32 devices in a mesh: dp: 8 (over z, x), fsdp: 4 (over y, core).
Axes of the slice: x: 2, y: 2, z: 4, core: 2. Of those that a mesh axis runs over, the one named last changes fastest.
Arguments:
- tokens: bfloat16 [5120, 768], P(('dp', 'fsdp')), may hold values from -6 to 6
- image_tokens: bfloat16 [128, 256, 768], P(('dp', 'fsdp')), may hold values from -6 to 6
- caption_lengths: int32 [32, 4], P(('dp', 'fsdp')), may hold values from 1 to 64, 160 in all within a row
- arrival_order: int32 [32, 160], P(('dp', 'fsdp')), may hold values from 0 to 159, each once within a row
- w_qkv: bfloat16 [1769472], P(('dp', 'fsdp')), may hold values from -0.21875 to 0.21875
- w_out: bfloat16 [589824], P(('dp', 'fsdp')), may hold values from -0.4375 to 0.4375
- w_cross_q: bfloat16 [589824], P(('dp', 'fsdp')), may hold values from -0.21875 to 0.21875
- w_cross_kv: bfloat16 [1179648], P(('dp', 'fsdp')), may hold values from -0.21875 to 0.21875
- w_cross_out: bfloat16 [589824], P(('dp', 'fsdp')), may hold values from -0.875 to 0.875
- w_up: bfloat16 [2359296], P(('dp', 'fsdp')), may hold values from -0.21875 to 0.21875
- w_down: bfloat16 [2359296], P(('dp', 'fsdp')), may hold values from -0.109375 to 0.109375
- small_params: bfloat16 [8448], P(('dp', 'fsdp')), may hold values from -0.5 to 1.5
- cotangent: bfloat16 [5120, 768], P(('dp', 'fsdp')), may hold values from -6 to 6
Outputs:
- layer_out: bfloat16 [5120, 768], P(('dp', 'fsdp'))
- grad_tokens: bfloat16 [5120, 768], P(('dp', 'fsdp'))
- grad_image: bfloat16 [128, 256, 768], P(('dp', 'fsdp'))
- grad_qkv: float32 [1769472], P(('dp', 'fsdp'))
- grad_out: float32 [589824], P(('dp', 'fsdp'))
- grad_cross_q: float32 [589824], P(('dp', 'fsdp'))
- grad_cross_kv: float32 [1179648], P(('dp', 'fsdp'))
- grad_cross_out: float32 [589824], P(('dp', 'fsdp'))
- grad_up: float32 [2359296], P(('dp', 'fsdp'))
- grad_down: float32 [2359296], P(('dp', 'fsdp'))
- grad_small: float32 [8448], P(('dp', 'fsdp'))
The draws below stay inside these ranges and needn't reach their ends.
All inputs are finite; a program needn't handle non-finite values.
Results may differ from the reference program's by a relative error of at most 0.018.
Values may be sent and summed in bfloat16 or wider, within the bound.
No kernel may reach another device: no remote copies, remote signals or barrier semaphores. Data moves between devices by JAX's collectives and lax.ppermute only.
A program may use at most 128 MiB of HBM per device.

```python
import math
import jax
import jax.numpy as jnp
import numpy as np
from jax import lax

D = 768
HEAD_DIM = 64
FF = 3072
V = 768
IMG = 256
CAP_LEN = 64
CAP_DEV = 4
ROW_DEV = 160
TOKENS = 5120
CAPTIONS = 128
N_FSDP = 4
DEVICES = 32


def draw_small_params(key, part):
    key = jax.random.fold_in(key, 11)
    gain_key, shift_key, bias_key = jax.random.split(key, 3)
    norm_gains = jax.random.uniform(gain_key, (3 * D,), jnp.float32, 0.5, 1.5)
    shifts = jax.random.uniform(shift_key, (3 * D,), jnp.float32, -0.5, 0.5)
    biases = jax.random.uniform(bias_key, (FF + D,), jnp.float32, -0.5, 0.5)
    return jnp.concatenate([norm_gains, shifts, biases]).astype(jnp.bfloat16)


def level_of(key, shape, cuts, least, high):
    level, own = 1.0, jax.random.fold_in(key, 6)
    for position, blocks in cuts:
        steps = jnp.exp(jax.random.uniform(jax.random.fold_in(own, position), (blocks,), jnp.float32, least / len(cuts), high / len(cuts)))
        level = level * jnp.repeat(steps, shape[position] // blocks).reshape([-1 if axis == position else 1 for axis in range(len(shape))])
    return level


def length_profile(number_of, total, reach, skew):
    portions = [(1 << 20) // math.isqrt(rank ** skew) + 1 for rank in range(2, number_of + 1)]
    spare, given = total - reach - (number_of - 1), [1] * (number_of - 1)
    while spare > 0:
        free = [i for i in range(number_of - 1) if given[i] < reach]
        pool, remaining = sum([portions[i] for i in free]), spare
        for i in free:
            extra = min(reach - given[i], max(1, remaining * portions[i] // pool), spare)
            given[i] = given[i] + extra
            spare = spare - extra
    return np.array([reach] + given)


def uneven_parts(own_key, count, total, most, slope):
    if count == 2:
        one = jax.random.randint(own_key, (), max(1, total - most), min(most, total - 1) + 1)
        return jnp.stack([one, total - one])
    sizes = jnp.asarray(length_profile(count, total, most, slope), jnp.int32)
    twos = (count - 1) // 2
    donor, sink = sizes[1:1 + 2 * twos:2], sizes[2:2 + 2 * twos:2]
    slack = jnp.minimum(donor - 1, most - sink)
    moved = jax.random.randint(jax.random.fold_in(own_key, 1), (twos,), 0, 1 << 20) % (slack + 1)
    sizes = sizes.at[1:1 + 2 * twos:2].set(donor - moved).at[2:2 + 2 * twos:2].set(sink + moved)
    return sizes[jax.random.permutation(jax.random.fold_in(own_key, 2), count)]


def gaussian(key, extent, width, most, cuts=(), kind=jnp.bfloat16):
    drawn = jax.random.normal(key, extent, jnp.float32) * width
    if len(cuts) > 0:
        drawn = level_of(key, extent, cuts, -0.22, 0.18) * drawn
    return jnp.clip(drawn, min=-most, max=most).astype(kind)


def setup_inputs(seed: int = 0) -> dict:
    streams_of = jax.random.split(jax.random.key(seed), 14)
    tokens = gaussian(streams_of[0], (TOKENS, D), 1.0, 6.0, ((0, 32),))
    image_tokens = gaussian(streams_of[1], (CAPTIONS, IMG, V), 1.0, 6.0, ((0, 32),))
    caption_lengths = jax.vmap(lambda own: uneven_parts(own, CAP_DEV, ROW_DEV, CAP_LEN, 1))(jax.random.split(streams_of[2], DEVICES)).reshape((DEVICES, CAP_DEV)).astype(jnp.int32)
    arrival_order = jax.vmap(lambda own: jax.random.permutation(own, ROW_DEV))(jax.random.split(streams_of[3], DEVICES)).reshape((DEVICES, ROW_DEV)).astype(jnp.int32)
    w_qkv = gaussian(streams_of[4], (3 * D * D,), D ** -0.5, 0.21875, ((0, 32),))
    w_out = gaussian(streams_of[5], (D * D,), (D // 4) ** -0.5, 0.4375, ((0, 32),))
    w_cross_q = gaussian(streams_of[6], (D * D,), D ** -0.5, 0.21875, ((0, 32),))
    w_cross_kv = gaussian(streams_of[7], (2 * V * D,), V ** -0.5, 0.21875, ((0, 32),))
    w_cross_out = gaussian(streams_of[8], (D * D,), (D // 16) ** -0.5, 0.875, ((0, 32),))
    w_up = gaussian(streams_of[9], (D * FF,), D ** -0.5, 0.21875, ((0, 32),))
    w_down = gaussian(streams_of[10], (FF * D,), FF ** -0.5, 0.109375, ((0, 32),))
    small_params = draw_small_params(jax.random.fold_in(streams_of[13], 71), 0)
    cotangent = gaussian(streams_of[12], (TOKENS, D), 1.0, 6.0, ((0, 32),))
    return dict(tokens=tokens, image_tokens=image_tokens, caption_lengths=caption_lengths, arrival_order=arrival_order, w_qkv=w_qkv, w_out=w_out, w_cross_q=w_cross_q, w_cross_kv=w_cross_kv, w_cross_out=w_cross_out, w_up=w_up, w_down=w_down, small_params=small_params, cotangent=cotangent)


epsilon = 1e-05
masked_fill = 1e+30

@jax.custom_vjp
def low(v):
    return lax.optimization_barrier(v.astype(jnp.bfloat16)).astype(jnp.float32)

@jax.custom_vjp
def low_back(v):
    return v

def low_keep(v):
    return (low(v), None)

def low_pass(kept, grad):
    return (grad,)

def back_keep(v):
    return (v, None)

def back_low(kept, grad):
    return (low(grad),)
low.defvjp(low_keep, low_pass)
low_back.defvjp(back_keep, back_low)

def low_both(inputs):
    return low(low_back(inputs))

def matmul(left, right):
    return jnp.dot(left, right, precision=lax.Precision.HIGHEST)

def norm_rows(inputs, gain_vec, shift_vec):
    centred = inputs - lax.optimization_barrier(jnp.mean(inputs, axis=-1, keepdims=True))
    variance = lax.optimization_barrier(jnp.mean(centred * centred, axis=-1, keepdims=True))
    return centred * lax.rsqrt(variance + epsilon) * gain_vec + shift_vec

def softmax_rows(scores):
    shifted = jnp.exp(scores - lax.optimization_barrier(jnp.max(scores, axis=-1, keepdims=True)))
    return shifted / lax.optimization_barrier(jnp.sum(shifted, axis=-1, keepdims=True))

def attention(queries, keys_in, values, allowed):
    scores = low_back(HEAD_DIM ** (-0.5) * jnp.einsum('cqhd,ckhd->chqk', queries, keys_in, precision=lax.Precision.HIGHEST))
    scores = jnp.where(allowed, scores, -masked_fill)
    attn_weights = low(softmax_rows(scores))
    return low_both(jnp.einsum('chqk,ckhd->cqhd', attn_weights, values, precision=lax.Precision.HIGHEST))

def unpack_params(flat_params):
    flat_qkv, flat_out, flat_cross_q, flat_cross_kv, flat_cross_out, flat_up, flat_down, flat_small = flat_params
    return (flat_qkv.reshape(D, 3 * D), flat_out.reshape(D, D), flat_cross_q.reshape(D, D), flat_cross_kv.reshape(V, 2 * D), flat_cross_out.reshape(D, D), flat_up.reshape(D, FF), flat_down.reshape(FF, D), flat_small[:3 * D].reshape(3, D), flat_small[3 * D:6 * D].reshape(3, D), flat_small[6 * D:6 * D + FF], flat_small[6 * D + FF:])

def caption_block(slotted, image_rows, lengths, params):
    mat_qkv, mat_out, mat_cross_q, mat_cross_kv, mat_cross_out, mat_up, mat_down, norm_gains, shifts, up_bias, down_bias = params
    captions = slotted.shape[0]
    head_count = D // HEAD_DIM
    positions = jnp.arange(CAP_LEN, dtype=jnp.int32)
    allowed = (positions[None, :] <= positions[:, None])[None, None] & (positions[None, None, None, :] < lengths[:, None, None, None])
    open_mask = jnp.ones((1, 1, 1, 1), jnp.bool_)
    normed_self = low(norm_rows(slotted, norm_gains[0], shifts[0]))
    projected = low_both(matmul(normed_self, mat_qkv)).reshape(captions, CAP_LEN, 3, head_count, HEAD_DIM)
    self_mixed = attention(projected[:, :, 0], projected[:, :, 1], projected[:, :, 2], allowed).reshape(captions, CAP_LEN, D)
    after_self = slotted + low_back(matmul(self_mixed, mat_out))
    normed_cross = low(norm_rows(after_self, norm_gains[1], shifts[1]))
    cross_query = low_both(matmul(normed_cross, mat_cross_q)).reshape(captions, CAP_LEN, head_count, HEAD_DIM)
    image_kv = low_both(matmul(image_rows, mat_cross_kv)).reshape(captions, IMG, 2, head_count, HEAD_DIM)
    cross_mixed = attention(cross_query, image_kv[:, :, 0], image_kv[:, :, 1], open_mask).reshape(captions, CAP_LEN, D)
    after_cross = after_self + low_back(matmul(cross_mixed, mat_cross_out))
    normed_mlp = low(norm_rows(after_cross, norm_gains[2], shifts[2]))
    hidden = low_back(matmul(normed_mlp, mat_up) + up_bias)
    activated = low(jax.nn.gelu(hidden, approximate=False))
    return after_cross + low_back(matmul(activated, mat_down) + down_bias)

def reference(tokens, image_tokens, caption_lengths, arrival_order, w_qkv, w_out, w_cross_q, w_cross_kv, w_cross_out, w_up, w_down, small_params, cotangent):
    device_count = caption_lengths.shape[0]
    per_peer = ROW_DEV // N_FSDP
    run_ends = jnp.cumsum(caption_lengths, axis=1).astype(jnp.int32)
    starts = run_ends - caption_lengths
    caption = lax.optimization_barrier(jnp.sum((run_ends[:, None, :] <= arrival_order[:, :, None]).astype(jnp.int32), axis=2))
    first_row = jnp.take_along_axis(starts, caption, axis=1).astype(jnp.int32)
    device = jnp.arange(device_count, dtype=jnp.int32)[:, None]
    arrival = jnp.arange(ROW_DEV, dtype=jnp.int32)[None, :]
    source = ((device // N_FSDP * N_FSDP + arrival // per_peer) * ROW_DEV + device % N_FSDP * per_peer + arrival % per_peer).reshape(-1)
    target = (device * (CAP_DEV * CAP_LEN) + caption * CAP_LEN + arrival_order - first_row).reshape(-1)

    def whole_layer(token_rows, image_all, *flat_params):
        params = unpack_params(flat_params)
        slotted = jnp.zeros((CAPTIONS * CAP_LEN, D), jnp.float32).at[target].set(token_rows[source])
        slotted = slotted.reshape(device_count, CAP_DEV, CAP_LEN, D)
        images = image_all.reshape(device_count, CAP_DEV, IMG, V)

        def per_device(pieces):
            return caption_block(pieces[0], pieces[1], pieces[2], params)
        result = lax.map(jax.checkpoint(per_device), (slotted, images, caption_lengths))
        result = result.reshape(CAPTIONS * CAP_LEN, D)
        return jnp.zeros((TOKENS, D), jnp.float32).at[source].set(result[target])
    inputs = tuple((array_in.astype(jnp.float32) for array_in in (tokens, image_tokens, w_qkv, w_out, w_cross_q, w_cross_kv, w_cross_out, w_up, w_down, small_params)))
    result, pullback = jax.vjp(whole_layer, *inputs)
    gradients = pullback(cotangent.astype(jnp.float32))
    return (result.astype(jnp.bfloat16), gradients[0].astype(jnp.bfloat16), gradients[1].astype(jnp.bfloat16), gradients[2], gradients[3], gradients[4], gradients[5], gradients[6], gradients[7], gradients[8], gradients[9])
```

```python
import functools

import jax
import jax.numpy as jnp
from jax import lax
from jax.experimental import pallas as pl
from jax.experimental.pallas import tpu as pltpu
from jax.sharding import Mesh
from jax.sharding import PartitionSpec as P

D = 768
HEAD_DIM = 64
FF = 3072
IMG = 256
CAP_LEN = 64
LANES = 128
PAIRS = D // LANES
FOLD = FF // D
SCALE = HEAD_DIM ** (-0.5)
epsilon = 1e-05
masked_fill = 1e30

BF = jnp.bfloat16
F32 = jnp.float32
AXES = ("z", "x", "y", "c")
COLS = {}
_at = 0
for _name, _width in (
    ("qkv", 3 * D),
    ("out", D),
    ("cross_q", D),
    ("cross_kv", 2 * D),
    ("cross_out", D),
    ("up", FF),
    ("down", FF),
):
    COLS[_name] = (_at, _width)
    _at += _width
TOTAL_COLS = _at


def mm(a, b):
    return lax.dot_general(a, b, (((1,), (0,)), ((), ())), preferred_element_type=F32)


def mm_t(a, b):
    return lax.dot_general(a, b, (((1,), (1,)), ((), ())), preferred_element_type=F32)


def t_mm(a, b):
    return lax.dot_general(a, b, (((0,), (0,)), ((), ())), preferred_element_type=F32)


def norm_rows(inputs, gain_vec, shift_vec):
    centred = inputs - jnp.mean(inputs, axis=-1, keepdims=True)
    variance = jnp.mean(centred * centred, axis=-1, keepdims=True)
    return centred * lax.rsqrt(variance + epsilon) * gain_vec + shift_vec


def norm_back(inputs, gain_vec, grad_normed):
    centred = inputs - jnp.mean(inputs, axis=-1, keepdims=True)
    variance = jnp.mean(centred * centred, axis=-1, keepdims=True)
    scale = lax.rsqrt(variance + epsilon)
    unit = centred * scale
    weighted = grad_normed * gain_vec
    grad_in = scale * (
        weighted
        - jnp.mean(weighted, axis=-1, keepdims=True)
        - unit * jnp.mean(weighted * unit, axis=-1, keepdims=True)
    )
    grad_gain = jnp.sum(grad_normed * unit, axis=0, keepdims=True)
    grad_shift = jnp.sum(grad_normed, axis=0, keepdims=True)
    return grad_in, grad_gain, grad_shift


def arrival_pick(arr_ref):
    rows = arr_ref.shape[1]
    place = lax.broadcasted_iota(jnp.int32, (rows, rows), 0)
    return jnp.where(place == arr_ref[...], 1.0, 0.0).astype(BF)


def caption_of(index, lens_ref):
    end = jnp.int32(0)
    found = jnp.zeros_like(index)
    for c in range(lens_ref.shape[1] - 1):
        end = end + lens_ref[0, c]
        found = found + jnp.where(index >= end, 1, 0)
    return found


def slot_pick(lens_ref, rows):
    captions = lens_ref.shape[1]
    shape = (captions * CAP_LEN, rows)
    slot = lax.broadcasted_iota(jnp.int32, shape, 0)
    row = lax.broadcasted_iota(jnp.int32, shape, 1)
    start = jnp.int32(0)
    hit = jnp.zeros(shape, F32)
    for c in range(captions):
        length = lens_ref[0, c]
        inside = slot - c * CAP_LEN
        ok = (inside >= 0) & (inside < length) & (row - start == inside)
        hit = hit + jnp.where(ok, 1.0, 0.0)
        start = start + length
    return hit.astype(BF)


def pair_mask(rows):
    shape = (2 * rows, LANES)
    top = lax.broadcasted_iota(jnp.int32, shape, 0) < rows
    left = lax.broadcasted_iota(jnp.int32, shape, 1) < HEAD_DIM
    return jnp.where(top == left, 1.0, 0.0).astype(BF)


def stack_pair(block, mask):
    return jnp.concatenate([block, block], axis=0) * mask


def merge_pair(stacked):
    rows = stacked.shape[0] // 2
    left = lax.broadcasted_iota(jnp.int32, (rows, LANES), 1) < HEAD_DIM
    return jnp.where(left, stacked[:rows], stacked[rows:])


def softmax_rows(scores):
    shifted = jnp.exp(scores - jnp.max(scores, axis=-1, keepdims=True))
    return shifted / jnp.sum(shifted, axis=-1, keepdims=True)


def load_cols(weights_ref, name, target, sem):
    at, width = COLS[name]
    copy = pltpu.make_async_copy(weights_ref.at[:, pl.ds(at, width)], target, sem)
    copy.start()
    return copy


def place_kernel(arr, tok, cot, table, slotted, normed, grad_slot):
    pick = arrival_pick(arr)
    rows = mm(pick, tok[...])
    slotted[...] = rows.astype(BF)
    normed[...] = norm_rows(rows, table[0:1, :], table[3:4, :]).astype(BF)
    grad_slot[...] = mm(pick, cot[...]).astype(BF)


def kv_kernel(img, weights, kv, w_kv, sem):
    copy = load_cols(weights, "cross_kv", w_kv, sem.at[0])
    copy.wait()
    for c in range(img.shape[0] // IMG):
        rows = pl.ds(c * IMG, IMG)
        kv[rows, :] = mm(img[rows, :], w_kv[...]).astype(BF)


def self_kernel(
    lens, slotted, normed, table, weights,
    projected, probs, mixed, after_self, normed_cross, query_slots,
    w_qkv, w_out, w_cq, sem,
):
    copies = [
        load_cols(weights, "qkv", w_qkv, sem.at[0]),
        load_cols(weights, "out", w_out, sem.at[1]),
        load_cols(weights, "cross_q", w_cq, sem.at[2]),
    ]
    rows = slotted.shape[0]
    copies[0].wait()
    projected[...] = mm(normed[...], w_qkv[...]).astype(BF)
    place = lax.broadcasted_iota(jnp.int32, (2 * rows, rows), 0)
    query_at = jnp.where(place >= rows, place - rows, place)
    key_at = lax.broadcasted_iota(jnp.int32, (2 * rows, rows), 1)
    allowed = (caption_of(query_at, lens) == caption_of(key_at, lens)) & (key_at <= query_at)
    mask = pair_mask(rows)
    for p in range(PAIRS):
        cols = slice(p * LANES, (p + 1) * LANES)
        query = stack_pair(projected[:, cols], mask)
        key = projected[:, D + p * LANES : D + (p + 1) * LANES]
        value = projected[:, 2 * D + p * LANES : 2 * D + (p + 1) * LANES]
        scores = jnp.where(allowed, mm_t(query, key) * SCALE, -masked_fill)
        weights_low = softmax_rows(scores).astype(BF)
        probs[p] = weights_low
        mixed[:, cols] = merge_pair(mm(weights_low, value)).astype(BF)
    copies[1].wait()
    state = slotted[...].astype(F32) + mm(mixed[...], w_out[...])
    after_self[...] = state
    low = norm_rows(state, table[1:2, :], table[4:5, :]).astype(BF)
    normed_cross[...] = low
    copies[2].wait()
    query = mm(low, w_cq[...]).astype(BF)
    query_slots[...] = mm(slot_pick(lens, rows), query).astype(BF)


def cross_kernel(
    lens, query_slots, kv, after_self, table, weights,
    probs, mixed, after_cross, normed_mlp,
    w_co, mixed_slots, sem,
):
    copy = load_cols(weights, "cross_out", w_co, sem.at[0])
    rows = after_self.shape[0]
    mask = pair_mask(CAP_LEN)
    for c in range(lens.shape[1]):
        slots = slice(c * CAP_LEN, (c + 1) * CAP_LEN)
        images = slice(c * IMG, (c + 1) * IMG)
        for p in range(PAIRS):
            cols = slice(p * LANES, (p + 1) * LANES)
            query = stack_pair(query_slots[slots, cols], mask)
            scores = mm_t(query, kv[images, cols]) * SCALE
            weights_low = softmax_rows(scores).astype(BF)
            probs[c * PAIRS + p] = weights_low
            value = kv[images, D + p * LANES : D + (p + 1) * LANES]
            mixed_slots[slots, cols] = merge_pair(mm(weights_low, value)).astype(BF)
    low = t_mm(slot_pick(lens, rows), mixed_slots[...]).astype(BF)
    mixed[...] = low
    copy.wait()
    state = after_self[...] + mm(low, w_co[...])
    after_cross[...] = state
    normed_mlp[...] = norm_rows(state, table[2:3, :], table[5:6, :]).astype(BF)


def mlp_kernel(
    arr, after_cross, normed_mlp, grad_slot, table, weights,
    active, grad_hidden, layer_rows, grad_after, small,
    w_up, w_down, sem,
):
    copies = []
    for j in range(FOLD):
        for k, (name, target) in enumerate((("up", w_up), ("down", w_down))):
            at = COLS[name][0] + j * D
            copy = pltpu.make_async_copy(
                weights.at[:, pl.ds(at, D)], target.at[j], sem.at[2 * j + k]
            )
            copy.start()
            copies.append(copy)
    low = normed_mlp[...]
    grad_low = grad_slot[...]
    result = after_cross[...] + table[10:11, :]
    grad_normed = jnp.zeros(result.shape, F32)
    for j in range(FOLD):
        cols = slice(j * D, (j + 1) * D)
        copies[2 * j].wait()
        hidden = mm(low, w_up[j]) + table[6 + j : 7 + j, :]
        half = 0.5 + 0.5 * lax.erf(hidden * (0.5**0.5))
        act = (hidden * half).astype(BF)
        active[:, cols] = act
        slope = half + hidden * (jnp.exp(hidden * hidden * -0.5) * 0.3989422804014327)
        copies[2 * j + 1].wait()
        result = result + mm(act, w_down[j])
        grad_hid = (mm_t(grad_low, w_down[j]) * slope).astype(BF)
        grad_hidden[:, cols] = grad_hid
        small[2 + j : 3 + j, :] = jnp.sum(grad_hid.astype(F32), axis=0, keepdims=True)
        grad_normed = grad_normed + mm_t(grad_hid, w_up[j])
    layer_rows[...] = t_mm(arrival_pick(arr), result.astype(BF)).astype(BF)
    grad_full = grad_low.astype(F32)
    grad_in, grad_gain, grad_shift = norm_back(after_cross[...], table[2:3, :], grad_normed)
    grad_after[...] = grad_full + grad_in
    small[0:1, :] = grad_gain
    small[1:2, :] = grad_shift
    small[6:7, :] = jnp.sum(grad_full, axis=0, keepdims=True)
    small[7:8, :] = jnp.zeros_like(grad_gain)


def cross_back_kernel(
    lens, grad_after, probs, query_slots, kv, after_self, table, weights,
    grad_branch, grad_query, grad_kv, grad_state, small,
    w_co, w_cq, mixed_slots, query_grad_slots, sem,
):
    copies = [
        load_cols(weights, "cross_out", w_co, sem.at[0]),
        load_cols(weights, "cross_q", w_cq, sem.at[1]),
    ]
    rows = after_self.shape[0]
    branch = grad_after[...].astype(BF)
    grad_branch[...] = branch
    pick = slot_pick(lens, rows)
    copies[0].wait()
    mixed_slots[...] = mm(pick, mm_t(branch, w_co[...]).astype(BF)).astype(BF)
    mask = pair_mask(CAP_LEN)
    for c in range(lens.shape[1]):
        slots = slice(c * CAP_LEN, (c + 1) * CAP_LEN)
        images = slice(c * IMG, (c + 1) * IMG)
        for p in range(PAIRS):
            cols = slice(p * LANES, (p + 1) * LANES)
            value_cols = slice(D + p * LANES, D + (p + 1) * LANES)
            grad_mixed = stack_pair(mixed_slots[slots, cols], mask)
            query = stack_pair(query_slots[slots, cols], mask)
            weights_low = probs[c * PAIRS + p]
            attn = weights_low.astype(F32)
            grad_weights = mm_t(grad_mixed, kv[images, value_cols])
            centre = jnp.sum(attn * grad_weights, axis=-1, keepdims=True)
            grad_scores = (attn * (grad_weights - centre)).astype(BF)
            query_grad_slots[slots, cols] = (
                merge_pair(mm(grad_scores, kv[images, cols])) * SCALE
            ).astype(BF)
            grad_kv[images, cols] = (t_mm(grad_scores, query) * SCALE).astype(BF)
            grad_kv[images, value_cols] = t_mm(weights_low, grad_mixed).astype(BF)
    query_low = t_mm(pick, query_grad_slots[...]).astype(BF)
    grad_query[...] = query_low
    copies[1].wait()
    grad_in, grad_gain, grad_shift = norm_back(
        after_self[...], table[1:2, :], mm_t(query_low, w_cq[...])
    )
    grad_state[...] = grad_after[...] + grad_in
    small[0:1, :] = grad_gain
    small[1:2, :] = grad_shift
    small[2:8, :] = jnp.zeros((6, D), F32)


def self_back_kernel(
    arr, grad_state, probs, projected, slotted, table, weights,
    grad_branch, grad_projected, token_rows, small,
    w_out, w_qkv, mixed, sem,
):
    copies = [
        load_cols(weights, "out", w_out, sem.at[0]),
        load_cols(weights, "qkv", w_qkv, sem.at[1]),
    ]
    rows = slotted.shape[0]
    branch = grad_state[...].astype(BF)
    grad_branch[...] = branch
    copies[0].wait()
    mixed[...] = mm_t(branch, w_out[...]).astype(BF)
    mask = pair_mask(rows)
    for p in range(PAIRS):
        cols = slice(p * LANES, (p + 1) * LANES)
        key_cols = slice(D + p * LANES, D + (p + 1) * LANES)
        value_cols = slice(2 * D + p * LANES, 2 * D + (p + 1) * LANES)
        grad_mixed = stack_pair(mixed[:, cols], mask)
        query = stack_pair(projected[:, cols], mask)
        weights_low = probs[p]
        attn = weights_low.astype(F32)
        grad_weights = mm_t(grad_mixed, projected[:, value_cols])
        centre = jnp.sum(attn * grad_weights, axis=-1, keepdims=True)
        grad_scores = (attn * (grad_weights - centre)).astype(BF)
        grad_projected[:, cols] = (
            merge_pair(mm(grad_scores, projected[:, key_cols])) * SCALE
        ).astype(BF)
        grad_projected[:, key_cols] = (t_mm(grad_scores, query) * SCALE).astype(BF)
        grad_projected[:, value_cols] = t_mm(weights_low, grad_mixed).astype(BF)
    copies[1].wait()
    grad_in, grad_gain, grad_shift = norm_back(
        slotted[...].astype(F32), table[0:1, :], mm_t(grad_projected[...], w_qkv[...])
    )
    grad_slotted = (grad_state[...] + grad_in).astype(BF)
    token_rows[...] = t_mm(arrival_pick(arr), grad_slotted).astype(BF)
    small[0:1, :] = grad_gain
    small[1:2, :] = grad_shift
    small[2:8, :] = jnp.zeros((6, D), F32)


def put_blocks(grads, me, keep, send, at, first):
    _, _, nz, height, _ = keep.shape
    width = grads.shape[1]
    own_x, own_y, own_c = me[0, 1], me[0, 2], me[0, 3]
    for z in range(nz):
        for x in range(2):
            for y in range(2):
                low = (((z * 2 + x) * 2 + y) * 2) * height
                even = grads[low : low + height, :]
                odd = grads[low + height : low + 2 * height, :]
                far_x, far_y = lax.bitwise_xor(own_x, x), lax.bitwise_xor(own_y, y)
                i, j = (far_x, far_y) if first == "x" else (far_y, far_x)
                keep[i, j, z, :, at : at + width] = jnp.where(own_c == 0, even, odd).astype(BF)
                send[i, j, z, :, at : at + width] = jnp.where(own_c == 0, odd, even).astype(BF)


def weight_grad_kernel(first, pieces, me, *refs):
    keep, send = refs[-2:]
    for left, left_at, right, right_at, width, at in pieces:
        for lo in range(0, width, D):
            grads = t_mm(
                refs[left][:, left_at : left_at + D],
                refs[right][:, right_at + lo : right_at + lo + D],
            )
            put_blocks(grads, me, keep, send, at + lo, first)


def image_grad_kernel(grad_kv, weights, grad_image, w_kv, sem):
    copy = load_cols(weights, "cross_kv", w_kv, sem.at[0])
    copy.wait()
    for c in range(grad_kv.shape[0] // IMG):
        rows = pl.ds(c * IMG, IMG)
        grad_image[rows, :] = mm_t(grad_kv[rows, :], w_kv[...]).astype(BF)


VM = pl.BlockSpec(memory_space=pltpu.VMEM)
SM = pl.BlockSpec(memory_space=pltpu.SMEM)
HB = pl.BlockSpec(memory_space=pl.ANY)


def run(kernel, outs, specs, scratch, flops, *args, mib=44):
    shapes = [jax.ShapeDtypeStruct(s, t) for s, t in outs]
    moved = sum(a.size * a.dtype.itemsize for a in args) + sum(
        s.size * s.dtype.itemsize for s in shapes
    )
    return pl.pallas_call(
        kernel,
        out_shape=shapes,
        in_specs=specs,
        out_specs=[VM] * len(shapes),
        scratch_shapes=scratch,
        compiler_params=pltpu.CompilerParams(vmem_limit_bytes=mib * 2**20),
        cost_estimate=pl.CostEstimate(flops=flops, bytes_accessed=moved, transcendentals=0),
    )(*args)


def flip(value, axis):
    return lax.ppermute(value, axis, [(0, 1), (1, 0)])


def swap_all(value, axes):
    return lax.all_to_all(value, axes, split_axis=0, concat_axis=0, tiled=True)


def reduce_unit(keep, send, first, second):
    far = flip(send, "c").astype(F32)
    near = keep.astype(F32)
    one = flip((near[1] + far[1]).astype(BF), first).astype(F32)
    two = flip((near[0, 1] + far[0, 1] + one[1]).astype(BF), second).astype(F32)
    part = (near[0, 0] + far[0, 0] + one[0] + two).astype(BF)
    return jnp.sum(swap_all(part, "z").astype(F32), axis=0)


def on_device(
    tokens,
    image_tokens,
    caption_lengths,
    arrival_order,
    w_qkv,
    w_out,
    w_cross_q,
    w_cross_kv,
    w_cross_out,
    w_up,
    w_down,
    small_params,
    cotangent,
):
    sizes = [lax.axis_size(a) for a in AXES]
    devices = sizes[0] * sizes[1] * sizes[2] * sizes[3]
    height = D // devices
    rows = tokens.shape[0]
    captions = caption_lengths.shape[1]
    slots = captions * CAP_LEN
    images = captions * IMG
    me = jnp.stack([lax.axis_index(a) for a in AXES]).astype(jnp.int32).reshape(1, 4)

    own = jnp.concatenate(
        [
            w_qkv.reshape(height, -1),
            w_out.reshape(height, -1),
            w_cross_q.reshape(height, -1),
            w_cross_kv.reshape(height, -1),
            w_cross_out.reshape(height, -1),
            w_up.reshape(height, D, FOLD).swapaxes(1, 2).reshape(height, FF),
            w_down.reshape(height, FF),
        ],
        axis=1,
    )
    weights = lax.all_gather(own, AXES, axis=0, tiled=True)

    tok = swap_all(tokens, ("y", "c"))
    cot = swap_all(cotangent, ("y", "c"))
    flat = swap_all(
        jnp.broadcast_to(small_params[None, None], (devices, 1, small_params.shape[0])), AXES
    )
    table = flat.reshape(-1, D).astype(F32)
    table = jnp.concatenate(
        [table[:6], table[6 : 6 + FOLD].reshape(D, FOLD).T, table[6 + FOLD :]], axis=0
    )
    img = image_tokens.reshape(images, D)

    slotted, normed_self, grad_slot = run(
        place_kernel,
        [((rows, D), BF)] * 3,
        [VM] * 4,
        [],
        4 * rows * rows * D,
        arrival_order, tok, cot, table,
    )
    sems = lambda n: pltpu.SemaphoreType.DMA((n,))
    vmem = pltpu.VMEM
    (kv,) = run(
        kv_kernel,
        [((images, 2 * D), BF)],
        [VM, HB],
        [vmem((D, 2 * D), BF), sems(1)],
        4 * images * D * D,
        img, weights,
    )
    projected, self_probs, self_mixed, after_self, normed_cross, query_slots = run(
        self_kernel,
        [
            ((rows, 3 * D), BF),
            ((PAIRS, 2 * rows, rows), BF),
            ((rows, D), BF),
            ((rows, D), F32),
            ((rows, D), BF),
            ((slots, D), BF),
        ],
        [SM, VM, VM, VM, HB],
        [vmem((D, 3 * D), BF), vmem((D, D), BF), vmem((D, D), BF), sems(3)],
        10 * rows * D * D,
        caption_lengths, slotted, normed_self, table, weights,
    )
    cross_probs, cross_mixed, after_cross, normed_mlp = run(
        cross_kernel,
        [
            ((captions * PAIRS, 2 * CAP_LEN, IMG), BF),
            ((rows, D), BF),
            ((rows, D), F32),
            ((rows, D), BF),
        ],
        [SM, VM, VM, VM, VM, HB],
        [vmem((D, D), BF), vmem((slots, D), BF), sems(1)],
        10 * rows * D * D,
        caption_lengths, query_slots, kv, after_self, table, weights,
    )
    active, grad_hidden, layer_rows, grad_after, small_mlp = run(
        mlp_kernel,
        [
            ((rows, FF), BF),
            ((rows, FF), BF),
            ((rows, D), BF),
            ((rows, D), F32),
            ((8, D), F32),
        ],
        [VM, VM, VM, VM, VM, HB],
        [vmem((FOLD, D, D), BF), vmem((FOLD, D, D), BF), sems(2 * FOLD)],
        8 * rows * D * FF,
        arrival_order, after_cross, normed_mlp, grad_slot, table, weights,
    )

    def weight_grads(first, pieces, *args):
        shape = (2, 2, sizes[0], height, FF)
        return run(
            functools.partial(weight_grad_kernel, first, pieces),
            [(shape, BF)] * 2,
            [SM] + [VM] * len(args),
            [],
            2 * rows * D * FF,
            me, *args,
        )

    def owned_sum(first, pieces, *args):
        second = "x" if first == "y" else "y"
        if height % 8 == 0 and sizes[1] == 2 and sizes[2] == 2:
            return reduce_unit(*weight_grads(first, pieces, *args), first, second)
        whole = jnp.concatenate(
            [
                t_mm(args[a][:, a0 : a0 + D], args[b][:, b0 : b0 + width])
                for a, a0, b, b0, width, _ in pieces
            ],
            axis=1,
        )
        parts = whole.astype(BF).reshape(devices, height, FF)
        return jnp.sum(swap_all(parts, AXES).astype(F32), axis=0)

    sum_down = owned_sum(
        "y", [(0, j * D, 1, 0, D, j * D) for j in range(FOLD)], active, grad_slot
    )
    sum_up = owned_sum("x", [(0, 0, 1, 0, FF, 0)], normed_mlp, grad_hidden)

    branch_cross, grad_query, grad_kv, grad_state, small_cross = run(
        cross_back_kernel,
        [
            ((rows, D), BF),
            ((rows, D), BF),
            ((images, 2 * D), BF),
            ((rows, D), F32),
            ((8, D), F32),
        ],
        [SM, VM, VM, VM, VM, VM, VM, HB],
        [
            vmem((D, D), BF),
            vmem((D, D), BF),
            vmem((slots, D), BF),
            vmem((slots, D), BF),
            sems(2),
        ],
        14 * rows * D * D,
        caption_lengths, grad_after, cross_probs, query_slots, kv, after_self, table, weights,
    )
    sum_cross = owned_sum(
        "y",
        [(0, 0, 1, 0, D, 0), (2, 0, 3, 0, 2 * D, D), (4, 0, 5, 0, D, 3 * D)],
        normed_cross, grad_query, img, grad_kv, cross_mixed, branch_cross,
    )
    branch_self, grad_projected, token_rows, small_self = run(
        self_back_kernel,
        [
            ((rows, D), BF),
            ((rows, 3 * D), BF),
            ((rows, D), BF),
            ((8, D), F32),
        ],
        [VM, VM, VM, VM, VM, VM, HB],
        [vmem((D, D), BF), vmem((D, 3 * D), BF), vmem((rows, D), BF), sems(2)],
        14 * rows * D * D,
        arrival_order, grad_state, self_probs, projected, slotted, table, weights,
    )
    sum_self = owned_sum(
        "x",
        [(0, 0, 1, 0, 3 * D, 0), (2, 0, 3, 0, D, 3 * D)],
        normed_self, grad_projected, self_mixed, branch_self,
    )
    (grad_image,) = run(
        image_grad_kernel,
        [((images, D), BF)],
        [VM, HB],
        [vmem((D, 2 * D), BF), sems(1)],
        4 * images * D * D,
        grad_kv, weights,
    )

    grad_small = jnp.concatenate(
        [
            small_self[0:1],
            small_cross[0:1],
            small_mlp[0:1],
            small_self[1:2],
            small_cross[1:2],
            small_mlp[1:2],
            small_mlp[2 : 2 + FOLD].T.reshape(FOLD, D),
            small_mlp[6:7],
        ],
        axis=0,
    )
    parts = grad_small.astype(BF).reshape(devices, 1, -1)
    sum_small = jnp.sum(swap_all(parts, AXES).astype(F32), axis=(0, 1))

    layer_out = swap_all(layer_rows, ("y", "c"))
    grad_tokens = swap_all(token_rows, ("y", "c"))
    return (
        layer_out,
        grad_tokens,
        grad_image.reshape(image_tokens.shape),
        sum_self[:, : 3 * D].reshape(-1),
        sum_self[:, 3 * D :].reshape(-1),
        sum_cross[:, :D].reshape(-1),
        sum_cross[:, D : 3 * D].reshape(-1),
        sum_cross[:, 3 * D :].reshape(-1),
        sum_up.reshape(height, FOLD, D).swapaxes(1, 2).reshape(-1),
        sum_down.reshape(-1),
        sum_small,
    )


def solution(mesh):
    dp, fsdp = mesh.shape["dp"], mesh.shape["fsdp"]
    split = Mesh(mesh.devices.reshape(dp // 2, 2, fsdp // 2, 2), AXES)
    rows, flat = P(AXES, None), P(AXES)
    cube = P(AXES, None, None)
    return jax.shard_map(
        on_device,
        mesh=split,
        in_specs=(rows, cube, rows, rows) + (flat,) * 8 + (rows,),
        out_specs=(rows, rows, cube) + (flat,) * 8,
        check_vma=False,
    )
```

```python
import functools

import jax
import jax.numpy as jnp
from jax import lax
from jax.experimental import pallas as pl
from jax.experimental.pallas import tpu as pltpu
from jax.sharding import Mesh
from jax.sharding import PartitionSpec as P

D = 768
HEAD_DIM = 64
FF = 3072
V = 768
IMG = 256
CAP_LEN = 64
LANES = 128
PAIRS = D // LANES
HALF = D // 2
HALF_PAIRS = PAIRS // 2
FOLD = FF // D
GROUP = FOLD * LANES
GROUPS = FF // GROUP
TOKENS_AT = 32
SCALE = HEAD_DIM ** (-0.5)
epsilon = 1e-05
masked_fill = 1e30

BF = jnp.bfloat16
F32 = jnp.float32
AXES = ("z", "x", "y", "c")


def mm(a, b):
    return lax.dot_general(a, b, (((1,), (0,)), ((), ())), preferred_element_type=F32)


def mm_t(a, b):
    return lax.dot_general(a, b, (((1,), (1,)), ((), ())), preferred_element_type=F32)


def t_mm(a, b):
    return lax.dot_general(a, b, (((0,), (0,)), ((), ())), preferred_element_type=F32)


def wide(value):
    return value.astype(F32)


def norm_rows(inputs, gain_vec, shift_vec):
    centred = inputs - jnp.mean(inputs, axis=-1, keepdims=True)
    variance = jnp.mean(centred * centred, axis=-1, keepdims=True)
    return centred * lax.rsqrt(variance + epsilon) * gain_vec + shift_vec


def norm_back(inputs, gain_vec, grad_normed):
    centred = inputs - jnp.mean(inputs, axis=-1, keepdims=True)
    variance = jnp.mean(centred * centred, axis=-1, keepdims=True)
    scale = lax.rsqrt(variance + epsilon)
    unit = centred * scale
    weighted = grad_normed * gain_vec
    grad_in = scale * (
        weighted
        - jnp.mean(weighted, axis=-1, keepdims=True)
        - unit * jnp.mean(weighted * unit, axis=-1, keepdims=True)
    )
    grad_gain = jnp.sum(grad_normed * unit, axis=0, keepdims=True)
    grad_shift = jnp.sum(grad_normed, axis=0, keepdims=True)
    return grad_in, grad_gain, grad_shift


def arrival_pick(arr_ref):
    rows = arr_ref.shape[1]
    place = lax.broadcasted_iota(jnp.int32, (rows, rows), 0)
    return jnp.where(place == arr_ref[...], 1.0, 0.0).astype(BF)


def caption_of(index, lens_ref):
    end = jnp.int32(0)
    found = jnp.zeros_like(index)
    for c in range(lens_ref.shape[1] - 1):
        end = end + lens_ref[0, c]
        found = found + jnp.where(index >= end, 1, 0)
    return found


def slot_pick(lens_ref, rows):
    captions = lens_ref.shape[1]
    shape = (captions * CAP_LEN, rows)
    slot = lax.broadcasted_iota(jnp.int32, shape, 0)
    row = lax.broadcasted_iota(jnp.int32, shape, 1)
    start = jnp.int32(0)
    hit = jnp.zeros(shape, F32)
    for c in range(captions):
        length = lens_ref[0, c]
        inside = slot - c * CAP_LEN
        ok = (inside >= 0) & (inside < length) & (row - start == inside)
        hit = hit + jnp.where(ok, 1.0, 0.0)
        start = start + length
    return hit.astype(BF)


def fold_pick(back):
    source = lax.broadcasted_iota(jnp.int32, (GROUP, GROUP), 1 if back else 0)
    target = lax.broadcasted_iota(jnp.int32, (GROUP, GROUP), 0 if back else 1)
    return jnp.where(target == (source % FOLD) * LANES + source // FOLD, 1.0, 0.0).astype(BF)


def pair_mask(rows):
    shape = (2 * rows, LANES)
    top = lax.broadcasted_iota(jnp.int32, shape, 0) < rows
    left = lax.broadcasted_iota(jnp.int32, shape, 1) < HEAD_DIM
    return jnp.where(top == left, 1.0, 0.0).astype(BF)


def stack_pair(block, mask):
    return jnp.concatenate([block, block], axis=0) * mask


def merge_pair(stacked):
    rows = stacked.shape[0] // 2
    left = lax.broadcasted_iota(jnp.int32, (rows, LANES), 1) < HEAD_DIM
    return jnp.where(left, stacked[:rows], stacked[rows:])


def softmax_rows(scores):
    shifted = jnp.exp(scores - jnp.max(scores, axis=-1, keepdims=True))
    return shifted * (1.0 / jnp.sum(shifted, axis=-1, keepdims=True))


def lanes_at(start, width):
    return pl.ds(pl.multiple_of(start, LANES), width)


def pack_kernel(
    me, w_qkv, w_out, w_cross_q, w_cross_kv, w_cross_out, w_up, w_down, tokens, cotangent,
    attend, near, core, chip, rows, parts,
):
    height, depth = attend.shape[2], attend.shape[0]
    pieces = HALF // LANES

    def chunk(count, index):
        return rows[pl.ds(index, height, stride=count), :].astype(BF)

    place = 0
    for shard, mats in ((w_qkv, 3), (w_out, 1), (w_cross_q, 1), (w_cross_kv, 2), (w_cross_out, 1)):
        rows[: shard.shape[0], :] = wide(shard[...])
        for mat in range(mats):
            for half in range(2):
                for i in range(pieces):
                    value = chunk(mats * PAIRS, mat * PAIRS + half * pieces + i)
                    at = place + i * LANES
                    for z in range(depth):
                        attend[z, half, :, at : at + LANES] = value
            place += HALF
    rows[...] = wide(w_up[...])
    pick = fold_pick(False)
    for t in range(GROUPS):
        group = jnp.concatenate(
            [chunk(FF // LANES, t * FOLD + k) for k in range(FOLD)], axis=1
        )
        folded = mm(group, pick).astype(BF)
        for j in range(FOLD):
            parts[j, :height, t * LANES : (t + 1) * LANES] = folded[
                :, j * LANES : (j + 1) * LANES
            ]
    rows[...] = wide(w_down[...])
    for j in range(FOLD):
        for i in range(PAIRS):
            at = D + i * LANES
            parts[j, :height, at : at + LANES] = chunk(FF // LANES, j * PAIRS + i)
        parts[j, TOKENS_AT : TOKENS_AT + tokens.shape[1], :D] = tokens[j]
        parts[j, TOKENS_AT : TOKENS_AT + tokens.shape[1], D:] = cotangent[j]
    near[...] = parts[part_of(me, 0, 0)]
    core[...] = parts[part_of(me, 0, 1)]
    for c in range(2):
        chip[c] = parts[part_of(me, 1, c)]


def part_of(me, far_y, far_c):
    return lax.bitwise_xor(me[0, 2], far_y) * 2 + lax.bitwise_xor(me[0, 3], far_c)


def spread_kernel(me, near, chip, core, both, hidden, tok_cot):
    height, count = hidden.shape[2], tok_cot.shape[1]
    for value, far_y, far_c in ((near[...], 0, 0), (chip[0], 1, 0), (core[...], 0, 1), (both[...], 1, 1)):
        index = part_of(me, far_y, far_c)
        for z in range(hidden.shape[0]):
            hidden[z, index] = value[:height]
        tok_cot[index] = value[TOKENS_AT : TOKENS_AT + count]


def unpack_hidden_kernel(got, up, down):
    depth, height = got.shape[0], got.shape[2]
    chunks = FF // LANES
    pick = fold_pick(True)
    for t in range(GROUPS):
        total = jnp.zeros((height, GROUP), F32)
        for z in range(depth):
            group = jnp.concatenate(
                [got[z, j, :, t * LANES : (t + 1) * LANES] for j in range(FOLD)], axis=1
            )
            total = total + mm(group, pick)
        for k in range(FOLD):
            up[pl.ds(t * FOLD + k, height, stride=chunks), :] = total[
                :, k * LANES : (k + 1) * LANES
            ]
    for j in range(FOLD):
        for i in range(PAIRS):
            at = D + i * LANES
            total = wide(got[0, j, :, at : at + LANES])
            for z in range(1, depth):
                total = total + wide(got[z, j, :, at : at + LANES])
            down[pl.ds(j * PAIRS + i, height, stride=chunks), :] = total


def unpack_halves_kernel(got, *outs):
    depth, height = got.shape[0], got.shape[2]
    parts = HALF // LANES
    place = 0
    for out in outs:
        chunks = out.shape[0] // height
        for mat in range(chunks // PAIRS):
            for half in range(2):
                for i in range(parts):
                    at = place + i * LANES
                    total = wide(got[0, half, :, at : at + LANES])
                    for z in range(1, depth):
                        total = total + wide(got[z, half, :, at : at + LANES])
                    index = mat * PAIRS + half * parts + i
                    out[pl.ds(index, height, stride=chunks), :] = total
            place += HALF


class Fetch:
    def __init__(self, sems):
        self.sems = sems
        self.used = 0

    def start(self, source, target):
        copy = pltpu.make_async_copy(source, target, self.sems.at[self.used])
        self.used += 1
        copy.start()
        return copy

    def columns(self, pieces, me, piece_at, target, target_at):
        copies = []
        for index, piece in enumerate(pieces):
            half = lax.bitwise_xor(me[0, 3], index // 4)
            x = lax.bitwise_xor(me[0, 1], index // 2 % 2)
            y = lax.bitwise_xor(me[0, 2], index % 2)
            copies.append(
                self.start(
                    piece.at[:, :, pl.ds(piece_at, HALF)],
                    target.at[:, x, y, :, lanes_at(target_at + half * HALF, HALF)],
                )
            )
        return copies


def wait(copies):
    for copy in copies:
        copy.wait()


def matrix(ref):
    shape = ref.shape
    return ref[...].reshape(shape[0] * shape[1] * shape[2] * shape[3], shape[4])


def place_kernel(arr, tok_cot, table, slotted, normed, grad_slot):
    pick = arrival_pick(arr)
    rows = mm(pick, tok_cot[:, :D])
    slotted[...] = rows.astype(BF)
    normed[...] = norm_rows(rows, table[0:1, :], table[3:4, :]).astype(BF)
    grad_slot[...] = mm(pick, tok_cot[:, D:]).astype(BF)


def forward_kernel(lens, me, slotted, normed, table, img, *refs):
    pieces_a, pieces_b = refs[:8], refs[8:16]
    (
        projected, probs_self, saved, after_self, after_cross, normed_mlp, query_slots, kv,
        probs_cross, w_qkv, w_out, w_cq, w_kv, w_co, mixed_slots, sems,
    ) = refs[16:]
    fetch = Fetch(sems)
    got_qkv = []
    for mat in range(3):
        got_qkv += fetch.columns(pieces_a, me, mat * HALF, w_qkv, mat * D)
    got_out = fetch.columns(pieces_a, me, 3 * HALF, w_out, 0)
    got_cq = fetch.columns(pieces_b, me, 0, w_cq, 0)
    got_kv = fetch.columns(pieces_b, me, HALF, w_kv, 0)
    got_kv += fetch.columns(pieces_b, me, 2 * HALF, w_kv, D)
    got_co = fetch.columns(pieces_b, me, 3 * HALF, w_co, 0)
    rows = slotted.shape[0]
    saved[:, :D] = normed[...]
    wait(got_qkv)
    projected[...] = mm(normed[...], matrix(w_qkv)).astype(BF)
    place = lax.broadcasted_iota(jnp.int32, (2 * rows, rows), 0)
    query_at = jnp.where(place >= rows, place - rows, place)
    key_at = lax.broadcasted_iota(jnp.int32, (2 * rows, rows), 1)
    allowed = (caption_of(query_at, lens) == caption_of(key_at, lens)) & (key_at <= query_at)
    mask = pair_mask(rows)
    for p in range(PAIRS):
        query = stack_pair(projected[:, p * LANES : (p + 1) * LANES], mask)
        key = projected[:, D + p * LANES : D + (p + 1) * LANES]
        value = projected[:, 2 * D + p * LANES : 2 * D + (p + 1) * LANES]
        scores = jnp.where(allowed, mm_t(query, key) * SCALE, -masked_fill)
        weights_low = softmax_rows(scores).astype(BF)
        probs_self[p] = weights_low
        saved[:, D + p * LANES : D + (p + 1) * LANES] = merge_pair(
            mm(weights_low, value)
        ).astype(BF)
    wait(got_out)
    state = wide(slotted[...]) + mm(saved[:, D : 2 * D], matrix(w_out))
    after_self[...] = state
    low = norm_rows(state, table[1:2, :], table[4:5, :]).astype(BF)
    saved[:, 2 * D : 3 * D] = low
    wait(got_cq)
    pick = slot_pick(lens, rows)
    query_slots[...] = mm(pick, mm(low, matrix(w_cq)).astype(BF)).astype(BF)
    wait(got_kv)
    kv_mat = matrix(w_kv)
    mask = pair_mask(CAP_LEN)
    for c in range(lens.shape[1]):
        slots = slice(c * CAP_LEN, (c + 1) * CAP_LEN)
        images = slice(c * IMG, (c + 1) * IMG)
        kv[images, :] = mm(img[images, :], kv_mat).astype(BF)
        for p in range(PAIRS):
            cols = slice(p * LANES, (p + 1) * LANES)
            query = stack_pair(query_slots[slots, cols], mask)
            weights_low = softmax_rows(mm_t(query, kv[images, cols]) * SCALE).astype(BF)
            probs_cross[c * PAIRS + p] = weights_low
            value = kv[images, D + p * LANES : D + (p + 1) * LANES]
            mixed_slots[slots, cols] = merge_pair(mm(weights_low, value)).astype(BF)
    low = t_mm(pick, mixed_slots[...]).astype(BF)
    saved[:, 3 * D :] = low
    wait(got_co)
    state = after_self[...] + mm(low, matrix(w_co))
    after_cross[...] = state
    normed_mlp[...] = norm_rows(state, table[2:3, :], table[5:6, :]).astype(BF)


def put_small(small, row, value):
    for k in range(PAIRS):
        at = row * PAIRS + k
        small[at : at + 1, :] = value[:, k * LANES : (k + 1) * LANES]


def own_part(value, me):
    part = me[0, 2] * 2 + me[0, 3]
    out = value[:, :LANES]
    for j in range(1, FOLD):
        out = jnp.where(part == j, value[:, j * LANES : (j + 1) * LANES], out)
    return out


def mlp_kernel(me, table, up_bias, *refs):
    inputs, grads, ups, downs = refs[:4], refs[4:8], refs[8:10], refs[10:12]
    (
        grad_keep, grad_send, out_keep, out_send, active, grad_hidden, small,
        all_in, all_grad, w_up, w_down, sems,
    ) = refs[12:]
    fetch = Fetch(sems)
    got_up, got_down = [], []
    for index in range(2):
        x = lax.bitwise_xor(me[0, 1], index)
        got_up.append(fetch.start(ups[index], w_up.at[:, x]))
        got_down.append(fetch.start(downs[index], w_down.at[:, x]))
    rows = inputs[0].shape[0]
    for n in range(4):
        all_in[n * rows : (n + 1) * rows, :] = inputs[n][...]
        all_grad[n * rows : (n + 1) * rows, :] = grads[n][...]
    bias = own_part(mm(up_bias[...], fold_pick(False)), me)
    bias = jnp.concatenate([bias[t : t + 1, :] for t in range(GROUPS)], axis=1)
    wait(got_up)
    up_mat = w_up[...].reshape(D, D)
    hidden = mm(all_in[...], up_mat) + bias
    half = 0.5 + 0.5 * lax.erf(hidden * (0.5**0.5))
    act = (hidden * half).astype(BF)
    active[...] = act
    slope = half + hidden * (jnp.exp(hidden * hidden * -0.5) * 0.3989422804014327)
    wait(got_down)
    down_mat = w_down[...].reshape(D, D)
    grad_hid = (mm_t(all_grad[...], down_mat) * slope).astype(BF)
    grad_hidden[...] = grad_hid
    grad_part = mm_t(grad_hid, up_mat)
    out_part = mm(act, down_mat)
    for y in range(2):
        own, other = slice(2 * y * rows, (2 * y + 1) * rows), slice((2 * y + 1) * rows, 2 * (y + 1) * rows)
        grad_keep[y] = grad_part[own]
        out_keep[y] = out_part[own]
        grad_send[y] = grad_part[other].astype(BF)
        out_send[y] = out_part[other].astype(BF)
    sums = jnp.sum(wide(grad_hid), axis=0, keepdims=True).astype(BF)
    sums = jnp.concatenate(
        [sums[:, t * LANES : (t + 1) * LANES] for t in range(GROUPS)] + [sums[:, :LANES]] * 2,
        axis=0,
    )
    part = me[0, 2] * 2 + me[0, 3]
    spread = jnp.concatenate(
        [jnp.where(part == j, sums, jnp.zeros_like(sums)) for j in range(FOLD)], axis=1
    )
    natural = mm(spread, fold_pick(True))
    small[...] = jnp.zeros_like(small)
    for n in range(FF // LANES):
        at = 6 * PAIRS + n
        small[at : at + 1, :] = natural[
            n // FOLD : n // FOLD + 1, n % FOLD * LANES : (n % FOLD + 1) * LANES
        ]
    put_small(small, 10, jnp.sum(wide(grads[0][...]), axis=0, keepdims=True))


def hidden_grad_kernel(me, *refs):
    normed, grad_slot = refs[:4], refs[4:8]
    active, grad_hidden, keep_up, send_up, keep_down, send_down = refs[8:]
    depth, height = keep_up.shape[:2]
    for keep, send, left, right in (
        (keep_up, send_up, [r[...] for r in normed], [grad_hidden[...]]),
        (keep_down, send_down, [active[...]], [r[...] for r in grad_slot]),
    ):
        grads = t_mm(jnp.concatenate(left, axis=0), jnp.concatenate(right, axis=0))
        for z in range(depth):
            low = grads[2 * z * height : (2 * z + 1) * height, :]
            high = grads[(2 * z + 1) * height : (2 * z + 2) * height, :]
            keep[z] = jnp.where(me[0, 1] == 0, low, high).astype(BF)
            send[z] = jnp.where(me[0, 1] == 0, high, low).astype(BF)


def combine_kernel(grad_keep, out_keep, grad_far, out_far, grad_own, out_own, grad_send, out_send):
    grad_own[...] = grad_keep[0] + wide(grad_far[0])
    out_own[...] = out_keep[0] + wide(out_far[0])
    grad_send[...] = (grad_keep[1] + wide(grad_far[1])).astype(BF)
    out_send[...] = (out_keep[1] + wide(out_far[1])).astype(BF)


def cross_back_kernel(
    lens, me, grad_own, grad_far, after_cross, grad_slot, probs, query_slots, kv, after_self,
    table, small_in, *refs,
):
    pieces = refs[:8]
    (
        grad_state, small, half_keep, half_send, kv_keep, kv_send,
        w_co, w_cq, mixed_slots, query_grads, sems,
    ) = refs[8:]
    fetch = Fetch(sems)
    got_co = fetch.columns(pieces, me, 3 * HALF, w_co, 0)
    got_cq = fetch.columns(pieces, me, 0, w_cq, 0)
    rows = after_self.shape[0]
    halves = ((0, half_keep, kv_keep), (1, half_send, kv_send))
    small[...] = small_in[...]
    grad_in, grad_gain, grad_shift = norm_back(
        after_cross[...], table[2:3, :], grad_own[...] + wide(grad_far[...])
    )
    put_small(small, 2, grad_gain)
    put_small(small, 5, grad_shift)
    grad_after = wide(grad_slot[...]) + grad_in
    grad_state[...] = grad_after
    pick = slot_pick(lens, rows)
    wait(got_co)
    query_grads[:rows, :] = grad_after.astype(BF)
    mixed_slots[...] = mm(pick, mm_t(query_grads[:rows, :], matrix(w_co)).astype(BF)).astype(BF)
    for rel, half_out, _ in halves:
        at = lax.bitwise_xor(me[0, 3], rel) * HALF
        half_out[:, HALF : 2 * HALF] = query_grads[:rows, lanes_at(at, HALF)]
    mask = pair_mask(CAP_LEN)
    for c in range(lens.shape[1]):
        slots = slice(c * CAP_LEN, (c + 1) * CAP_LEN)
        images = slice(c * IMG, (c + 1) * IMG)
        for rel, _, kv_out in halves:
            half = lax.bitwise_xor(me[0, 3], rel)
            for i in range(HALF_PAIRS):
                cols = lanes_at(half * HALF + i * LANES, LANES)
                grad_mixed = stack_pair(mixed_slots[slots, cols], mask)
                query = stack_pair(query_slots[slots, cols], mask)
                key = kv[images, cols]
                value = kv[images, lanes_at(half * HALF + D + i * LANES, LANES)]
                weights_low = probs[c * PAIRS + half * HALF_PAIRS + i]
                attn = wide(weights_low)
                grad_weights = mm_t(grad_mixed, value)
                centre = jnp.sum(attn * grad_weights, axis=-1, keepdims=True)
                grad_scores = (attn * (grad_weights - centre)).astype(BF)
                query_grads[slots, cols] = (merge_pair(mm(grad_scores, key)) * SCALE).astype(BF)
                at = i * LANES
                kv_out[images, at : at + LANES] = (t_mm(grad_scores, query) * SCALE).astype(BF)
                at = HALF + i * LANES
                kv_out[images, at : at + LANES] = t_mm(weights_low, grad_mixed).astype(BF)
    mixed_slots[:rows, :] = t_mm(pick, query_grads[...]).astype(BF)
    wait(got_cq)
    grad_in, grad_gain, grad_shift = norm_back(
        after_self[...], table[1:2, :], mm_t(mixed_slots[:rows, :], matrix(w_cq))
    )
    put_small(small, 1, grad_gain)
    put_small(small, 4, grad_shift)
    grad_after = grad_state[...] + grad_in
    grad_state[...] = grad_after
    query_grads[:rows, :] = grad_after.astype(BF)
    for rel, half_out, _ in halves:
        at = lax.bitwise_xor(me[0, 3], rel) * HALF
        half_out[:, :HALF] = mixed_slots[:rows, lanes_at(at, HALF)]
        half_out[:, 2 * HALF :] = query_grads[:rows, lanes_at(at, HALF)]


def self_back_kernel(me, grad_state, probs, projected, slotted, table, small_in, *refs):
    pieces = refs[:8]
    (
        grad_rows, small, keep, send,
        w_out, w_qkv, mixed, grad_projected, sems,
    ) = refs[8:]
    fetch = Fetch(sems)
    got_out = fetch.columns(pieces, me, 3 * HALF, w_out, 0)
    got_qkv = []
    for mat in range(3):
        got_qkv += fetch.columns(pieces, me, mat * HALF, w_qkv, mat * D)
    rows = slotted.shape[0]
    wait(got_out)
    mixed[...] = mm_t(grad_state[...].astype(BF), matrix(w_out)).astype(BF)
    mask = pair_mask(rows)
    for p in range(PAIRS):
        cols = slice(p * LANES, (p + 1) * LANES)
        key_cols = slice(D + p * LANES, D + (p + 1) * LANES)
        value_cols = slice(2 * D + p * LANES, 2 * D + (p + 1) * LANES)
        grad_mixed = stack_pair(mixed[:, cols], mask)
        query = stack_pair(projected[:, cols], mask)
        weights_low = probs[p]
        attn = wide(weights_low)
        grad_weights = mm_t(grad_mixed, projected[:, value_cols])
        centre = jnp.sum(attn * grad_weights, axis=-1, keepdims=True)
        grad_scores = (attn * (grad_weights - centre)).astype(BF)
        grad_projected[:, cols] = (
            merge_pair(mm(grad_scores, projected[:, key_cols])) * SCALE
        ).astype(BF)
        grad_projected[:, key_cols] = (t_mm(grad_scores, query) * SCALE).astype(BF)
        grad_projected[:, value_cols] = t_mm(weights_low, grad_mixed).astype(BF)
    for mat in range(3):
        for rel, out in ((0, keep), (1, send)):
            at = lax.bitwise_xor(me[0, 3], rel) * HALF + mat * D
            out[:, mat * HALF : (mat + 1) * HALF] = grad_projected[:, lanes_at(at, HALF)]
    wait(got_qkv)
    grad_in, grad_gain, grad_shift = norm_back(
        wide(slotted[...]), table[0:1, :], mm_t(grad_projected[...], matrix(w_qkv))
    )
    grad_slotted = (grad_state[...] + grad_in).astype(BF)
    grad_rows[...] = grad_slotted
    small[...] = small_in[...]
    put_small(small, 0, grad_gain)
    put_small(small, 3, grad_shift)


def put_quadrants(grads, me, outs, at):
    depth, height = outs[0].shape[:2]
    width = grads.shape[1]
    for index, out in enumerate(outs):
        x = lax.bitwise_xor(me[0, 1], index // 2)
        y = lax.bitwise_xor(me[0, 2], index % 2)
        for z in range(depth):
            low = pl.multiple_of(((z * 2 + x) * 2 + y) * height, 16)
            out[z, :, at : at + width] = grads[pl.ds(low, height), :].astype(BF)


def half_grads(pieces, me, outs, grads):
    at = 0
    for left, far_left, right, far_right in pieces:
        width = right.shape[1]
        grads[:, :width] = t_mm(left, right) + t_mm(far_left, far_right)
        put_quadrants(grads.at[:, :width], me, outs, at)
        at += width


def cross_grad_kernel(
    me, saved, saved_far, img, img_far, half, half_far, kv, kv_far, *refs
):
    outs, grads = refs[:4], refs[4]
    part = lambda ref, n, width: ref[:, n * width : (n + 1) * width]
    half_grads(
        [
            (part(saved, 2, D), part(saved_far, 2, D), part(half, 0, HALF), part(half_far, 0, HALF)),
            (img[...], img_far[...], kv[...], kv_far[...]),
            (part(saved, 3, D), part(saved_far, 3, D), part(half, 1, HALF), part(half_far, 1, HALF)),
            (part(saved, 1, D), part(saved_far, 1, D), part(half, 2, HALF), part(half_far, 2, HALF)),
        ],
        me, outs, grads,
    )


def owner_rows(small, blocks, share):
    height = blocks.shape[0] // (small.shape[0] * LANES // share)
    lane = lax.broadcasted_iota(jnp.int32, (3, LANES), 1)
    blocks[...] = jnp.zeros_like(blocks)
    table = jnp.concatenate([small[...], jnp.zeros((6, LANES), F32)], axis=0)
    for owner in range(small.shape[0] * LANES // share):
        row, shift = divmod(owner * share, LANES)
        if shift == 0:
            value = table[row : row + 3]
        else:
            moved = pltpu.roll(table[row : row + 4], LANES - shift, axis=1)
            value = jnp.where(lane < LANES - shift, moved[:3], moved[1:4])
        blocks[owner * height : owner * height + 3, :] = value


def self_grad_kernel(share, me, saved, saved_far, half, half_far, small, *refs):
    outs, grads = refs[:4], refs[4]
    half_grads(
        [(saved[:, :D], saved_far[:, :D], half[...], half_far[...])], me, outs, grads
    )
    blocks = grads.at[:, :LANES]
    owner_rows(small, blocks, share)
    put_quadrants(blocks, me, outs, 3 * HALF)


def unpack_self_kernel(got, qkv, small):
    depth = got.shape[0]
    unpack_halves_kernel(got, qkv)
    total = jnp.zeros((8, LANES), F32)
    for z in range(depth):
        for c in range(2):
            total = total + wide(got[z, c, :8, 3 * HALF :])
    small[...] = total


def return_kernel(
    me, arr, after_cross, table, own, far, grad_rows, near, core, chip, rows
):
    pick = arrival_pick(arr)
    count = near.shape[0]
    result = after_cross[...] + own[...] + wide(far[...]) + table[10:11, :]
    rows[:, :D] = t_mm(pick, result.astype(BF))
    rows[:, D:] = t_mm(pick, grad_rows[...])

    def part(far_y, far_c):
        at = pl.multiple_of(part_of(me, far_y, far_c) * count, 8)
        return rows[pl.ds(at, count), :].astype(BF)

    near[...] = part(0, 0)
    core[...] = part(0, 1)
    for c in range(2):
        chip[c] = part(1, c)


def collect_kernel(me, near, chip, core, both, layer_out, grad_tokens):
    for value, far_y, far_c in ((near[...], 0, 0), (chip[0], 1, 0), (core[...], 0, 1), (both[...], 1, 1)):
        index = part_of(me, far_y, far_c)
        layer_out[index] = value[:, :D]
        grad_tokens[index] = value[:, D:]


def image_grad_kernel(kv_keep, kv_send, *refs):
    me, pieces = refs[0], refs[1:9]
    grad_image, w_kv, sems = refs[9:]
    fetch = Fetch(sems)
    copies = []
    for index, piece in enumerate(pieces):
        x = lax.bitwise_xor(me[0, 1], index // 2 % 2)
        y = lax.bitwise_xor(me[0, 2], index % 2)
        copies.append(
            fetch.start(piece.at[:, :, pl.ds(HALF, D)], w_kv.at[index // 4, :, x, y])
        )
    wait(copies)
    near, far = w_kv[0].reshape(D, D), w_kv[1].reshape(D, D)
    for c in range(kv_keep.shape[0] // IMG):
        rows = pl.ds(c * IMG, IMG)
        grad_image[rows, :] = (mm_t(kv_keep[rows, :], near) + mm_t(kv_send[rows, :], far)).astype(
            BF
        )


def add_kernel(sums, *refs):
    out, each = refs[-1], (len(refs) - 1) // sums
    width = refs[0].shape[-1]
    for n in range(sums):
        total = wide(refs[n * each][...])
        for ref in refs[n * each + 1 : (n + 1) * each]:
            total = total + wide(ref[...])
        out[:, :, n * width : (n + 1) * width] = total.astype(BF)


VM = pl.BlockSpec(memory_space=pltpu.VMEM)
SM = pl.BlockSpec(memory_space=pltpu.SMEM)
HB = pl.BlockSpec(memory_space=pl.ANY)


def run(kernel, outs, specs, scratch, *args, mib=58):
    return pl.pallas_call(
        kernel,
        out_shape=[jax.ShapeDtypeStruct(s, t) for s, t in outs],
        in_specs=specs,
        out_specs=[VM] * len(outs),
        scratch_shapes=scratch,
        compiler_params=pltpu.CompilerParams(vmem_limit_bytes=mib * 2**20),
        name=(kernel.func if isinstance(kernel, functools.partial) else kernel).__name__,
    )(*args)


def add_up(*args, sums=1):
    depth, height, width = args[0].shape
    spec = pl.BlockSpec((1, height, width), lambda z: (z, 0, 0))
    return pl.pallas_call(
        functools.partial(add_kernel, sums),
        grid=(depth,),
        out_shape=jax.ShapeDtypeStruct((depth, height, sums * width), BF),
        in_specs=[spec] * len(args),
        out_specs=pl.BlockSpec((1, height, sums * width), lambda z: (z, 0, 0)),
        compiler_params=pltpu.CompilerParams(vmem_limit_bytes=16 * 2**20),
        name="add_kernel",
    )(*args)


def flip(value, axis):
    return lax.ppermute(value, axis, [(0, 1), (1, 0)])


def swap_all(value, axes):
    return lax.all_to_all(value, axes, split_axis=0, concat_axis=0, tiled=True)


def tie(*values):
    return lax.optimization_barrier(values)


def group_parts(near, chip, core):
    chip = flip(chip, "y")
    return near, chip, flip(core, "c"), flip(chip[1], "c")


def on_device(
    tokens,
    image_tokens,
    caption_lengths,
    arrival_order,
    w_qkv,
    w_out,
    w_cross_q,
    w_cross_kv,
    w_cross_out,
    w_up,
    w_down,
    small_params,
    cotangent,
):
    depth = lax.axis_size("z")
    height = D // (8 * depth)
    rows = tokens.shape[0]
    captions = caption_lengths.shape[1]
    slots = captions * CAP_LEN
    images = captions * IMG
    lens, arr = caption_lengths, arrival_order
    me = jnp.stack([lax.axis_index(a) for a in AXES]).astype(jnp.int32).reshape(1, 4)
    owner = ((me[0, 0] * 2 + me[0, 1]) * 2 + me[0, 2]) * 2 + me[0, 3]
    vmem = pltpu.VMEM
    sems = lambda n: pltpu.SemaphoreType.DMA((n,))
    shards = (w_qkv, w_out, w_cross_q, w_cross_kv, w_cross_out, w_up, w_down)

    part = ((TOKENS_AT + 48, 2 * D), BF)
    attend, near, core, chip = run(
        pack_kernel,
        [((depth, 2, height, 8 * HALF), BF), part, part, ((2,) + part[0], BF)],
        [SM] + [VM] * 9,
        [vmem((w_up.shape[0] // LANES, LANES), F32), vmem((FOLD,) + part[0], BF)],
        me,
        *(w.reshape(-1, LANES) for w in shards),
        tokens.reshape(FOLD, -1, D),
        cotangent.reshape(FOLD, -1, D),
    )
    attend = swap_all(attend.reshape(2 * depth, height, 8 * HALF), ("z", "c"))
    attend = attend.reshape(depth, 2 * height, 8 * HALF)
    hidden, tok_cot = run(
        spread_kernel,
        [((depth, FOLD, height, 2 * D), BF), ((FOLD, rows // FOLD, 2 * D), BF)],
        [SM] + [VM] * 4,
        [],
        me, *group_parts(near, chip, core),
    )
    table = jnp.zeros((8 * depth, small_params.shape[0]), BF)
    table = lax.dynamic_update_slice(table, small_params[None], (owner, 0))
    table = table.reshape(-1, LANES)
    for axis in ("c", "y", "x"):
        table = table + flip(table, axis)
    img = image_tokens.reshape(images, V)
    hidden, attend, table, img, tok_cot = tie(hidden, attend, table, img, tok_cot)
    a, b = attend[:, :, : 4 * HALF], attend[:, :, 4 * HALF :]
    ax, by, ay, bx = flip(a, "x"), flip(b, "y"), flip(a, "y"), flip(b, "x")
    hidden = swap_all(hidden.reshape(depth, FOLD * height, 2 * D), "z")
    step = 1
    while step < depth:
        table = table + lax.ppermute(table, "z", [(i, i ^ step) for i in range(depth)])
        step *= 2
    up_bias = table.reshape(-1)[6 * D : 6 * D + FF].reshape(GROUPS, GROUP)
    table = wide(table.reshape(-1, D))
    slotted, normed_self, grad_slot = run(
        place_kernel, [((rows, D), BF)] * 3, [VM] * 3, [],
        arr, tok_cot.reshape(rows, 2 * D), table,
    )
    img_far = flip(img, "c")
    a, b, ax, by, ay, bx, hidden, slotted, normed_self, grad_slot, img_far = tie(
        a, b, ax, by, ay, bx, hidden, slotted, normed_self, grad_slot, img_far
    )
    axy, byx = flip(ax, "y"), flip(by, "x")
    near = (a, ay, ax, b, by, bx)
    far = tuple(flip(p, "c") for p in near)
    axy, byx, hidden, far = tie(axy, byx, hidden, far)
    hidden_up, hidden_down = hidden[:, :, :D], hidden[:, :, D:]
    pieces_a = near[:3] + (axy,) + far[:3] + (flip(axy, "c"),)
    pieces_b = near[3:] + (byx,) + far[3:] + (flip(byx, "c"),)
    hidden_up, hidden_down, pieces_a, pieces_b = tie(hidden_up, hidden_down, pieces_a, pieces_b)
    hidden_up_far = flip(hidden_up, "x")

    def group_rows(value):
        far = flip(value, "y")
        return (value, flip(value, "c"), far, flip(far, "c"))

    grad_slots = group_rows(grad_slot)
    weight_shape = lambda n: vmem((depth, 2, 2, 2 * height, n * D), BF)
    (
        projected, probs_self, saved, after_self, after_cross, normed_mlp, query_slots, kv,
        probs_cross,
    ) = run(
        forward_kernel,
        [
            ((rows, 3 * D), BF),
            ((PAIRS, 2 * rows, rows), BF),
            ((rows, 4 * D), BF),
            ((rows, D), F32),
            ((rows, D), F32),
            ((rows, D), BF),
            ((slots, D), BF),
            ((images, 2 * D), BF),
            ((captions * PAIRS, 2 * CAP_LEN, IMG), BF),
        ],
        [SM, SM] + [VM] * 4 + [HB] * 16,
        [
            weight_shape(3),
            weight_shape(1),
            weight_shape(1),
            weight_shape(2),
            weight_shape(1),
            vmem((slots, D), BF),
            sems(64),
        ],
        lens, me, slotted, normed_self, table, img, *pieces_a, *pieces_b,
    )
    normed_mlp, grad_slots, hidden_up_far, hidden_down = tie(
        normed_mlp, grad_slots, hidden_up_far, hidden_down
    )
    hidden_down_far = flip(hidden_down, "x")
    inputs = group_rows(normed_mlp)
    small_shape = ((11 * PAIRS, LANES), F32)
    saved_far = flip(saved, "c")
    (
        grad_keep, grad_send, out_keep, out_send, active, grad_hidden, small,
    ) = run(
        mlp_kernel,
        [
            ((2, rows, D), F32),
            ((2, rows, D), BF),
            ((2, rows, D), F32),
            ((2, rows, D), BF),
            ((4 * rows, D), BF),
            ((4 * rows, D), BF),
            small_shape,
        ],
        [SM] + [VM] * 10 + [HB] * 4,
        [
            vmem((4 * rows, D), BF),
            vmem((4 * rows, D), BF),
            vmem((depth, 2, FOLD * height, D), BF),
            vmem((depth, 2, FOLD * height, D), BF),
            sems(4),
        ],
        me, table, up_bias, *inputs, *grad_slots,
        hidden_up, hidden_up_far, hidden_down, hidden_down_far,
    )

    grad_own, out_own, grad_back, out_back = run(
        combine_kernel,
        [((rows, D), F32)] * 2 + [((rows, D), BF)] * 2,
        [VM] * 4,
        [],
        grad_keep, out_keep, flip(grad_send, "c"), flip(out_send, "c"),
        mib=16,
    )
    grad_far = flip(grad_back, "y")
    keep_up, send_up, keep_down, send_down = run(
        hidden_grad_kernel,
        [((depth, FOLD * height, D), BF)] * 4,
        [SM] + [VM] * 10,
        [],
        me, *inputs, *grad_slots, active, grad_hidden,
    )
    grad_far, send_up, send_down, saved_far = tie(grad_far, send_up, send_down, saved_far)
    far_up = flip(send_up, "x")
    grad_state, small, half_keep, half_send, kv_keep, kv_send = run(
        cross_back_kernel,
        [
            ((rows, D), F32),
            small_shape,
            ((rows, 3 * HALF), BF),
            ((rows, 3 * HALF), BF),
            ((images, D), BF),
            ((images, D), BF),
        ],
        [SM, SM] + [VM] * 10 + [HB] * 8,
        [
            weight_shape(1),
            weight_shape(1),
            vmem((slots, D), BF),
            vmem((slots, D), BF),
            sems(16),
        ],
        lens, me, grad_own, grad_far, after_cross, grad_slot, probs_cross, query_slots, kv,
        after_self, table, small, *pieces_b,
    )
    far_up, send_down, grad_state, half_send, kv_send, out_back = tie(
        far_up, send_down, grad_state, half_send, kv_send, out_back
    )
    far_down, out_far = flip(send_down, "x"), flip(out_back, "y")
    half_far, kv_far = flip(half_send, "c"), flip(kv_send, "c")
    block = lambda n: ((depth, 2 * height, n * HALF), BF)
    cross_00, cross_01, cross_10, cross_11 = run(
        cross_grad_kernel,
        [block(5)] * 4,
        [SM] + [VM] * 8,
        [vmem((D, D), F32)],
        me, saved, saved_far, img, img_far, half_keep, half_far, kv_keep, kv_far,
    )
    cross_11, cross_01, grad_state, out_far = tie(cross_11, cross_01, grad_state, out_far)
    cross_11 = flip(cross_11, "y")
    grad_rows, small, self_keep, self_send = run(
        self_back_kernel,
        [
            ((rows, D), BF),
            small_shape,
            ((rows, 3 * HALF), BF),
            ((rows, 3 * HALF), BF),
        ],
        [SM] + [VM] * 6 + [HB] * 8,
        [
            weight_shape(1),
            weight_shape(3),
            vmem((rows, D), BF),
            vmem((rows, 3 * D), BF),
            sems(32),
        ],
        me, grad_state, probs_self, projected, slotted, table, small, *pieces_a,
    )
    self_block = ((depth, 2 * height, 3 * HALF + LANES), BF)
    self_00, self_01, self_10, self_11 = run(
        functools.partial(self_grad_kernel, small_params.shape[0]),
        [self_block] * 4,
        [SM] + [VM] * 5,
        [vmem((D, 3 * HALF), F32)],
        me, saved, saved_far, self_keep, flip(self_send, "c"), small,
    )
    cross_11, self_11, self_10, grad_rows, far_down, cross_01, kv_send = tie(
        cross_11, self_11, self_10, grad_rows, far_down, cross_01, kv_send
    )
    self_11, cross_01 = flip(self_11, "x"), flip(cross_01, "y")
    cross_10 = flip(add_up(cross_10, cross_11), "x")
    hidden_sum = add_up(keep_up, far_up, keep_down, far_down, sums=2)
    part = ((rows // FOLD, 2 * D), BF)
    near, core, chip = run(
        return_kernel,
        [part, part, ((2,) + part[0], BF)],
        [SM] + [VM] * 6,
        [vmem((rows, 2 * D), F32)],
        me, arr, after_cross, table, out_own, out_far, grad_rows,
    )

    def owned(value, parts, axes):
        got = swap_all(value.reshape(parts * depth, height, -1), axes)
        return got.reshape(depth, parts, height, -1)

    flat = lambda n: ((height * n * PAIRS, LANES), F32)
    hidden_got = owned(hidden_sum, FOLD, ("z", "y", "c"))
    (grad_image,) = run(
        image_grad_kernel,
        [((images, D), BF)],
        [VM, VM, SM] + [HB] * 8,
        [vmem((2, depth, 2, 2, 2 * height, D), BF), sems(8)],
        kv_keep, kv_send, me, *pieces_b,
    )
    self_11, hidden_got, grad_image, self_10, cross_10, cross_01 = tie(
        self_11, hidden_got, grad_image, self_10, cross_10, cross_01
    )
    self_10 = flip(self_10, "x")
    self_01 = flip(add_up(self_01, self_11), "y")
    got = owned(add_up(cross_00, cross_01, cross_10), 2, ("z", "c"))
    returned = group_parts(near, chip, core)
    grad_up, grad_down = run(
        unpack_hidden_kernel, [flat(FOLD)] * 2, [VM], [], hidden_got, mib=16
    )
    got, self_01, self_10, returned, grad_up, grad_down = tie(
        got, self_01, self_10, returned, grad_up, grad_down
    )
    grad_cq, grad_ckv, grad_co, grad_out = run(
        unpack_halves_kernel, [flat(n) for n in (1, 2, 1, 1)], [VM], [], got, mib=16
    )
    got = owned(add_up(self_00, self_10, self_01), 2, ("z", "c"))
    layer_out, grad_tokens = run(
        collect_kernel, [((FOLD, rows // FOLD, D), BF)] * 2, [SM] + [VM] * 4, [],
        me, *returned,
    )
    grad_qkv, grad_small = run(
        unpack_self_kernel, [flat(3), ((8, LANES), F32)], [VM], [], got, mib=16
    )
    return (
        layer_out.reshape(tokens.shape),
        grad_tokens.reshape(tokens.shape),
        grad_image.reshape(image_tokens.shape),
        *(
            g.reshape(-1)
            for g in (grad_qkv, grad_out, grad_cq, grad_ckv, grad_co, grad_up, grad_down)
        ),
        grad_small.reshape(-1)[: small_params.shape[0]],
    )


def general_norm_rows(inputs, gain_vec, shift_vec):
    centred = inputs - jnp.mean(inputs, axis=-1, keepdims=True)
    variance = jnp.mean(centred * centred, axis=-1, keepdims=True)
    return centred * lax.rsqrt(variance + epsilon) * gain_vec + shift_vec


def general_norm_back(inputs, gain_vec, shift_vec, grad_normed):
    _, pullback = jax.vjp(general_norm_rows, inputs, gain_vec, shift_vec)
    return pullback(grad_normed)


def general_gelu_exact(inputs):
    return jax.nn.gelu(inputs, approximate=False)


def general_gelu_back(inputs, grad_active):
    _, pullback = jax.vjp(general_gelu_exact, inputs)
    return pullback(grad_active)[0]


def general_slot_index(lengths, arrivals):
    run_ends = jnp.cumsum(lengths)
    starts = run_ends - lengths
    caption = jnp.sum((run_ends[None, :] <= arrivals[:, None]).astype(jnp.int32), axis=1)
    picked = caption[:, None] == jnp.arange(lengths.shape[0], dtype=jnp.int32)[None, :]
    first_row = jnp.sum(jnp.where(picked, starts[None, :], 0), axis=1)
    return caption * CAP_LEN + arrivals - first_row


def general_score_block(queries, keys_in, allowed):
    scores = jnp.einsum(
        "cqhd,ckhd->chqk", queries, keys_in, preferred_element_type=jnp.float32
    ) * HEAD_DIM ** (-0.5)
    return jnp.where(allowed, scores, -masked_fill)


def general_attention(queries, keys_in, values, allowed):
    scores = general_score_block(queries, keys_in, allowed)
    row_max = jnp.max(scores, axis=-1, keepdims=True)
    log_total = row_max + jnp.log(jnp.sum(jnp.exp(scores - row_max), axis=-1, keepdims=True))
    attn_weights = jnp.exp(scores - log_total).astype(jnp.bfloat16)
    mixed_out = jnp.einsum(
        "chqk,ckhd->cqhd", attn_weights, values, preferred_element_type=jnp.float32
    ).astype(jnp.bfloat16)
    return (mixed_out, log_total)


def general_attention_back(queries, keys_in, values, log_total, grad_mixed, allowed):
    scores = general_score_block(queries, keys_in, allowed)
    attn_weights = jnp.exp(scores - log_total)
    grad_weights = jnp.einsum(
        "cqhd,ckhd->chqk", grad_mixed, values, preferred_element_type=jnp.float32
    )
    centre = jnp.sum(attn_weights * grad_weights, axis=-1, keepdims=True)
    grad_scores = (attn_weights * (grad_weights - centre)).astype(jnp.bfloat16)
    grad_queries = jnp.einsum(
        "chqk,ckhd->cqhd", grad_scores, keys_in, preferred_element_type=jnp.float32
    ) * HEAD_DIM ** (-0.5)
    grad_keys = jnp.einsum(
        "chqk,cqhd->ckhd", grad_scores, queries, preferred_element_type=jnp.float32
    ) * HEAD_DIM ** (-0.5)
    grad_values = jnp.einsum(
        "chqk,cqhd->ckhd",
        attn_weights.astype(jnp.bfloat16),
        grad_mixed,
        preferred_element_type=jnp.float32,
    )
    return (grad_queries, grad_keys, grad_values)


def general_unpack_params(gathered):
    (
        flat_qkv,
        flat_out,
        flat_cross_q,
        flat_cross_kv,
        flat_cross_out,
        flat_up,
        flat_down,
        flat_small,
    ) = gathered
    small_vals = flat_small.astype(jnp.float32)
    return (
        flat_qkv.reshape(D, 3 * D),
        flat_out.reshape(D, D),
        flat_cross_q.reshape(D, D),
        flat_cross_kv.reshape(V, 2 * D),
        flat_cross_out.reshape(D, D),
        flat_up.reshape(D, FF),
        flat_down.reshape(FF, D),
        small_vals[: 3 * D].reshape(3, D),
        small_vals[3 * D : 6 * D].reshape(3, D),
        small_vals[6 * D : 6 * D + FF],
        small_vals[6 * D + FF :],
    )


def general_forward(slotted, image_rows, params, allowed, open_mask):
    (
        mat_qkv,
        mat_out,
        mat_cross_q,
        mat_cross_kv,
        mat_cross_out,
        mat_up,
        mat_down,
        norm_gains,
        shifts,
        up_bias,
        down_bias,
    ) = params
    captions = slotted.shape[0] // CAP_LEN
    head_count = D // HEAD_DIM
    normed_self = general_norm_rows(slotted, norm_gains[0], shifts[0]).astype(jnp.bfloat16)
    projected = jnp.dot(normed_self, mat_qkv, preferred_element_type=jnp.float32).astype(
        jnp.bfloat16
    )
    projected = projected.reshape(captions, CAP_LEN, 3, head_count, HEAD_DIM)
    self_mixed, self_total = general_attention(
        projected[:, :, 0], projected[:, :, 1], projected[:, :, 2], allowed
    )
    self_mixed = self_mixed.reshape(-1, D)
    after_self = slotted + jnp.dot(self_mixed, mat_out, preferred_element_type=jnp.float32)
    normed_cross = general_norm_rows(after_self, norm_gains[1], shifts[1]).astype(jnp.bfloat16)
    cross_query = jnp.dot(normed_cross, mat_cross_q, preferred_element_type=jnp.float32).astype(
        jnp.bfloat16
    )
    cross_query = cross_query.reshape(captions, CAP_LEN, head_count, HEAD_DIM)
    image_kv = jnp.dot(image_rows, mat_cross_kv, preferred_element_type=jnp.float32).astype(
        jnp.bfloat16
    )
    image_kv = image_kv.reshape(captions, IMG, 2, head_count, HEAD_DIM)
    cross_mixed, cross_total = general_attention(
        cross_query, image_kv[:, :, 0], image_kv[:, :, 1], open_mask
    )
    cross_mixed = cross_mixed.reshape(-1, D)
    after_cross = after_self + jnp.dot(
        cross_mixed, mat_cross_out, preferred_element_type=jnp.float32
    )
    normed_mlp = general_norm_rows(after_cross, norm_gains[2], shifts[2]).astype(jnp.bfloat16)
    hidden = jnp.dot(normed_mlp, mat_up, preferred_element_type=jnp.float32) + up_bias
    activated = general_gelu_exact(hidden).astype(jnp.bfloat16)
    result = (
        after_cross + jnp.dot(activated, mat_down, preferred_element_type=jnp.float32) + down_bias
    )
    saved_state = (
        slotted,
        normed_self,
        projected,
        self_total,
        self_mixed,
        after_self,
        normed_cross,
        cross_query,
        image_kv,
        cross_total,
        cross_mixed,
        after_cross,
        normed_mlp,
        hidden,
        activated,
    )
    return (result, saved_state)


def general_backward(saved_state, grad_slot, image_rows, params, allowed, open_mask):
    (
        mat_qkv,
        mat_out,
        mat_cross_q,
        mat_cross_kv,
        mat_cross_out,
        mat_up,
        mat_down,
        norm_gains,
        shifts,
        up_bias,
        down_bias,
    ) = params
    (
        slotted,
        normed_self,
        projected,
        self_total,
        self_mixed,
        after_self,
        normed_cross,
        cross_query,
        image_kv,
        cross_total,
        cross_mixed,
        after_cross,
        normed_mlp,
        hidden,
        activated,
    ) = saved_state
    captions = slotted.shape[0] // CAP_LEN
    head_count = D // HEAD_DIM
    grad_branch = grad_slot.astype(jnp.bfloat16)
    grad_down = jnp.einsum("rf,rd->fd", activated, grad_branch, preferred_element_type=jnp.float32)
    grad_down_bias = jnp.sum(grad_slot, axis=0)
    grad_active = jnp.einsum("rd,fd->rf", grad_branch, mat_down, preferred_element_type=jnp.float32)
    grad_hidden = general_gelu_back(hidden, grad_active).astype(jnp.bfloat16)
    grad_up = jnp.einsum("rd,rf->df", normed_mlp, grad_hidden, preferred_element_type=jnp.float32)
    grad_up_bias = jnp.sum(grad_hidden.astype(jnp.float32), axis=0)
    grad_normed = jnp.einsum("rf,df->rd", grad_hidden, mat_up, preferred_element_type=jnp.float32)
    grad_cross_in, grad_gain3, grad_shift3 = general_norm_back(
        after_cross, norm_gains[2], shifts[2], grad_normed
    )
    grad_after_cross = grad_slot + grad_cross_in
    grad_branch = grad_after_cross.astype(jnp.bfloat16)
    grad_cross_out = jnp.einsum(
        "rd,re->de", cross_mixed, grad_branch, preferred_element_type=jnp.float32
    )
    grad_mixed = jnp.einsum(
        "re,de->rd", grad_branch, mat_cross_out, preferred_element_type=jnp.float32
    ).astype(jnp.bfloat16)
    grad_mixed = grad_mixed.reshape(captions, CAP_LEN, head_count, HEAD_DIM)
    grad_query, grad_key, grad_value = general_attention_back(
        cross_query, image_kv[:, :, 0], image_kv[:, :, 1], cross_total, grad_mixed, open_mask
    )
    grad_query = grad_query.reshape(-1, D).astype(jnp.bfloat16)
    grad_kv = jnp.stack([grad_key, grad_value], axis=2).reshape(-1, 2 * D).astype(jnp.bfloat16)
    grad_cross_q = jnp.einsum(
        "rd,re->de", normed_cross, grad_query, preferred_element_type=jnp.float32
    )
    grad_cross_kv = jnp.einsum("iv,ie->ve", image_rows, grad_kv, preferred_element_type=jnp.float32)
    grad_image = jnp.einsum(
        "ie,ve->iv", grad_kv, mat_cross_kv, preferred_element_type=jnp.float32
    ).astype(jnp.bfloat16)
    grad_normed = jnp.einsum(
        "re,de->rd", grad_query, mat_cross_q, preferred_element_type=jnp.float32
    )
    grad_self_in, grad_gain2, grad_shift2 = general_norm_back(
        after_self, norm_gains[1], shifts[1], grad_normed
    )
    grad_after_self = grad_after_cross + grad_self_in
    grad_branch = grad_after_self.astype(jnp.bfloat16)
    grad_out = jnp.einsum("rd,re->de", self_mixed, grad_branch, preferred_element_type=jnp.float32)
    grad_mixed = jnp.einsum(
        "re,de->rd", grad_branch, mat_out, preferred_element_type=jnp.float32
    ).astype(jnp.bfloat16)
    grad_mixed = grad_mixed.reshape(captions, CAP_LEN, head_count, HEAD_DIM)
    grad_query, grad_key, grad_value = general_attention_back(
        projected[:, :, 0], projected[:, :, 1], projected[:, :, 2], self_total, grad_mixed, allowed
    )
    grad_projected = (
        jnp.stack([grad_query, grad_key, grad_value], axis=2)
        .reshape(-1, 3 * D)
        .astype(jnp.bfloat16)
    )
    grad_w_qkv = jnp.einsum(
        "rd,re->de", normed_self, grad_projected, preferred_element_type=jnp.float32
    )
    grad_normed = jnp.einsum(
        "re,de->rd", grad_projected, mat_qkv, preferred_element_type=jnp.float32
    )
    grad_input, grad_gain1, grad_shift1 = general_norm_back(slotted, norm_gains[0], shifts[0], grad_normed)
    grad_input = grad_input + grad_after_self
    grad_small = jnp.concatenate(
        [
            grad_gain1,
            grad_gain2,
            grad_gain3,
            grad_shift1,
            grad_shift2,
            grad_shift3,
            grad_up_bias,
            grad_down_bias,
        ]
    )
    flat_grads = (
        grad_w_qkv.reshape(-1),
        grad_out.reshape(-1),
        grad_cross_q.reshape(-1),
        grad_cross_kv.reshape(-1),
        grad_cross_out.reshape(-1),
        grad_up.reshape(-1),
        grad_down.reshape(-1),
        grad_small,
    )
    return (grad_input, grad_image, flat_grads)


def general_sum_to_owners(flat_grads):
    summed = []
    for grad_vec in flat_grads:
        for axis in ("dp", "fsdp"):
            parts = grad_vec.reshape(lax.axis_size(axis), -1).astype(jnp.bfloat16)
            if axis == "dp":
                parts = grad_vec.reshape(lax.axis_size("dp"), lax.axis_size("fsdp"), -1)
                parts = parts.astype(jnp.bfloat16)
            got = lax.all_to_all(parts, axis, split_axis=0, concat_axis=0, tiled=True)
            grad_vec = jnp.sum(got.astype(jnp.float32), axis=0)
        summed.append(grad_vec)
    return tuple(summed)


def general_device(
    tokens,
    image_tokens,
    caption_lengths,
    arrival_order,
    w_qkv,
    w_out,
    w_cross_q,
    w_cross_kv,
    w_cross_out,
    w_up,
    w_down,
    small_params,
    cotangent,
):
    lengths = caption_lengths[0]
    slot_rows = general_slot_index(lengths, arrival_order[0])
    captions = lengths.shape[0]
    slot_total = captions * CAP_LEN
    arrived, arrived_grad = (
        lax.all_to_all(tokens, "fsdp", split_axis=0, concat_axis=0, tiled=True),
        lax.all_to_all(cotangent, "fsdp", split_axis=0, concat_axis=0, tiled=True),
    )
    slotted = jnp.zeros((slot_total, D), jnp.float32).at[slot_rows].set(arrived.astype(jnp.float32))
    grad_slot = (
        jnp.zeros((slot_total, D), jnp.float32).at[slot_rows].set(arrived_grad.astype(jnp.float32))
    )
    positions = jnp.arange(CAP_LEN, dtype=jnp.int32)
    allowed = (positions[None, :] <= positions[:, None])[None, None] & (
        positions[None, None, None, :] < lengths[:, None, None, None]
    )
    open_mask = jnp.ones((1, 1, 1, 1), jnp.bool_)
    image_rows = image_tokens.reshape(-1, V)
    owned_shards = (w_qkv, w_out, w_cross_q, w_cross_kv, w_cross_out, w_up, w_down, small_params)
    params = general_unpack_params(
        tuple(lax.all_gather(w, ("dp", "fsdp"), axis=0, tiled=True) for w in owned_shards)
    )
    result, saved_state = general_forward(slotted, image_rows, params, allowed, open_mask)
    grad_input, grad_image, flat_grads = general_backward(
        saved_state, grad_slot, image_rows, params, allowed, open_mask
    )
    summed = general_sum_to_owners(flat_grads)
    out_rows = result[slot_rows].astype(jnp.bfloat16)
    grad_rows = grad_input[slot_rows].astype(jnp.bfloat16)
    layer_out, grad_tokens = (
        lax.all_to_all(out_rows, "fsdp", split_axis=0, concat_axis=0, tiled=True),
        lax.all_to_all(grad_rows, "fsdp", split_axis=0, concat_axis=0, tiled=True),
    )
    return (layer_out, grad_tokens, grad_image.reshape(image_tokens.shape)) + tuple(summed)


def solution(mesh):
    dp, fsdp = mesh.shape["dp"], mesh.shape["fsdp"]
    inner, specs_of = on_device, ("dp", "fsdp")
    if fsdp == 4 and dp % 2 == 0 and D % (dp * fsdp * 8) == 0:
        mesh = Mesh(mesh.devices.reshape(dp // 2, 2, 2, 2), AXES)
        specs_of = AXES
    else:
        inner = general_device
    rows, flat, cube = P(specs_of, None), P(specs_of), P(specs_of, None, None)
    return jax.shard_map(
        inner,
        mesh=mesh,
        in_specs=(rows, cube, rows, rows) + (flat,) * 8 + (rows,),
        out_specs=(rows, rows, cube) + (flat,) * 8,
        check_vma=False,
    )
```

```python
import functools

import jax
import jax.numpy as jnp
from jax import lax
from jax.experimental import pallas as pl
from jax.experimental.pallas import tpu as pltpu
from jax.sharding import Mesh
from jax.sharding import PartitionSpec as P

D = 768
HEAD_DIM = 64
FF = 3072
V = 768
IMG = 256
CAP_LEN = 64
LANES = 128
PAIRS = D // LANES
HALF = D // 2
HEADS = 4
WIDE = HEADS * HEAD_DIM
BATCHES = D // WIDE
FOLD = FF // D
GROUP = FOLD * LANES
GROUPS = FF // GROUP
TOKENS_AT = 32
SCALE = HEAD_DIM ** (-0.5)
epsilon = 1e-05
masked_fill = 1e30

BF = jnp.bfloat16
F32 = jnp.float32
AXES = ("z", "x", "y", "c")


def mm(a, b):
    return lax.dot_general(a, b, (((1,), (0,)), ((), ())), preferred_element_type=F32)


def mm_t(a, b):
    return lax.dot_general(a, b, (((1,), (1,)), ((), ())), preferred_element_type=F32)


def t_mm(a, b):
    return lax.dot_general(a, b, (((0,), (0,)), ((), ())), preferred_element_type=F32)


def wide(value):
    return value.astype(F32)


def norm_rows(inputs, gain_vec, shift_vec):
    centred = inputs - jnp.mean(inputs, axis=-1, keepdims=True)
    variance = jnp.mean(centred * centred, axis=-1, keepdims=True)
    return centred * lax.rsqrt(variance + epsilon) * gain_vec + shift_vec


def norm_back(inputs, gain_vec, grad_normed):
    centred = inputs - jnp.mean(inputs, axis=-1, keepdims=True)
    variance = jnp.mean(centred * centred, axis=-1, keepdims=True)
    scale = lax.rsqrt(variance + epsilon)
    unit = centred * scale
    weighted = grad_normed * gain_vec
    grad_in = scale * (
        weighted
        - jnp.mean(weighted, axis=-1, keepdims=True)
        - unit * jnp.mean(weighted * unit, axis=-1, keepdims=True)
    )
    grad_gain = jnp.sum(grad_normed * unit, axis=0, keepdims=True)
    grad_shift = jnp.sum(grad_normed, axis=0, keepdims=True)
    return grad_in, grad_gain, grad_shift


def arrival_pick(arr_ref):
    rows = arr_ref.shape[1]
    place = lax.broadcasted_iota(jnp.int32, (rows, rows), 0)
    return jnp.where(place == arr_ref[...], 1.0, 0.0).astype(BF)


def caption_of(index, lens_ref):
    end = jnp.int32(0)
    found = jnp.zeros_like(index)
    for c in range(lens_ref.shape[1] - 1):
        end = end + lens_ref[0, c]
        found = found + jnp.where(index >= end, 1, 0)
    return found


def slot_pick(lens_ref, rows):
    captions = lens_ref.shape[1]
    shape = (captions * CAP_LEN, rows)
    slot = lax.broadcasted_iota(jnp.int32, shape, 0)
    row = lax.broadcasted_iota(jnp.int32, shape, 1)
    start = jnp.int32(0)
    hit = jnp.zeros(shape, F32)
    for c in range(captions):
        length = lens_ref[0, c]
        inside = slot - c * CAP_LEN
        ok = (inside >= 0) & (inside < length) & (row - start == inside)
        hit = hit + jnp.where(ok, 1.0, 0.0)
        start = start + length
    return hit.astype(BF)


def fold_pick(back):
    source = lax.broadcasted_iota(jnp.int32, (GROUP, GROUP), 1 if back else 0)
    target = lax.broadcasted_iota(jnp.int32, (GROUP, GROUP), 0 if back else 1)
    return jnp.where(target == (source % FOLD) * LANES + source // FOLD, 1.0, 0.0).astype(BF)


def head_mask(rows):
    shape = (HEADS * rows, WIDE)
    head = lax.broadcasted_iota(jnp.int32, shape, 1) // HEAD_DIM
    row = lax.broadcasted_iota(jnp.int32, shape, 0)
    inside = (row >= head * rows) & (row < (head + 1) * rows)
    return jnp.where(inside, 1.0, 0.0).astype(BF)


def stack_heads(block, mask):
    return jnp.concatenate([block] * HEADS, axis=0) * mask


def merge_heads(stacked):
    rows = stacked.shape[0] // HEADS
    head = lax.broadcasted_iota(jnp.int32, (rows, WIDE), 1) // HEAD_DIM
    out = stacked[:rows]
    for n in range(1, HEADS):
        out = jnp.where(head == n, stacked[n * rows : (n + 1) * rows], out)
    return out


def softmax_rows(scores):
    shifted = jnp.exp(scores - jnp.max(scores, axis=-1, keepdims=True))
    return shifted * (1.0 / jnp.sum(shifted, axis=-1, keepdims=True))


def lanes_at(start, width):
    return pl.ds(pl.multiple_of(start, LANES), width)


def pack_kernel(
    me, w_qkv, w_out, w_cross_q, w_cross_kv, w_cross_out, w_up, w_down, small, tokens, cotangent,
    attend, near, core, chip, rows, parts,
):
    height, depth = attend.shape[2], attend.shape[0]
    pieces = HALF // LANES

    def chunk(count, index):
        return rows[pl.ds(index, height, stride=count), :].astype(BF)

    place = 0
    for shard, mats in ((w_qkv, 3), (w_out, 1), (w_cross_q, 1), (w_cross_kv, 2), (w_cross_out, 1)):
        rows[: shard.shape[0], :] = wide(shard[...])
        for mat in range(mats):
            for half in range(2):
                for i in range(pieces):
                    value = chunk(mats * PAIRS, mat * PAIRS + half * pieces + i)
                    at = place + i * LANES
                    for z in range(depth):
                        attend[z, half, :, at : at + LANES] = value
            place += HALF
            if place == 4 * HALF:
                for z in range(depth):
                    for half in range(2):
                        attend[z, half, :, place : place + LANES] = small[...]
                place += LANES
    rows[...] = wide(w_up[...])
    pick = fold_pick(False)
    for t in range(GROUPS):
        group = jnp.concatenate(
            [chunk(FF // LANES, t * FOLD + k) for k in range(FOLD)], axis=1
        )
        folded = mm(group, pick).astype(BF)
        for j in range(FOLD):
            parts[j, :height, t * LANES : (t + 1) * LANES] = folded[
                :, j * LANES : (j + 1) * LANES
            ]
    rows[...] = wide(w_down[...])
    for j in range(FOLD):
        for i in range(PAIRS):
            at = D + i * LANES
            parts[j, :height, at : at + LANES] = chunk(FF // LANES, j * PAIRS + i)
        parts[j, TOKENS_AT : TOKENS_AT + tokens.shape[1], :D] = tokens[j]
        parts[j, TOKENS_AT : TOKENS_AT + tokens.shape[1], D:] = cotangent[j]
    near[...] = parts[part_of(me, 0, 0)]
    core[...] = parts[part_of(me, 0, 1)]
    for c in range(2):
        chip[c] = parts[part_of(me, 1, c)]


def part_of(me, far_y, far_c):
    return lax.bitwise_xor(me[0, 2], far_y) * 2 + lax.bitwise_xor(me[0, 3], far_c)


def spread_kernel(me, arr, near, chip, core, both, hidden, slotted, grad_slot, arrived):
    height, count = hidden.shape[2], arrived.shape[0] // FOLD
    for value, far_y, far_c in (
        (near[...], 0, 0), (chip[0], 1, 0), (core[...], 0, 1), (both[...], 1, 1),
    ):
        index = part_of(me, far_y, far_c)
        for z in range(hidden.shape[0]):
            hidden[z, index] = value[:height]
        at = pl.multiple_of(index * count, 8)
        arrived[pl.ds(at, count), :] = wide(value[TOKENS_AT : TOKENS_AT + count])
    pick = arrival_pick(arr)
    slotted[...] = mm(pick, arrived[:, :D].astype(BF)).astype(BF)
    grad_slot[...] = mm(pick, arrived[:, D:].astype(BF)).astype(BF)


def fill_table(share, me, pieces, flat, table):
    depth, height = pieces.shape[1], pieces.shape[2] // 2
    lane = lax.broadcasted_iota(jnp.int32, (3, LANES), 1)
    flat[...] = jnp.zeros_like(flat)
    for owner in range(8 * depth):
        z, x, y, c = owner // 8, owner // 4 % 2, owner // 2 % 2, owner % 2
        index = lax.bitwise_xor(me[0, 1], x) * 2 + lax.bitwise_xor(me[0, 2], y)
        value = wide(pieces[index, z])[c * height : c * height + 3, :]
        row, shift = divmod(owner * share, LANES)
        if shift == 0:
            flat[row : row + 3, :] += value
        else:
            moved = pltpu.roll(value, shift, axis=1)
            flat[row : row + 3, :] += jnp.where(lane >= shift, moved, 0.0)
            flat[row + 1 : row + 4, :] += jnp.where(lane < shift, moved, 0.0)
    for n in range(table.shape[0] * PAIRS):
        row, lanes = n // PAIRS, slice(n % PAIRS * LANES, (n % PAIRS + 1) * LANES)
        table[row : row + 1, lanes] = flat[n : n + 1, :]


def depth_sum_kernel(me, got, near, core, chip, total):
    height = near.shape[0]
    value = wide(got[0])
    for z in range(1, got.shape[0]):
        value = value + wide(got[z])
    total[...] = value

    def part(far_y, far_c):
        at = pl.multiple_of(part_of(me, far_y, far_c) * height, 8)
        return total[pl.ds(at, height), :].astype(BF)

    near[...] = part(0, 0)
    core[...] = part(0, 1)
    for c in range(2):
        chip[c] = part(1, c)


def unpack_hidden_kernel(me, near, chip, core, both, up, down, got):
    for value, far_y, far_c in (
        (near[...], 0, 0), (chip[0], 1, 0), (core[...], 0, 1), (both[...], 1, 1),
    ):
        got[part_of(me, far_y, far_c)] = value
    height = got.shape[1]
    chunks = FF // LANES
    pick = fold_pick(True)
    for t in range(GROUPS):
        group = jnp.concatenate(
            [got[j, :, t * LANES : (t + 1) * LANES] for j in range(FOLD)], axis=1
        )
        natural = mm(group, pick)
        for k in range(FOLD):
            up[pl.ds(t * FOLD + k, height, stride=chunks), :] = natural[
                :, k * LANES : (k + 1) * LANES
            ]
    for j in range(FOLD):
        for i in range(PAIRS):
            at = D + i * LANES
            down[pl.ds(j * PAIRS + i, height, stride=chunks), :] = wide(
                got[j, :, at : at + LANES]
            )


def unpack_halves_kernel(got, *outs):
    depth, height = got.shape[0], got.shape[2]
    parts = HALF // LANES
    place = 0
    for out in outs:
        chunks = out.shape[0] // height
        for mat in range(chunks // PAIRS):
            for half in range(2):
                for i in range(parts):
                    at = place + i * LANES
                    total = wide(got[0, half, :, at : at + LANES])
                    for z in range(1, depth):
                        total = total + wide(got[z, half, :, at : at + LANES])
                    index = mat * PAIRS + half * parts + i
                    out[pl.ds(index, height, stride=chunks), :] = total
            place += HALF


class Fetch:
    def __init__(self, sems):
        self.sems = sems
        self.used = 0

    def start(self, source, target):
        copy = pltpu.make_async_copy(source, target, self.sems.at[self.used])
        self.used += 1
        copy.start()
        return copy

    def columns(self, pieces, me, piece_at, target, target_at):
        copies = []
        for index, piece in enumerate(pieces):
            half = lax.bitwise_xor(me[0, 3], index // 4)
            x = lax.bitwise_xor(me[0, 1], index // 2 % 2)
            y = lax.bitwise_xor(me[0, 2], index % 2)
            copies.append(
                self.start(
                    piece.at[:, :, pl.ds(piece_at, HALF)],
                    target.at[:, x, y, :, lanes_at(target_at + half * HALF, HALF)],
                )
            )
        return copies


def wait(copies):
    for copy in copies:
        copy.wait()


def matrix(ref):
    shape = ref.shape
    return ref[...].reshape(shape[0] * shape[1] * shape[2] * shape[3], shape[4])


def forward_kernel(share, lens, me, slotted, img, *refs):
    pieces_a, pieces_b = refs[:8], refs[8:16]
    (
        table,
        projected, probs_self, saved, after_self, after_cross, normed_mlp, query_slots,
        kv_out, probs_out, kv, probs_cross, w_qkv, w_out, w_cq, w_kv, w_co, mixed_slots, small, flat, sems,
    ) = refs[16:]
    fetch = Fetch(sems)
    got_small = [
        fetch.start(pieces_a[n].at[:, :, pl.ds(4 * HALF, LANES)], small.at[n]) for n in range(4)
    ]
    got_qkv = []
    for mat in range(3):
        got_qkv += fetch.columns(pieces_a, me, mat * HALF, w_qkv, mat * D)
    got_out = fetch.columns(pieces_a, me, 3 * HALF, w_out, 0)
    got_cq = fetch.columns(pieces_b, me, 0, w_cq, 0)
    got_kv = fetch.columns(pieces_b, me, HALF, w_kv, 0)
    got_kv += fetch.columns(pieces_b, me, 2 * HALF, w_kv, D)
    got_co = fetch.columns(pieces_b, me, 3 * HALF, w_co, 0)
    rows = slotted.shape[0]
    wait(got_small)
    fill_table(share, me, small, flat, table)
    saved[:, :D] = norm_rows(wide(slotted[...]), table[0:1, :], table[3:4, :]).astype(BF)
    wait(got_qkv)
    projected[...] = mm(saved[:, :D], matrix(w_qkv)).astype(BF)
    query_at = lax.broadcasted_iota(jnp.int32, (rows, rows), 0)
    key_at = lax.broadcasted_iota(jnp.int32, (rows, rows), 1)
    same = caption_of(query_at, lens) == caption_of(key_at, lens)
    block = jnp.where(same & (key_at <= query_at), 0.0, -masked_fill)
    barred = jnp.concatenate([block] * HEADS, axis=0)
    mask = head_mask(rows)
    for n in range(BATCHES):
        query, key, value = (
            projected[:, m * D + n * WIDE : m * D + (n + 1) * WIDE] for m in range(3)
        )
        scores = mm_t(stack_heads(query, mask), key) * SCALE + barred
        weights_low = softmax_rows(scores).astype(BF)
        probs_self[n] = weights_low
        saved[:, D + n * WIDE : D + (n + 1) * WIDE] = merge_heads(
            mm(weights_low, value)
        ).astype(BF)
    wait(got_out)
    state = wide(slotted[...]) + mm(saved[:, D : 2 * D], matrix(w_out))
    after_self[...] = state
    low = norm_rows(state, table[1:2, :], table[4:5, :]).astype(BF)
    saved[:, 2 * D : 3 * D] = low
    wait(got_cq)
    pick = slot_pick(lens, rows)
    query_slots[...] = mm(pick, mm(low, matrix(w_cq)).astype(BF)).astype(BF)
    wait(got_kv)
    kv_mat = matrix(w_kv)
    mask = head_mask(CAP_LEN)
    sent = []
    for c in range(lens.shape[1]):
        slots = slice(c * CAP_LEN, (c + 1) * CAP_LEN)
        images = slice(c * IMG, (c + 1) * IMG)
        kv[images, :] = mm(img[images, :], kv_mat).astype(BF)
        for n in range(BATCHES):
            cols = slice(n * WIDE, (n + 1) * WIDE)
            query = stack_heads(query_slots[slots, cols], mask)
            weights_low = softmax_rows(mm_t(query, kv[images, cols]) * SCALE).astype(BF)
            probs_cross[c * BATCHES + n] = weights_low
            value = kv[images, D + n * WIDE : D + (n + 1) * WIDE]
            mixed_slots[slots, cols] = merge_heads(mm(weights_low, value)).astype(BF)
        batch = slice(c * BATCHES, (c + 1) * BATCHES)
        sent.append(fetch.start(kv.at[images], kv_out.at[images]))
        sent.append(fetch.start(probs_cross.at[batch], probs_out.at[batch]))
    low = t_mm(pick, mixed_slots[...]).astype(BF)
    saved[:, 3 * D :] = low
    wait(got_co)
    state = after_self[...] + mm(low, matrix(w_co))
    after_cross[...] = state
    normed_mlp[...] = norm_rows(state, table[2:3, :], table[5:6, :]).astype(BF)
    wait(sent)


def put_small(small, row, value):
    for k in range(PAIRS):
        at = row * PAIRS + k
        small[at : at + 1, :] = value[:, k * LANES : (k + 1) * LANES]


def own_part(value, me):
    part = me[0, 2] * 2 + me[0, 3]
    out = value[:, :LANES]
    for j in range(1, FOLD):
        out = jnp.where(part == j, value[:, j * LANES : (j + 1) * LANES], out)
    return out


def mlp_kernel(me, table, *refs):
    inputs, grads, pieces = refs[:4], refs[4:8], refs[8:10]
    (
        grad_near, grad_keep, grad_send, out_near, out_keep, out_send, active, grad_hidden, small,
        all_in, all_grad, w_up, w_down, sems,
    ) = refs[10:]
    fetch = Fetch(sems)
    got_up, got_down = [], []
    for index in range(2):
        x = lax.bitwise_xor(me[0, 1], index)
        got_up.append(fetch.start(pieces[index].at[:, :, pl.ds(0, D)], w_up.at[:, x]))
        got_down.append(fetch.start(pieces[index].at[:, :, pl.ds(D, D)], w_down.at[:, x]))
    rows = inputs[0].shape[0]
    for n in range(4):
        all_in[n * rows : (n + 1) * rows, :] = inputs[n][...]
        all_grad[n * rows : (n + 1) * rows, :] = grads[n][...]
    bias = [
        table[6 + n // PAIRS : 7 + n // PAIRS, n % PAIRS * LANES : (n % PAIRS + 1) * LANES]
        for n in range(FF // LANES)
    ]
    bias = jnp.concatenate(
        [jnp.concatenate(bias[t * FOLD : (t + 1) * FOLD], axis=1) for t in range(GROUPS)], axis=0
    )
    bias = own_part(mm(bias.astype(BF), fold_pick(False)), me)
    bias = jnp.concatenate([bias[t : t + 1, :] for t in range(GROUPS)], axis=1)
    wait(got_up)
    up_mat = w_up[...].reshape(D, D)
    hidden = mm(all_in[...], up_mat) + bias
    half = 0.5 + 0.5 * lax.erf(hidden * (0.5**0.5))
    act = (hidden * half).astype(BF)
    active[...] = act
    slope = half + hidden * (jnp.exp(hidden * hidden * -0.5) * 0.3989422804014327)
    wait(got_down)
    down_mat = w_down[...].reshape(D, D)
    grad_hid = (mm_t(all_grad[...], down_mat) * slope).astype(BF)
    grad_hidden[...] = grad_hid
    grad_part = mm_t(grad_hid, up_mat)
    out_part = mm(act, down_mat)
    for y, grad_own, out_own in ((0, grad_near, out_near), (1, grad_keep, out_keep)):
        own = slice(2 * y * rows, (2 * y + 1) * rows)
        other = slice((2 * y + 1) * rows, (2 * y + 2) * rows)
        grad_own[...] = grad_part[own]
        out_own[...] = out_part[own]
        grad_send[y] = grad_part[other].astype(BF)
        out_send[y] = out_part[other].astype(BF)
    sums = jnp.sum(wide(grad_hid), axis=0, keepdims=True).astype(BF)
    sums = jnp.concatenate(
        [sums[:, t * LANES : (t + 1) * LANES] for t in range(GROUPS)] + [sums[:, :LANES]] * 2,
        axis=0,
    )
    part = me[0, 2] * 2 + me[0, 3]
    spread = jnp.concatenate(
        [jnp.where(part == j, sums, jnp.zeros_like(sums)) for j in range(FOLD)], axis=1
    )
    natural = mm(spread, fold_pick(True))
    small[...] = jnp.zeros_like(small)
    for n in range(FF // LANES):
        at = 6 * PAIRS + n
        small[at : at + 1, :] = natural[
            n // FOLD : n // FOLD + 1, n % FOLD * LANES : (n % FOLD + 1) * LANES
        ]
    put_small(small, 10, jnp.sum(wide(grads[0][...]), axis=0, keepdims=True))


def hidden_grad_kernel(me, *refs):
    normed, grad_slot = refs[:4], refs[4:8]
    active, grad_hidden, keep_up, send_up, keep_down, send_down = refs[8:]
    depth, height = keep_up.shape[:2]
    for keep, send, left, right in (
        (keep_up, send_up, [r[...] for r in normed], [grad_hidden[...]]),
        (keep_down, send_down, [active[...]], [r[...] for r in grad_slot]),
    ):
        grads = t_mm(jnp.concatenate(left, axis=0), jnp.concatenate(right, axis=0))
        for z in range(depth):
            low = grads[2 * z * height : (2 * z + 1) * height, :]
            high = grads[(2 * z + 1) * height : (2 * z + 2) * height, :]
            keep[z] = jnp.where(me[0, 1] == 0, low, high).astype(BF)
            send[z] = jnp.where(me[0, 1] == 0, high, low).astype(BF)


def combine_kernel(keep, far, out):
    out[...] = (keep[...] + wide(far[1])).astype(BF)


def cross_back_kernel(
    lens, me, grad_near, grad_core, grad_far, after_cross, grad_slot, probs_in, query_slots, kv_in,
    after_self, table, small_in, *refs,
):
    pieces = refs[:8]
    (
        grad_state, small, half_keep, half_send, keep_out, send_out,
        w_co, w_cq, mixed_slots, query_grads, grad_kv, kv_keep, kv_send, kv, probs, sems,
    ) = refs[8:]
    fetch = Fetch(sems)
    got_co = fetch.columns(pieces, me, 3 * HALF, w_co, 0)
    got_kv = [fetch.start(kv_in, kv), fetch.start(probs_in, probs)]
    got_cq = fetch.columns(pieces, me, 0, w_cq, 0)
    rows = after_self.shape[0]
    sent = []
    halves = ((0, half_keep, kv_keep), (1, half_send, kv_send))
    small[...] = small_in[...]
    grad_in, grad_gain, grad_shift = norm_back(
        after_cross[...],
        table[2:3, :],
        grad_near[...] + wide(grad_core[0]) + wide(grad_far[...]),
    )
    put_small(small, 2, grad_gain)
    put_small(small, 5, grad_shift)
    grad_after = wide(grad_slot[...]) + grad_in
    grad_state[...] = grad_after
    pick = slot_pick(lens, rows)
    wait(got_co)
    query_grads[:rows, :] = grad_after.astype(BF)
    mixed_slots[...] = mm(pick, mm_t(query_grads[:rows, :], matrix(w_co)).astype(BF)).astype(BF)
    for rel, half_out, _ in halves:
        at = lax.bitwise_xor(me[0, 3], rel) * HALF
        half_out[:, HALF : 2 * HALF] = query_grads[:rows, lanes_at(at, HALF)]
    mask = head_mask(CAP_LEN)
    wait(got_kv)
    for c in range(lens.shape[1]):
        slots = slice(c * CAP_LEN, (c + 1) * CAP_LEN)
        images = slice(c * IMG, (c + 1) * IMG)
        for n in range(BATCHES):
            cols = slice(n * WIDE, (n + 1) * WIDE)
            value_cols = slice(D + n * WIDE, D + (n + 1) * WIDE)
            grad_mixed = stack_heads(mixed_slots[slots, cols], mask)
            query = stack_heads(query_slots[slots, cols], mask)
            weights_low = probs[c * BATCHES + n]
            attn = wide(weights_low)
            grad_weights = mm_t(grad_mixed, kv[images, value_cols])
            centre = jnp.sum(attn * grad_weights, axis=-1, keepdims=True)
            grad_scores = (attn * (grad_weights - centre)).astype(BF)
            query_grads[slots, cols] = (
                merge_heads(mm(grad_scores, kv[images, cols])) * SCALE
            ).astype(BF)
            grad_kv[images, cols] = (t_mm(grad_scores, query) * SCALE).astype(BF)
            grad_kv[images, value_cols] = t_mm(weights_low, grad_mixed).astype(BF)
        for rel, _, kv_half in halves:
            at = lax.bitwise_xor(me[0, 3], rel) * HALF
            kv_half[images, :HALF] = grad_kv[images, lanes_at(at, HALF)]
            kv_half[images, HALF:] = grad_kv[images, lanes_at(at + D, HALF)]
        sent.append(fetch.start(kv_send.at[images], send_out.at[images]))
        sent.append(fetch.start(kv_keep.at[images], keep_out.at[images]))
    mixed_slots[:rows, :] = t_mm(pick, query_grads[...]).astype(BF)
    wait(got_cq)
    grad_in, grad_gain, grad_shift = norm_back(
        after_self[...], table[1:2, :], mm_t(mixed_slots[:rows, :], matrix(w_cq))
    )
    put_small(small, 1, grad_gain)
    put_small(small, 4, grad_shift)
    grad_after = grad_state[...] + grad_in
    grad_state[...] = grad_after
    query_grads[:rows, :] = grad_after.astype(BF)
    for rel, half_out, _ in halves:
        at = lax.bitwise_xor(me[0, 3], rel) * HALF
        half_out[:, :HALF] = mixed_slots[:rows, lanes_at(at, HALF)]
        half_out[:, 2 * HALF :] = query_grads[:rows, lanes_at(at, HALF)]
    wait(sent)


def self_back_kernel(me, grad_state, probs, projected, slotted, table, small_in, *refs):
    pieces = refs[:8]
    (
        grad_rows, small, keep, send,
        w_out, w_qkv, mixed, grad_projected, sems,
    ) = refs[8:]
    fetch = Fetch(sems)
    got_out = fetch.columns(pieces, me, 3 * HALF, w_out, 0)
    got_qkv = []
    for mat in range(3):
        got_qkv += fetch.columns(pieces, me, mat * HALF, w_qkv, mat * D)
    rows = slotted.shape[0]
    wait(got_out)
    mixed[...] = mm_t(grad_state[...].astype(BF), matrix(w_out)).astype(BF)
    mask = head_mask(rows)
    for n in range(BATCHES):
        cols, key_cols, value_cols = (
            slice(m * D + n * WIDE, m * D + (n + 1) * WIDE) for m in range(3)
        )
        grad_mixed = stack_heads(mixed[:, cols], mask)
        query = stack_heads(projected[:, cols], mask)
        weights_low = probs[n]
        attn = wide(weights_low)
        grad_weights = mm_t(grad_mixed, projected[:, value_cols])
        centre = jnp.sum(attn * grad_weights, axis=-1, keepdims=True)
        grad_scores = (attn * (grad_weights - centre)).astype(BF)
        grad_projected[:, cols] = (
            merge_heads(mm(grad_scores, projected[:, key_cols])) * SCALE
        ).astype(BF)
        grad_projected[:, key_cols] = (t_mm(grad_scores, query) * SCALE).astype(BF)
        grad_projected[:, value_cols] = t_mm(weights_low, grad_mixed).astype(BF)
    for mat in range(3):
        for rel, out in ((0, keep), (1, send)):
            at = lax.bitwise_xor(me[0, 3], rel) * HALF + mat * D
            out[:, mat * HALF : (mat + 1) * HALF] = grad_projected[:, lanes_at(at, HALF)]
    wait(got_qkv)
    grad_in, grad_gain, grad_shift = norm_back(
        wide(slotted[...]), table[0:1, :], mm_t(grad_projected[...], matrix(w_qkv))
    )
    grad_slotted = (grad_state[...] + grad_in).astype(BF)
    grad_rows[...] = grad_slotted
    small[...] = small_in[...]
    put_small(small, 0, grad_gain)
    put_small(small, 3, grad_shift)


def put_quadrants(grads, me, outs, at, first):
    depth, height = outs[0].shape[1:3]
    width = grads.shape[1]
    for i, out in enumerate(outs):
        for j in range(2):
            far_x, far_y = (i, j) if first == "x" else (j, i)
            x, y = lax.bitwise_xor(me[0, 1], far_x), lax.bitwise_xor(me[0, 2], far_y)
            for z in range(depth):
                low = pl.multiple_of(((z * 2 + x) * 2 + y) * height, 16)
                out[j, z, :, at : at + width] = grads[pl.ds(low, height), :].astype(BF)


def half_grads(pieces, me, outs, grads, first, at=0):
    for left, far_left, right, far_right in pieces:
        width = right.shape[1]
        grads[:, :width] = t_mm(left, right) + t_mm(far_left, far_right)
        put_quadrants(grads.at[:, :width], me, outs, at, first)
        at += width


def cross_grad_kernel(
    me, saved, saved_far, half, half_far, img_in, img_far_in, kv_in, kv_far_in, *refs
):
    grads, sems = refs[4], refs[9]
    fetch = Fetch(sems)
    sources = (img_in, img_far_in, kv_in, kv_far_in)
    copies = [fetch.start(source, target) for source, target in zip(sources, refs[5:9])]
    part = lambda ref, n, width: ref[:, n * width : (n + 1) * width]
    piece = lambda left, right: (
        part(saved, left, D), part(saved_far, left, D),
        part(half, right, HALF), part(half_far, right, HALF),
    )
    half_grads([piece(3, 1), piece(1, 2)], me, refs[2:4], grads, "y")
    half_grads([piece(2, 0)], me, refs[:2], grads, "x")
    wait(copies)
    half_grads([tuple(ref[...] for ref in refs[5:9])], me, refs[:2], grads, "x", HALF)


def owner_rows(small, blocks, share):
    height = blocks.shape[0] // (small.shape[0] * LANES // share)
    lane = lax.broadcasted_iota(jnp.int32, (3, LANES), 1)
    blocks[...] = jnp.zeros_like(blocks)
    table = jnp.concatenate([small[...], jnp.zeros((6, LANES), F32)], axis=0)
    for owner in range(small.shape[0] * LANES // share):
        row, shift = divmod(owner * share, LANES)
        if shift == 0:
            value = table[row : row + 3]
        else:
            moved = pltpu.roll(table[row : row + 4], LANES - shift, axis=1)
            value = jnp.where(lane < LANES - shift, moved[:3], moved[1:4])
        blocks[owner * height : owner * height + 3, :] = value


def self_grad_kernel(share, me, saved, saved_far, half, half_far, small, *refs):
    first, second, grads = refs[:2], refs[2:4], refs[4]
    own, far = saved[:, :D], saved_far[:, :D]
    half_grads([(own, far, half[:, :D], half_far[:, :D])], me, first, grads, "y")
    half_grads([(own, far, half[:, D:], half_far[:, D:])], me, second, grads, "x")
    blocks = grads.at[:, :LANES]
    owner_rows(small, blocks, share)
    put_quadrants(blocks, me, second, HALF, "x")


def unpack_self_kernel(got, qkv, small):
    depth = got.shape[0]
    unpack_halves_kernel(got, qkv)
    total = jnp.zeros((8, LANES), F32)
    for z in range(depth):
        for c in range(2):
            total = total + wide(got[z, c, :8, 3 * HALF :])
    small[...] = total


def return_kernel(
    me, arr, after_cross, table, out_near, out_core, out_far, grad_rows, near, core, chip, rows
):
    pick = arrival_pick(arr)
    count = near.shape[0]
    result = after_cross[...] + out_near[...] + wide(out_core[0]) + wide(out_far[...])
    result = result + table[10:11, :]
    rows[:, :D] = t_mm(pick, result.astype(BF))
    rows[:, D:] = t_mm(pick, grad_rows[...])

    def part(far_y, far_c):
        at = pl.multiple_of(part_of(me, far_y, far_c) * count, 8)
        return rows[pl.ds(at, count), :].astype(BF)

    near[...] = part(0, 0)
    core[...] = part(0, 1)
    for c in range(2):
        chip[c] = part(1, c)


def collect_kernel(me, near, chip, core, both, layer_out, grad_tokens):
    for value, far_y, far_c in ((near[...], 0, 0), (chip[0], 1, 0), (core[...], 0, 1), (both[...], 1, 1)):
        index = part_of(me, far_y, far_c)
        layer_out[index] = value[:, :D]
        grad_tokens[index] = value[:, D:]


def image_grad_kernel(kv_keep, kv_send, *refs):
    me, pieces = refs[0], refs[1:9]
    grad_image, w_kv, sems = refs[9:]
    fetch = Fetch(sems)
    copies = []
    for index, piece in enumerate(pieces):
        x = lax.bitwise_xor(me[0, 1], index // 2 % 2)
        y = lax.bitwise_xor(me[0, 2], index % 2)
        copies.append(
            fetch.start(piece.at[:, :, pl.ds(HALF, D)], w_kv.at[index // 4, :, x, y])
        )
    wait(copies)
    near, far = w_kv[0].reshape(D, D), w_kv[1].reshape(D, D)
    for c in range(kv_keep.shape[0] // IMG):
        rows = pl.ds(c * IMG, IMG)
        grad_image[rows, :] = (mm_t(kv_keep[rows, :], near) + mm_t(kv_send[rows, :], far)).astype(
            BF
        )


def add_kernel(counts, *refs):
    out = refs[-1]
    first = at = 0
    for count in counts:
        total = wide(refs[first][...])
        for ref in refs[first + 1 : first + count]:
            total = total + wide(ref[...])
        width = total.shape[-1]
        out[:, :, at : at + width] = total.astype(BF)
        first, at = first + count, at + width


VM = pl.BlockSpec(memory_space=pltpu.VMEM)
SM = pl.BlockSpec(memory_space=pltpu.SMEM)
HB = pl.BlockSpec(memory_space=pl.ANY)


def run(kernel, outs, specs, scratch, *args, mib=58, copied=0):
    return pl.pallas_call(
        kernel,
        out_shape=[jax.ShapeDtypeStruct(s, t) for s, t in outs],
        in_specs=specs,
        out_specs=[VM] * (len(outs) - copied) + [HB] * copied,
        scratch_shapes=scratch,
        compiler_params=pltpu.CompilerParams(vmem_limit_bytes=mib * 2**20),
        name=(kernel.func if isinstance(kernel, functools.partial) else kernel).__name__,
    )(*args)


def add_up(*sums):
    args, specs, width = [], [], 0
    for terms in sums:
        for term in terms:
            array, index = term if isinstance(term, tuple) else (term, None)
            depth, height, last = array.shape[-3:]
            if index is None:
                specs.append(pl.BlockSpec((1, height, last), lambda z: (z, 0, 0)))
            else:
                specs.append(
                    pl.BlockSpec((None, 1, height, last), lambda z, i=index: (i, z, 0, 0))
                )
            args.append(array)
        width += last
    return pl.pallas_call(
        functools.partial(add_kernel, [len(terms) for terms in sums]),
        grid=(depth,),
        out_shape=jax.ShapeDtypeStruct((depth, height, width), BF),
        in_specs=specs,
        out_specs=pl.BlockSpec((1, height, width), lambda z: (z, 0, 0)),
        compiler_params=pltpu.CompilerParams(vmem_limit_bytes=16 * 2**20),
        name="add_kernel",
    )(*args)


def flip(value, axis):
    return lax.ppermute(value, axis, [(0, 1), (1, 0)])


def swap_all(value, axes):
    return lax.all_to_all(value, axes, split_axis=0, concat_axis=0, tiled=True)


def tie(*values):
    return lax.optimization_barrier(values)


def on_device(
    tokens,
    image_tokens,
    caption_lengths,
    arrival_order,
    w_qkv,
    w_out,
    w_cross_q,
    w_cross_kv,
    w_cross_out,
    w_up,
    w_down,
    small_params,
    cotangent,
):
    depth = lax.axis_size("z")
    height = D // (8 * depth)
    rows = tokens.shape[0]
    captions = caption_lengths.shape[1]
    slots = captions * CAP_LEN
    images = captions * IMG
    lens, arr = caption_lengths, arrival_order
    me = jnp.stack([lax.axis_index(a) for a in AXES]).astype(jnp.int32).reshape(1, 4)
    vmem = pltpu.VMEM
    sems = lambda n: pltpu.SemaphoreType.DMA((n,))
    shards = (w_qkv, w_out, w_cross_q, w_cross_kv, w_cross_out, w_up, w_down)

    part = ((TOKENS_AT + 48, 2 * D), BF)
    share = small_params.shape[0]
    small = jnp.zeros((height * LANES,), BF).at[:share].set(small_params).reshape(height, LANES)
    attend, near, core, chip = run(
        pack_kernel,
        [((depth, 2, height, 8 * HALF + LANES), BF), part, part, ((2,) + part[0], BF)],
        [SM] + [VM] * 10,
        [vmem((w_up.shape[0] // LANES, LANES), F32), vmem((FOLD,) + part[0], BF)],
        me,
        *(w.reshape(-1, LANES) for w in shards),
        small,
        tokens.reshape(FOLD, -1, D),
        cotangent.reshape(FOLD, -1, D),
    )
    attend = swap_all(attend.reshape(2 * depth, height, -1), ("z", "c"))
    attend = attend.reshape(depth, 2 * height, -1)
    chip = flip(chip, "y")
    hidden, slotted, grad_slot = run(
        spread_kernel,
        [((depth, FOLD, height, 2 * D), BF), ((rows, D), BF), ((rows, D), BF)],
        [SM] + [VM] * 5,
        [vmem((rows, 2 * D), F32)],
        me, arr, near, chip, flip(core, "c"), flip(chip[1], "c"),
    )

    def group_rows(value):
        far = flip(value, "y")
        return (value, flip(value, "c"), far, flip(far, "c"))

    grad_slots = group_rows(grad_slot)
    img = image_tokens.reshape(images, V)
    img_far = flip(img, "c")
    hidden, attend, grad_slots, img_far = tie(hidden, attend, grad_slots, img_far)
    wide_a = 4 * HALF + LANES
    a, b = attend[:, :, :wide_a], attend[:, :, wide_a:]
    ax, by, ay, bx = flip(a, "x"), flip(b, "y"), flip(a, "y"), flip(b, "x")
    hidden = swap_all(hidden.reshape(depth, FOLD * height, 2 * D), "z")
    far_a, far_b = flip(a, "c"), flip(b, "c")
    a, b, ax, by, ay, bx, far_a, far_b = tie(a, b, ax, by, ay, bx, far_a, far_b)
    axy, byx = flip(ax, "y"), flip(by, "x")
    near = (a, ay, ax, b, by, bx)
    far = tuple(flip(p, "c") for p in (ay, ax, by, bx))
    axy, byx, hidden, far = tie(axy, byx, hidden, far)
    pieces_a = near[:3] + (axy, far_a) + far[:2] + (flip(axy, "c"),)
    pieces_b = near[3:] + (byx, far_b) + far[2:] + (flip(byx, "c"),)
    hidden, pieces_a, pieces_b = tie(hidden, pieces_a, pieces_b)
    hidden_far = flip(hidden, "x")

    weight_shape = lambda n: vmem((depth, 2, 2, 2 * height, n * D), BF)
    (
        table, projected, probs_self, saved, after_self, after_cross, normed_mlp, query_slots, kv,
        probs_cross,
    ) = run(
        functools.partial(forward_kernel, share),
        [
            ((8 * depth * share // D, D), F32),
            ((rows, 3 * D), BF),
            ((BATCHES, HEADS * rows, rows), BF),
            ((rows, 4 * D), BF),
            ((rows, D), F32),
            ((rows, D), F32),
            ((rows, D), BF),
            ((slots, D), BF),
            ((images, 2 * D), BF),
            ((captions * BATCHES, HEADS * CAP_LEN, IMG), BF),
        ],
        [SM, SM] + [VM] * 2 + [HB] * 16,
        [
            vmem((images, 2 * D), BF),
            vmem((captions * BATCHES, HEADS * CAP_LEN, IMG), BF),
            weight_shape(3),
            weight_shape(1),
            weight_shape(1),
            weight_shape(2),
            weight_shape(1),
            vmem((slots, D), BF),
            vmem((4, depth, 2 * height, LANES), BF),
            vmem((72, LANES), F32),
            sems(68 + 2 * captions),
        ],
        lens, me, slotted, img, *pieces_a, *pieces_b,
        copied=2,
    )
    inputs = group_rows(normed_mlp)
    small_shape = ((11 * PAIRS, LANES), F32)
    saved_far = flip(saved, "c")
    (
        grad_near, grad_keep, grad_send, out_near, out_keep, out_send, active, grad_hidden, small,
    ) = run(
        mlp_kernel,
        [
            ((rows, D), F32),
            ((rows, D), F32),
            ((2, rows, D), BF),
            ((rows, D), F32),
            ((rows, D), F32),
            ((2, rows, D), BF),
            ((4 * rows, D), BF),
            ((4 * rows, D), BF),
            small_shape,
        ],
        [SM] + [VM] * 9 + [HB] * 2,
        [
            vmem((4 * rows, D), BF),
            vmem((4 * rows, D), BF),
            vmem((depth, 2, FOLD * height, D), BF),
            vmem((depth, 2, FOLD * height, D), BF),
            sems(4),
        ],
        me, table, *inputs, *grad_slots,
        hidden, hidden_far,
    )

    def owned(value, parts, axes):
        got = swap_all(value.reshape(parts * depth, height, -1), axes)
        return got.reshape(depth, parts, height, -1)

    flat = lambda n: ((height * n * PAIRS, LANES), F32)

    def combined(keep, far):
        return run(combine_kernel, [((rows, D), BF)], [VM] * 2, [], keep, far, mib=16)[0]

    grad_core = flip(grad_send, "c")
    grad_far = flip(combined(grad_keep, grad_core), "y")
    keep_up, send_up, keep_down, send_down = run(
        hidden_grad_kernel,
        [((depth, FOLD * height, D), BF)] * 4,
        [SM] + [VM] * 10,
        [],
        me, *inputs, *grad_slots, active, grad_hidden,
    )
    grad_far, send_up, send_down, saved_far, out_send = tie(
        grad_far, send_up, send_down, saved_far, out_send
    )
    far_up, far_down = flip(send_up, "x"), flip(send_down, "x")
    out_core = flip(out_send, "c")
    grad_state, small, half_keep, half_send, kv_keep, kv_send = run(
        cross_back_kernel,
        [
            ((rows, D), F32),
            small_shape,
            ((rows, 3 * HALF), BF),
            ((rows, 3 * HALF), BF),
            ((images, D), BF),
            ((images, D), BF),
        ],
        [SM, SM] + [VM] * 5 + [HB, VM, HB] + [VM] * 3 + [HB] * 8,
        [
            weight_shape(1),
            weight_shape(1),
            vmem((slots, D), BF),
            vmem((slots, D), BF),
            vmem((images, 2 * D), BF),
            vmem((images, D), BF),
            vmem((images, D), BF),
            vmem((images, 2 * D), BF),
            vmem((captions * BATCHES, HEADS * CAP_LEN, IMG), BF),
            sems(18 + 2 * captions),
        ],
        lens, me, grad_near, grad_core, grad_far, after_cross, grad_slot, probs_cross, query_slots,
        kv, after_self, table, small, *pieces_b,
        copied=2,
    )
    far_up, grad_state, half_send, kv_send, out_core = tie(
        far_up, grad_state, half_send, kv_send, out_core
    )
    half_far, kv_far = flip(half_send, "c"), flip(kv_send, "c")
    out_far = flip(combined(out_keep, out_core), "y")
    block = lambda n: ((2, depth, 2 * height, n), BF)
    kv_0, kv_1, mix_0, mix_1 = run(
        cross_grad_kernel,
        [block(3 * HALF)] * 2 + [block(2 * HALF)] * 2,
        [SM] + [VM] * 4 + [HB] * 4,
        [vmem((D, D), F32)] + [vmem((images, D), BF)] * 4 + [sems(4)],
        me, saved, saved_far, half_keep, half_far, img, img_far, kv_keep, kv_far,
    )
    kv_0, kv_1, mix_0, mix_1, grad_state, out_far, far_down = tie(
        kv_0, kv_1, mix_0, mix_1, grad_state, out_far, far_down
    )
    kv_1, mix_1 = flip(kv_1, "x"), flip(mix_1, "y")
    grad_rows, small, self_keep, self_send = run(
        self_back_kernel,
        [
            ((rows, D), BF),
            small_shape,
            ((rows, 3 * HALF), BF),
            ((rows, 3 * HALF), BF),
        ],
        [SM] + [VM] * 6 + [HB] * 8,
        [
            weight_shape(1),
            weight_shape(3),
            vmem((rows, D), BF),
            vmem((rows, 3 * D), BF),
            sems(32),
        ],
        me, grad_state, probs_self, projected, slotted, table, small, *pieces_a,
    )
    self_far = flip(self_send, "c")
    hidden_got = swap_all(add_up((keep_up, far_up), (keep_down, far_down)), "z")
    q_0, q_1, v_0, v_1 = run(
        functools.partial(self_grad_kernel, share),
        [block(D)] * 2 + [block(HALF + LANES)] * 2,
        [SM] + [VM] * 5,
        [vmem((D, D), F32)],
        me, saved, saved_far, self_keep, self_far, small,
    )
    q_1, v_1, kv_1, mix_1, grad_rows = tie(q_1, v_1, kv_1, mix_1, grad_rows)
    kv_2 = flip(add_up(((kv_0, 1), (kv_1, 1))), "y")
    mix_2 = flip(add_up(((mix_0, 1), (mix_1, 1))), "x")
    q_1, v_1 = flip(q_1, "y"), flip(v_1, "x")
    kv_2, mix_2, q_1, v_1, hidden_got, grad_rows = tie(
        kv_2, mix_2, q_1, v_1, hidden_got, grad_rows
    )
    got = owned(
        add_up(((kv_0, 0), (kv_1, 0), kv_2), ((mix_0, 0), (mix_1, 0), mix_2)), 2, ("z", "c")
    )
    hidden_part = ((height, 2 * D), BF)
    hidden_near, hidden_core, hidden_chip = run(
        depth_sum_kernel,
        [hidden_part, hidden_part, ((2,) + hidden_part[0], BF)],
        [SM, VM],
        [vmem((FOLD * height, 2 * D), F32)],
        me, hidden_got,
    )
    q_2 = flip(add_up(((q_0, 1), (q_1, 1))), "x")
    v_2 = flip(add_up(((v_0, 1), (v_1, 1))), "y")
    part = ((rows // FOLD, 2 * D), BF)
    near, core, chip = run(
        return_kernel,
        [part, part, ((2,) + part[0], BF)],
        [SM] + [VM] * 7,
        [vmem((rows, 2 * D), F32)],
        me, arr, after_cross, table, out_near, out_core, out_far, grad_rows,
    )
    chip, hidden_chip = flip(chip, "y"), flip(hidden_chip, "y")
    q_2, v_2, kv_send, got = tie(q_2, v_2, kv_send, got)
    self_got = owned(
        add_up(((q_0, 0), (q_1, 0), q_2), ((v_0, 0), (v_1, 0), v_2)), 2, ("z", "c")
    )
    (grad_image,) = run(
        image_grad_kernel,
        [((images, D), BF)],
        [VM, VM, SM] + [HB] * 8,
        [vmem((2, depth, 2, 2, 2 * height, D), BF), sems(8)],
        kv_keep, kv_send, me, *pieces_b,
    )
    grad_up, grad_down = run(
        unpack_hidden_kernel, [flat(FOLD)] * 2, [SM] + [VM] * 4,
        [vmem((FOLD, height, 2 * D), BF)],
        me, hidden_near, hidden_chip, flip(hidden_core, "c"), flip(hidden_chip[1], "c"),
    )
    layer_out, grad_tokens = run(
        collect_kernel, [((FOLD, rows // FOLD, D), BF)] * 2, [SM] + [VM] * 4, [],
        me, near, chip, flip(core, "c"), flip(chip[1], "c"),
    )
    grad_cq, grad_ckv, grad_co, grad_out = run(
        unpack_halves_kernel, [flat(n) for n in (1, 2, 1, 1)], [VM], [], got, mib=16
    )
    grad_qkv, grad_small = run(
        unpack_self_kernel, [flat(3), ((8, LANES), F32)], [VM], [], self_got, mib=16
    )
    return (
        layer_out.reshape(tokens.shape),
        grad_tokens.reshape(tokens.shape),
        grad_image.reshape(image_tokens.shape),
        *(
            g.reshape(-1)
            for g in (grad_qkv, grad_out, grad_cq, grad_ckv, grad_co, grad_up, grad_down)
        ),
        grad_small.reshape(-1)[: small_params.shape[0]],
    )


def general_norm_rows(inputs, gain_vec, shift_vec):
    centred = inputs - jnp.mean(inputs, axis=-1, keepdims=True)
    variance = jnp.mean(centred * centred, axis=-1, keepdims=True)
    return centred * lax.rsqrt(variance + epsilon) * gain_vec + shift_vec


def general_norm_back(inputs, gain_vec, shift_vec, grad_normed):
    _, pullback = jax.vjp(general_norm_rows, inputs, gain_vec, shift_vec)
    return pullback(grad_normed)


def general_gelu_exact(inputs):
    return jax.nn.gelu(inputs, approximate=False)


def general_gelu_back(inputs, grad_active):
    _, pullback = jax.vjp(general_gelu_exact, inputs)
    return pullback(grad_active)[0]


def general_slot_index(lengths, arrivals):
    run_ends = jnp.cumsum(lengths)
    starts = run_ends - lengths
    caption = jnp.sum((run_ends[None, :] <= arrivals[:, None]).astype(jnp.int32), axis=1)
    picked = caption[:, None] == jnp.arange(lengths.shape[0], dtype=jnp.int32)[None, :]
    first_row = jnp.sum(jnp.where(picked, starts[None, :], 0), axis=1)
    return caption * CAP_LEN + arrivals - first_row


def general_score_block(queries, keys_in, allowed):
    scores = jnp.einsum(
        "cqhd,ckhd->chqk", queries, keys_in, preferred_element_type=jnp.float32
    ) * HEAD_DIM ** (-0.5)
    return jnp.where(allowed, scores, -masked_fill)


def general_attention(queries, keys_in, values, allowed):
    scores = general_score_block(queries, keys_in, allowed)
    row_max = jnp.max(scores, axis=-1, keepdims=True)
    log_total = row_max + jnp.log(jnp.sum(jnp.exp(scores - row_max), axis=-1, keepdims=True))
    attn_weights = jnp.exp(scores - log_total).astype(jnp.bfloat16)
    mixed_out = jnp.einsum(
        "chqk,ckhd->cqhd", attn_weights, values, preferred_element_type=jnp.float32
    ).astype(jnp.bfloat16)
    return (mixed_out, log_total)


def general_attention_back(queries, keys_in, values, log_total, grad_mixed, allowed):
    scores = general_score_block(queries, keys_in, allowed)
    attn_weights = jnp.exp(scores - log_total)
    grad_weights = jnp.einsum(
        "cqhd,ckhd->chqk", grad_mixed, values, preferred_element_type=jnp.float32
    )
    centre = jnp.sum(attn_weights * grad_weights, axis=-1, keepdims=True)
    grad_scores = (attn_weights * (grad_weights - centre)).astype(jnp.bfloat16)
    grad_queries = jnp.einsum(
        "chqk,ckhd->cqhd", grad_scores, keys_in, preferred_element_type=jnp.float32
    ) * HEAD_DIM ** (-0.5)
    grad_keys = jnp.einsum(
        "chqk,cqhd->ckhd", grad_scores, queries, preferred_element_type=jnp.float32
    ) * HEAD_DIM ** (-0.5)
    grad_values = jnp.einsum(
        "chqk,cqhd->ckhd",
        attn_weights.astype(jnp.bfloat16),
        grad_mixed,
        preferred_element_type=jnp.float32,
    )
    return (grad_queries, grad_keys, grad_values)


def general_unpack_params(gathered):
    (
        flat_qkv,
        flat_out,
        flat_cross_q,
        flat_cross_kv,
        flat_cross_out,
        flat_up,
        flat_down,
        flat_small,
    ) = gathered
    small_vals = flat_small.astype(jnp.float32)
    return (
        flat_qkv.reshape(D, 3 * D),
        flat_out.reshape(D, D),
        flat_cross_q.reshape(D, D),
        flat_cross_kv.reshape(V, 2 * D),
        flat_cross_out.reshape(D, D),
        flat_up.reshape(D, FF),
        flat_down.reshape(FF, D),
        small_vals[: 3 * D].reshape(3, D),
        small_vals[3 * D : 6 * D].reshape(3, D),
        small_vals[6 * D : 6 * D + FF],
        small_vals[6 * D + FF :],
    )


def general_forward(slotted, image_rows, params, allowed, open_mask):
    (
        mat_qkv,
        mat_out,
        mat_cross_q,
        mat_cross_kv,
        mat_cross_out,
        mat_up,
        mat_down,
        norm_gains,
        shifts,
        up_bias,
        down_bias,
    ) = params
    captions = slotted.shape[0] // CAP_LEN
    head_count = D // HEAD_DIM
    normed_self = general_norm_rows(slotted, norm_gains[0], shifts[0]).astype(jnp.bfloat16)
    projected = jnp.dot(normed_self, mat_qkv, preferred_element_type=jnp.float32).astype(
        jnp.bfloat16
    )
    projected = projected.reshape(captions, CAP_LEN, 3, head_count, HEAD_DIM)
    self_mixed, self_total = general_attention(
        projected[:, :, 0], projected[:, :, 1], projected[:, :, 2], allowed
    )
    self_mixed = self_mixed.reshape(-1, D)
    after_self = slotted + jnp.dot(self_mixed, mat_out, preferred_element_type=jnp.float32)
    normed_cross = general_norm_rows(after_self, norm_gains[1], shifts[1]).astype(jnp.bfloat16)
    cross_query = jnp.dot(normed_cross, mat_cross_q, preferred_element_type=jnp.float32).astype(
        jnp.bfloat16
    )
    cross_query = cross_query.reshape(captions, CAP_LEN, head_count, HEAD_DIM)
    image_kv = jnp.dot(image_rows, mat_cross_kv, preferred_element_type=jnp.float32).astype(
        jnp.bfloat16
    )
    image_kv = image_kv.reshape(captions, IMG, 2, head_count, HEAD_DIM)
    cross_mixed, cross_total = general_attention(
        cross_query, image_kv[:, :, 0], image_kv[:, :, 1], open_mask
    )
    cross_mixed = cross_mixed.reshape(-1, D)
    after_cross = after_self + jnp.dot(
        cross_mixed, mat_cross_out, preferred_element_type=jnp.float32
    )
    normed_mlp = general_norm_rows(after_cross, norm_gains[2], shifts[2]).astype(jnp.bfloat16)
    hidden = jnp.dot(normed_mlp, mat_up, preferred_element_type=jnp.float32) + up_bias
    activated = general_gelu_exact(hidden).astype(jnp.bfloat16)
    result = (
        after_cross + jnp.dot(activated, mat_down, preferred_element_type=jnp.float32) + down_bias
    )
    saved_state = (
        slotted,
        normed_self,
        projected,
        self_total,
        self_mixed,
        after_self,
        normed_cross,
        cross_query,
        image_kv,
        cross_total,
        cross_mixed,
        after_cross,
        normed_mlp,
        hidden,
        activated,
    )
    return (result, saved_state)


def general_backward(saved_state, grad_slot, image_rows, params, allowed, open_mask):
    (
        mat_qkv,
        mat_out,
        mat_cross_q,
        mat_cross_kv,
        mat_cross_out,
        mat_up,
        mat_down,
        norm_gains,
        shifts,
        up_bias,
        down_bias,
    ) = params
    (
        slotted,
        normed_self,
        projected,
        self_total,
        self_mixed,
        after_self,
        normed_cross,
        cross_query,
        image_kv,
        cross_total,
        cross_mixed,
        after_cross,
        normed_mlp,
        hidden,
        activated,
    ) = saved_state
    captions = slotted.shape[0] // CAP_LEN
    head_count = D // HEAD_DIM
    grad_branch = grad_slot.astype(jnp.bfloat16)
    grad_down = jnp.einsum("rf,rd->fd", activated, grad_branch, preferred_element_type=jnp.float32)
    grad_down_bias = jnp.sum(grad_slot, axis=0)
    grad_active = jnp.einsum("rd,fd->rf", grad_branch, mat_down, preferred_element_type=jnp.float32)
    grad_hidden = general_gelu_back(hidden, grad_active).astype(jnp.bfloat16)
    grad_up = jnp.einsum("rd,rf->df", normed_mlp, grad_hidden, preferred_element_type=jnp.float32)
    grad_up_bias = jnp.sum(grad_hidden.astype(jnp.float32), axis=0)
    grad_normed = jnp.einsum("rf,df->rd", grad_hidden, mat_up, preferred_element_type=jnp.float32)
    grad_cross_in, grad_gain3, grad_shift3 = general_norm_back(
        after_cross, norm_gains[2], shifts[2], grad_normed
    )
    grad_after_cross = grad_slot + grad_cross_in
    grad_branch = grad_after_cross.astype(jnp.bfloat16)
    grad_cross_out = jnp.einsum(
        "rd,re->de", cross_mixed, grad_branch, preferred_element_type=jnp.float32
    )
    grad_mixed = jnp.einsum(
        "re,de->rd", grad_branch, mat_cross_out, preferred_element_type=jnp.float32
    ).astype(jnp.bfloat16)
    grad_mixed = grad_mixed.reshape(captions, CAP_LEN, head_count, HEAD_DIM)
    grad_query, grad_key, grad_value = general_attention_back(
        cross_query, image_kv[:, :, 0], image_kv[:, :, 1], cross_total, grad_mixed, open_mask
    )
    grad_query = grad_query.reshape(-1, D).astype(jnp.bfloat16)
    grad_kv = jnp.stack([grad_key, grad_value], axis=2).reshape(-1, 2 * D).astype(jnp.bfloat16)
    grad_cross_q = jnp.einsum(
        "rd,re->de", normed_cross, grad_query, preferred_element_type=jnp.float32
    )
    grad_cross_kv = jnp.einsum("iv,ie->ve", image_rows, grad_kv, preferred_element_type=jnp.float32)
    grad_image = jnp.einsum(
        "ie,ve->iv", grad_kv, mat_cross_kv, preferred_element_type=jnp.float32
    ).astype(jnp.bfloat16)
    grad_normed = jnp.einsum(
        "re,de->rd", grad_query, mat_cross_q, preferred_element_type=jnp.float32
    )
    grad_self_in, grad_gain2, grad_shift2 = general_norm_back(
        after_self, norm_gains[1], shifts[1], grad_normed
    )
    grad_after_self = grad_after_cross + grad_self_in
    grad_branch = grad_after_self.astype(jnp.bfloat16)
    grad_out = jnp.einsum("rd,re->de", self_mixed, grad_branch, preferred_element_type=jnp.float32)
    grad_mixed = jnp.einsum(
        "re,de->rd", grad_branch, mat_out, preferred_element_type=jnp.float32
    ).astype(jnp.bfloat16)
    grad_mixed = grad_mixed.reshape(captions, CAP_LEN, head_count, HEAD_DIM)
    grad_query, grad_key, grad_value = general_attention_back(
        projected[:, :, 0], projected[:, :, 1], projected[:, :, 2], self_total, grad_mixed, allowed
    )
    grad_projected = (
        jnp.stack([grad_query, grad_key, grad_value], axis=2)
        .reshape(-1, 3 * D)
        .astype(jnp.bfloat16)
    )
    grad_w_qkv = jnp.einsum(
        "rd,re->de", normed_self, grad_projected, preferred_element_type=jnp.float32
    )
    grad_normed = jnp.einsum(
        "re,de->rd", grad_projected, mat_qkv, preferred_element_type=jnp.float32
    )
    grad_input, grad_gain1, grad_shift1 = general_norm_back(slotted, norm_gains[0], shifts[0], grad_normed)
    grad_input = grad_input + grad_after_self
    grad_small = jnp.concatenate(
        [
            grad_gain1,
            grad_gain2,
            grad_gain3,
            grad_shift1,
            grad_shift2,
            grad_shift3,
            grad_up_bias,
            grad_down_bias,
        ]
    )
    flat_grads = (
        grad_w_qkv.reshape(-1),
        grad_out.reshape(-1),
        grad_cross_q.reshape(-1),
        grad_cross_kv.reshape(-1),
        grad_cross_out.reshape(-1),
        grad_up.reshape(-1),
        grad_down.reshape(-1),
        grad_small,
    )
    return (grad_input, grad_image, flat_grads)


def general_sum_to_owners(flat_grads):
    summed = []
    for grad_vec in flat_grads:
        for axis in ("dp", "fsdp"):
            parts = grad_vec.reshape(lax.axis_size(axis), -1).astype(jnp.bfloat16)
            if axis == "dp":
                parts = grad_vec.reshape(lax.axis_size("dp"), lax.axis_size("fsdp"), -1)
                parts = parts.astype(jnp.bfloat16)
            got = lax.all_to_all(parts, axis, split_axis=0, concat_axis=0, tiled=True)
            grad_vec = jnp.sum(got.astype(jnp.float32), axis=0)
        summed.append(grad_vec)
    return tuple(summed)


def general_device(
    tokens,
    image_tokens,
    caption_lengths,
    arrival_order,
    w_qkv,
    w_out,
    w_cross_q,
    w_cross_kv,
    w_cross_out,
    w_up,
    w_down,
    small_params,
    cotangent,
):
    lengths = caption_lengths[0]
    slot_rows = general_slot_index(lengths, arrival_order[0])
    captions = lengths.shape[0]
    slot_total = captions * CAP_LEN
    arrived, arrived_grad = (
        lax.all_to_all(tokens, "fsdp", split_axis=0, concat_axis=0, tiled=True),
        lax.all_to_all(cotangent, "fsdp", split_axis=0, concat_axis=0, tiled=True),
    )
    slotted = jnp.zeros((slot_total, D), jnp.float32).at[slot_rows].set(arrived.astype(jnp.float32))
    grad_slot = (
        jnp.zeros((slot_total, D), jnp.float32).at[slot_rows].set(arrived_grad.astype(jnp.float32))
    )
    positions = jnp.arange(CAP_LEN, dtype=jnp.int32)
    allowed = (positions[None, :] <= positions[:, None])[None, None] & (
        positions[None, None, None, :] < lengths[:, None, None, None]
    )
    open_mask = jnp.ones((1, 1, 1, 1), jnp.bool_)
    image_rows = image_tokens.reshape(-1, V)
    owned_shards = (w_qkv, w_out, w_cross_q, w_cross_kv, w_cross_out, w_up, w_down, small_params)
    params = general_unpack_params(
        tuple(lax.all_gather(w, ("dp", "fsdp"), axis=0, tiled=True) for w in owned_shards)
    )
    result, saved_state = general_forward(slotted, image_rows, params, allowed, open_mask)
    grad_input, grad_image, flat_grads = general_backward(
        saved_state, grad_slot, image_rows, params, allowed, open_mask
    )
    summed = general_sum_to_owners(flat_grads)
    out_rows = result[slot_rows].astype(jnp.bfloat16)
    grad_rows = grad_input[slot_rows].astype(jnp.bfloat16)
    layer_out, grad_tokens = (
        lax.all_to_all(out_rows, "fsdp", split_axis=0, concat_axis=0, tiled=True),
        lax.all_to_all(grad_rows, "fsdp", split_axis=0, concat_axis=0, tiled=True),
    )
    return (layer_out, grad_tokens, grad_image.reshape(image_tokens.shape)) + tuple(summed)


def solution(mesh):
    dp, fsdp = mesh.shape["dp"], mesh.shape["fsdp"]
    inner, specs_of = on_device, ("dp", "fsdp")
    if fsdp == 4 and dp % 2 == 0 and D % (dp * fsdp * 8) == 0:
        mesh = Mesh(mesh.devices.reshape(dp // 2, 2, 2, 2), AXES)
        specs_of = AXES
    else:
        inner = general_device
    rows, flat, cube = P(specs_of, None), P(specs_of), P(specs_of, None, None)
    return jax.shard_map(
        inner,
        mesh=mesh,
        in_specs=(rows, cube, rows, rows) + (flat,) * 8 + (rows,),
        out_specs=(rows, rows, cube) + (flat,) * 8,
        check_vma=False,
    )
```

```python
import functools

import jax
import jax.numpy as jnp
from jax import lax
from jax.experimental import pallas as pl
from jax.experimental.pallas import tpu as pltpu
from jax.sharding import Mesh
from jax.sharding import PartitionSpec as P

D = 768
HEAD_DIM = 64
FF = 3072
V = 768
IMG = 256
CAP_LEN = 64
LANES = 128
PAIRS = D // LANES
HALF = D // 2
HEADS = 4
WIDE = HEADS * HEAD_DIM
BATCHES = D // WIDE
FOLD = FF // D
GROUP = FOLD * LANES
GROUPS = FF // GROUP
TOKENS_AT = 32
SCALE = HEAD_DIM ** (-0.5)
epsilon = 1e-05
masked_fill = 1e30

BF = jnp.bfloat16
F32 = jnp.float32
AXES = ("z", "x", "y", "c")


def mm(a, b):
    return lax.dot_general(a, b, (((1,), (0,)), ((), ())), preferred_element_type=F32)


def mm_t(a, b):
    return lax.dot_general(a, b, (((1,), (1,)), ((), ())), preferred_element_type=F32)


def t_mm(a, b):
    return lax.dot_general(a, b, (((0,), (0,)), ((), ())), preferred_element_type=F32)


def wide(value):
    return value.astype(F32)


def norm_rows(inputs, gain_vec, shift_vec):
    centred = inputs - jnp.mean(inputs, axis=-1, keepdims=True)
    variance = jnp.mean(centred * centred, axis=-1, keepdims=True)
    return centred * lax.rsqrt(variance + epsilon) * gain_vec + shift_vec


def norm_back(inputs, gain_vec, grad_normed):
    centred = inputs - jnp.mean(inputs, axis=-1, keepdims=True)
    variance = jnp.mean(centred * centred, axis=-1, keepdims=True)
    scale = lax.rsqrt(variance + epsilon)
    unit = centred * scale
    weighted = grad_normed * gain_vec
    grad_in = scale * (
        weighted
        - jnp.mean(weighted, axis=-1, keepdims=True)
        - unit * jnp.mean(weighted * unit, axis=-1, keepdims=True)
    )
    grad_gain = jnp.sum(grad_normed * unit, axis=0, keepdims=True)
    grad_shift = jnp.sum(grad_normed, axis=0, keepdims=True)
    return grad_in, grad_gain, grad_shift


def arrival_pick(arr_ref):
    rows = arr_ref.shape[1]
    place = lax.broadcasted_iota(jnp.int32, (rows, rows), 0)
    return jnp.where(place == arr_ref[...], 1.0, 0.0).astype(BF)


def caption_of(index, lens_ref):
    end = jnp.int32(0)
    found = jnp.zeros_like(index)
    for c in range(lens_ref.shape[1] - 1):
        end = end + lens_ref[0, c]
        found = found + jnp.where(index >= end, 1, 0)
    return found


def slot_pick(lens_ref, rows):
    captions = lens_ref.shape[1]
    shape = (captions * CAP_LEN, rows)
    slot = lax.broadcasted_iota(jnp.int32, shape, 0)
    row = lax.broadcasted_iota(jnp.int32, shape, 1)
    start = jnp.int32(0)
    hit = jnp.zeros(shape, F32)
    for c in range(captions):
        length = lens_ref[0, c]
        inside = slot - c * CAP_LEN
        ok = (inside >= 0) & (inside < length) & (row - start == inside)
        hit = hit + jnp.where(ok, 1.0, 0.0)
        start = start + length
    return hit.astype(BF)


def fold_pick(back):
    source = lax.broadcasted_iota(jnp.int32, (GROUP, GROUP), 1 if back else 0)
    target = lax.broadcasted_iota(jnp.int32, (GROUP, GROUP), 0 if back else 1)
    return jnp.where(target == (source % FOLD) * LANES + source // FOLD, 1.0, 0.0).astype(BF)


def head_mask(rows):
    shape = (HEADS * rows, WIDE)
    head = lax.broadcasted_iota(jnp.int32, shape, 1) // HEAD_DIM
    row = lax.broadcasted_iota(jnp.int32, shape, 0)
    inside = (row >= head * rows) & (row < (head + 1) * rows)
    return jnp.where(inside, 1.0, 0.0).astype(BF)


def stack_heads(block, mask):
    return jnp.concatenate([block] * HEADS, axis=0) * mask


def merge_heads(stacked):
    rows = stacked.shape[0] // HEADS
    head = lax.broadcasted_iota(jnp.int32, (rows, WIDE), 1) // HEAD_DIM
    out = stacked[:rows]
    for n in range(1, HEADS):
        out = jnp.where(head == n, stacked[n * rows : (n + 1) * rows], out)
    return out


def softmax_rows(scores):
    shifted = jnp.exp(scores - jnp.max(scores, axis=-1, keepdims=True))
    return shifted * (1.0 / jnp.sum(shifted, axis=-1, keepdims=True))


def lanes_at(start, width):
    return pl.ds(pl.multiple_of(start, LANES), width)


def pack_halves(shards, out, rows, at=0):
    depth, _, height, _ = out.shape
    pieces = HALF // LANES
    for shard, mats in shards:
        rows[: shard.shape[0], :] = wide(shard[...])
        for mat in range(mats):
            for half in range(2):
                for i in range(pieces):
                    index = mat * PAIRS + half * pieces + i
                    value = rows[pl.ds(index, height, stride=mats * PAIRS), :].astype(BF)
                    lanes = slice(at + i * LANES, at + (i + 1) * LANES)
                    for z in range(depth):
                        out[z, half, :, lanes] = value
            at += HALF
    return at


def pack_self_kernel(w_qkv, w_out, attend, rows):
    pack_halves(((w_qkv, 3), (w_out, 1)), attend, rows)


def pack_cross_kernel(w_cross_q, w_cross_kv, w_cross_out, small, attend, rows):
    at = pack_halves(((w_cross_q, 1), (w_cross_kv, 2), (w_cross_out, 1)), attend, rows)
    depth, _, height, _ = attend.shape
    flat = wide(small[...])
    tail = jnp.zeros((1, LANES - small.shape[1] % LANES), F32)
    flat = jnp.concatenate([flat, tail], axis=1)
    parts = [flat[:, n : n + LANES] for n in range(0, flat.shape[1], LANES)]
    block = jnp.concatenate(parts + [jnp.zeros((height - len(parts), LANES), F32)], axis=0)
    for z in range(depth):
        for half in range(2):
            attend[z, half, :, at:] = block.astype(BF)


def pack_group_kernel(me, w_up, w_down, tokens, cotangent, near, core, chip, rows, parts):
    chunks = FF // LANES
    height = w_up.shape[0] // chunks

    def chunk(index):
        return rows[pl.ds(index, height, stride=chunks), :].astype(BF)

    rows[...] = wide(w_up[...])
    pick = fold_pick(False)
    for t in range(GROUPS):
        group = jnp.concatenate([chunk(t * FOLD + k) for k in range(FOLD)], axis=1)
        folded = mm(group, pick).astype(BF)
        for j in range(FOLD):
            parts[j, :height, t * LANES : (t + 1) * LANES] = folded[
                :, j * LANES : (j + 1) * LANES
            ]
    rows[...] = wide(w_down[...])
    for j in range(FOLD):
        for i in range(PAIRS):
            at = D + i * LANES
            parts[j, :height, at : at + LANES] = chunk(j * PAIRS + i)
        parts[j, TOKENS_AT : TOKENS_AT + tokens.shape[1], :D] = tokens[j]
        parts[j, TOKENS_AT : TOKENS_AT + tokens.shape[1], D:] = cotangent[j]
    near[...] = parts[part_of(me, 0, 0)]
    core[...] = parts[part_of(me, 0, 1)]
    for c in range(2):
        chip[c] = parts[part_of(me, 1, c)]


def transpose_kernel(img, out):
    for n in range(0, img.shape[0], IMG):
        out[:, n : n + IMG] = img[n : n + IMG, :].T


def part_of(me, far_y, far_c):
    return lax.bitwise_xor(me[0, 2], far_y) * 2 + lax.bitwise_xor(me[0, 3], far_c)


def spread_kernel(me, arr, near, chip, core, both, hidden, slotted, grad_slot, arrived):
    height, count = hidden.shape[2], arrived.shape[0] // FOLD
    for value, far_y, far_c in (
        (near[...], 0, 0), (chip[0], 1, 0), (core[...], 0, 1), (both[...], 1, 1),
    ):
        index = part_of(me, far_y, far_c)
        for z in range(hidden.shape[0]):
            hidden[z, index] = value[:height]
        at = pl.multiple_of(index * count, 8)
        arrived[pl.ds(at, count), :] = wide(value[TOKENS_AT : TOKENS_AT + count])
    pick = arrival_pick(arr)
    slotted[...] = mm(pick, arrived[:, :D].astype(BF)).astype(BF)
    grad_slot[...] = mm(pick, arrived[:, D:].astype(BF)).astype(BF)


def fill_table(share, me, pieces, flat, table):
    depth, height = pieces.shape[1], pieces.shape[2] // 2
    lane = lax.broadcasted_iota(jnp.int32, (3, LANES), 1)
    flat[...] = jnp.zeros_like(flat)
    for owner in range(8 * depth):
        z, x, y, c = owner // 8, owner // 4 % 2, owner // 2 % 2, owner % 2
        index = lax.bitwise_xor(me[0, 1], x) * 2 + lax.bitwise_xor(me[0, 2], y)
        value = wide(pieces[index, z])[c * height : c * height + 3, :]
        row, shift = divmod(owner * share, LANES)
        if shift == 0:
            flat[row : row + 3, :] += value
        else:
            moved = pltpu.roll(value, shift, axis=1)
            flat[row : row + 3, :] += jnp.where(lane >= shift, moved, 0.0)
            flat[row + 1 : row + 4, :] += jnp.where(lane < shift, moved, 0.0)
    for n in range(table.shape[0] * PAIRS):
        row, lanes = n // PAIRS, slice(n % PAIRS * LANES, (n % PAIRS + 1) * LANES)
        table[row : row + 1, lanes] = flat[n : n + 1, :]


def depth_sum_kernel(me, got, near, core, chip, total):
    height = near.shape[0]
    value = wide(got[0])
    for z in range(1, got.shape[0]):
        value = value + wide(got[z])
    total[...] = value

    def part(far_y, far_c):
        at = pl.multiple_of(part_of(me, far_y, far_c) * height, 8)
        return total[pl.ds(at, height), :].astype(BF)

    near[...] = part(0, 0)
    core[...] = part(0, 1)
    for c in range(2):
        chip[c] = part(1, c)


def unpack_hidden_kernel(me, near, chip, core, both, up, down, got):
    for value, far_y, far_c in (
        (near[...], 0, 0), (chip[0], 1, 0), (core[...], 0, 1), (both[...], 1, 1),
    ):
        got[part_of(me, far_y, far_c)] = value
    height = got.shape[1]
    chunks = FF // LANES
    pick = fold_pick(True)
    for t in range(GROUPS):
        group = jnp.concatenate(
            [got[j, :, t * LANES : (t + 1) * LANES] for j in range(FOLD)], axis=1
        )
        natural = mm(group, pick)
        for k in range(FOLD):
            up[pl.ds(t * FOLD + k, height, stride=chunks), :] = natural[
                :, k * LANES : (k + 1) * LANES
            ]
    for j in range(FOLD):
        for i in range(PAIRS):
            at = D + i * LANES
            down[pl.ds(j * PAIRS + i, height, stride=chunks), :] = wide(
                got[j, :, at : at + LANES]
            )


def unpack_halves(got, outs):
    depth, height = got.shape[0], got.shape[2]
    parts = HALF // LANES
    place = 0
    for out in outs:
        chunks = out.shape[0] // height
        for mat in range(chunks // PAIRS):
            for half in range(2):
                for i in range(parts):
                    at = place + i * LANES
                    total = wide(got[0, half, :, at : at + LANES])
                    for z in range(1, depth):
                        total = total + wide(got[z, half, :, at : at + LANES])
                    index = mat * PAIRS + half * parts + i
                    out[pl.ds(index, height, stride=chunks), :] = total
            place += HALF
    return place


class Fetch:
    def __init__(self, sems):
        self.sems = sems
        self.used = 0

    def start(self, source, target):
        copy = pltpu.make_async_copy(source, target, self.sems.at[self.used])
        self.used += 1
        copy.start()
        return copy

    def columns(self, pieces, me, piece_at, target, target_at):
        copies = []
        for index, piece in enumerate(pieces):
            half = lax.bitwise_xor(me[0, 3], index // 4)
            x = lax.bitwise_xor(me[0, 1], index // 2 % 2)
            y = lax.bitwise_xor(me[0, 2], index % 2)
            copies.append(
                self.start(
                    piece.at[:, :, pl.ds(piece_at, HALF)],
                    target.at[:, x, y, :, lanes_at(target_at + half * HALF, HALF)],
                )
            )
        return copies


def wait(copies):
    for copy in copies:
        copy.wait()


def matrix(ref):
    shape = ref.shape
    return ref[...].reshape(shape[0] * shape[1] * shape[2] * shape[3], shape[4])


def forward_kernel(share, lens, me, slotted, img, *refs):
    pieces_a, pieces_b = refs[:8], refs[8:16]
    (
        table, saved, after_self, after_cross, normed_mlp,
        projected_out, self_out, slots_out, kv_out, probs_out,
        projected, probs_self, query_slots, kv, probs_cross,
        w_qkv, w_out, w_cq, w_kv, w_co, mixed_slots, small, flat, sems,
    ) = refs[16:]
    fetch = Fetch(sems)
    got_small = [
        fetch.start(pieces_b[n].at[:, :, pl.ds(4 * HALF, LANES)], small.at[n]) for n in range(4)
    ]
    got_qkv = []
    for mat in range(3):
        got_qkv += fetch.columns(pieces_a, me, mat * HALF, w_qkv, mat * D)
    got_out = fetch.columns(pieces_a, me, 3 * HALF, w_out, 0)
    got_cq = fetch.columns(pieces_b, me, 0, w_cq, 0)
    got_kv = fetch.columns(pieces_b, me, HALF, w_kv, 0)
    got_kv += fetch.columns(pieces_b, me, 2 * HALF, w_kv, D)
    got_co = fetch.columns(pieces_b, me, 3 * HALF, w_co, 0)
    rows = slotted.shape[0]
    wait(got_small)
    fill_table(share, me, small, flat, table)
    saved[:, :D] = norm_rows(wide(slotted[...]), table[0:1, :], table[3:4, :]).astype(BF)
    wait(got_qkv)
    projected[...] = mm(saved[:, :D], matrix(w_qkv)).astype(BF)
    query_at = lax.broadcasted_iota(jnp.int32, (rows, rows), 0)
    key_at = lax.broadcasted_iota(jnp.int32, (rows, rows), 1)
    same = caption_of(query_at, lens) == caption_of(key_at, lens)
    block = jnp.where(same & (key_at <= query_at), 0.0, -masked_fill)
    barred = jnp.concatenate([block] * HEADS, axis=0)
    mask = head_mask(rows)
    for n in range(BATCHES):
        query, key, value = (
            projected[:, m * D + n * WIDE : m * D + (n + 1) * WIDE] for m in range(3)
        )
        scores = mm_t(stack_heads(query, mask), key) * SCALE + barred
        weights_low = softmax_rows(scores).astype(BF)
        probs_self[n] = weights_low
        saved[:, D + n * WIDE : D + (n + 1) * WIDE] = merge_heads(
            mm(weights_low, value)
        ).astype(BF)
    wait(got_out)
    state = wide(slotted[...]) + mm(saved[:, D : 2 * D], matrix(w_out))
    after_self[...] = state
    low = norm_rows(state, table[1:2, :], table[4:5, :]).astype(BF)
    saved[:, 2 * D : 3 * D] = low
    wait(got_cq)
    pick = slot_pick(lens, rows)
    query_slots[...] = mm(pick, mm(low, matrix(w_cq)).astype(BF)).astype(BF)
    sent = [
        fetch.start(projected, projected_out),
        fetch.start(probs_self, self_out),
        fetch.start(query_slots, slots_out),
    ]
    wait(got_kv)
    kv_mat = matrix(w_kv)
    mask = head_mask(CAP_LEN)
    for c in range(lens.shape[1]):
        slots = slice(c * CAP_LEN, (c + 1) * CAP_LEN)
        images = slice(c * IMG, (c + 1) * IMG)
        kv[images, :] = mm(img[images, :], kv_mat).astype(BF)
        for n in range(BATCHES):
            cols = slice(n * WIDE, (n + 1) * WIDE)
            query = stack_heads(query_slots[slots, cols], mask)
            weights_low = softmax_rows(mm_t(query, kv[images, cols]) * SCALE).astype(BF)
            probs_cross[c * BATCHES + n] = weights_low
            value = kv[images, D + n * WIDE : D + (n + 1) * WIDE]
            mixed_slots[slots, cols] = merge_heads(mm(weights_low, value)).astype(BF)
        batch = slice(c * BATCHES, (c + 1) * BATCHES)
        sent.append(fetch.start(kv.at[images], kv_out.at[images]))
        sent.append(fetch.start(probs_cross.at[batch], probs_out.at[batch]))
    low = t_mm(pick, mixed_slots[...]).astype(BF)
    saved[:, 3 * D :] = low
    wait(got_co)
    state = after_self[...] + mm(low, matrix(w_co))
    after_cross[...] = state
    normed_mlp[...] = norm_rows(state, table[2:3, :], table[5:6, :]).astype(BF)
    wait(sent)


def put_small(small, row, value):
    for k in range(PAIRS):
        at = row * PAIRS + k
        small[at : at + 1, :] = value[:, k * LANES : (k + 1) * LANES]


def own_part(value, me):
    part = me[0, 2] * 2 + me[0, 3]
    out = value[:, :LANES]
    for j in range(1, FOLD):
        out = jnp.where(part == j, value[:, j * LANES : (j + 1) * LANES], out)
    return out


def mlp_kernel(me, table, *refs):
    inputs, grads, pieces = refs[:4], refs[4:8], refs[8:10]
    (
        grad_near, grad_keep, grad_send, grad_send_y, active, grad_hidden, small,
        all_in, all_grad, w_hidden, grad_part, sems,
    ) = refs[10:]
    fetch = Fetch(sems)
    got = [
        fetch.start(piece, w_hidden.at[:, lax.bitwise_xor(me[0, 1], index)])
        for index, piece in enumerate(pieces)
    ]
    rows = inputs[0].shape[0]
    for n in range(4):
        all_in[n * rows : (n + 1) * rows, :] = inputs[n][...]
        all_grad[n * rows : (n + 1) * rows, :] = grads[n][...]
    bias = [
        table[6 + n // PAIRS : 7 + n // PAIRS, n % PAIRS * LANES : (n % PAIRS + 1) * LANES]
        for n in range(FF // LANES)
    ]
    bias = jnp.concatenate(
        [jnp.concatenate(bias[t * FOLD : (t + 1) * FOLD], axis=1) for t in range(GROUPS)], axis=0
    )
    bias = own_part(mm(bias.astype(BF), fold_pick(False)), me)
    bias = jnp.concatenate([bias[t : t + 1, :] for t in range(GROUPS)], axis=1)
    wait(got)
    up_mat = w_hidden[:, :, :, :D].reshape(D, D)
    down_mat = w_hidden[:, :, :, D:].reshape(D, D)

    def rows_of(n, total):
        at = slice(n * 2 * rows, (n + 1) * 2 * rows)
        hidden = mm(all_in[at, :], up_mat) + bias
        half = 0.5 + 0.5 * lax.erf(hidden * (0.5**0.5))
        act = (hidden * half).astype(BF)
        active[at, :] = act
        slope = half + hidden * (jnp.exp(hidden * hidden * -0.5) * 0.3989422804014327)
        grad_hid = (mm_t(all_grad[at, :], down_mat) * slope).astype(BF)
        grad_hidden[at, :] = grad_hid
        grad_part[n] = mm_t(grad_hid, up_mat)
        return total + jnp.sum(wide(grad_hid), axis=0, keepdims=True)

    sums = rows_of(1, rows_of(0, jnp.zeros((1, D), F32))).astype(BF)
    for n, out in enumerate((grad_near, grad_send, grad_keep, grad_send_y)):
        out[...] = grad_part[n // 2, n % 2 * rows : (n % 2 + 1) * rows].astype(out.dtype)
    sums = jnp.concatenate(
        [sums[:, t * LANES : (t + 1) * LANES] for t in range(GROUPS)] + [sums[:, :LANES]] * 2,
        axis=0,
    )
    part = me[0, 2] * 2 + me[0, 3]
    spread = jnp.concatenate(
        [jnp.where(part == j, sums, jnp.zeros_like(sums)) for j in range(FOLD)], axis=1
    )
    natural = mm(spread, fold_pick(True))
    small[...] = jnp.zeros_like(small)
    for n in range(FF // LANES):
        at = 6 * PAIRS + n
        small[at : at + 1, :] = natural[
            n // FOLD : n // FOLD + 1, n % FOLD * LANES : (n % FOLD + 1) * LANES
        ]
    put_small(small, 10, jnp.sum(wide(grads[0][...]), axis=0, keepdims=True))


def hidden_grad_kernel(me, *refs):
    sources, pieces = refs[:10], refs[10:12]
    (
        out_near, out_keep, out_send, out_send_y, out,
        normed, grads, grad_hidden, active, made, w_down, sems,
    ) = refs[12:]
    fetch = Fetch(sems)
    rows = sources[0].shape[0]
    places = [normed.at[n * rows : (n + 1) * rows] for n in range(4)]
    places += [grad_hidden, active]
    places += [grads.at[n * rows : (n + 1) * rows] for n in range(4)]
    copies = [fetch.start(source, place) for source, place in zip(sources, places)]
    got = [
        fetch.start(
            piece.at[:, :, pl.ds(D, D)], w_down.at[:, lax.bitwise_xor(me[0, 1], index)]
        )
        for index, piece in enumerate(pieces)
    ]
    wait(copies[:5])
    made[0] = t_mm(normed[...], grad_hidden[...]).astype(BF)
    sent = [fetch.start(made.at[0], out.at[:, pl.ds(0, D)])]
    wait(copies[5:])
    made[1] = t_mm(active[...], grads[...]).astype(BF)
    sent.append(fetch.start(made.at[1], out.at[:, pl.ds(D, D)]))
    wait(got)
    part = mm(active[...], w_down[...].reshape(D, D))
    for n, target in enumerate((out_near, out_send, out_keep, out_send_y)):
        target[...] = part[n * rows : (n + 1) * rows].astype(target.dtype)
    wait(sent)


def combine_kernel(keep, far, out):
    out[...] = (wide(keep[...]) + wide(far[...])).astype(BF)


def cross_back_kernel(
    lens, me, grad_near, grad_core, grad_far, after_cross, grad_slot, probs_in, query_slots, kv_in,
    after_self, table, small_in, *refs,
):
    pieces = refs[:8]
    (
        grad_state, small, half_keep, half_send, keep_out, send_out,
        w_co, w_cq, mixed_slots, query_grads, grad_kv, kv_keep, kv_send, kv, probs, sems,
    ) = refs[8:]
    fetch = Fetch(sems)
    got_co = fetch.columns(pieces, me, 3 * HALF, w_co, 0)
    got_kv = [fetch.start(kv_in, kv), fetch.start(probs_in, probs)]
    got_cq = fetch.columns(pieces, me, 0, w_cq, 0)
    rows = after_self.shape[0]
    sent = []
    halves = ((0, half_keep, kv_keep), (1, half_send, kv_send))
    small[...] = small_in[...]
    grad_in, grad_gain, grad_shift = norm_back(
        after_cross[...],
        table[2:3, :],
        grad_near[...] + wide(grad_core[...]) + wide(grad_far[...]),
    )
    put_small(small, 2, grad_gain)
    put_small(small, 5, grad_shift)
    grad_after = wide(grad_slot[...]) + grad_in
    grad_state[...] = grad_after
    pick = slot_pick(lens, rows)
    wait(got_co)
    query_grads[:rows, :] = grad_after.astype(BF)
    mixed_slots[...] = mm(pick, mm_t(query_grads[:rows, :], matrix(w_co)).astype(BF)).astype(BF)
    for rel, half_out, _ in halves:
        at = lax.bitwise_xor(me[0, 3], rel) * HALF
        half_out[:, HALF : 2 * HALF] = query_grads[:rows, lanes_at(at, HALF)]
    mask = head_mask(CAP_LEN)
    wait(got_kv)
    for c in range(lens.shape[1]):
        slots = slice(c * CAP_LEN, (c + 1) * CAP_LEN)
        images = slice(c * IMG, (c + 1) * IMG)
        for n in range(BATCHES):
            cols = slice(n * WIDE, (n + 1) * WIDE)
            value_cols = slice(D + n * WIDE, D + (n + 1) * WIDE)
            grad_mixed = stack_heads(mixed_slots[slots, cols], mask)
            query = stack_heads(query_slots[slots, cols], mask)
            weights_low = probs[c * BATCHES + n]
            attn = wide(weights_low)
            grad_weights = mm_t(grad_mixed, kv[images, value_cols])
            centre = jnp.sum(attn * grad_weights, axis=-1, keepdims=True)
            grad_scores = (attn * (grad_weights - centre)).astype(BF)
            query_grads[slots, cols] = (
                merge_heads(mm(grad_scores, kv[images, cols])) * SCALE
            ).astype(BF)
            grad_kv[images, cols] = (t_mm(grad_scores, query) * SCALE).astype(BF)
            grad_kv[images, value_cols] = t_mm(weights_low, grad_mixed).astype(BF)
        for rel, _, kv_half in halves:
            at = lax.bitwise_xor(me[0, 3], rel) * HALF
            kv_half[images, :HALF] = grad_kv[images, lanes_at(at, HALF)]
            kv_half[images, HALF:] = grad_kv[images, lanes_at(at + D, HALF)]
        sent.append(fetch.start(kv_send.at[images], send_out.at[images]))
        sent.append(fetch.start(kv_keep.at[images], keep_out.at[images]))
    mixed_slots[:rows, :] = t_mm(pick, query_grads[...]).astype(BF)
    wait(got_cq)
    grad_in, grad_gain, grad_shift = norm_back(
        after_self[...], table[1:2, :], mm_t(mixed_slots[:rows, :], matrix(w_cq))
    )
    put_small(small, 1, grad_gain)
    put_small(small, 4, grad_shift)
    grad_after = grad_state[...] + grad_in
    grad_state[...] = grad_after
    query_grads[:rows, :] = grad_after.astype(BF)
    for rel, half_out, _ in halves:
        at = lax.bitwise_xor(me[0, 3], rel) * HALF
        half_out[:, :HALF] = mixed_slots[:rows, lanes_at(at, HALF)]
        half_out[:, 2 * HALF :] = query_grads[:rows, lanes_at(at, HALF)]
    wait(sent)


def self_back_kernel(me, grad_state, slotted, table, small_in, probs_in, projected_in, *refs):
    pieces = refs[:8]
    (
        grad_rows, small, keep, send,
        w_out, w_qkv, mixed, grad_projected, probs, projected, sems,
    ) = refs[8:]
    fetch = Fetch(sems)
    got_out = fetch.columns(pieces, me, 3 * HALF, w_out, 0)
    got_probs = [fetch.start(projected_in, projected), fetch.start(probs_in, probs)]
    got_qkv = []
    for mat in range(3):
        got_qkv += fetch.columns(pieces, me, mat * HALF, w_qkv, mat * D)
    rows = slotted.shape[0]
    wait(got_out)
    mixed[...] = mm_t(grad_state[...].astype(BF), matrix(w_out)).astype(BF)
    mask = head_mask(rows)
    wait(got_probs)
    for n in range(BATCHES):
        cols, key_cols, value_cols = (
            slice(m * D + n * WIDE, m * D + (n + 1) * WIDE) for m in range(3)
        )
        grad_mixed = stack_heads(mixed[:, cols], mask)
        query = stack_heads(projected[:, cols], mask)
        weights_low = probs[n]
        attn = wide(weights_low)
        grad_weights = mm_t(grad_mixed, projected[:, value_cols])
        centre = jnp.sum(attn * grad_weights, axis=-1, keepdims=True)
        grad_scores = (attn * (grad_weights - centre)).astype(BF)
        grad_projected[:, cols] = (
            merge_heads(mm(grad_scores, projected[:, key_cols])) * SCALE
        ).astype(BF)
        grad_projected[:, key_cols] = (t_mm(grad_scores, query) * SCALE).astype(BF)
        grad_projected[:, value_cols] = t_mm(weights_low, grad_mixed).astype(BF)
    for mat in range(3):
        for rel, out in ((0, keep), (1, send)):
            at = lax.bitwise_xor(me[0, 3], rel) * HALF + mat * D
            out[:, mat * HALF : (mat + 1) * HALF] = grad_projected[:, lanes_at(at, HALF)]
    wait(got_qkv)
    grad_in, grad_gain, grad_shift = norm_back(
        wide(slotted[...]), table[0:1, :], mm_t(grad_projected[...], matrix(w_qkv))
    )
    grad_slotted = (grad_state[...] + grad_in).astype(BF)
    grad_rows[...] = grad_slotted
    small[...] = small_in[...]
    put_small(small, 0, grad_gain)
    put_small(small, 3, grad_shift)


def put_quadrants(grads, me, outs, at, first):
    depth, height = outs[0].shape[1:3]
    width = grads.shape[1]
    for i, out in enumerate(outs):
        for j in range(2):
            far_x, far_y = (i, j) if first == "x" else (j, i)
            x, y = lax.bitwise_xor(me[0, 1], far_x), lax.bitwise_xor(me[0, 2], far_y)
            for z in range(depth):
                low = pl.multiple_of(((z * 2 + x) * 2 + y) * height, 16)
                out[j, z, :, at : at + width] = grads[pl.ds(low, height), :].astype(BF)


def half_grads(pieces, me, outs, grads, first, at=0):
    for left, far_left, right, far_right in pieces:
        width = right.shape[1]
        grads[:, :width] = t_mm(left, right) + t_mm(far_left, far_right)
        put_quadrants(grads.at[:, :width], me, outs, at, first)
        at += width


def cross_grad_kernel(me, *refs):
    sources, targets, landed, made, grads, sems = (
        refs[:8], refs[8:12], refs[12:20], refs[20:24], refs[24], refs[25],
    )
    fetch = Fetch(sems)
    copies = [fetch.start(source, target) for source, target in zip(sources, landed)]
    saved, saved_far, half, half_far, img_t, img_t_far, kv, kv_far = landed
    part = lambda ref, n, width: ref[:, n * width : (n + 1) * width]
    piece = lambda left, right: (
        part(saved, left, D), part(saved_far, left, D),
        part(half, right, HALF), part(half_far, right, HALF),
    )
    wait(copies[:4])
    half_grads([piece(3, 1), piece(1, 2)], me, made[2:], grads, "y")
    sent = [fetch.start(made[n], targets[n]) for n in (3, 2)]
    half_grads([piece(2, 0)], me, made[:2], grads, "x")
    wait(copies[4:])
    grads[...] = mm(img_t[...], kv[...]) + mm(img_t_far[...], kv_far[...])
    put_quadrants(grads, me, made[:2], HALF, "x")
    sent += [fetch.start(made[n], targets[n]) for n in (1, 0)]
    wait(sent)


def owner_rows(small, blocks, share):
    height = blocks.shape[0] // (small.shape[0] * LANES // share)
    lane = lax.broadcasted_iota(jnp.int32, (3, LANES), 1)
    blocks[...] = jnp.zeros_like(blocks)
    table = jnp.concatenate([small[...], jnp.zeros((6, LANES), F32)], axis=0)
    for owner in range(small.shape[0] * LANES // share):
        row, shift = divmod(owner * share, LANES)
        if shift == 0:
            value = table[row : row + 3]
        else:
            moved = pltpu.roll(table[row : row + 4], LANES - shift, axis=1)
            value = jnp.where(lane < LANES - shift, moved[:3], moved[1:4])
        blocks[owner * height : owner * height + 3, :] = value


def self_grad_kernel(share, me, saved, saved_far, half, half_far, small, *refs):
    first, second, grads = refs[:2], refs[2:4], refs[4]
    own, far = saved[:, :D], saved_far[:, :D]
    half_grads([(own, far, half[:, :D], half_far[:, :D])], me, first, grads, "y")
    half_grads([(own, far, half[:, D:], half_far[:, D:])], me, second, grads, "x")
    blocks = grads.at[:, :LANES]
    owner_rows(small, blocks, share)
    put_quadrants(blocks, me, second, HALF, "x")


def unpack_kernel(got, *outs):
    at = unpack_halves(got, outs[:-1])
    total = jnp.zeros((8, LANES), F32)
    for z in range(got.shape[0]):
        for c in range(2):
            total = total + wide(got[z, c, :8, at:])
    outs[-1][...] = total


def return_kernel(
    me, arr, after_cross, table, out_near, out_core, out_far, grad_rows, near, core, chip, rows
):
    pick = arrival_pick(arr)
    count = near.shape[0]
    result = after_cross[...] + out_near[...] + wide(out_core[...]) + wide(out_far[...])
    result = result + table[10:11, :]
    rows[:, :D] = t_mm(pick, result.astype(BF))
    rows[:, D:] = t_mm(pick, grad_rows[...])

    def part(far_y, far_c):
        at = pl.multiple_of(part_of(me, far_y, far_c) * count, 8)
        return rows[pl.ds(at, count), :].astype(BF)

    near[...] = part(0, 0)
    core[...] = part(0, 1)
    for c in range(2):
        chip[c] = part(1, c)


def collect_kernel(me, near, chip, core, both, layer_out, grad_tokens):
    for value, far_y, far_c in ((near[...], 0, 0), (chip[0], 1, 0), (core[...], 0, 1), (both[...], 1, 1)):
        index = part_of(me, far_y, far_c)
        layer_out[index] = value[:, :D]
        grad_tokens[index] = value[:, D:]


def image_grad_kernel(kv_keep, kv_send, *refs):
    me, pieces = refs[0], refs[1:9]
    grad_image, w_kv, sems = refs[9:]
    fetch = Fetch(sems)
    copies = []
    for index, piece in enumerate(pieces):
        x = lax.bitwise_xor(me[0, 1], index // 2 % 2)
        y = lax.bitwise_xor(me[0, 2], index % 2)
        copies.append(
            fetch.start(piece.at[:, :, pl.ds(HALF, D)], w_kv.at[index // 4, :, x, y])
        )
    wait(copies)
    near, far = w_kv[0].reshape(D, D), w_kv[1].reshape(D, D)
    for c in range(kv_keep.shape[0] // IMG):
        rows = pl.ds(c * IMG, IMG)
        grad_image[rows, :] = (mm_t(kv_keep[rows, :], near) + mm_t(kv_send[rows, :], far)).astype(
            BF
        )


def add_kernel(counts, joined, *refs):
    outs = refs[sum(counts) :]
    first = at = 0
    for n, count in enumerate(counts):
        for z in range(refs[first].shape[0]):
            total = wide(refs[first][z])
            for ref in refs[first + 1 : first + count]:
                total = total + wide(ref[z])
            if joined:
                outs[0][z, :, at : at + total.shape[-1]] = total.astype(BF)
            else:
                outs[n][z] = total.astype(BF)
        at += total.shape[-1]
        first += count


VM = pl.BlockSpec(memory_space=pltpu.VMEM)
SM = pl.BlockSpec(memory_space=pltpu.SMEM)
HB = pl.BlockSpec(memory_space=pl.ANY)


def run(kernel, outs, specs, scratch, *args, mib=58, copied=0):
    return pl.pallas_call(
        kernel,
        out_shape=[jax.ShapeDtypeStruct(s, t) for s, t in outs],
        in_specs=specs,
        out_specs=[VM] * (len(outs) - copied) + [HB] * copied,
        scratch_shapes=scratch,
        compiler_params=pltpu.CompilerParams(vmem_limit_bytes=mib * 2**20),
        name=(kernel.func if isinstance(kernel, functools.partial) else kernel).__name__,
    )(*args)


def add_up(*sums, joined=False):
    args, specs, shapes = [], [], []
    for terms in sums:
        for term in terms:
            array, index = term if isinstance(term, tuple) else (term, None)
            block = array.shape[-3:]
            if index is None:
                specs.append(pl.BlockSpec(block, lambda i: (0, 0, 0)))
            else:
                specs.append(pl.BlockSpec((None,) + block, lambda i, n=index: (n, 0, 0, 0)))
            args.append(array)
        shapes.append(block)
    if joined:
        shapes = [shapes[0][:2] + (sum(s[2] for s in shapes),)]
    return pl.pallas_call(
        functools.partial(add_kernel, [len(terms) for terms in sums], joined),
        grid=(1,),
        out_shape=[jax.ShapeDtypeStruct(s, BF) for s in shapes],
        in_specs=specs,
        out_specs=[pl.BlockSpec(s, lambda i: (0, 0, 0)) for s in shapes],
        compiler_params=pltpu.CompilerParams(vmem_limit_bytes=58 * 2**20),
        name="add_kernel",
    )(*args)


def flip(value, axis):
    return lax.ppermute(value, axis, [(0, 1), (1, 0)])


def swap_all(value, axes):
    return lax.all_to_all(value, axes, split_axis=0, concat_axis=0, tiled=True)


def tie(*values):
    return lax.optimization_barrier(values)


def on_device(
    tokens,
    image_tokens,
    caption_lengths,
    arrival_order,
    w_qkv,
    w_out,
    w_cross_q,
    w_cross_kv,
    w_cross_out,
    w_up,
    w_down,
    small_params,
    cotangent,
):
    depth = lax.axis_size("z")
    height = D // (8 * depth)
    rows = tokens.shape[0]
    captions = caption_lengths.shape[1]
    slots = captions * CAP_LEN
    images = captions * IMG
    lens, arr = caption_lengths, arrival_order
    me = jnp.stack([lax.axis_index(a) for a in AXES]).astype(jnp.int32).reshape(1, 4)
    vmem = pltpu.VMEM
    sems = lambda n: pltpu.SemaphoreType.DMA((n,))
    shards = (w_qkv, w_out, w_cross_q, w_cross_kv, w_cross_out, w_up, w_down)

    share = small_params.shape[0]
    flat_shards = [w.reshape(-1, LANES) for w in shards]
    packed = lambda n: [((depth, 2, height, n), BF)]
    chunked = [vmem((w_up.shape[0] // LANES, LANES), F32)]
    (a,) = run(pack_self_kernel, packed(4 * HALF), [VM] * 2, chunked, *flat_shards[:2])
    (b,) = run(
        pack_cross_kernel, packed(4 * HALF + LANES), [VM] * 4, chunked,
        *flat_shards[2:5], small_params.reshape(1, share),
    )
    part = ((TOKENS_AT + 48, 2 * D), BF)
    near, core, chip = run(
        pack_group_kernel,
        [part, part, ((2,) + part[0], BF)],
        [SM] + [VM] * 4,
        chunked + [vmem((FOLD,) + part[0], BF)],
        me, *flat_shards[5:], tokens.reshape(FOLD, -1, D), cotangent.reshape(FOLD, -1, D),
    )

    def along_z(packed):
        got = swap_all(packed.reshape(2 * depth, height, -1), ("z", "c"))
        return got.reshape(depth, 2 * height, -1)

    a, chip = along_z(a), flip(chip, "y")
    img = image_tokens.reshape(images, V)
    (img_t,) = run(transpose_kernel, [((V, images), BF)], [VM], [], img)
    a, b, chip, core, img_t = tie(a, b, chip, core, img_t)
    b = along_z(b)
    ax, ay = flip(a, "x"), flip(a, "y")
    img_t_far = flip(img_t, "c")
    hidden, slotted, grad_slot = run(
        spread_kernel,
        [((depth, FOLD, height, 2 * D), BF), ((rows, D), BF), ((rows, D), BF)],
        [SM] + [VM] * 5,
        [vmem((rows, 2 * D), F32)],
        me, arr, near, chip, flip(core, "c"), flip(chip[1], "c"),
    )
    a_far = flip(a, "c")
    b, ax, ay, hidden, grad_slot, img_t_far, a_far = tie(
        b, ax, ay, hidden, grad_slot, img_t_far, a_far
    )
    def group_rows(value):
        far = flip(value, "y")
        return (value, flip(value, "c"), far, flip(far, "c"))

    bx, by = flip(b, "x"), flip(b, "y")
    hidden = swap_all(hidden.reshape(depth, FOLD * height, 2 * D), "z")
    b_far, ax_far, ay_far = flip(b, "c"), flip(ax, "c"), flip(ay, "c")
    bx, by, ax, ax_far, ay_far, b_far = tie(bx, by, ax, ax_far, ay_far, b_far)
    axy, byx = flip(ax, "y"), flip(by, "x")
    by_far, bx_far = flip(by, "c"), flip(bx, "c")
    axy, byx, by_far, bx_far, hidden = tie(axy, byx, by_far, bx_far, hidden)
    pieces_a = (a, ay, ax, axy, a_far, ay_far, ax_far, flip(axy, "c"))
    pieces_b = (b, by, bx, byx, b_far, by_far, bx_far, flip(byx, "c"))
    hidden, pieces_a, pieces_b = tie(hidden, pieces_a, pieces_b)
    hidden_far = flip(hidden, "x")
    grad_slots = group_rows(grad_slot)

    weight_shape = lambda n: vmem((depth, 2, 2, 2 * height, n * D), BF)
    (
        table, saved, after_self, after_cross, normed_mlp,
        projected, probs_self, query_slots, kv, probs_cross,
    ) = run(
        functools.partial(forward_kernel, share),
        [
            ((8 * depth * share // D, D), F32),
            ((rows, 4 * D), BF),
            ((rows, D), F32),
            ((rows, D), F32),
            ((rows, D), BF),
            ((rows, 3 * D), BF),
            ((BATCHES, HEADS * rows, rows), BF),
            ((slots, D), BF),
            ((images, 2 * D), BF),
            ((captions * BATCHES, HEADS * CAP_LEN, IMG), BF),
        ],
        [SM, SM] + [VM] * 2 + [HB] * 16,
        [
            vmem((rows, 3 * D), BF),
            vmem((BATCHES, HEADS * rows, rows), BF),
            vmem((slots, D), BF),
            vmem((images, 2 * D), BF),
            vmem((captions * BATCHES, HEADS * CAP_LEN, IMG), BF),
            weight_shape(3),
            weight_shape(1),
            weight_shape(1),
            weight_shape(2),
            weight_shape(1),
            vmem((slots, D), BF),
            vmem((4, depth, 2 * height, LANES), BF),
            vmem((72, LANES), F32),
            sems(71 + 2 * captions),
        ],
        lens, me, slotted, img, *pieces_a, *pieces_b,
        copied=5,
    )
    inputs = group_rows(normed_mlp)
    small_shape = ((11 * PAIRS, LANES), F32)
    saved_far = flip(saved, "c")
    (
        grad_near, grad_keep, grad_send, grad_send_y, active, grad_hidden, small,
    ) = run(
        mlp_kernel,
        [
            ((rows, D), F32),
            ((rows, D), BF),
            ((rows, D), BF),
            ((rows, D), BF),
            ((4 * rows, D), BF),
            ((4 * rows, D), BF),
            small_shape,
        ],
        [SM] + [VM] * 9 + [HB] * 2,
        [
            vmem((4 * rows, D), BF),
            vmem((4 * rows, D), BF),
            vmem((depth, 2, FOLD * height, 2 * D), BF),
            vmem((2, 2 * rows, D), F32),
            sems(2),
        ],
        me, table, *inputs, *grad_slots,
        hidden, hidden_far,
    )

    def owned(value, parts, axes):
        got = swap_all(value.reshape(parts * depth, height, -1), axes)
        return got.reshape(depth, parts, height, -1)

    flat = lambda n: ((height * n * PAIRS, LANES), F32)

    def combined(keep, far):
        return run(combine_kernel, [((rows, D), BF)], [VM] * 2, [], keep, far, mib=16)[0]

    grad_far = flip(combined(grad_keep, flip(grad_send_y, "c")), "y")
    grad_core = flip(grad_send, "c")
    out_near, out_keep, out_send, out_send_y, hidden_grad = run(
        hidden_grad_kernel,
        [((rows, D), F32)] + [((rows, D), BF)] * 3 + [((D, 2 * D), BF)],
        [SM] + [HB] * 12,
        [vmem((4 * rows, D), BF)] * 4
        + [vmem((2, D, D), BF), vmem((depth, 2, FOLD * height, D), BF), sems(14)],
        me, *inputs, grad_hidden, active, *grad_slots, hidden, hidden_far,
        copied=1,
    )
    grad_far, grad_core, hidden_grad, saved_far, out_send, out_send_y = tie(
        grad_far, grad_core, hidden_grad, saved_far, out_send, out_send_y
    )
    hidden_got = swap_all(hidden_grad.reshape(2 * depth, FOLD * height, 2 * D), ("z", "x"))
    out_core, out_core_y = flip(out_send, "c"), flip(out_send_y, "c")
    grad_state, small, half_keep, half_send, kv_keep, kv_send = run(
        cross_back_kernel,
        [
            ((rows, D), F32),
            small_shape,
            ((rows, 3 * HALF), BF),
            ((rows, 3 * HALF), BF),
            ((images, D), BF),
            ((images, D), BF),
        ],
        [SM, SM] + [VM] * 5 + [HB, VM, HB] + [VM] * 3 + [HB] * 8,
        [
            weight_shape(1),
            weight_shape(1),
            vmem((slots, D), BF),
            vmem((slots, D), BF),
            vmem((images, 2 * D), BF),
            vmem((images, D), BF),
            vmem((images, D), BF),
            vmem((images, 2 * D), BF),
            vmem((captions * BATCHES, HEADS * CAP_LEN, IMG), BF),
            sems(18 + 2 * captions),
        ],
        lens, me, grad_near, grad_core, grad_far, after_cross, grad_slot, probs_cross, query_slots,
        kv, after_self, table, small, *pieces_b,
        copied=2,
    )
    grad_state, half_send, kv_send, out_core_y = tie(grad_state, half_send, kv_send, out_core_y)
    half_far, kv_far = flip(half_send, "c"), flip(kv_send, "c")
    out_far = flip(combined(out_keep, out_core_y), "y")
    grad_rows, small, self_keep, self_send = run(
        self_back_kernel,
        [
            ((rows, D), BF),
            small_shape,
            ((rows, 3 * HALF), BF),
            ((rows, 3 * HALF), BF),
        ],
        [SM] + [VM] * 4 + [HB] * 10,
        [
            weight_shape(1),
            weight_shape(3),
            vmem((rows, D), BF),
            vmem((rows, 3 * D), BF),
            vmem((BATCHES, HEADS * rows, rows), BF),
            vmem((rows, 3 * D), BF),
            sems(34),
        ],
        me, grad_state, slotted, table, small, probs_self, projected, *pieces_a,
    )
    self_send, grad_rows, half_far, kv_far, out_far = tie(
        self_send, grad_rows, half_far, kv_far, out_far
    )
    self_far = flip(self_send, "c")
    block = lambda n: ((2, depth, 2 * height, n), BF)
    kv_0, kv_1, mix_0, mix_1 = run(
        cross_grad_kernel,
        [block(3 * HALF)] * 2 + [block(2 * HALF)] * 2,
        [SM] + [HB] * 8,
        [vmem((rows, 4 * D), BF)] * 2
        + [vmem((rows, 3 * HALF), BF)] * 2
        + [vmem((V, images), BF)] * 2
        + [vmem((images, D), BF)] * 2
        + [vmem(block(n * HALF)[0], BF) for n in (3, 3, 2, 2)]
        + [vmem((D, D), F32), sems(12)],
        me, saved, saved_far, half_keep, half_far, img_t, img_t_far, kv_keep, kv_far,
        copied=4,
    )
    kv_0, kv_1, mix_0, mix_1, self_far, grad_rows = tie(
        kv_0, kv_1, mix_0, mix_1, self_far, grad_rows
    )
    kv_1, mix_1 = flip(kv_1, "x"), flip(mix_1, "y")
    q_0, q_1, v_0, v_1 = run(
        functools.partial(self_grad_kernel, share),
        [block(D)] * 2 + [block(HALF + LANES)] * 2,
        [SM] + [VM] * 5,
        [vmem((D, D), F32)],
        me, saved, saved_far, self_keep, self_far, small,
    )
    q_0, q_1, v_0, v_1, grad_rows = tie(q_0, q_1, v_0, v_1, grad_rows)
    q_1, v_1 = flip(q_1, "y"), flip(v_1, "x")
    part = ((rows // FOLD, 2 * D), BF)
    near, core, chip = run(
        return_kernel,
        [part, part, ((2,) + part[0], BF)],
        [SM] + [VM] * 7,
        [vmem((rows, 2 * D), F32)],
        me, arr, after_cross, table, out_near, out_core, out_far, grad_rows,
    )
    kv_1, mix_1, q_1, v_1, chip = tie(kv_1, mix_1, q_1, v_1, chip)
    kv_2, mix_2, q_2, v_2 = add_up(
        *([(near, 1), (got, 1)] for near, got in ((kv_0, kv_1), (mix_0, mix_1), (q_0, q_1), (v_0, v_1)))
    )
    kv_2, mix_2, q_2, v_2 = flip(kv_2, "y"), flip(mix_2, "x"), flip(q_2, "x"), flip(v_2, "y")
    kv_2, mix_2, q_2, v_2, hidden_got, kv_send, chip = tie(
        kv_2, mix_2, q_2, v_2, hidden_got, kv_send, chip
    )
    (got,) = add_up(
        [(kv_0, 0), (kv_1, 0), kv_2],
        [(mix_0, 0), (mix_1, 0), mix_2],
        [(q_0, 0), (q_1, 0), q_2],
        [(v_0, 0), (v_1, 0), v_2],
        joined=True,
    )
    got = owned(got, 2, ("z", "c"))
    chip = flip(chip, "y")
    hidden_part = ((height, 2 * D), BF)
    hidden_near, hidden_core, hidden_chip = run(
        depth_sum_kernel,
        [hidden_part, hidden_part, ((2,) + hidden_part[0], BF)],
        [SM, VM],
        [vmem((FOLD * height, 2 * D), F32)],
        me, hidden_got,
    )
    hidden_chip = flip(hidden_chip, "y")
    (grad_image,) = run(
        image_grad_kernel,
        [((images, D), BF)],
        [VM, VM, SM] + [HB] * 8,
        [vmem((2, depth, 2, 2, 2 * height, D), BF), sems(8)],
        kv_keep, kv_send, me, *pieces_b,
    )
    grad_up, grad_down = run(
        unpack_hidden_kernel, [flat(FOLD)] * 2, [SM] + [VM] * 4,
        [vmem((FOLD, height, 2 * D), BF)],
        me, hidden_near, hidden_chip, flip(hidden_core, "c"), flip(hidden_chip[1], "c"),
    )
    layer_out, grad_tokens = run(
        collect_kernel, [((FOLD, rows // FOLD, D), BF)] * 2, [SM] + [VM] * 4, [],
        me, near, chip, flip(core, "c"), flip(chip[1], "c"),
    )
    grad_cq, grad_ckv, grad_co, grad_out, grad_qkv, grad_small = run(
        unpack_kernel,
        [flat(n) for n in (1, 2, 1, 1, 3)] + [((8, LANES), F32)],
        [VM],
        [],
        got,
        mib=16,
    )
    return (
        layer_out.reshape(tokens.shape),
        grad_tokens.reshape(tokens.shape),
        grad_image.reshape(image_tokens.shape),
        *(
            g.reshape(-1)
            for g in (grad_qkv, grad_out, grad_cq, grad_ckv, grad_co, grad_up, grad_down)
        ),
        grad_small.reshape(-1)[: small_params.shape[0]],
    )


def general_norm_rows(inputs, gain_vec, shift_vec):
    centred = inputs - jnp.mean(inputs, axis=-1, keepdims=True)
    variance = jnp.mean(centred * centred, axis=-1, keepdims=True)
    return centred * lax.rsqrt(variance + epsilon) * gain_vec + shift_vec


def general_norm_back(inputs, gain_vec, shift_vec, grad_normed):
    _, pullback = jax.vjp(general_norm_rows, inputs, gain_vec, shift_vec)
    return pullback(grad_normed)


def general_gelu_exact(inputs):
    return jax.nn.gelu(inputs, approximate=False)


def general_gelu_back(inputs, grad_active):
    _, pullback = jax.vjp(general_gelu_exact, inputs)
    return pullback(grad_active)[0]


def general_slot_index(lengths, arrivals):
    run_ends = jnp.cumsum(lengths)
    starts = run_ends - lengths
    caption = jnp.sum((run_ends[None, :] <= arrivals[:, None]).astype(jnp.int32), axis=1)
    picked = caption[:, None] == jnp.arange(lengths.shape[0], dtype=jnp.int32)[None, :]
    first_row = jnp.sum(jnp.where(picked, starts[None, :], 0), axis=1)
    return caption * CAP_LEN + arrivals - first_row


def general_score_block(queries, keys_in, allowed):
    scores = jnp.einsum(
        "cqhd,ckhd->chqk", queries, keys_in, preferred_element_type=jnp.float32
    ) * HEAD_DIM ** (-0.5)
    return jnp.where(allowed, scores, -masked_fill)


def general_attention(queries, keys_in, values, allowed):
    scores = general_score_block(queries, keys_in, allowed)
    row_max = jnp.max(scores, axis=-1, keepdims=True)
    log_total = row_max + jnp.log(jnp.sum(jnp.exp(scores - row_max), axis=-1, keepdims=True))
    attn_weights = jnp.exp(scores - log_total).astype(jnp.bfloat16)
    mixed_out = jnp.einsum(
        "chqk,ckhd->cqhd", attn_weights, values, preferred_element_type=jnp.float32
    ).astype(jnp.bfloat16)
    return (mixed_out, log_total)


def general_attention_back(queries, keys_in, values, log_total, grad_mixed, allowed):
    scores = general_score_block(queries, keys_in, allowed)
    attn_weights = jnp.exp(scores - log_total)
    grad_weights = jnp.einsum(
        "cqhd,ckhd->chqk", grad_mixed, values, preferred_element_type=jnp.float32
    )
    centre = jnp.sum(attn_weights * grad_weights, axis=-1, keepdims=True)
    grad_scores = (attn_weights * (grad_weights - centre)).astype(jnp.bfloat16)
    grad_queries = jnp.einsum(
        "chqk,ckhd->cqhd", grad_scores, keys_in, preferred_element_type=jnp.float32
    ) * HEAD_DIM ** (-0.5)
    grad_keys = jnp.einsum(
        "chqk,cqhd->ckhd", grad_scores, queries, preferred_element_type=jnp.float32
    ) * HEAD_DIM ** (-0.5)
    grad_values = jnp.einsum(
        "chqk,cqhd->ckhd",
        attn_weights.astype(jnp.bfloat16),
        grad_mixed,
        preferred_element_type=jnp.float32,
    )
    return (grad_queries, grad_keys, grad_values)


def general_unpack_params(gathered):
    (
        flat_qkv,
        flat_out,
        flat_cross_q,
        flat_cross_kv,
        flat_cross_out,
        flat_up,
        flat_down,
        flat_small,
    ) = gathered
    small_vals = flat_small.astype(jnp.float32)
    return (
        flat_qkv.reshape(D, 3 * D),
        flat_out.reshape(D, D),
        flat_cross_q.reshape(D, D),
        flat_cross_kv.reshape(V, 2 * D),
        flat_cross_out.reshape(D, D),
        flat_up.reshape(D, FF),
        flat_down.reshape(FF, D),
        small_vals[: 3 * D].reshape(3, D),
        small_vals[3 * D : 6 * D].reshape(3, D),
        small_vals[6 * D : 6 * D + FF],
        small_vals[6 * D + FF :],
    )


def general_forward(slotted, image_rows, params, allowed, open_mask):
    (
        mat_qkv,
        mat_out,
        mat_cross_q,
        mat_cross_kv,
        mat_cross_out,
        mat_up,
        mat_down,
        norm_gains,
        shifts,
        up_bias,
        down_bias,
    ) = params
    captions = slotted.shape[0] // CAP_LEN
    head_count = D // HEAD_DIM
    normed_self = general_norm_rows(slotted, norm_gains[0], shifts[0]).astype(jnp.bfloat16)
    projected = jnp.dot(normed_self, mat_qkv, preferred_element_type=jnp.float32).astype(
        jnp.bfloat16
    )
    projected = projected.reshape(captions, CAP_LEN, 3, head_count, HEAD_DIM)
    self_mixed, self_total = general_attention(
        projected[:, :, 0], projected[:, :, 1], projected[:, :, 2], allowed
    )
    self_mixed = self_mixed.reshape(-1, D)
    after_self = slotted + jnp.dot(self_mixed, mat_out, preferred_element_type=jnp.float32)
    normed_cross = general_norm_rows(after_self, norm_gains[1], shifts[1]).astype(jnp.bfloat16)
    cross_query = jnp.dot(normed_cross, mat_cross_q, preferred_element_type=jnp.float32).astype(
        jnp.bfloat16
    )
    cross_query = cross_query.reshape(captions, CAP_LEN, head_count, HEAD_DIM)
    image_kv = jnp.dot(image_rows, mat_cross_kv, preferred_element_type=jnp.float32).astype(
        jnp.bfloat16
    )
    image_kv = image_kv.reshape(captions, IMG, 2, head_count, HEAD_DIM)
    cross_mixed, cross_total = general_attention(
        cross_query, image_kv[:, :, 0], image_kv[:, :, 1], open_mask
    )
    cross_mixed = cross_mixed.reshape(-1, D)
    after_cross = after_self + jnp.dot(
        cross_mixed, mat_cross_out, preferred_element_type=jnp.float32
    )
    normed_mlp = general_norm_rows(after_cross, norm_gains[2], shifts[2]).astype(jnp.bfloat16)
    hidden = jnp.dot(normed_mlp, mat_up, preferred_element_type=jnp.float32) + up_bias
    activated = general_gelu_exact(hidden).astype(jnp.bfloat16)
    result = (
        after_cross + jnp.dot(activated, mat_down, preferred_element_type=jnp.float32) + down_bias
    )
    saved_state = (
        slotted,
        normed_self,
        projected,
        self_total,
        self_mixed,
        after_self,
        normed_cross,
        cross_query,
        image_kv,
        cross_total,
        cross_mixed,
        after_cross,
        normed_mlp,
        hidden,
        activated,
    )
    return (result, saved_state)


def general_backward(saved_state, grad_slot, image_rows, params, allowed, open_mask):
    (
        mat_qkv,
        mat_out,
        mat_cross_q,
        mat_cross_kv,
        mat_cross_out,
        mat_up,
        mat_down,
        norm_gains,
        shifts,
        up_bias,
        down_bias,
    ) = params
    (
        slotted,
        normed_self,
        projected,
        self_total,
        self_mixed,
        after_self,
        normed_cross,
        cross_query,
        image_kv,
        cross_total,
        cross_mixed,
        after_cross,
        normed_mlp,
        hidden,
        activated,
    ) = saved_state
    captions = slotted.shape[0] // CAP_LEN
    head_count = D // HEAD_DIM
    grad_branch = grad_slot.astype(jnp.bfloat16)
    grad_down = jnp.einsum("rf,rd->fd", activated, grad_branch, preferred_element_type=jnp.float32)
    grad_down_bias = jnp.sum(grad_slot, axis=0)
    grad_active = jnp.einsum("rd,fd->rf", grad_branch, mat_down, preferred_element_type=jnp.float32)
    grad_hidden = general_gelu_back(hidden, grad_active).astype(jnp.bfloat16)
    grad_up = jnp.einsum("rd,rf->df", normed_mlp, grad_hidden, preferred_element_type=jnp.float32)
    grad_up_bias = jnp.sum(grad_hidden.astype(jnp.float32), axis=0)
    grad_normed = jnp.einsum("rf,df->rd", grad_hidden, mat_up, preferred_element_type=jnp.float32)
    grad_cross_in, grad_gain3, grad_shift3 = general_norm_back(
        after_cross, norm_gains[2], shifts[2], grad_normed
    )
    grad_after_cross = grad_slot + grad_cross_in
    grad_branch = grad_after_cross.astype(jnp.bfloat16)
    grad_cross_out = jnp.einsum(
        "rd,re->de", cross_mixed, grad_branch, preferred_element_type=jnp.float32
    )
    grad_mixed = jnp.einsum(
        "re,de->rd", grad_branch, mat_cross_out, preferred_element_type=jnp.float32
    ).astype(jnp.bfloat16)
    grad_mixed = grad_mixed.reshape(captions, CAP_LEN, head_count, HEAD_DIM)
    grad_query, grad_key, grad_value = general_attention_back(
        cross_query, image_kv[:, :, 0], image_kv[:, :, 1], cross_total, grad_mixed, open_mask
    )
    grad_query = grad_query.reshape(-1, D).astype(jnp.bfloat16)
    grad_kv = jnp.stack([grad_key, grad_value], axis=2).reshape(-1, 2 * D).astype(jnp.bfloat16)
    grad_cross_q = jnp.einsum(
        "rd,re->de", normed_cross, grad_query, preferred_element_type=jnp.float32
    )
    grad_cross_kv = jnp.einsum("iv,ie->ve", image_rows, grad_kv, preferred_element_type=jnp.float32)
    grad_image = jnp.einsum(
        "ie,ve->iv", grad_kv, mat_cross_kv, preferred_element_type=jnp.float32
    ).astype(jnp.bfloat16)
    grad_normed = jnp.einsum(
        "re,de->rd", grad_query, mat_cross_q, preferred_element_type=jnp.float32
    )
    grad_self_in, grad_gain2, grad_shift2 = general_norm_back(
        after_self, norm_gains[1], shifts[1], grad_normed
    )
    grad_after_self = grad_after_cross + grad_self_in
    grad_branch = grad_after_self.astype(jnp.bfloat16)
    grad_out = jnp.einsum("rd,re->de", self_mixed, grad_branch, preferred_element_type=jnp.float32)
    grad_mixed = jnp.einsum(
        "re,de->rd", grad_branch, mat_out, preferred_element_type=jnp.float32
    ).astype(jnp.bfloat16)
    grad_mixed = grad_mixed.reshape(captions, CAP_LEN, head_count, HEAD_DIM)
    grad_query, grad_key, grad_value = general_attention_back(
        projected[:, :, 0], projected[:, :, 1], projected[:, :, 2], self_total, grad_mixed, allowed
    )
    grad_projected = (
        jnp.stack([grad_query, grad_key, grad_value], axis=2)
        .reshape(-1, 3 * D)
        .astype(jnp.bfloat16)
    )
    grad_w_qkv = jnp.einsum(
        "rd,re->de", normed_self, grad_projected, preferred_element_type=jnp.float32
    )
    grad_normed = jnp.einsum(
        "re,de->rd", grad_projected, mat_qkv, preferred_element_type=jnp.float32
    )
    grad_input, grad_gain1, grad_shift1 = general_norm_back(slotted, norm_gains[0], shifts[0], grad_normed)
    grad_input = grad_input + grad_after_self
    grad_small = jnp.concatenate(
        [
            grad_gain1,
            grad_gain2,
            grad_gain3,
            grad_shift1,
            grad_shift2,
            grad_shift3,
            grad_up_bias,
            grad_down_bias,
        ]
    )
    flat_grads = (
        grad_w_qkv.reshape(-1),
        grad_out.reshape(-1),
        grad_cross_q.reshape(-1),
        grad_cross_kv.reshape(-1),
        grad_cross_out.reshape(-1),
        grad_up.reshape(-1),
        grad_down.reshape(-1),
        grad_small,
    )
    return (grad_input, grad_image, flat_grads)


def general_sum_to_owners(flat_grads):
    summed = []
    for grad_vec in flat_grads:
        for axis in ("dp", "fsdp"):
            parts = grad_vec.reshape(lax.axis_size(axis), -1).astype(jnp.bfloat16)
            if axis == "dp":
                parts = grad_vec.reshape(lax.axis_size("dp"), lax.axis_size("fsdp"), -1)
                parts = parts.astype(jnp.bfloat16)
            got = lax.all_to_all(parts, axis, split_axis=0, concat_axis=0, tiled=True)
            grad_vec = jnp.sum(got.astype(jnp.float32), axis=0)
        summed.append(grad_vec)
    return tuple(summed)


def general_device(
    tokens,
    image_tokens,
    caption_lengths,
    arrival_order,
    w_qkv,
    w_out,
    w_cross_q,
    w_cross_kv,
    w_cross_out,
    w_up,
    w_down,
    small_params,
    cotangent,
):
    lengths = caption_lengths[0]
    slot_rows = general_slot_index(lengths, arrival_order[0])
    captions = lengths.shape[0]
    slot_total = captions * CAP_LEN
    arrived, arrived_grad = (
        lax.all_to_all(tokens, "fsdp", split_axis=0, concat_axis=0, tiled=True),
        lax.all_to_all(cotangent, "fsdp", split_axis=0, concat_axis=0, tiled=True),
    )
    slotted = jnp.zeros((slot_total, D), jnp.float32).at[slot_rows].set(arrived.astype(jnp.float32))
    grad_slot = (
        jnp.zeros((slot_total, D), jnp.float32).at[slot_rows].set(arrived_grad.astype(jnp.float32))
    )
    positions = jnp.arange(CAP_LEN, dtype=jnp.int32)
    allowed = (positions[None, :] <= positions[:, None])[None, None] & (
        positions[None, None, None, :] < lengths[:, None, None, None]
    )
    open_mask = jnp.ones((1, 1, 1, 1), jnp.bool_)
    image_rows = image_tokens.reshape(-1, V)
    owned_shards = (w_qkv, w_out, w_cross_q, w_cross_kv, w_cross_out, w_up, w_down, small_params)
    params = general_unpack_params(
        tuple(lax.all_gather(w, ("dp", "fsdp"), axis=0, tiled=True) for w in owned_shards)
    )
    result, saved_state = general_forward(slotted, image_rows, params, allowed, open_mask)
    grad_input, grad_image, flat_grads = general_backward(
        saved_state, grad_slot, image_rows, params, allowed, open_mask
    )
    summed = general_sum_to_owners(flat_grads)
    out_rows = result[slot_rows].astype(jnp.bfloat16)
    grad_rows = grad_input[slot_rows].astype(jnp.bfloat16)
    layer_out, grad_tokens = (
        lax.all_to_all(out_rows, "fsdp", split_axis=0, concat_axis=0, tiled=True),
        lax.all_to_all(grad_rows, "fsdp", split_axis=0, concat_axis=0, tiled=True),
    )
    return (layer_out, grad_tokens, grad_image.reshape(image_tokens.shape)) + tuple(summed)


def solution(mesh):
    dp, fsdp = mesh.shape["dp"], mesh.shape["fsdp"]
    inner, specs_of = on_device, ("dp", "fsdp")
    if fsdp == 4 and dp % 2 == 0 and D % (dp * fsdp * 8) == 0:
        mesh = Mesh(mesh.devices.reshape(dp // 2, 2, 2, 2), AXES)
        specs_of = AXES
    else:
        inner = general_device
    rows, flat, cube = P(specs_of, None), P(specs_of), P(specs_of, None, None)
    return jax.shard_map(
        inner,
        mesh=mesh,
        in_specs=(rows, cube, rows, rows) + (flat,) * 8 + (rows,),
        out_specs=(rows, rows, cube) + (flat,) * 8,
        check_vma=False,
    )
```

```python
import functools

import jax
import jax.numpy as jnp
from jax import lax
from jax.experimental import pallas as pl
from jax.experimental.pallas import tpu as pltpu
from jax.sharding import Mesh
from jax.sharding import PartitionSpec as P

D = 768
HEAD_DIM = 64
FF = 3072
V = 768
IMG = 256
CAP_LEN = 64
LANES = 128
PAIRS = D // LANES
HALF = D // 2
HEADS = 4
WIDE = HEADS * HEAD_DIM
BATCHES = D // WIDE
FOLD = FF // D
GROUP = FOLD * LANES
GROUPS = FF // GROUP
TOKENS_AT = 32
SCALE = HEAD_DIM ** (-0.5)
epsilon = 1e-05
masked_fill = 1e30

BF = jnp.bfloat16
F32 = jnp.float32
AXES = ("z", "x", "y", "c")


def mm(a, b):
    return lax.dot_general(a, b, (((1,), (0,)), ((), ())), preferred_element_type=F32)


def mm_t(a, b):
    return lax.dot_general(a, b, (((1,), (1,)), ((), ())), preferred_element_type=F32)


def t_mm(a, b):
    return lax.dot_general(a, b, (((0,), (0,)), ((), ())), preferred_element_type=F32)


def wide(value):
    return value.astype(F32)


def norm_rows(inputs, gain_vec, shift_vec):
    centred = inputs - jnp.mean(inputs, axis=-1, keepdims=True)
    variance = jnp.mean(centred * centred, axis=-1, keepdims=True)
    return centred * lax.rsqrt(variance + epsilon) * gain_vec + shift_vec


def norm_back(inputs, gain_vec, grad_normed):
    centred = inputs - jnp.mean(inputs, axis=-1, keepdims=True)
    variance = jnp.mean(centred * centred, axis=-1, keepdims=True)
    scale = lax.rsqrt(variance + epsilon)
    unit = centred * scale
    weighted = grad_normed * gain_vec
    grad_in = scale * (
        weighted
        - jnp.mean(weighted, axis=-1, keepdims=True)
        - unit * jnp.mean(weighted * unit, axis=-1, keepdims=True)
    )
    grad_gain = jnp.sum(grad_normed * unit, axis=0, keepdims=True)
    grad_shift = jnp.sum(grad_normed, axis=0, keepdims=True)
    return grad_in, grad_gain, grad_shift


def arrival_pick(arr_ref):
    rows = arr_ref.shape[1]
    place = lax.broadcasted_iota(jnp.int32, (rows, rows), 0)
    return jnp.where(place == arr_ref[...], 1.0, 0.0).astype(BF)


def caption_of(index, lens_ref):
    end = jnp.int32(0)
    found = jnp.zeros_like(index)
    for c in range(lens_ref.shape[1] - 1):
        end = end + lens_ref[0, c]
        found = found + jnp.where(index >= end, 1, 0)
    return found


def slot_pick(lens_ref, rows):
    captions = lens_ref.shape[1]
    shape = (captions * CAP_LEN, rows)
    slot = lax.broadcasted_iota(jnp.int32, shape, 0)
    row = lax.broadcasted_iota(jnp.int32, shape, 1)
    start = jnp.int32(0)
    hit = jnp.zeros(shape, F32)
    for c in range(captions):
        length = lens_ref[0, c]
        inside = slot - c * CAP_LEN
        ok = (inside >= 0) & (inside < length) & (row - start == inside)
        hit = hit + jnp.where(ok, 1.0, 0.0)
        start = start + length
    return hit.astype(BF)


def fold_pick(back):
    source = lax.broadcasted_iota(jnp.int32, (GROUP, GROUP), 1 if back else 0)
    target = lax.broadcasted_iota(jnp.int32, (GROUP, GROUP), 0 if back else 1)
    return jnp.where(target == (source % FOLD) * LANES + source // FOLD, 1.0, 0.0).astype(BF)


def head_mask(rows):
    shape = (HEADS * rows, WIDE)
    head = lax.broadcasted_iota(jnp.int32, shape, 1) // HEAD_DIM
    row = lax.broadcasted_iota(jnp.int32, shape, 0)
    inside = (row >= head * rows) & (row < (head + 1) * rows)
    return jnp.where(inside, 1.0, 0.0).astype(BF)


def stack_heads(block, mask):
    return jnp.concatenate([block] * HEADS, axis=0) * mask


def merge_heads(stacked):
    rows = stacked.shape[0] // HEADS
    head = lax.broadcasted_iota(jnp.int32, (rows, WIDE), 1) // HEAD_DIM
    out = stacked[:rows]
    for n in range(1, HEADS):
        out = jnp.where(head == n, stacked[n * rows : (n + 1) * rows], out)
    return out


def softmax_rows(scores):
    shifted = jnp.exp(scores - jnp.max(scores, axis=-1, keepdims=True))
    return shifted * (1.0 / jnp.sum(shifted, axis=-1, keepdims=True))


def lanes_at(start, width):
    return pl.ds(pl.multiple_of(start, LANES), width)


def pack_halves(shards, out, rows, at=0):
    depth, _, height, _ = out.shape
    pieces = HALF // LANES
    for shard, mats in shards:
        rows[: shard.shape[0], :] = wide(shard[...])
        for mat in range(mats):
            for half in range(2):
                for i in range(pieces):
                    index = mat * PAIRS + half * pieces + i
                    value = rows[pl.ds(index, height, stride=mats * PAIRS), :].astype(BF)
                    lanes = slice(at + i * LANES, at + (i + 1) * LANES)
                    for z in range(depth):
                        out[z, half, :, lanes] = value
            at += HALF
    return at


def pack_self_kernel(w_qkv, w_out, attend, rows):
    pack_halves(((w_qkv, 3), (w_out, 1)), attend, rows)


def pack_cross_kernel(w_cross_q, w_cross_kv, w_cross_out, small, attend, rows):
    at = pack_halves(((w_cross_q, 1), (w_cross_kv, 2), (w_cross_out, 1)), attend, rows)
    depth, _, height, _ = attend.shape
    flat = wide(small[...])
    tail = jnp.zeros((1, LANES - small.shape[1] % LANES), F32)
    flat = jnp.concatenate([flat, tail], axis=1)
    parts = [flat[:, n : n + LANES] for n in range(0, flat.shape[1], LANES)]
    block = jnp.concatenate(parts + [jnp.zeros((height - len(parts), LANES), F32)], axis=0)
    for z in range(depth):
        for half in range(2):
            attend[z, half, :, at:] = block.astype(BF)


def pack_group_kernel(me, w_up, w_down, tokens, cotangent, near, core, chip, rows, parts):
    chunks = FF // LANES
    height = w_up.shape[0] // chunks

    def chunk(index):
        return rows[pl.ds(index, height, stride=chunks), :].astype(BF)

    rows[...] = wide(w_up[...])
    pick = fold_pick(False)
    for t in range(GROUPS):
        group = jnp.concatenate([chunk(t * FOLD + k) for k in range(FOLD)], axis=1)
        folded = mm(group, pick).astype(BF)
        for j in range(FOLD):
            parts[j, :height, t * LANES : (t + 1) * LANES] = folded[
                :, j * LANES : (j + 1) * LANES
            ]
    rows[...] = wide(w_down[...])
    for j in range(FOLD):
        for i in range(PAIRS):
            at = D + i * LANES
            parts[j, :height, at : at + LANES] = chunk(j * PAIRS + i)
        parts[j, TOKENS_AT : TOKENS_AT + tokens.shape[1], :D] = tokens[j]
        parts[j, TOKENS_AT : TOKENS_AT + tokens.shape[1], D:] = cotangent[j]
    near[...] = parts[part_of(me, 0, 0)]
    core[...] = parts[part_of(me, 0, 1)]
    for c in range(2):
        chip[c] = parts[part_of(me, 1, c)]


def transpose_kernel(img, out):
    for n in range(0, img.shape[0], IMG):
        out[:, n : n + IMG] = img[n : n + IMG, :].T


def part_of(me, far_y, far_c):
    return lax.bitwise_xor(me[0, 2], far_y) * 2 + lax.bitwise_xor(me[0, 3], far_c)


def spread_kernel(me, arr, near, chip, core, both, hidden, slotted, grad_slot, arrived):
    height, count = hidden.shape[2], arrived.shape[0] // FOLD
    for value, far_y, far_c in (
        (near[...], 0, 0), (chip[0], 1, 0), (core[...], 0, 1), (both[...], 1, 1),
    ):
        index = part_of(me, far_y, far_c)
        for z in range(hidden.shape[0]):
            hidden[z, index] = value[:height]
        at = pl.multiple_of(index * count, 8)
        arrived[pl.ds(at, count), :] = wide(value[TOKENS_AT : TOKENS_AT + count])
    pick = arrival_pick(arr)
    slotted[...] = mm(pick, arrived[:, :D].astype(BF)).astype(BF)
    grad_slot[...] = mm(pick, arrived[:, D:].astype(BF)).astype(BF)


def fill_table(share, me, pieces, flat, table):
    depth, height = pieces.shape[1], pieces.shape[2] // 2
    lane = lax.broadcasted_iota(jnp.int32, (3, LANES), 1)
    flat[...] = jnp.zeros_like(flat)
    for owner in range(8 * depth):
        z, x, y, c = owner // 8, owner // 4 % 2, owner // 2 % 2, owner % 2
        index = lax.bitwise_xor(me[0, 1], x) * 2 + lax.bitwise_xor(me[0, 2], y)
        value = wide(pieces[index, z])[c * height : c * height + 3, :]
        row, shift = divmod(owner * share, LANES)
        if shift == 0:
            flat[row : row + 3, :] += value
        else:
            moved = pltpu.roll(value, shift, axis=1)
            flat[row : row + 3, :] += jnp.where(lane >= shift, moved, 0.0)
            flat[row + 1 : row + 4, :] += jnp.where(lane < shift, moved, 0.0)
    for n in range(table.shape[0] * PAIRS):
        row, lanes = n // PAIRS, slice(n % PAIRS * LANES, (n % PAIRS + 1) * LANES)
        table[row : row + 1, lanes] = flat[n : n + 1, :]


def depth_sum_kernel(me, got, near, core, chip, total):
    height = near.shape[0]
    value = wide(got[0])
    for z in range(1, got.shape[0]):
        value = value + wide(got[z])
    total[...] = value

    def part(far_y, far_c):
        at = pl.multiple_of(part_of(me, far_y, far_c) * height, 8)
        return total[pl.ds(at, height), :].astype(BF)

    near[...] = part(0, 0)
    core[...] = part(0, 1)
    for c in range(2):
        chip[c] = part(1, c)


def unpack_hidden_kernel(me, near, chip, core, both, up, down, got):
    for value, far_y, far_c in (
        (near[...], 0, 0), (chip[0], 1, 0), (core[...], 0, 1), (both[...], 1, 1),
    ):
        got[part_of(me, far_y, far_c)] = value
    height = got.shape[1]
    chunks = FF // LANES
    pick = fold_pick(True)
    for t in range(GROUPS):
        group = jnp.concatenate(
            [got[j, :, t * LANES : (t + 1) * LANES] for j in range(FOLD)], axis=1
        )
        natural = mm(group, pick)
        for k in range(FOLD):
            up[pl.ds(t * FOLD + k, height, stride=chunks), :] = natural[
                :, k * LANES : (k + 1) * LANES
            ]
    for j in range(FOLD):
        for i in range(PAIRS):
            at = D + i * LANES
            down[pl.ds(j * PAIRS + i, height, stride=chunks), :] = wide(
                got[j, :, at : at + LANES]
            )


def unpack_halves(got, outs):
    depth, height = got.shape[0], got.shape[2]
    parts = HALF // LANES
    place = 0
    for out in outs:
        chunks = out.shape[0] // height
        for mat in range(chunks // PAIRS):
            for half in range(2):
                for i in range(parts):
                    at = place + i * LANES
                    total = wide(got[0, half, :, at : at + LANES])
                    for z in range(1, depth):
                        total = total + wide(got[z, half, :, at : at + LANES])
                    index = mat * PAIRS + half * parts + i
                    out[pl.ds(index, height, stride=chunks), :] = total
            place += HALF
    return place


class Fetch:
    def __init__(self, sems):
        self.sems = sems
        self.used = 0

    def start(self, source, target):
        copy = pltpu.make_async_copy(source, target, self.sems.at[self.used])
        self.used += 1
        copy.start()
        return copy

    def columns(self, pieces, me, piece_at, target, target_at):
        copies = []
        for index, piece in enumerate(pieces):
            half = lax.bitwise_xor(me[0, 3], index // 4)
            x = lax.bitwise_xor(me[0, 1], index // 2 % 2)
            y = lax.bitwise_xor(me[0, 2], index % 2)
            copies.append(
                self.start(
                    piece.at[:, :, pl.ds(piece_at, HALF)],
                    target.at[:, x, y, :, lanes_at(target_at + half * HALF, HALF)],
                )
            )
        return copies


def wait(copies):
    for copy in copies:
        copy.wait()


def matrix(ref):
    shape = ref.shape
    return ref[...].reshape(shape[0] * shape[1] * shape[2] * shape[3], shape[4])


def forward_kernel(share, lens, me, slotted, img, *refs):
    pieces_a, pieces_b = refs[:8], refs[8:16]
    (
        table,
        projected, probs_self, saved, after_self, after_cross, normed_mlp, query_slots,
        kv_out, probs_out, kv, probs_cross, w_qkv, w_out, w_cq, w_kv, w_co, mixed_slots, small, flat, sems,
    ) = refs[16:]
    fetch = Fetch(sems)
    got_small = [
        fetch.start(pieces_b[n].at[:, :, pl.ds(4 * HALF, LANES)], small.at[n]) for n in range(4)
    ]
    got_qkv = []
    for mat in range(3):
        got_qkv += fetch.columns(pieces_a, me, mat * HALF, w_qkv, mat * D)
    got_out = fetch.columns(pieces_a, me, 3 * HALF, w_out, 0)
    got_cq = fetch.columns(pieces_b, me, 0, w_cq, 0)
    got_kv = fetch.columns(pieces_b, me, HALF, w_kv, 0)
    got_kv += fetch.columns(pieces_b, me, 2 * HALF, w_kv, D)
    got_co = fetch.columns(pieces_b, me, 3 * HALF, w_co, 0)
    rows = slotted.shape[0]
    wait(got_small)
    fill_table(share, me, small, flat, table)
    saved[:, :D] = norm_rows(wide(slotted[...]), table[0:1, :], table[3:4, :]).astype(BF)
    wait(got_qkv)
    projected[...] = mm(saved[:, :D], matrix(w_qkv)).astype(BF)
    query_at = lax.broadcasted_iota(jnp.int32, (rows, rows), 0)
    key_at = lax.broadcasted_iota(jnp.int32, (rows, rows), 1)
    same = caption_of(query_at, lens) == caption_of(key_at, lens)
    block = jnp.where(same & (key_at <= query_at), 0.0, -masked_fill)
    barred = jnp.concatenate([block] * HEADS, axis=0)
    mask = head_mask(rows)
    for n in range(BATCHES):
        query, key, value = (
            projected[:, m * D + n * WIDE : m * D + (n + 1) * WIDE] for m in range(3)
        )
        scores = mm_t(stack_heads(query, mask), key) * SCALE + barred
        weights_low = softmax_rows(scores).astype(BF)
        probs_self[n] = weights_low
        saved[:, D + n * WIDE : D + (n + 1) * WIDE] = merge_heads(
            mm(weights_low, value)
        ).astype(BF)
    wait(got_out)
    state = wide(slotted[...]) + mm(saved[:, D : 2 * D], matrix(w_out))
    after_self[...] = state
    low = norm_rows(state, table[1:2, :], table[4:5, :]).astype(BF)
    saved[:, 2 * D : 3 * D] = low
    wait(got_cq)
    pick = slot_pick(lens, rows)
    query_slots[...] = mm(pick, mm(low, matrix(w_cq)).astype(BF)).astype(BF)
    wait(got_kv)
    kv_mat = matrix(w_kv)
    mask = head_mask(CAP_LEN)
    sent = []
    for c in range(lens.shape[1]):
        slots = slice(c * CAP_LEN, (c + 1) * CAP_LEN)
        images = slice(c * IMG, (c + 1) * IMG)
        kv[images, :] = mm(img[images, :], kv_mat).astype(BF)
        for n in range(BATCHES):
            cols = slice(n * WIDE, (n + 1) * WIDE)
            query = stack_heads(query_slots[slots, cols], mask)
            weights_low = softmax_rows(mm_t(query, kv[images, cols]) * SCALE).astype(BF)
            probs_cross[c * BATCHES + n] = weights_low
            value = kv[images, D + n * WIDE : D + (n + 1) * WIDE]
            mixed_slots[slots, cols] = merge_heads(mm(weights_low, value)).astype(BF)
        batch = slice(c * BATCHES, (c + 1) * BATCHES)
        sent.append(fetch.start(kv.at[images], kv_out.at[images]))
        sent.append(fetch.start(probs_cross.at[batch], probs_out.at[batch]))
    low = t_mm(pick, mixed_slots[...]).astype(BF)
    saved[:, 3 * D :] = low
    wait(got_co)
    state = after_self[...] + mm(low, matrix(w_co))
    after_cross[...] = state
    normed_mlp[...] = norm_rows(state, table[2:3, :], table[5:6, :]).astype(BF)
    wait(sent)


def put_small(small, row, value):
    for k in range(PAIRS):
        at = row * PAIRS + k
        small[at : at + 1, :] = value[:, k * LANES : (k + 1) * LANES]


def own_part(value, me):
    part = me[0, 2] * 2 + me[0, 3]
    out = value[:, :LANES]
    for j in range(1, FOLD):
        out = jnp.where(part == j, value[:, j * LANES : (j + 1) * LANES], out)
    return out


def mlp_kernel(me, table, *refs):
    inputs, grads, pieces = refs[:4], refs[4:8], refs[8:10]
    (
        grad_near, grad_keep, grad_send, grad_send_y, out_near, out_keep, out_send, out_send_y,
        active, grad_hidden, small, all_in, all_grad, w_up, w_down, grad_part, out_part, sems,
    ) = refs[10:]
    fetch = Fetch(sems)
    got_up, got_down = [], []
    for index in range(2):
        x = lax.bitwise_xor(me[0, 1], index)
        got_up.append(fetch.start(pieces[index].at[:, :, pl.ds(0, D)], w_up.at[:, x]))
        got_down.append(fetch.start(pieces[index].at[:, :, pl.ds(D, D)], w_down.at[:, x]))
    rows = inputs[0].shape[0]
    for n in range(4):
        all_in[n * rows : (n + 1) * rows, :] = inputs[n][...]
        all_grad[n * rows : (n + 1) * rows, :] = grads[n][...]
    bias = [
        table[6 + n // PAIRS : 7 + n // PAIRS, n % PAIRS * LANES : (n % PAIRS + 1) * LANES]
        for n in range(FF // LANES)
    ]
    bias = jnp.concatenate(
        [jnp.concatenate(bias[t * FOLD : (t + 1) * FOLD], axis=1) for t in range(GROUPS)], axis=0
    )
    bias = own_part(mm(bias.astype(BF), fold_pick(False)), me)
    bias = jnp.concatenate([bias[t : t + 1, :] for t in range(GROUPS)], axis=1)
    wait(got_up)
    up_mat = w_up[...].reshape(D, D)
    wait(got_down)
    down_mat = w_down[...].reshape(D, D)

    def rows_of(n, total):
        at = pl.ds(pl.multiple_of(n * 2 * rows, 64), 2 * rows)
        hidden = mm(all_in[at, :], up_mat) + bias
        half = 0.5 + 0.5 * lax.erf(hidden * (0.5**0.5))
        act = (hidden * half).astype(BF)
        active[at, :] = act
        slope = half + hidden * (jnp.exp(hidden * hidden * -0.5) * 0.3989422804014327)
        grad_hid = (mm_t(all_grad[at, :], down_mat) * slope).astype(BF)
        grad_hidden[at, :] = grad_hid
        grad_part[n] = mm_t(grad_hid, up_mat)
        out_part[n] = mm(act, down_mat)
        return total + jnp.sum(wide(grad_hid), axis=0, keepdims=True)

    sums = lax.fori_loop(0, 2, rows_of, jnp.zeros((1, D), F32)).astype(BF)
    for part, outs in (
        (grad_part, (grad_near, grad_send, grad_keep, grad_send_y)),
        (out_part, (out_near, out_send, out_keep, out_send_y)),
    ):
        for n, out in enumerate(outs):
            out[...] = part[n // 2, n % 2 * rows : (n % 2 + 1) * rows].astype(out.dtype)
    sums = jnp.concatenate(
        [sums[:, t * LANES : (t + 1) * LANES] for t in range(GROUPS)] + [sums[:, :LANES]] * 2,
        axis=0,
    )
    part = me[0, 2] * 2 + me[0, 3]
    spread = jnp.concatenate(
        [jnp.where(part == j, sums, jnp.zeros_like(sums)) for j in range(FOLD)], axis=1
    )
    natural = mm(spread, fold_pick(True))
    small[...] = jnp.zeros_like(small)
    for n in range(FF // LANES):
        at = 6 * PAIRS + n
        small[at : at + 1, :] = natural[
            n // FOLD : n // FOLD + 1, n % FOLD * LANES : (n % FOLD + 1) * LANES
        ]
    put_small(small, 10, jnp.sum(wide(grads[0][...]), axis=0, keepdims=True))


def hidden_grad_kernel(*refs):
    normed, grad_slot = refs[:4], refs[4:8]
    active, grad_hidden, out = refs[8:]
    rows = lambda parts: jnp.concatenate([r[...] for r in parts], axis=0)
    out[:, :D] = t_mm(rows(normed), grad_hidden[...]).astype(BF)
    out[:, D:] = t_mm(active[...], rows(grad_slot)).astype(BF)


def combine_kernel(keep, far, out):
    out[...] = (wide(keep[...]) + wide(far[...])).astype(BF)


def cross_back_kernel(
    lens, me, grad_near, grad_core, grad_far, after_cross, grad_slot, probs_in, query_slots, kv_in,
    after_self, table, small_in, *refs,
):
    pieces = refs[:8]
    (
        grad_state, small, half_keep, half_send, keep_out, send_out,
        w_co, w_cq, mixed_slots, query_grads, grad_kv, kv_keep, kv_send, kv, probs, sems,
    ) = refs[8:]
    fetch = Fetch(sems)
    got_co = fetch.columns(pieces, me, 3 * HALF, w_co, 0)
    got_kv = [fetch.start(kv_in, kv), fetch.start(probs_in, probs)]
    got_cq = fetch.columns(pieces, me, 0, w_cq, 0)
    rows = after_self.shape[0]
    sent = []
    halves = ((0, half_keep, kv_keep), (1, half_send, kv_send))
    small[...] = small_in[...]
    grad_in, grad_gain, grad_shift = norm_back(
        after_cross[...],
        table[2:3, :],
        grad_near[...] + wide(grad_core[...]) + wide(grad_far[...]),
    )
    put_small(small, 2, grad_gain)
    put_small(small, 5, grad_shift)
    grad_after = wide(grad_slot[...]) + grad_in
    grad_state[...] = grad_after
    pick = slot_pick(lens, rows)
    wait(got_co)
    query_grads[:rows, :] = grad_after.astype(BF)
    mixed_slots[...] = mm(pick, mm_t(query_grads[:rows, :], matrix(w_co)).astype(BF)).astype(BF)
    for rel, half_out, _ in halves:
        at = lax.bitwise_xor(me[0, 3], rel) * HALF
        half_out[:, HALF : 2 * HALF] = query_grads[:rows, lanes_at(at, HALF)]
    mask = head_mask(CAP_LEN)
    wait(got_kv)
    for c in range(lens.shape[1]):
        slots = slice(c * CAP_LEN, (c + 1) * CAP_LEN)
        images = slice(c * IMG, (c + 1) * IMG)
        for n in range(BATCHES):
            cols = slice(n * WIDE, (n + 1) * WIDE)
            value_cols = slice(D + n * WIDE, D + (n + 1) * WIDE)
            grad_mixed = stack_heads(mixed_slots[slots, cols], mask)
            query = stack_heads(query_slots[slots, cols], mask)
            weights_low = probs[c * BATCHES + n]
            attn = wide(weights_low)
            grad_weights = mm_t(grad_mixed, kv[images, value_cols])
            centre = jnp.sum(attn * grad_weights, axis=-1, keepdims=True)
            grad_scores = (attn * (grad_weights - centre)).astype(BF)
            query_grads[slots, cols] = (
                merge_heads(mm(grad_scores, kv[images, cols])) * SCALE
            ).astype(BF)
            grad_kv[images, cols] = (t_mm(grad_scores, query) * SCALE).astype(BF)
            grad_kv[images, value_cols] = t_mm(weights_low, grad_mixed).astype(BF)
        for rel, _, kv_half in halves:
            at = lax.bitwise_xor(me[0, 3], rel) * HALF
            kv_half[images, :HALF] = grad_kv[images, lanes_at(at, HALF)]
            kv_half[images, HALF:] = grad_kv[images, lanes_at(at + D, HALF)]
        sent.append(fetch.start(kv_send.at[images], send_out.at[images]))
        sent.append(fetch.start(kv_keep.at[images], keep_out.at[images]))
    mixed_slots[:rows, :] = t_mm(pick, query_grads[...]).astype(BF)
    wait(got_cq)
    grad_in, grad_gain, grad_shift = norm_back(
        after_self[...], table[1:2, :], mm_t(mixed_slots[:rows, :], matrix(w_cq))
    )
    put_small(small, 1, grad_gain)
    put_small(small, 4, grad_shift)
    grad_after = grad_state[...] + grad_in
    grad_state[...] = grad_after
    query_grads[:rows, :] = grad_after.astype(BF)
    for rel, half_out, _ in halves:
        at = lax.bitwise_xor(me[0, 3], rel) * HALF
        half_out[:, :HALF] = mixed_slots[:rows, lanes_at(at, HALF)]
        half_out[:, 2 * HALF :] = query_grads[:rows, lanes_at(at, HALF)]
    wait(sent)


def self_back_kernel(me, grad_state, probs, projected, slotted, table, small_in, *refs):
    pieces = refs[:8]
    (
        grad_rows, small, keep, send,
        w_out, w_qkv, mixed, grad_projected, sems,
    ) = refs[8:]
    fetch = Fetch(sems)
    got_out = fetch.columns(pieces, me, 3 * HALF, w_out, 0)
    got_qkv = []
    for mat in range(3):
        got_qkv += fetch.columns(pieces, me, mat * HALF, w_qkv, mat * D)
    rows = slotted.shape[0]
    wait(got_out)
    mixed[...] = mm_t(grad_state[...].astype(BF), matrix(w_out)).astype(BF)
    mask = head_mask(rows)
    for n in range(BATCHES):
        cols, key_cols, value_cols = (
            slice(m * D + n * WIDE, m * D + (n + 1) * WIDE) for m in range(3)
        )
        grad_mixed = stack_heads(mixed[:, cols], mask)
        query = stack_heads(projected[:, cols], mask)
        weights_low = probs[n]
        attn = wide(weights_low)
        grad_weights = mm_t(grad_mixed, projected[:, value_cols])
        centre = jnp.sum(attn * grad_weights, axis=-1, keepdims=True)
        grad_scores = (attn * (grad_weights - centre)).astype(BF)
        grad_projected[:, cols] = (
            merge_heads(mm(grad_scores, projected[:, key_cols])) * SCALE
        ).astype(BF)
        grad_projected[:, key_cols] = (t_mm(grad_scores, query) * SCALE).astype(BF)
        grad_projected[:, value_cols] = t_mm(weights_low, grad_mixed).astype(BF)
    for mat in range(3):
        for rel, out in ((0, keep), (1, send)):
            at = lax.bitwise_xor(me[0, 3], rel) * HALF + mat * D
            out[:, mat * HALF : (mat + 1) * HALF] = grad_projected[:, lanes_at(at, HALF)]
    wait(got_qkv)
    grad_in, grad_gain, grad_shift = norm_back(
        wide(slotted[...]), table[0:1, :], mm_t(grad_projected[...], matrix(w_qkv))
    )
    grad_slotted = (grad_state[...] + grad_in).astype(BF)
    grad_rows[...] = grad_slotted
    small[...] = small_in[...]
    put_small(small, 0, grad_gain)
    put_small(small, 3, grad_shift)


def put_quadrants(grads, me, outs, at, first):
    depth, height = outs[0].shape[1:3]
    width = grads.shape[1]
    for i, out in enumerate(outs):
        for j in range(2):
            far_x, far_y = (i, j) if first == "x" else (j, i)
            x, y = lax.bitwise_xor(me[0, 1], far_x), lax.bitwise_xor(me[0, 2], far_y)
            for z in range(depth):
                low = pl.multiple_of(((z * 2 + x) * 2 + y) * height, 16)
                out[j, z, :, at : at + width] = grads[pl.ds(low, height), :].astype(BF)


def half_grads(pieces, me, outs, grads, first, at=0):
    for left, far_left, right, far_right in pieces:
        width = right.shape[1]
        grads[:, :width] = t_mm(left, right) + t_mm(far_left, far_right)
        put_quadrants(grads.at[:, :width], me, outs, at, first)
        at += width


def cross_grad_kernel(me, *refs):
    sources, targets, landed, made, grads, sems = (
        refs[:8], refs[8:12], refs[12:20], refs[20:24], refs[24], refs[25],
    )
    fetch = Fetch(sems)
    copies = [fetch.start(source, target) for source, target in zip(sources, landed)]
    saved, saved_far, half, half_far, img_t, img_t_far, kv, kv_far = landed
    part = lambda ref, n, width: ref[:, n * width : (n + 1) * width]
    piece = lambda left, right: (
        part(saved, left, D), part(saved_far, left, D),
        part(half, right, HALF), part(half_far, right, HALF),
    )
    wait(copies[:4])
    half_grads([piece(3, 1), piece(1, 2)], me, made[2:], grads, "y")
    sent = [fetch.start(made[n], targets[n]) for n in (3, 2)]
    half_grads([piece(2, 0)], me, made[:2], grads, "x")
    wait(copies[4:])
    grads[...] = mm(img_t[...], kv[...]) + mm(img_t_far[...], kv_far[...])
    put_quadrants(grads, me, made[:2], HALF, "x")
    sent += [fetch.start(made[n], targets[n]) for n in (1, 0)]
    wait(sent)


def owner_rows(small, blocks, share):
    height = blocks.shape[0] // (small.shape[0] * LANES // share)
    lane = lax.broadcasted_iota(jnp.int32, (3, LANES), 1)
    blocks[...] = jnp.zeros_like(blocks)
    table = jnp.concatenate([small[...], jnp.zeros((6, LANES), F32)], axis=0)
    for owner in range(small.shape[0] * LANES // share):
        row, shift = divmod(owner * share, LANES)
        if shift == 0:
            value = table[row : row + 3]
        else:
            moved = pltpu.roll(table[row : row + 4], LANES - shift, axis=1)
            value = jnp.where(lane < LANES - shift, moved[:3], moved[1:4])
        blocks[owner * height : owner * height + 3, :] = value


def self_grad_kernel(share, me, small, *refs):
    sources, targets, landed, made, grads, sems = (
        refs[:4], refs[4:8], refs[8:12], refs[12:16], refs[16], refs[17],
    )
    fetch = Fetch(sems)
    sources = [sources[0].at[:, pl.ds(0, D)], sources[1].at[:, pl.ds(0, D)], *sources[2:]]
    copies = [fetch.start(source, target) for source, target in zip(sources, landed)]
    own, far, half, half_far = landed
    wait(copies)
    half_grads([(own[...], far[...], half[:, :D], half_far[:, :D])], me, made[:2], grads, "y")
    sent = [fetch.start(made[n], targets[n]) for n in (1, 0)]
    half_grads([(own[...], far[...], half[:, D:], half_far[:, D:])], me, made[2:], grads, "x")
    blocks = grads.at[:, :LANES]
    owner_rows(small, blocks, share)
    put_quadrants(blocks, me, made[2:], HALF, "x")
    sent += [fetch.start(made[n], targets[n]) for n in (3, 2)]
    wait(sent)


def unpack_kernel(got, *outs):
    at = unpack_halves(got, outs[:-1])
    total = jnp.zeros((8, LANES), F32)
    for z in range(got.shape[0]):
        for c in range(2):
            total = total + wide(got[z, c, :8, at:])
    outs[-1][...] = total


def return_kernel(
    me, arr, after_cross, table, out_near, out_core, out_far, grad_rows, near, core, chip, rows
):
    pick = arrival_pick(arr)
    count = near.shape[0]
    result = after_cross[...] + out_near[...] + wide(out_core[...]) + wide(out_far[...])
    result = result + table[10:11, :]
    rows[:, :D] = t_mm(pick, result.astype(BF))
    rows[:, D:] = t_mm(pick, grad_rows[...])

    def part(far_y, far_c):
        at = pl.multiple_of(part_of(me, far_y, far_c) * count, 8)
        return rows[pl.ds(at, count), :].astype(BF)

    near[...] = part(0, 0)
    core[...] = part(0, 1)
    for c in range(2):
        chip[c] = part(1, c)


def collect_kernel(me, near, chip, core, both, layer_out, grad_tokens):
    for value, far_y, far_c in ((near[...], 0, 0), (chip[0], 1, 0), (core[...], 0, 1), (both[...], 1, 1)):
        index = part_of(me, far_y, far_c)
        layer_out[index] = value[:, :D]
        grad_tokens[index] = value[:, D:]


def image_grad_kernel(kv_keep, kv_send, *refs):
    me, pieces = refs[0], refs[1:9]
    grad_image, w_kv, sems = refs[9:]
    fetch = Fetch(sems)
    copies = []
    for index, piece in enumerate(pieces):
        x = lax.bitwise_xor(me[0, 1], index // 2 % 2)
        y = lax.bitwise_xor(me[0, 2], index % 2)
        copies.append(
            fetch.start(piece.at[:, :, pl.ds(HALF, D)], w_kv.at[index // 4, :, x, y])
        )
    wait(copies)
    near, far = w_kv[0].reshape(D, D), w_kv[1].reshape(D, D)
    for c in range(kv_keep.shape[0] // IMG):
        rows = pl.ds(c * IMG, IMG)
        grad_image[rows, :] = (mm_t(kv_keep[rows, :], near) + mm_t(kv_send[rows, :], far)).astype(
            BF
        )


def add_kernel(counts, joined, *refs):
    outs = refs[sum(counts) :]
    first = at = 0
    for n, count in enumerate(counts):
        for z in range(refs[first].shape[0]):
            total = wide(refs[first][z])
            for ref in refs[first + 1 : first + count]:
                total = total + wide(ref[z])
            if joined:
                outs[0][z, :, at : at + total.shape[-1]] = total.astype(BF)
            else:
                outs[n][z] = total.astype(BF)
        at += total.shape[-1]
        first += count


VM = pl.BlockSpec(memory_space=pltpu.VMEM)
SM = pl.BlockSpec(memory_space=pltpu.SMEM)
HB = pl.BlockSpec(memory_space=pl.ANY)


def run(kernel, outs, specs, scratch, *args, mib=58, copied=0):
    return pl.pallas_call(
        kernel,
        out_shape=[jax.ShapeDtypeStruct(s, t) for s, t in outs],
        in_specs=specs,
        out_specs=[VM] * (len(outs) - copied) + [HB] * copied,
        scratch_shapes=scratch,
        compiler_params=pltpu.CompilerParams(vmem_limit_bytes=mib * 2**20),
        name=(kernel.func if isinstance(kernel, functools.partial) else kernel).__name__,
    )(*args)


def add_up(*sums, joined=False):
    args, specs, shapes = [], [], []
    for terms in sums:
        for term in terms:
            array, index = term if isinstance(term, tuple) else (term, None)
            block = array.shape[-3:]
            if index is None:
                specs.append(pl.BlockSpec(block, lambda i: (0, 0, 0)))
            else:
                specs.append(pl.BlockSpec((None,) + block, lambda i, n=index: (n, 0, 0, 0)))
            args.append(array)
        shapes.append(block)
    if joined:
        shapes = [shapes[0][:2] + (sum(s[2] for s in shapes),)]
    return pl.pallas_call(
        functools.partial(add_kernel, [len(terms) for terms in sums], joined),
        grid=(1,),
        out_shape=[jax.ShapeDtypeStruct(s, BF) for s in shapes],
        in_specs=specs,
        out_specs=[pl.BlockSpec(s, lambda i: (0, 0, 0)) for s in shapes],
        compiler_params=pltpu.CompilerParams(vmem_limit_bytes=58 * 2**20),
        name="add_kernel",
    )(*args)


def flip(value, axis):
    return lax.ppermute(value, axis, [(0, 1), (1, 0)])


def swap_all(value, axes):
    return lax.all_to_all(value, axes, split_axis=0, concat_axis=0, tiled=True)


def tie(*values):
    return lax.optimization_barrier(values)


def on_device(
    tokens,
    image_tokens,
    caption_lengths,
    arrival_order,
    w_qkv,
    w_out,
    w_cross_q,
    w_cross_kv,
    w_cross_out,
    w_up,
    w_down,
    small_params,
    cotangent,
):
    depth = lax.axis_size("z")
    height = D // (8 * depth)
    rows = tokens.shape[0]
    captions = caption_lengths.shape[1]
    slots = captions * CAP_LEN
    images = captions * IMG
    lens, arr = caption_lengths, arrival_order
    me = jnp.stack([lax.axis_index(a) for a in AXES]).astype(jnp.int32).reshape(1, 4)
    vmem = pltpu.VMEM
    sems = lambda n: pltpu.SemaphoreType.DMA((n,))
    shards = (w_qkv, w_out, w_cross_q, w_cross_kv, w_cross_out, w_up, w_down)

    share = small_params.shape[0]
    flat_shards = [w.reshape(-1, LANES) for w in shards]
    packed = lambda n: [((depth, 2, height, n), BF)]
    chunked = [vmem((w_up.shape[0] // LANES, LANES), F32)]
    (a,) = run(pack_self_kernel, packed(4 * HALF), [VM] * 2, chunked, *flat_shards[:2])
    (b,) = run(
        pack_cross_kernel, packed(4 * HALF + LANES), [VM] * 4, chunked,
        *flat_shards[2:5], small_params.reshape(1, share),
    )
    part = ((TOKENS_AT + 48, 2 * D), BF)
    near, core, chip = run(
        pack_group_kernel,
        [part, part, ((2,) + part[0], BF)],
        [SM] + [VM] * 4,
        chunked + [vmem((FOLD,) + part[0], BF)],
        me, *flat_shards[5:], tokens.reshape(FOLD, -1, D), cotangent.reshape(FOLD, -1, D),
    )

    def along_z(packed):
        got = swap_all(packed.reshape(2 * depth, height, -1), ("z", "c"))
        return got.reshape(depth, 2 * height, -1)

    a, chip = along_z(a), flip(chip, "y")
    img = image_tokens.reshape(images, V)
    (img_t,) = run(transpose_kernel, [((V, images), BF)], [VM], [], img)
    a, b, chip, core, img_t = tie(a, b, chip, core, img_t)
    b = along_z(b)
    ax, ay = flip(a, "x"), flip(a, "y")
    img_t_far = flip(img_t, "c")
    hidden, slotted, grad_slot = run(
        spread_kernel,
        [((depth, FOLD, height, 2 * D), BF), ((rows, D), BF), ((rows, D), BF)],
        [SM] + [VM] * 5,
        [vmem((rows, 2 * D), F32)],
        me, arr, near, chip, flip(core, "c"), flip(chip[1], "c"),
    )
    a_far = flip(a, "c")
    b, ax, ay, hidden, grad_slot, img_t_far, a_far = tie(
        b, ax, ay, hidden, grad_slot, img_t_far, a_far
    )
    def group_rows(value):
        far = flip(value, "y")
        return (value, flip(value, "c"), far, flip(far, "c"))

    bx, by = flip(b, "x"), flip(b, "y")
    hidden = swap_all(hidden.reshape(depth, FOLD * height, 2 * D), "z")
    b_far, ax_far, ay_far = flip(b, "c"), flip(ax, "c"), flip(ay, "c")
    bx, by, ax, ax_far, ay_far, b_far = tie(bx, by, ax, ax_far, ay_far, b_far)
    axy, byx = flip(ax, "y"), flip(by, "x")
    by_far, bx_far = flip(by, "c"), flip(bx, "c")
    axy, byx, by_far, bx_far, hidden = tie(axy, byx, by_far, bx_far, hidden)
    pieces_a = (a, ay, ax, axy, a_far, ay_far, ax_far, flip(axy, "c"))
    pieces_b = (b, by, bx, byx, b_far, by_far, bx_far, flip(byx, "c"))
    hidden, pieces_a, pieces_b = tie(hidden, pieces_a, pieces_b)
    hidden_far = flip(hidden, "x")
    grad_slots = group_rows(grad_slot)

    weight_shape = lambda n: vmem((depth, 2, 2, 2 * height, n * D), BF)
    (
        table, projected, probs_self, saved, after_self, after_cross, normed_mlp, query_slots, kv,
        probs_cross,
    ) = run(
        functools.partial(forward_kernel, share),
        [
            ((8 * depth * share // D, D), F32),
            ((rows, 3 * D), BF),
            ((BATCHES, HEADS * rows, rows), BF),
            ((rows, 4 * D), BF),
            ((rows, D), F32),
            ((rows, D), F32),
            ((rows, D), BF),
            ((slots, D), BF),
            ((images, 2 * D), BF),
            ((captions * BATCHES, HEADS * CAP_LEN, IMG), BF),
        ],
        [SM, SM] + [VM] * 2 + [HB] * 16,
        [
            vmem((images, 2 * D), BF),
            vmem((captions * BATCHES, HEADS * CAP_LEN, IMG), BF),
            weight_shape(3),
            weight_shape(1),
            weight_shape(1),
            weight_shape(2),
            weight_shape(1),
            vmem((slots, D), BF),
            vmem((4, depth, 2 * height, LANES), BF),
            vmem((72, LANES), F32),
            sems(68 + 2 * captions),
        ],
        lens, me, slotted, img, *pieces_a, *pieces_b,
        copied=2,
    )
    inputs = group_rows(normed_mlp)
    small_shape = ((11 * PAIRS, LANES), F32)
    saved_far = flip(saved, "c")
    (
        grad_near, grad_keep, grad_send, grad_send_y, out_near, out_keep, out_send, out_send_y,
        active, grad_hidden, small,
    ) = run(
        mlp_kernel,
        [
            ((rows, D), F32),
            ((rows, D), BF),
            ((rows, D), BF),
            ((rows, D), BF),
            ((rows, D), F32),
            ((rows, D), BF),
            ((rows, D), BF),
            ((rows, D), BF),
            ((4 * rows, D), BF),
            ((4 * rows, D), BF),
            small_shape,
        ],
        [SM] + [VM] * 9 + [HB] * 2,
        [
            vmem((4 * rows, D), BF),
            vmem((4 * rows, D), BF),
            vmem((depth, 2, FOLD * height, D), BF),
            vmem((depth, 2, FOLD * height, D), BF),
            vmem((2, 2 * rows, D), F32),
            vmem((2, 2 * rows, D), F32),
            sems(4),
        ],
        me, table, *inputs, *grad_slots,
        hidden, hidden_far,
    )

    def owned(value, parts, axes):
        got = swap_all(value.reshape(parts * depth, height, -1), axes)
        return got.reshape(depth, parts, height, -1)

    flat = lambda n: ((height * n * PAIRS, LANES), F32)

    def combined(keep, far):
        return run(combine_kernel, [((rows, D), BF)], [VM] * 2, [], keep, far, mib=16)[0]

    grad_far = flip(combined(grad_keep, flip(grad_send_y, "c")), "y")
    grad_core = flip(grad_send, "c")
    (hidden_grad,) = run(
        hidden_grad_kernel,
        [((D, 2 * D), BF)],
        [VM] * 10,
        [],
        *inputs, *grad_slots, active, grad_hidden,
    )
    grad_far, grad_core, hidden_grad, saved_far, out_send, out_send_y = tie(
        grad_far, grad_core, hidden_grad, saved_far, out_send, out_send_y
    )
    hidden_got = swap_all(hidden_grad.reshape(2 * depth, FOLD * height, 2 * D), ("z", "x"))
    out_core, out_core_y = flip(out_send, "c"), flip(out_send_y, "c")
    grad_state, small, half_keep, half_send, kv_keep, kv_send = run(
        cross_back_kernel,
        [
            ((rows, D), F32),
            small_shape,
            ((rows, 3 * HALF), BF),
            ((rows, 3 * HALF), BF),
            ((images, D), BF),
            ((images, D), BF),
        ],
        [SM, SM] + [VM] * 5 + [HB, VM, HB] + [VM] * 3 + [HB] * 8,
        [
            weight_shape(1),
            weight_shape(1),
            vmem((slots, D), BF),
            vmem((slots, D), BF),
            vmem((images, 2 * D), BF),
            vmem((images, D), BF),
            vmem((images, D), BF),
            vmem((images, 2 * D), BF),
            vmem((captions * BATCHES, HEADS * CAP_LEN, IMG), BF),
            sems(18 + 2 * captions),
        ],
        lens, me, grad_near, grad_core, grad_far, after_cross, grad_slot, probs_cross, query_slots,
        kv, after_self, table, small, *pieces_b,
        copied=2,
    )
    grad_state, half_send, kv_send, out_core_y = tie(grad_state, half_send, kv_send, out_core_y)
    half_far, kv_far = flip(half_send, "c"), flip(kv_send, "c")
    out_far = flip(combined(out_keep, out_core_y), "y")
    grad_rows, small, self_keep, self_send = run(
        self_back_kernel,
        [
            ((rows, D), BF),
            small_shape,
            ((rows, 3 * HALF), BF),
            ((rows, 3 * HALF), BF),
        ],
        [SM] + [VM] * 6 + [HB] * 8,
        [
            weight_shape(1),
            weight_shape(3),
            vmem((rows, D), BF),
            vmem((rows, 3 * D), BF),
            sems(32),
        ],
        me, grad_state, probs_self, projected, slotted, table, small, *pieces_a,
    )
    self_send, grad_rows, half_far, kv_far, out_far = tie(
        self_send, grad_rows, half_far, kv_far, out_far
    )
    self_far = flip(self_send, "c")
    block = lambda n: ((2, depth, 2 * height, n), BF)
    kv_0, kv_1, mix_0, mix_1 = run(
        cross_grad_kernel,
        [block(3 * HALF)] * 2 + [block(2 * HALF)] * 2,
        [SM] + [HB] * 8,
        [vmem((rows, 4 * D), BF)] * 2
        + [vmem((rows, 3 * HALF), BF)] * 2
        + [vmem((V, images), BF)] * 2
        + [vmem((images, D), BF)] * 2
        + [vmem(block(n * HALF)[0], BF) for n in (3, 3, 2, 2)]
        + [vmem((D, D), F32), sems(12)],
        me, saved, saved_far, half_keep, half_far, img_t, img_t_far, kv_keep, kv_far,
        copied=4,
    )
    kv_0, kv_1, mix_0, mix_1, self_far, grad_rows = tie(
        kv_0, kv_1, mix_0, mix_1, self_far, grad_rows
    )
    kv_1, mix_1 = flip(kv_1, "x"), flip(mix_1, "y")
    q_0, q_1, v_0, v_1 = run(
        functools.partial(self_grad_kernel, share),
        [block(D)] * 2 + [block(HALF + LANES)] * 2,
        [SM, VM] + [HB] * 4,
        [vmem((rows, D), BF)] * 2
        + [vmem((rows, 3 * HALF), BF)] * 2
        + [vmem(block(n)[0], BF) for n in (D, D, HALF + LANES, HALF + LANES)]
        + [vmem((D, D), F32), sems(8)],
        me, small, saved, saved_far, self_keep, self_far,
        copied=4,
    )
    q_0, q_1, v_0, v_1, grad_rows = tie(q_0, q_1, v_0, v_1, grad_rows)
    q_1, v_1 = flip(q_1, "y"), flip(v_1, "x")
    part = ((rows // FOLD, 2 * D), BF)
    near, core, chip = run(
        return_kernel,
        [part, part, ((2,) + part[0], BF)],
        [SM] + [VM] * 7,
        [vmem((rows, 2 * D), F32)],
        me, arr, after_cross, table, out_near, out_core, out_far, grad_rows,
    )
    kv_1, mix_1, q_1, v_1, chip = tie(kv_1, mix_1, q_1, v_1, chip)
    kv_2, mix_2, q_2, v_2 = add_up(
        *([(near, 1), (got, 1)] for near, got in ((kv_0, kv_1), (mix_0, mix_1), (q_0, q_1), (v_0, v_1)))
    )
    kv_2, mix_2, q_2, v_2 = flip(kv_2, "y"), flip(mix_2, "x"), flip(q_2, "x"), flip(v_2, "y")
    kv_2, mix_2, q_2, v_2, hidden_got, kv_send, chip = tie(
        kv_2, mix_2, q_2, v_2, hidden_got, kv_send, chip
    )
    (got,) = add_up(
        [(kv_0, 0), (kv_1, 0), kv_2],
        [(mix_0, 0), (mix_1, 0), mix_2],
        [(q_0, 0), (q_1, 0), q_2],
        [(v_0, 0), (v_1, 0), v_2],
        joined=True,
    )
    got = owned(got, 2, ("z", "c"))
    chip = flip(chip, "y")
    hidden_part = ((height, 2 * D), BF)
    hidden_near, hidden_core, hidden_chip = run(
        depth_sum_kernel,
        [hidden_part, hidden_part, ((2,) + hidden_part[0], BF)],
        [SM, VM],
        [vmem((FOLD * height, 2 * D), F32)],
        me, hidden_got,
    )
    hidden_chip = flip(hidden_chip, "y")
    (grad_image,) = run(
        image_grad_kernel,
        [((images, D), BF)],
        [VM, VM, SM] + [HB] * 8,
        [vmem((2, depth, 2, 2, 2 * height, D), BF), sems(8)],
        kv_keep, kv_send, me, *pieces_b,
    )
    grad_up, grad_down = run(
        unpack_hidden_kernel, [flat(FOLD)] * 2, [SM] + [VM] * 4,
        [vmem((FOLD, height, 2 * D), BF)],
        me, hidden_near, hidden_chip, flip(hidden_core, "c"), flip(hidden_chip[1], "c"),
    )
    layer_out, grad_tokens = run(
        collect_kernel, [((FOLD, rows // FOLD, D), BF)] * 2, [SM] + [VM] * 4, [],
        me, near, chip, flip(core, "c"), flip(chip[1], "c"),
    )
    grad_cq, grad_ckv, grad_co, grad_out, grad_qkv, grad_small = run(
        unpack_kernel,
        [flat(n) for n in (1, 2, 1, 1, 3)] + [((8, LANES), F32)],
        [VM],
        [],
        got,
        mib=16,
    )
    return (
        layer_out.reshape(tokens.shape),
        grad_tokens.reshape(tokens.shape),
        grad_image.reshape(image_tokens.shape),
        *(
            g.reshape(-1)
            for g in (grad_qkv, grad_out, grad_cq, grad_ckv, grad_co, grad_up, grad_down)
        ),
        grad_small.reshape(-1)[: small_params.shape[0]],
    )


def general_norm_rows(inputs, gain_vec, shift_vec):
    centred = inputs - jnp.mean(inputs, axis=-1, keepdims=True)
    variance = jnp.mean(centred * centred, axis=-1, keepdims=True)
    return centred * lax.rsqrt(variance + epsilon) * gain_vec + shift_vec


def general_norm_back(inputs, gain_vec, shift_vec, grad_normed):
    _, pullback = jax.vjp(general_norm_rows, inputs, gain_vec, shift_vec)
    return pullback(grad_normed)


def general_gelu_exact(inputs):
    return jax.nn.gelu(inputs, approximate=False)


def general_gelu_back(inputs, grad_active):
    _, pullback = jax.vjp(general_gelu_exact, inputs)
    return pullback(grad_active)[0]


def general_slot_index(lengths, arrivals):
    run_ends = jnp.cumsum(lengths)
    starts = run_ends - lengths
    caption = jnp.sum((run_ends[None, :] <= arrivals[:, None]).astype(jnp.int32), axis=1)
    picked = caption[:, None] == jnp.arange(lengths.shape[0], dtype=jnp.int32)[None, :]
    first_row = jnp.sum(jnp.where(picked, starts[None, :], 0), axis=1)
    return caption * CAP_LEN + arrivals - first_row


def general_score_block(queries, keys_in, allowed):
    scores = jnp.einsum(
        "cqhd,ckhd->chqk", queries, keys_in, preferred_element_type=jnp.float32
    ) * HEAD_DIM ** (-0.5)
    return jnp.where(allowed, scores, -masked_fill)


def general_attention(queries, keys_in, values, allowed):
    scores = general_score_block(queries, keys_in, allowed)
    row_max = jnp.max(scores, axis=-1, keepdims=True)
    log_total = row_max + jnp.log(jnp.sum(jnp.exp(scores - row_max), axis=-1, keepdims=True))
    attn_weights = jnp.exp(scores - log_total).astype(jnp.bfloat16)
    mixed_out = jnp.einsum(
        "chqk,ckhd->cqhd", attn_weights, values, preferred_element_type=jnp.float32
    ).astype(jnp.bfloat16)
    return (mixed_out, log_total)


def general_attention_back(queries, keys_in, values, log_total, grad_mixed, allowed):
    scores = general_score_block(queries, keys_in, allowed)
    attn_weights = jnp.exp(scores - log_total)
    grad_weights = jnp.einsum(
        "cqhd,ckhd->chqk", grad_mixed, values, preferred_element_type=jnp.float32
    )
    centre = jnp.sum(attn_weights * grad_weights, axis=-1, keepdims=True)
    grad_scores = (attn_weights * (grad_weights - centre)).astype(jnp.bfloat16)
    grad_queries = jnp.einsum(
        "chqk,ckhd->cqhd", grad_scores, keys_in, preferred_element_type=jnp.float32
    ) * HEAD_DIM ** (-0.5)
    grad_keys = jnp.einsum(
        "chqk,cqhd->ckhd", grad_scores, queries, preferred_element_type=jnp.float32
    ) * HEAD_DIM ** (-0.5)
    grad_values = jnp.einsum(
        "chqk,cqhd->ckhd",
        attn_weights.astype(jnp.bfloat16),
        grad_mixed,
        preferred_element_type=jnp.float32,
    )
    return (grad_queries, grad_keys, grad_values)


def general_unpack_params(gathered):
    (
        flat_qkv,
        flat_out,
        flat_cross_q,
        flat_cross_kv,
        flat_cross_out,
        flat_up,
        flat_down,
        flat_small,
    ) = gathered
    small_vals = flat_small.astype(jnp.float32)
    return (
        flat_qkv.reshape(D, 3 * D),
        flat_out.reshape(D, D),
        flat_cross_q.reshape(D, D),
        flat_cross_kv.reshape(V, 2 * D),
        flat_cross_out.reshape(D, D),
        flat_up.reshape(D, FF),
        flat_down.reshape(FF, D),
        small_vals[: 3 * D].reshape(3, D),
        small_vals[3 * D : 6 * D].reshape(3, D),
        small_vals[6 * D : 6 * D + FF],
        small_vals[6 * D + FF :],
    )


def general_forward(slotted, image_rows, params, allowed, open_mask):
    (
        mat_qkv,
        mat_out,
        mat_cross_q,
        mat_cross_kv,
        mat_cross_out,
        mat_up,
        mat_down,
        norm_gains,
        shifts,
        up_bias,
        down_bias,
    ) = params
    captions = slotted.shape[0] // CAP_LEN
    head_count = D // HEAD_DIM
    normed_self = general_norm_rows(slotted, norm_gains[0], shifts[0]).astype(jnp.bfloat16)
    projected = jnp.dot(normed_self, mat_qkv, preferred_element_type=jnp.float32).astype(
        jnp.bfloat16
    )
    projected = projected.reshape(captions, CAP_LEN, 3, head_count, HEAD_DIM)
    self_mixed, self_total = general_attention(
        projected[:, :, 0], projected[:, :, 1], projected[:, :, 2], allowed
    )
    self_mixed = self_mixed.reshape(-1, D)
    after_self = slotted + jnp.dot(self_mixed, mat_out, preferred_element_type=jnp.float32)
    normed_cross = general_norm_rows(after_self, norm_gains[1], shifts[1]).astype(jnp.bfloat16)
    cross_query = jnp.dot(normed_cross, mat_cross_q, preferred_element_type=jnp.float32).astype(
        jnp.bfloat16
    )
    cross_query = cross_query.reshape(captions, CAP_LEN, head_count, HEAD_DIM)
    image_kv = jnp.dot(image_rows, mat_cross_kv, preferred_element_type=jnp.float32).astype(
        jnp.bfloat16
    )
    image_kv = image_kv.reshape(captions, IMG, 2, head_count, HEAD_DIM)
    cross_mixed, cross_total = general_attention(
        cross_query, image_kv[:, :, 0], image_kv[:, :, 1], open_mask
    )
    cross_mixed = cross_mixed.reshape(-1, D)
    after_cross = after_self + jnp.dot(
        cross_mixed, mat_cross_out, preferred_element_type=jnp.float32
    )
    normed_mlp = general_norm_rows(after_cross, norm_gains[2], shifts[2]).astype(jnp.bfloat16)
    hidden = jnp.dot(normed_mlp, mat_up, preferred_element_type=jnp.float32) + up_bias
    activated = general_gelu_exact(hidden).astype(jnp.bfloat16)
    result = (
        after_cross + jnp.dot(activated, mat_down, preferred_element_type=jnp.float32) + down_bias
    )
    saved_state = (
        slotted,
        normed_self,
        projected,
        self_total,
        self_mixed,
        after_self,
        normed_cross,
        cross_query,
        image_kv,
        cross_total,
        cross_mixed,
        after_cross,
        normed_mlp,
        hidden,
        activated,
    )
    return (result, saved_state)


def general_backward(saved_state, grad_slot, image_rows, params, allowed, open_mask):
    (
        mat_qkv,
        mat_out,
        mat_cross_q,
        mat_cross_kv,
        mat_cross_out,
        mat_up,
        mat_down,
        norm_gains,
        shifts,
        up_bias,
        down_bias,
    ) = params
    (
        slotted,
        normed_self,
        projected,
        self_total,
        self_mixed,
        after_self,
        normed_cross,
        cross_query,
        image_kv,
        cross_total,
        cross_mixed,
        after_cross,
        normed_mlp,
        hidden,
        activated,
    ) = saved_state
    captions = slotted.shape[0] // CAP_LEN
    head_count = D // HEAD_DIM
    grad_branch = grad_slot.astype(jnp.bfloat16)
    grad_down = jnp.einsum("rf,rd->fd", activated, grad_branch, preferred_element_type=jnp.float32)
    grad_down_bias = jnp.sum(grad_slot, axis=0)
    grad_active = jnp.einsum("rd,fd->rf", grad_branch, mat_down, preferred_element_type=jnp.float32)
    grad_hidden = general_gelu_back(hidden, grad_active).astype(jnp.bfloat16)
    grad_up = jnp.einsum("rd,rf->df", normed_mlp, grad_hidden, preferred_element_type=jnp.float32)
    grad_up_bias = jnp.sum(grad_hidden.astype(jnp.float32), axis=0)
    grad_normed = jnp.einsum("rf,df->rd", grad_hidden, mat_up, preferred_element_type=jnp.float32)
    grad_cross_in, grad_gain3, grad_shift3 = general_norm_back(
        after_cross, norm_gains[2], shifts[2], grad_normed
    )
    grad_after_cross = grad_slot + grad_cross_in
    grad_branch = grad_after_cross.astype(jnp.bfloat16)
    grad_cross_out = jnp.einsum(
        "rd,re->de", cross_mixed, grad_branch, preferred_element_type=jnp.float32
    )
    grad_mixed = jnp.einsum(
        "re,de->rd", grad_branch, mat_cross_out, preferred_element_type=jnp.float32
    ).astype(jnp.bfloat16)
    grad_mixed = grad_mixed.reshape(captions, CAP_LEN, head_count, HEAD_DIM)
    grad_query, grad_key, grad_value = general_attention_back(
        cross_query, image_kv[:, :, 0], image_kv[:, :, 1], cross_total, grad_mixed, open_mask
    )
    grad_query = grad_query.reshape(-1, D).astype(jnp.bfloat16)
    grad_kv = jnp.stack([grad_key, grad_value], axis=2).reshape(-1, 2 * D).astype(jnp.bfloat16)
    grad_cross_q = jnp.einsum(
        "rd,re->de", normed_cross, grad_query, preferred_element_type=jnp.float32
    )
    grad_cross_kv = jnp.einsum("iv,ie->ve", image_rows, grad_kv, preferred_element_type=jnp.float32)
    grad_image = jnp.einsum(
        "ie,ve->iv", grad_kv, mat_cross_kv, preferred_element_type=jnp.float32
    ).astype(jnp.bfloat16)
    grad_normed = jnp.einsum(
        "re,de->rd", grad_query, mat_cross_q, preferred_element_type=jnp.float32
    )
    grad_self_in, grad_gain2, grad_shift2 = general_norm_back(
        after_self, norm_gains[1], shifts[1], grad_normed
    )
    grad_after_self = grad_after_cross + grad_self_in
    grad_branch = grad_after_self.astype(jnp.bfloat16)
    grad_out = jnp.einsum("rd,re->de", self_mixed, grad_branch, preferred_element_type=jnp.float32)
    grad_mixed = jnp.einsum(
        "re,de->rd", grad_branch, mat_out, preferred_element_type=jnp.float32
    ).astype(jnp.bfloat16)
    grad_mixed = grad_mixed.reshape(captions, CAP_LEN, head_count, HEAD_DIM)
    grad_query, grad_key, grad_value = general_attention_back(
        projected[:, :, 0], projected[:, :, 1], projected[:, :, 2], self_total, grad_mixed, allowed
    )
    grad_projected = (
        jnp.stack([grad_query, grad_key, grad_value], axis=2)
        .reshape(-1, 3 * D)
        .astype(jnp.bfloat16)
    )
    grad_w_qkv = jnp.einsum(
        "rd,re->de", normed_self, grad_projected, preferred_element_type=jnp.float32
    )
    grad_normed = jnp.einsum(
        "re,de->rd", grad_projected, mat_qkv, preferred_element_type=jnp.float32
    )
    grad_input, grad_gain1, grad_shift1 = general_norm_back(slotted, norm_gains[0], shifts[0], grad_normed)
    grad_input = grad_input + grad_after_self
    grad_small = jnp.concatenate(
        [
            grad_gain1,
            grad_gain2,
            grad_gain3,
            grad_shift1,
            grad_shift2,
            grad_shift3,
            grad_up_bias,
            grad_down_bias,
        ]
    )
    flat_grads = (
        grad_w_qkv.reshape(-1),
        grad_out.reshape(-1),
        grad_cross_q.reshape(-1),
        grad_cross_kv.reshape(-1),
        grad_cross_out.reshape(-1),
        grad_up.reshape(-1),
        grad_down.reshape(-1),
        grad_small,
    )
    return (grad_input, grad_image, flat_grads)


def general_sum_to_owners(flat_grads):
    summed = []
    for grad_vec in flat_grads:
        for axis in ("dp", "fsdp"):
            parts = grad_vec.reshape(lax.axis_size(axis), -1).astype(jnp.bfloat16)
            if axis == "dp":
                parts = grad_vec.reshape(lax.axis_size("dp"), lax.axis_size("fsdp"), -1)
                parts = parts.astype(jnp.bfloat16)
            got = lax.all_to_all(parts, axis, split_axis=0, concat_axis=0, tiled=True)
            grad_vec = jnp.sum(got.astype(jnp.float32), axis=0)
        summed.append(grad_vec)
    return tuple(summed)


def general_device(
    tokens,
    image_tokens,
    caption_lengths,
    arrival_order,
    w_qkv,
    w_out,
    w_cross_q,
    w_cross_kv,
    w_cross_out,
    w_up,
    w_down,
    small_params,
    cotangent,
):
    lengths = caption_lengths[0]
    slot_rows = general_slot_index(lengths, arrival_order[0])
    captions = lengths.shape[0]
    slot_total = captions * CAP_LEN
    arrived, arrived_grad = (
        lax.all_to_all(tokens, "fsdp", split_axis=0, concat_axis=0, tiled=True),
        lax.all_to_all(cotangent, "fsdp", split_axis=0, concat_axis=0, tiled=True),
    )
    slotted = jnp.zeros((slot_total, D), jnp.float32).at[slot_rows].set(arrived.astype(jnp.float32))
    grad_slot = (
        jnp.zeros((slot_total, D), jnp.float32).at[slot_rows].set(arrived_grad.astype(jnp.float32))
    )
    positions = jnp.arange(CAP_LEN, dtype=jnp.int32)
    allowed = (positions[None, :] <= positions[:, None])[None, None] & (
        positions[None, None, None, :] < lengths[:, None, None, None]
    )
    open_mask = jnp.ones((1, 1, 1, 1), jnp.bool_)
    image_rows = image_tokens.reshape(-1, V)
    owned_shards = (w_qkv, w_out, w_cross_q, w_cross_kv, w_cross_out, w_up, w_down, small_params)
    params = general_unpack_params(
        tuple(lax.all_gather(w, ("dp", "fsdp"), axis=0, tiled=True) for w in owned_shards)
    )
    result, saved_state = general_forward(slotted, image_rows, params, allowed, open_mask)
    grad_input, grad_image, flat_grads = general_backward(
        saved_state, grad_slot, image_rows, params, allowed, open_mask
    )
    summed = general_sum_to_owners(flat_grads)
    out_rows = result[slot_rows].astype(jnp.bfloat16)
    grad_rows = grad_input[slot_rows].astype(jnp.bfloat16)
    layer_out, grad_tokens = (
        lax.all_to_all(out_rows, "fsdp", split_axis=0, concat_axis=0, tiled=True),
        lax.all_to_all(grad_rows, "fsdp", split_axis=0, concat_axis=0, tiled=True),
    )
    return (layer_out, grad_tokens, grad_image.reshape(image_tokens.shape)) + tuple(summed)


def solution(mesh):
    dp, fsdp = mesh.shape["dp"], mesh.shape["fsdp"]
    inner, specs_of = on_device, ("dp", "fsdp")
    if fsdp == 4 and dp % 2 == 0 and D % (dp * fsdp * 8) == 0:
        mesh = Mesh(mesh.devices.reshape(dp // 2, 2, 2, 2), AXES)
        specs_of = AXES
    else:
        inner = general_device
    rows, flat, cube = P(specs_of, None), P(specs_of), P(specs_of, None, None)
    return jax.shard_map(
        inner,
        mesh=mesh,
        in_specs=(rows, cube, rows, rows) + (flat,) * 8 + (rows,),
        out_specs=(rows, rows, cube) + (flat,) * 8,
        check_vma=False,
    )
```

```python
import functools

import jax
import jax.numpy as jnp
from jax import lax
from jax.experimental import pallas as pl
from jax.experimental.pallas import tpu as pltpu
from jax.sharding import Mesh
from jax.sharding import PartitionSpec as P

D = 768
HEAD_DIM = 64
FF = 3072
V = 768
IMG = 256
CAP_LEN = 64
LANES = 128
PAIRS = D // LANES
HALF = D // 2
HEADS = 4
WIDE = HEADS * HEAD_DIM
BATCHES = D // WIDE
FOLD = FF // D
GROUP = FOLD * LANES
GROUPS = FF // GROUP
TOKENS_AT = 32
SCALE = HEAD_DIM ** (-0.5)
epsilon = 1e-05
masked_fill = 1e30

BF = jnp.bfloat16
F32 = jnp.float32
AXES = ("z", "x", "y", "c")


def mm(a, b):
    return lax.dot_general(a, b, (((1,), (0,)), ((), ())), preferred_element_type=F32)


def mm_t(a, b):
    return lax.dot_general(a, b, (((1,), (1,)), ((), ())), preferred_element_type=F32)


def t_mm(a, b):
    return lax.dot_general(a, b, (((0,), (0,)), ((), ())), preferred_element_type=F32)


def wide(value):
    return value.astype(F32)


def norm_rows(inputs, gain_vec, shift_vec):
    centred = inputs - jnp.mean(inputs, axis=-1, keepdims=True)
    variance = jnp.mean(centred * centred, axis=-1, keepdims=True)
    return centred * lax.rsqrt(variance + epsilon) * gain_vec + shift_vec


def norm_back(inputs, gain_vec, grad_normed):
    centred = inputs - jnp.mean(inputs, axis=-1, keepdims=True)
    variance = jnp.mean(centred * centred, axis=-1, keepdims=True)
    scale = lax.rsqrt(variance + epsilon)
    unit = centred * scale
    weighted = grad_normed * gain_vec
    grad_in = scale * (
        weighted
        - jnp.mean(weighted, axis=-1, keepdims=True)
        - unit * jnp.mean(weighted * unit, axis=-1, keepdims=True)
    )
    grad_gain = jnp.sum(grad_normed * unit, axis=0, keepdims=True)
    grad_shift = jnp.sum(grad_normed, axis=0, keepdims=True)
    return grad_in, grad_gain, grad_shift


def arrival_pick(arr_ref):
    rows = arr_ref.shape[1]
    place = lax.broadcasted_iota(jnp.int32, (rows, rows), 0)
    return jnp.where(place == arr_ref[...], 1.0, 0.0).astype(BF)


def caption_of(index, lens_ref):
    end = jnp.int32(0)
    found = jnp.zeros_like(index)
    for c in range(lens_ref.shape[1] - 1):
        end = end + lens_ref[0, c]
        found = found + jnp.where(index >= end, 1, 0)
    return found


def slot_pick(lens_ref, rows):
    captions = lens_ref.shape[1]
    shape = (captions * CAP_LEN, rows)
    slot = lax.broadcasted_iota(jnp.int32, shape, 0)
    row = lax.broadcasted_iota(jnp.int32, shape, 1)
    start = jnp.int32(0)
    hit = jnp.zeros(shape, F32)
    for c in range(captions):
        length = lens_ref[0, c]
        inside = slot - c * CAP_LEN
        ok = (inside >= 0) & (inside < length) & (row - start == inside)
        hit = hit + jnp.where(ok, 1.0, 0.0)
        start = start + length
    return hit.astype(BF)


def fold_pick(back):
    source = lax.broadcasted_iota(jnp.int32, (GROUP, GROUP), 1 if back else 0)
    target = lax.broadcasted_iota(jnp.int32, (GROUP, GROUP), 0 if back else 1)
    return jnp.where(target == (source % FOLD) * LANES + source // FOLD, 1.0, 0.0).astype(BF)


def head_mask(rows):
    shape = (HEADS * rows, WIDE)
    head = lax.broadcasted_iota(jnp.int32, shape, 1) // HEAD_DIM
    row = lax.broadcasted_iota(jnp.int32, shape, 0)
    inside = (row >= head * rows) & (row < (head + 1) * rows)
    return jnp.where(inside, 1.0, 0.0).astype(BF)


def stack_heads(block, mask):
    return jnp.concatenate([block] * HEADS, axis=0) * mask


def merge_heads(stacked):
    rows = stacked.shape[0] // HEADS
    head = lax.broadcasted_iota(jnp.int32, (rows, WIDE), 1) // HEAD_DIM
    out = stacked[:rows]
    for n in range(1, HEADS):
        out = jnp.where(head == n, stacked[n * rows : (n + 1) * rows], out)
    return out


def softmax_rows(scores):
    shifted = jnp.exp(scores - jnp.max(scores, axis=-1, keepdims=True))
    return shifted * (1.0 / jnp.sum(shifted, axis=-1, keepdims=True))


def lanes_at(start, width):
    return pl.ds(pl.multiple_of(start, LANES), width)


def pack_halves(shards, out, rows, at=0):
    depth, _, height, _ = out.shape
    pieces = HALF // LANES
    for shard, mats in shards:
        rows[: shard.shape[0], :] = wide(shard[...])
        for mat in range(mats):
            for half in range(2):
                for i in range(pieces):
                    index = mat * PAIRS + half * pieces + i
                    value = rows[pl.ds(index, height, stride=mats * PAIRS), :].astype(BF)
                    lanes = slice(at + i * LANES, at + (i + 1) * LANES)
                    for z in range(depth):
                        out[z, half, :, lanes] = value
            at += HALF
    return at


def pack_self_kernel(w_qkv, w_out, attend, rows):
    pack_halves(((w_qkv, 3), (w_out, 1)), attend, rows)


def pack_cross_kernel(w_cross_q, w_cross_kv, w_cross_out, small, attend, rows):
    at = pack_halves(((w_cross_q, 1), (w_cross_kv, 2), (w_cross_out, 1)), attend, rows)
    depth, _, height, _ = attend.shape
    flat = wide(small[...])
    tail = jnp.zeros((1, LANES - small.shape[1] % LANES), F32)
    flat = jnp.concatenate([flat, tail], axis=1)
    parts = [flat[:, n : n + LANES] for n in range(0, flat.shape[1], LANES)]
    block = jnp.concatenate(parts + [jnp.zeros((height - len(parts), LANES), F32)], axis=0)
    for z in range(depth):
        for half in range(2):
            attend[z, half, :, at:] = block.astype(BF)


def pack_group_kernel(me, w_up, w_down, tokens, cotangent, near, core, chip, rows, parts):
    chunks = FF // LANES
    height = w_up.shape[0] // chunks

    def chunk(index):
        return rows[pl.ds(index, height, stride=chunks), :].astype(BF)

    rows[...] = wide(w_up[...])
    pick = fold_pick(False)
    for t in range(GROUPS):
        group = jnp.concatenate([chunk(t * FOLD + k) for k in range(FOLD)], axis=1)
        folded = mm(group, pick).astype(BF)
        for j in range(FOLD):
            parts[j, :height, t * LANES : (t + 1) * LANES] = folded[
                :, j * LANES : (j + 1) * LANES
            ]
    rows[...] = wide(w_down[...])
    for j in range(FOLD):
        for i in range(PAIRS):
            at = D + i * LANES
            parts[j, :height, at : at + LANES] = chunk(j * PAIRS + i)
        parts[j, TOKENS_AT : TOKENS_AT + tokens.shape[1], :D] = tokens[j]
        parts[j, TOKENS_AT : TOKENS_AT + tokens.shape[1], D:] = cotangent[j]
    near[...] = parts[part_of(me, 0, 0)]
    core[...] = parts[part_of(me, 0, 1)]
    for c in range(2):
        chip[c] = parts[part_of(me, 1, c)]


def transpose_kernel(img, out):
    for n in range(0, img.shape[0], IMG):
        out[:, n : n + IMG] = img[n : n + IMG, :].T


def part_of(me, far_y, far_c):
    return lax.bitwise_xor(me[0, 2], far_y) * 2 + lax.bitwise_xor(me[0, 3], far_c)


def spread_kernel(me, arr, near, chip, core, both, hidden, slotted, grad_slot, arrived):
    height, count = hidden.shape[2], arrived.shape[0] // FOLD
    for value, far_y, far_c in (
        (near[...], 0, 0), (chip[0], 1, 0), (core[...], 0, 1), (both[...], 1, 1),
    ):
        index = part_of(me, far_y, far_c)
        for z in range(hidden.shape[0]):
            hidden[z, index] = value[:height]
        at = pl.multiple_of(index * count, 8)
        arrived[pl.ds(at, count), :] = wide(value[TOKENS_AT : TOKENS_AT + count])
    pick = arrival_pick(arr)
    slotted[...] = mm(pick, arrived[:, :D].astype(BF)).astype(BF)
    grad_slot[...] = mm(pick, arrived[:, D:].astype(BF)).astype(BF)


def fill_table(share, me, pieces, flat, table):
    depth, height = pieces.shape[1], pieces.shape[2] // 2
    lane = lax.broadcasted_iota(jnp.int32, (3, LANES), 1)
    flat[...] = jnp.zeros_like(flat)
    for owner in range(8 * depth):
        z, x, y, c = owner // 8, owner // 4 % 2, owner // 2 % 2, owner % 2
        index = lax.bitwise_xor(me[0, 1], x) * 2 + lax.bitwise_xor(me[0, 2], y)
        value = wide(pieces[index, z])[c * height : c * height + 3, :]
        row, shift = divmod(owner * share, LANES)
        if shift == 0:
            flat[row : row + 3, :] += value
        else:
            moved = pltpu.roll(value, shift, axis=1)
            flat[row : row + 3, :] += jnp.where(lane >= shift, moved, 0.0)
            flat[row + 1 : row + 4, :] += jnp.where(lane < shift, moved, 0.0)
    for n in range(table.shape[0] * PAIRS):
        row, lanes = n // PAIRS, slice(n % PAIRS * LANES, (n % PAIRS + 1) * LANES)
        table[row : row + 1, lanes] = flat[n : n + 1, :]


def depth_sum_kernel(me, got, near, core, chip, total):
    height = near.shape[0]
    value = wide(got[0])
    for z in range(1, got.shape[0]):
        value = value + wide(got[z])
    total[...] = value

    def part(far_y, far_c):
        at = pl.multiple_of(part_of(me, far_y, far_c) * height, 8)
        return total[pl.ds(at, height), :].astype(BF)

    near[...] = part(0, 0)
    core[...] = part(0, 1)
    for c in range(2):
        chip[c] = part(1, c)


def unpack_hidden_kernel(me, near, chip, core, both, up, down, got):
    for value, far_y, far_c in (
        (near[...], 0, 0), (chip[0], 1, 0), (core[...], 0, 1), (both[...], 1, 1),
    ):
        got[part_of(me, far_y, far_c)] = value
    height = got.shape[1]
    chunks = FF // LANES
    pick = fold_pick(True)
    for t in range(GROUPS):
        group = jnp.concatenate(
            [got[j, :, t * LANES : (t + 1) * LANES] for j in range(FOLD)], axis=1
        )
        natural = mm(group, pick)
        for k in range(FOLD):
            up[pl.ds(t * FOLD + k, height, stride=chunks), :] = natural[
                :, k * LANES : (k + 1) * LANES
            ]
    for j in range(FOLD):
        for i in range(PAIRS):
            at = D + i * LANES
            down[pl.ds(j * PAIRS + i, height, stride=chunks), :] = wide(
                got[j, :, at : at + LANES]
            )


def unpack_halves(got, outs):
    depth, height = got.shape[0], got.shape[2]
    parts = HALF // LANES
    place = 0
    for out in outs:
        chunks = out.shape[0] // height
        for mat in range(chunks // PAIRS):
            for half in range(2):
                for i in range(parts):
                    at = place + i * LANES
                    total = wide(got[0, half, :, at : at + LANES])
                    for z in range(1, depth):
                        total = total + wide(got[z, half, :, at : at + LANES])
                    index = mat * PAIRS + half * parts + i
                    out[pl.ds(index, height, stride=chunks), :] = total
            place += HALF
    return place


class Fetch:
    def __init__(self, sems):
        self.sems = sems
        self.used = 0

    def start(self, source, target):
        copy = pltpu.make_async_copy(source, target, self.sems.at[self.used])
        self.used += 1
        copy.start()
        return copy

    def columns(self, pieces, me, piece_at, target, target_at):
        copies = []
        for index, piece in enumerate(pieces):
            half = lax.bitwise_xor(me[0, 3], index // 4)
            x = lax.bitwise_xor(me[0, 1], index // 2 % 2)
            y = lax.bitwise_xor(me[0, 2], index % 2)
            copies.append(
                self.start(
                    piece.at[:, :, pl.ds(piece_at, HALF)],
                    target.at[:, x, y, :, lanes_at(target_at + half * HALF, HALF)],
                )
            )
        return copies


def wait(copies):
    for copy in copies:
        copy.wait()


def matrix(ref):
    shape = ref.shape
    return ref[...].reshape(shape[0] * shape[1] * shape[2] * shape[3], shape[4])


def forward_kernel(share, lens, me, slotted, img, *refs):
    pieces_a, pieces_b = refs[:8], refs[8:16]
    (
        table,
        projected, probs_self, saved, after_self, after_cross, normed_mlp, query_slots,
        kv_out, probs_out, kv, probs_cross, w_qkv, w_out, w_cq, w_kv, w_co, mixed_slots, small, flat, sems,
    ) = refs[16:]
    fetch = Fetch(sems)
    got_small = [
        fetch.start(pieces_b[n].at[:, :, pl.ds(4 * HALF, LANES)], small.at[n]) for n in range(4)
    ]
    got_qkv = []
    for mat in range(3):
        got_qkv += fetch.columns(pieces_a, me, mat * HALF, w_qkv, mat * D)
    got_out = fetch.columns(pieces_a, me, 3 * HALF, w_out, 0)
    got_cq = fetch.columns(pieces_b, me, 0, w_cq, 0)
    got_kv = fetch.columns(pieces_b, me, HALF, w_kv, 0)
    got_kv += fetch.columns(pieces_b, me, 2 * HALF, w_kv, D)
    got_co = fetch.columns(pieces_b, me, 3 * HALF, w_co, 0)
    rows = slotted.shape[0]
    wait(got_small)
    fill_table(share, me, small, flat, table)
    saved[:, :D] = norm_rows(wide(slotted[...]), table[0:1, :], table[3:4, :]).astype(BF)
    wait(got_qkv)
    projected[...] = mm(saved[:, :D], matrix(w_qkv)).astype(BF)
    query_at = lax.broadcasted_iota(jnp.int32, (rows, rows), 0)
    key_at = lax.broadcasted_iota(jnp.int32, (rows, rows), 1)
    same = caption_of(query_at, lens) == caption_of(key_at, lens)
    block = jnp.where(same & (key_at <= query_at), 0.0, -masked_fill)
    barred = jnp.concatenate([block] * HEADS, axis=0)
    mask = head_mask(rows)
    for n in range(BATCHES):
        query, key, value = (
            projected[:, m * D + n * WIDE : m * D + (n + 1) * WIDE] for m in range(3)
        )
        scores = mm_t(stack_heads(query, mask), key) * SCALE + barred
        weights_low = softmax_rows(scores).astype(BF)
        probs_self[n] = weights_low
        saved[:, D + n * WIDE : D + (n + 1) * WIDE] = merge_heads(
            mm(weights_low, value)
        ).astype(BF)
    wait(got_out)
    state = wide(slotted[...]) + mm(saved[:, D : 2 * D], matrix(w_out))
    after_self[...] = state
    low = norm_rows(state, table[1:2, :], table[4:5, :]).astype(BF)
    saved[:, 2 * D : 3 * D] = low
    wait(got_cq)
    pick = slot_pick(lens, rows)
    query_slots[...] = mm(pick, mm(low, matrix(w_cq)).astype(BF)).astype(BF)
    wait(got_kv)
    kv_mat = matrix(w_kv)
    mask = head_mask(CAP_LEN)
    sent = []
    for c in range(lens.shape[1]):
        slots = slice(c * CAP_LEN, (c + 1) * CAP_LEN)
        images = slice(c * IMG, (c + 1) * IMG)
        kv[images, :] = mm(img[images, :], kv_mat).astype(BF)
        for n in range(BATCHES):
            cols = slice(n * WIDE, (n + 1) * WIDE)
            query = stack_heads(query_slots[slots, cols], mask)
            weights_low = softmax_rows(mm_t(query, kv[images, cols]) * SCALE).astype(BF)
            probs_cross[c * BATCHES + n] = weights_low
            value = kv[images, D + n * WIDE : D + (n + 1) * WIDE]
            mixed_slots[slots, cols] = merge_heads(mm(weights_low, value)).astype(BF)
        batch = slice(c * BATCHES, (c + 1) * BATCHES)
        sent.append(fetch.start(kv.at[images], kv_out.at[images]))
        sent.append(fetch.start(probs_cross.at[batch], probs_out.at[batch]))
    low = t_mm(pick, mixed_slots[...]).astype(BF)
    saved[:, 3 * D :] = low
    wait(got_co)
    state = after_self[...] + mm(low, matrix(w_co))
    after_cross[...] = state
    normed_mlp[...] = norm_rows(state, table[2:3, :], table[5:6, :]).astype(BF)
    wait(sent)


def put_small(small, row, value):
    for k in range(PAIRS):
        at = row * PAIRS + k
        small[at : at + 1, :] = value[:, k * LANES : (k + 1) * LANES]


def own_part(value, me):
    part = me[0, 2] * 2 + me[0, 3]
    out = value[:, :LANES]
    for j in range(1, FOLD):
        out = jnp.where(part == j, value[:, j * LANES : (j + 1) * LANES], out)
    return out


def mlp_kernel(me, table, *refs):
    inputs, grads, pieces = refs[:4], refs[4:8], refs[8:10]
    (
        grad_near, grad_keep, grad_send, grad_send_y, out_near, out_keep, out_send, out_send_y,
        active, grad_hidden, small, all_in, all_grad, w_up, w_down, grad_part, out_part, sems,
    ) = refs[10:]
    fetch = Fetch(sems)
    got_up, got_down = [], []
    for index in range(2):
        x = lax.bitwise_xor(me[0, 1], index)
        got_up.append(fetch.start(pieces[index].at[:, :, pl.ds(0, D)], w_up.at[:, x]))
        got_down.append(fetch.start(pieces[index].at[:, :, pl.ds(D, D)], w_down.at[:, x]))
    rows = inputs[0].shape[0]
    for n in range(4):
        all_in[n * rows : (n + 1) * rows, :] = inputs[n][...]
        all_grad[n * rows : (n + 1) * rows, :] = grads[n][...]
    bias = [
        table[6 + n // PAIRS : 7 + n // PAIRS, n % PAIRS * LANES : (n % PAIRS + 1) * LANES]
        for n in range(FF // LANES)
    ]
    bias = jnp.concatenate(
        [jnp.concatenate(bias[t * FOLD : (t + 1) * FOLD], axis=1) for t in range(GROUPS)], axis=0
    )
    bias = own_part(mm(bias.astype(BF), fold_pick(False)), me)
    bias = jnp.concatenate([bias[t : t + 1, :] for t in range(GROUPS)], axis=1)
    wait(got_up)
    up_mat = w_up[...].reshape(D, D)
    wait(got_down)
    down_mat = w_down[...].reshape(D, D)

    def rows_of(n, total):
        at = pl.ds(pl.multiple_of(n * 2 * rows, 64), 2 * rows)
        hidden = mm(all_in[at, :], up_mat) + bias
        half = 0.5 + 0.5 * lax.erf(hidden * (0.5**0.5))
        act = (hidden * half).astype(BF)
        active[at, :] = act
        slope = half + hidden * (jnp.exp(hidden * hidden * -0.5) * 0.3989422804014327)
        grad_hid = (mm_t(all_grad[at, :], down_mat) * slope).astype(BF)
        grad_hidden[at, :] = grad_hid
        grad_part[n] = mm_t(grad_hid, up_mat)
        out_part[n] = mm(act, down_mat)
        return total + jnp.sum(wide(grad_hid), axis=0, keepdims=True)

    sums = lax.fori_loop(0, 2, rows_of, jnp.zeros((1, D), F32)).astype(BF)
    for part, outs in (
        (grad_part, (grad_near, grad_send, grad_keep, grad_send_y)),
        (out_part, (out_near, out_send, out_keep, out_send_y)),
    ):
        for n, out in enumerate(outs):
            out[...] = part[n // 2, n % 2 * rows : (n % 2 + 1) * rows].astype(out.dtype)
    sums = jnp.concatenate(
        [sums[:, t * LANES : (t + 1) * LANES] for t in range(GROUPS)] + [sums[:, :LANES]] * 2,
        axis=0,
    )
    part = me[0, 2] * 2 + me[0, 3]
    spread = jnp.concatenate(
        [jnp.where(part == j, sums, jnp.zeros_like(sums)) for j in range(FOLD)], axis=1
    )
    natural = mm(spread, fold_pick(True))
    small[...] = jnp.zeros_like(small)
    for n in range(FF // LANES):
        at = 6 * PAIRS + n
        small[at : at + 1, :] = natural[
            n // FOLD : n // FOLD + 1, n % FOLD * LANES : (n % FOLD + 1) * LANES
        ]
    put_small(small, 10, jnp.sum(wide(grads[0][...]), axis=0, keepdims=True))


def hidden_grad_kernel(*refs):
    normed, grad_slot = refs[:4], refs[4:8]
    active, grad_hidden, out = refs[8:]
    rows = lambda parts: jnp.concatenate([r[...] for r in parts], axis=0)
    out[:, :D] = t_mm(rows(normed), grad_hidden[...]).astype(BF)
    out[:, D:] = t_mm(active[...], rows(grad_slot)).astype(BF)


def combine_kernel(keep, far, out):
    out[...] = (wide(keep[...]) + wide(far[...])).astype(BF)


def cross_back_kernel(
    lens, me, grad_near, grad_core, grad_far, after_cross, grad_slot, probs_in, query_slots, kv_in,
    after_self, table, small_in, *refs,
):
    pieces = refs[:8]
    (
        grad_state, small, half_keep, half_send, keep_out, send_out,
        w_co, w_cq, mixed_slots, query_grads, grad_kv, kv_keep, kv_send, kv, probs, sems,
    ) = refs[8:]
    fetch = Fetch(sems)
    got_co = fetch.columns(pieces, me, 3 * HALF, w_co, 0)
    got_kv = [fetch.start(kv_in, kv), fetch.start(probs_in, probs)]
    got_cq = fetch.columns(pieces, me, 0, w_cq, 0)
    rows = after_self.shape[0]
    sent = []
    halves = ((0, half_keep, kv_keep), (1, half_send, kv_send))
    small[...] = small_in[...]
    grad_in, grad_gain, grad_shift = norm_back(
        after_cross[...],
        table[2:3, :],
        grad_near[...] + wide(grad_core[...]) + wide(grad_far[...]),
    )
    put_small(small, 2, grad_gain)
    put_small(small, 5, grad_shift)
    grad_after = wide(grad_slot[...]) + grad_in
    grad_state[...] = grad_after
    pick = slot_pick(lens, rows)
    wait(got_co)
    query_grads[:rows, :] = grad_after.astype(BF)
    mixed_slots[...] = mm(pick, mm_t(query_grads[:rows, :], matrix(w_co)).astype(BF)).astype(BF)
    for rel, half_out, _ in halves:
        at = lax.bitwise_xor(me[0, 3], rel) * HALF
        half_out[:, HALF : 2 * HALF] = query_grads[:rows, lanes_at(at, HALF)]
    mask = head_mask(CAP_LEN)
    wait(got_kv)
    for c in range(lens.shape[1]):
        slots = slice(c * CAP_LEN, (c + 1) * CAP_LEN)
        images = slice(c * IMG, (c + 1) * IMG)
        for n in range(BATCHES):
            cols = slice(n * WIDE, (n + 1) * WIDE)
            value_cols = slice(D + n * WIDE, D + (n + 1) * WIDE)
            grad_mixed = stack_heads(mixed_slots[slots, cols], mask)
            query = stack_heads(query_slots[slots, cols], mask)
            weights_low = probs[c * BATCHES + n]
            attn = wide(weights_low)
            grad_weights = mm_t(grad_mixed, kv[images, value_cols])
            centre = jnp.sum(attn * grad_weights, axis=-1, keepdims=True)
            grad_scores = (attn * (grad_weights - centre)).astype(BF)
            query_grads[slots, cols] = (
                merge_heads(mm(grad_scores, kv[images, cols])) * SCALE
            ).astype(BF)
            grad_kv[images, cols] = (t_mm(grad_scores, query) * SCALE).astype(BF)
            grad_kv[images, value_cols] = t_mm(weights_low, grad_mixed).astype(BF)
        for rel, _, kv_half in halves:
            at = lax.bitwise_xor(me[0, 3], rel) * HALF
            kv_half[images, :HALF] = grad_kv[images, lanes_at(at, HALF)]
            kv_half[images, HALF:] = grad_kv[images, lanes_at(at + D, HALF)]
        sent.append(fetch.start(kv_send.at[images], send_out.at[images]))
        sent.append(fetch.start(kv_keep.at[images], keep_out.at[images]))
    mixed_slots[:rows, :] = t_mm(pick, query_grads[...]).astype(BF)
    wait(got_cq)
    grad_in, grad_gain, grad_shift = norm_back(
        after_self[...], table[1:2, :], mm_t(mixed_slots[:rows, :], matrix(w_cq))
    )
    put_small(small, 1, grad_gain)
    put_small(small, 4, grad_shift)
    grad_after = grad_state[...] + grad_in
    grad_state[...] = grad_after
    query_grads[:rows, :] = grad_after.astype(BF)
    for rel, half_out, _ in halves:
        at = lax.bitwise_xor(me[0, 3], rel) * HALF
        half_out[:, :HALF] = mixed_slots[:rows, lanes_at(at, HALF)]
        half_out[:, 2 * HALF :] = query_grads[:rows, lanes_at(at, HALF)]
    wait(sent)


def self_back_kernel(me, grad_state, probs, projected, slotted, table, small_in, *refs):
    pieces = refs[:8]
    (
        grad_rows, small, keep, send,
        w_out, w_qkv, mixed, grad_projected, sems,
    ) = refs[8:]
    fetch = Fetch(sems)
    got_out = fetch.columns(pieces, me, 3 * HALF, w_out, 0)
    got_qkv = []
    for mat in range(3):
        got_qkv += fetch.columns(pieces, me, mat * HALF, w_qkv, mat * D)
    rows = slotted.shape[0]
    wait(got_out)
    mixed[...] = mm_t(grad_state[...].astype(BF), matrix(w_out)).astype(BF)
    mask = head_mask(rows)
    for n in range(BATCHES):
        cols, key_cols, value_cols = (
            slice(m * D + n * WIDE, m * D + (n + 1) * WIDE) for m in range(3)
        )
        grad_mixed = stack_heads(mixed[:, cols], mask)
        query = stack_heads(projected[:, cols], mask)
        weights_low = probs[n]
        attn = wide(weights_low)
        grad_weights = mm_t(grad_mixed, projected[:, value_cols])
        centre = jnp.sum(attn * grad_weights, axis=-1, keepdims=True)
        grad_scores = (attn * (grad_weights - centre)).astype(BF)
        grad_projected[:, cols] = (
            merge_heads(mm(grad_scores, projected[:, key_cols])) * SCALE
        ).astype(BF)
        grad_projected[:, key_cols] = (t_mm(grad_scores, query) * SCALE).astype(BF)
        grad_projected[:, value_cols] = t_mm(weights_low, grad_mixed).astype(BF)
    for mat in range(3):
        for rel, out in ((0, keep), (1, send)):
            at = lax.bitwise_xor(me[0, 3], rel) * HALF + mat * D
            out[:, mat * HALF : (mat + 1) * HALF] = grad_projected[:, lanes_at(at, HALF)]
    wait(got_qkv)
    grad_in, grad_gain, grad_shift = norm_back(
        wide(slotted[...]), table[0:1, :], mm_t(grad_projected[...], matrix(w_qkv))
    )
    grad_slotted = (grad_state[...] + grad_in).astype(BF)
    grad_rows[...] = grad_slotted
    small[...] = small_in[...]
    put_small(small, 0, grad_gain)
    put_small(small, 3, grad_shift)


def put_quadrants(grads, me, outs, at, first):
    depth, height = outs[0].shape[1:3]
    width = grads.shape[1]
    for i, out in enumerate(outs):
        for j in range(2):
            far_x, far_y = (i, j) if first == "x" else (j, i)
            x, y = lax.bitwise_xor(me[0, 1], far_x), lax.bitwise_xor(me[0, 2], far_y)
            for z in range(depth):
                low = pl.multiple_of(((z * 2 + x) * 2 + y) * height, 16)
                out[j, z, :, at : at + width] = grads[pl.ds(low, height), :].astype(BF)


def half_grads(pieces, me, outs, grads, first, at=0):
    for left, far_left, right, far_right in pieces:
        width = right.shape[1]
        grads[:, :width] = t_mm(left, right) + t_mm(far_left, far_right)
        put_quadrants(grads.at[:, :width], me, outs, at, first)
        at += width


def cross_grad_kernel(me, *refs):
    sources, targets, landed, made, grads, sems = (
        refs[:8], refs[8:12], refs[12:20], refs[20:24], refs[24], refs[25],
    )
    fetch = Fetch(sems)
    copies = [fetch.start(source, target) for source, target in zip(sources, landed)]
    saved, saved_far, half, half_far, img_t, img_t_far, kv, kv_far = landed
    part = lambda ref, n, width: ref[:, n * width : (n + 1) * width]
    piece = lambda left, right: (
        part(saved, left, D), part(saved_far, left, D),
        part(half, right, HALF), part(half_far, right, HALF),
    )
    wait(copies[:4])
    half_grads([piece(3, 1), piece(1, 2)], me, made[2:], grads, "y")
    sent = [fetch.start(made[n], targets[n]) for n in (3, 2)]
    half_grads([piece(2, 0)], me, made[:2], grads, "x")
    wait(copies[4:])
    grads[...] = mm(img_t[...], kv[...]) + mm(img_t_far[...], kv_far[...])
    put_quadrants(grads, me, made[:2], HALF, "x")
    sent += [fetch.start(made[n], targets[n]) for n in (1, 0)]
    wait(sent)


def owner_rows(small, blocks, share):
    height = blocks.shape[0] // (small.shape[0] * LANES // share)
    lane = lax.broadcasted_iota(jnp.int32, (3, LANES), 1)
    blocks[...] = jnp.zeros_like(blocks)
    table = jnp.concatenate([small[...], jnp.zeros((6, LANES), F32)], axis=0)
    for owner in range(small.shape[0] * LANES // share):
        row, shift = divmod(owner * share, LANES)
        if shift == 0:
            value = table[row : row + 3]
        else:
            moved = pltpu.roll(table[row : row + 4], LANES - shift, axis=1)
            value = jnp.where(lane < LANES - shift, moved[:3], moved[1:4])
        blocks[owner * height : owner * height + 3, :] = value


def self_grad_kernel(share, me, saved, saved_far, half, half_far, small, *refs):
    first, second, grads = refs[:2], refs[2:4], refs[4]
    own, far = saved[:, :D], saved_far[:, :D]
    half_grads([(own, far, half[:, :D], half_far[:, :D])], me, first, grads, "y")
    half_grads([(own, far, half[:, D:], half_far[:, D:])], me, second, grads, "x")
    blocks = grads.at[:, :LANES]
    owner_rows(small, blocks, share)
    put_quadrants(blocks, me, second, HALF, "x")


def unpack_kernel(got, *outs):
    at = unpack_halves(got, outs[:-1])
    total = jnp.zeros((8, LANES), F32)
    for z in range(got.shape[0]):
        for c in range(2):
            total = total + wide(got[z, c, :8, at:])
    outs[-1][...] = total


def return_kernel(
    me, arr, after_cross, table, out_near, out_core, out_far, grad_rows, near, core, chip, rows
):
    pick = arrival_pick(arr)
    count = near.shape[0]
    result = after_cross[...] + out_near[...] + wide(out_core[...]) + wide(out_far[...])
    result = result + table[10:11, :]
    rows[:, :D] = t_mm(pick, result.astype(BF))
    rows[:, D:] = t_mm(pick, grad_rows[...])

    def part(far_y, far_c):
        at = pl.multiple_of(part_of(me, far_y, far_c) * count, 8)
        return rows[pl.ds(at, count), :].astype(BF)

    near[...] = part(0, 0)
    core[...] = part(0, 1)
    for c in range(2):
        chip[c] = part(1, c)


def collect_kernel(me, near, chip, core, both, layer_out, grad_tokens):
    for value, far_y, far_c in ((near[...], 0, 0), (chip[0], 1, 0), (core[...], 0, 1), (both[...], 1, 1)):
        index = part_of(me, far_y, far_c)
        layer_out[index] = value[:, :D]
        grad_tokens[index] = value[:, D:]


def image_grad_kernel(kv_keep, kv_send, *refs):
    me, pieces = refs[0], refs[1:9]
    grad_image, w_kv, sems = refs[9:]
    fetch = Fetch(sems)
    copies = []
    for index, piece in enumerate(pieces):
        x = lax.bitwise_xor(me[0, 1], index // 2 % 2)
        y = lax.bitwise_xor(me[0, 2], index % 2)
        copies.append(
            fetch.start(piece.at[:, :, pl.ds(HALF, D)], w_kv.at[index // 4, :, x, y])
        )
    wait(copies)
    near, far = w_kv[0].reshape(D, D), w_kv[1].reshape(D, D)
    for c in range(kv_keep.shape[0] // IMG):
        rows = pl.ds(c * IMG, IMG)
        grad_image[rows, :] = (mm_t(kv_keep[rows, :], near) + mm_t(kv_send[rows, :], far)).astype(
            BF
        )


def add_kernel(counts, joined, *refs):
    outs = refs[sum(counts) :]
    first = at = 0
    for n, count in enumerate(counts):
        for z in range(refs[first].shape[0]):
            total = wide(refs[first][z])
            for ref in refs[first + 1 : first + count]:
                total = total + wide(ref[z])
            if joined:
                outs[0][z, :, at : at + total.shape[-1]] = total.astype(BF)
            else:
                outs[n][z] = total.astype(BF)
        at += total.shape[-1]
        first += count


VM = pl.BlockSpec(memory_space=pltpu.VMEM)
SM = pl.BlockSpec(memory_space=pltpu.SMEM)
HB = pl.BlockSpec(memory_space=pl.ANY)


def run(kernel, outs, specs, scratch, *args, mib=58, copied=0):
    return pl.pallas_call(
        kernel,
        out_shape=[jax.ShapeDtypeStruct(s, t) for s, t in outs],
        in_specs=specs,
        out_specs=[VM] * (len(outs) - copied) + [HB] * copied,
        scratch_shapes=scratch,
        compiler_params=pltpu.CompilerParams(vmem_limit_bytes=mib * 2**20),
        name=(kernel.func if isinstance(kernel, functools.partial) else kernel).__name__,
    )(*args)


def add_up(*sums, joined=False):
    args, specs, shapes = [], [], []
    for terms in sums:
        for term in terms:
            array, index = term if isinstance(term, tuple) else (term, None)
            block = array.shape[-3:]
            if index is None:
                specs.append(pl.BlockSpec(block, lambda i: (0, 0, 0)))
            else:
                specs.append(pl.BlockSpec((None,) + block, lambda i, n=index: (n, 0, 0, 0)))
            args.append(array)
        shapes.append(block)
    if joined:
        shapes = [shapes[0][:2] + (sum(s[2] for s in shapes),)]
    return pl.pallas_call(
        functools.partial(add_kernel, [len(terms) for terms in sums], joined),
        grid=(1,),
        out_shape=[jax.ShapeDtypeStruct(s, BF) for s in shapes],
        in_specs=specs,
        out_specs=[pl.BlockSpec(s, lambda i: (0, 0, 0)) for s in shapes],
        compiler_params=pltpu.CompilerParams(vmem_limit_bytes=58 * 2**20),
        name="add_kernel",
    )(*args)


def flip(value, axis):
    return lax.ppermute(value, axis, [(0, 1), (1, 0)])


def swap_all(value, axes):
    return lax.all_to_all(value, axes, split_axis=0, concat_axis=0, tiled=True)


def tie(*values):
    return lax.optimization_barrier(values)


def on_device(
    tokens,
    image_tokens,
    caption_lengths,
    arrival_order,
    w_qkv,
    w_out,
    w_cross_q,
    w_cross_kv,
    w_cross_out,
    w_up,
    w_down,
    small_params,
    cotangent,
):
    depth = lax.axis_size("z")
    height = D // (8 * depth)
    rows = tokens.shape[0]
    captions = caption_lengths.shape[1]
    slots = captions * CAP_LEN
    images = captions * IMG
    lens, arr = caption_lengths, arrival_order
    me = jnp.stack([lax.axis_index(a) for a in AXES]).astype(jnp.int32).reshape(1, 4)
    vmem = pltpu.VMEM
    sems = lambda n: pltpu.SemaphoreType.DMA((n,))
    shards = (w_qkv, w_out, w_cross_q, w_cross_kv, w_cross_out, w_up, w_down)

    share = small_params.shape[0]
    flat_shards = [w.reshape(-1, LANES) for w in shards]
    packed = lambda n: [((depth, 2, height, n), BF)]
    chunked = [vmem((w_up.shape[0] // LANES, LANES), F32)]
    (a,) = run(pack_self_kernel, packed(4 * HALF), [VM] * 2, chunked, *flat_shards[:2])
    (b,) = run(
        pack_cross_kernel, packed(4 * HALF + LANES), [VM] * 4, chunked,
        *flat_shards[2:5], small_params.reshape(1, share),
    )
    part = ((TOKENS_AT + 48, 2 * D), BF)
    near, core, chip = run(
        pack_group_kernel,
        [part, part, ((2,) + part[0], BF)],
        [SM] + [VM] * 4,
        chunked + [vmem((FOLD,) + part[0], BF)],
        me, *flat_shards[5:], tokens.reshape(FOLD, -1, D), cotangent.reshape(FOLD, -1, D),
    )

    def along_z(packed):
        got = swap_all(packed.reshape(2 * depth, height, -1), ("z", "c"))
        return got.reshape(depth, 2 * height, -1)

    a, chip = along_z(a), flip(chip, "y")
    img = image_tokens.reshape(images, V)
    (img_t,) = run(transpose_kernel, [((V, images), BF)], [VM], [], img)
    a, b, chip, core, img_t = tie(a, b, chip, core, img_t)
    b = along_z(b)
    ax, ay = flip(a, "x"), flip(a, "y")
    img_t_far = flip(img_t, "c")
    hidden, slotted, grad_slot = run(
        spread_kernel,
        [((depth, FOLD, height, 2 * D), BF), ((rows, D), BF), ((rows, D), BF)],
        [SM] + [VM] * 5,
        [vmem((rows, 2 * D), F32)],
        me, arr, near, chip, flip(core, "c"), flip(chip[1], "c"),
    )
    a_far = flip(a, "c")
    b, ax, ay, hidden, grad_slot, img_t_far, a_far = tie(
        b, ax, ay, hidden, grad_slot, img_t_far, a_far
    )
    def group_rows(value):
        far = flip(value, "y")
        return (value, flip(value, "c"), far, flip(far, "c"))

    bx, by = flip(b, "x"), flip(b, "y")
    hidden = swap_all(hidden.reshape(depth, FOLD * height, 2 * D), "z")
    b_far, ax_far, ay_far = flip(b, "c"), flip(ax, "c"), flip(ay, "c")
    bx, by, ax, ax_far, ay_far, b_far = tie(bx, by, ax, ax_far, ay_far, b_far)
    axy, byx = flip(ax, "y"), flip(by, "x")
    by_far, bx_far = flip(by, "c"), flip(bx, "c")
    axy, byx, by_far, bx_far = tie(axy, byx, by_far, bx_far)
    pieces_a = (a, ay, ax, axy, a_far, ay_far, ax_far, flip(axy, "c"))
    pieces_b = (b, by, bx, byx, b_far, by_far, bx_far, flip(byx, "c"))
    hidden_far = flip(hidden, "x")
    pieces_a, pieces_b = tie(pieces_a, pieces_b)
    grad_slots = group_rows(grad_slot)

    weight_shape = lambda n: vmem((depth, 2, 2, 2 * height, n * D), BF)
    (
        table, projected, probs_self, saved, after_self, after_cross, normed_mlp, query_slots, kv,
        probs_cross,
    ) = run(
        functools.partial(forward_kernel, share),
        [
            ((8 * depth * share // D, D), F32),
            ((rows, 3 * D), BF),
            ((BATCHES, HEADS * rows, rows), BF),
            ((rows, 4 * D), BF),
            ((rows, D), F32),
            ((rows, D), F32),
            ((rows, D), BF),
            ((slots, D), BF),
            ((images, 2 * D), BF),
            ((captions * BATCHES, HEADS * CAP_LEN, IMG), BF),
        ],
        [SM, SM] + [VM] * 2 + [HB] * 16,
        [
            vmem((images, 2 * D), BF),
            vmem((captions * BATCHES, HEADS * CAP_LEN, IMG), BF),
            weight_shape(3),
            weight_shape(1),
            weight_shape(1),
            weight_shape(2),
            weight_shape(1),
            vmem((slots, D), BF),
            vmem((4, depth, 2 * height, LANES), BF),
            vmem((72, LANES), F32),
            sems(68 + 2 * captions),
        ],
        lens, me, slotted, img, *pieces_a, *pieces_b,
        copied=2,
    )
    inputs = group_rows(normed_mlp)
    small_shape = ((11 * PAIRS, LANES), F32)
    saved_far = flip(saved, "c")
    (
        grad_near, grad_keep, grad_send, grad_send_y, out_near, out_keep, out_send, out_send_y,
        active, grad_hidden, small,
    ) = run(
        mlp_kernel,
        [
            ((rows, D), F32),
            ((rows, D), BF),
            ((rows, D), BF),
            ((rows, D), BF),
            ((rows, D), F32),
            ((rows, D), BF),
            ((rows, D), BF),
            ((rows, D), BF),
            ((4 * rows, D), BF),
            ((4 * rows, D), BF),
            small_shape,
        ],
        [SM] + [VM] * 9 + [HB] * 2,
        [
            vmem((4 * rows, D), BF),
            vmem((4 * rows, D), BF),
            vmem((depth, 2, FOLD * height, D), BF),
            vmem((depth, 2, FOLD * height, D), BF),
            vmem((2, 2 * rows, D), F32),
            vmem((2, 2 * rows, D), F32),
            sems(4),
        ],
        me, table, *inputs, *grad_slots,
        hidden, hidden_far,
    )

    def owned(value, parts, axes):
        got = swap_all(value.reshape(parts * depth, height, -1), axes)
        return got.reshape(depth, parts, height, -1)

    flat = lambda n: ((height * n * PAIRS, LANES), F32)

    def combined(keep, far):
        return run(combine_kernel, [((rows, D), BF)], [VM] * 2, [], keep, far, mib=16)[0]

    grad_far = flip(combined(grad_keep, flip(grad_send_y, "c")), "y")
    grad_core = flip(grad_send, "c")
    (hidden_grad,) = run(
        hidden_grad_kernel,
        [((D, 2 * D), BF)],
        [VM] * 10,
        [],
        *inputs, *grad_slots, active, grad_hidden,
    )
    grad_far, grad_core, hidden_grad, saved_far, out_send, out_send_y = tie(
        grad_far, grad_core, hidden_grad, saved_far, out_send, out_send_y
    )
    hidden_got = swap_all(hidden_grad.reshape(2 * depth, FOLD * height, 2 * D), ("z", "x"))
    out_core, out_core_y = flip(out_send, "c"), flip(out_send_y, "c")
    grad_state, small, half_keep, half_send, kv_keep, kv_send = run(
        cross_back_kernel,
        [
            ((rows, D), F32),
            small_shape,
            ((rows, 3 * HALF), BF),
            ((rows, 3 * HALF), BF),
            ((images, D), BF),
            ((images, D), BF),
        ],
        [SM, SM] + [VM] * 5 + [HB, VM, HB] + [VM] * 3 + [HB] * 8,
        [
            weight_shape(1),
            weight_shape(1),
            vmem((slots, D), BF),
            vmem((slots, D), BF),
            vmem((images, 2 * D), BF),
            vmem((images, D), BF),
            vmem((images, D), BF),
            vmem((images, 2 * D), BF),
            vmem((captions * BATCHES, HEADS * CAP_LEN, IMG), BF),
            sems(18 + 2 * captions),
        ],
        lens, me, grad_near, grad_core, grad_far, after_cross, grad_slot, probs_cross, query_slots,
        kv, after_self, table, small, *pieces_b,
        copied=2,
    )
    grad_state, half_send, kv_send, out_core_y = tie(grad_state, half_send, kv_send, out_core_y)
    half_far, kv_far = flip(half_send, "c"), flip(kv_send, "c")
    out_far = flip(combined(out_keep, out_core_y), "y")
    grad_rows, small, self_keep, self_send = run(
        self_back_kernel,
        [
            ((rows, D), BF),
            small_shape,
            ((rows, 3 * HALF), BF),
            ((rows, 3 * HALF), BF),
        ],
        [SM] + [VM] * 6 + [HB] * 8,
        [
            weight_shape(1),
            weight_shape(3),
            vmem((rows, D), BF),
            vmem((rows, 3 * D), BF),
            sems(32),
        ],
        me, grad_state, probs_self, projected, slotted, table, small, *pieces_a,
    )
    self_send, grad_rows, half_far, kv_far, out_far = tie(
        self_send, grad_rows, half_far, kv_far, out_far
    )
    self_far = flip(self_send, "c")
    block = lambda n: ((2, depth, 2 * height, n), BF)
    kv_0, kv_1, mix_0, mix_1 = run(
        cross_grad_kernel,
        [block(3 * HALF)] * 2 + [block(2 * HALF)] * 2,
        [SM] + [HB] * 8,
        [vmem((rows, 4 * D), BF)] * 2
        + [vmem((rows, 3 * HALF), BF)] * 2
        + [vmem((V, images), BF)] * 2
        + [vmem((images, D), BF)] * 2
        + [vmem(block(n * HALF)[0], BF) for n in (3, 3, 2, 2)]
        + [vmem((D, D), F32), sems(12)],
        me, saved, saved_far, half_keep, half_far, img_t, img_t_far, kv_keep, kv_far,
        copied=4,
    )
    kv_0, kv_1, mix_0, mix_1, self_far, grad_rows = tie(
        kv_0, kv_1, mix_0, mix_1, self_far, grad_rows
    )
    kv_1, mix_1 = flip(kv_1, "x"), flip(mix_1, "y")
    q_0, q_1, v_0, v_1 = run(
        functools.partial(self_grad_kernel, share),
        [block(D)] * 2 + [block(HALF + LANES)] * 2,
        [SM] + [VM] * 5,
        [vmem((D, D), F32)],
        me, saved, saved_far, self_keep, self_far, small,
    )
    q_0, q_1, v_0, v_1, grad_rows = tie(q_0, q_1, v_0, v_1, grad_rows)
    q_1, v_1 = flip(q_1, "y"), flip(v_1, "x")
    part = ((rows // FOLD, 2 * D), BF)
    near, core, chip = run(
        return_kernel,
        [part, part, ((2,) + part[0], BF)],
        [SM] + [VM] * 7,
        [vmem((rows, 2 * D), F32)],
        me, arr, after_cross, table, out_near, out_core, out_far, grad_rows,
    )
    kv_1, mix_1, q_1, v_1, chip = tie(kv_1, mix_1, q_1, v_1, chip)
    kv_2, mix_2, q_2, v_2 = add_up(
        *([(near, 1), (got, 1)] for near, got in ((kv_0, kv_1), (mix_0, mix_1), (q_0, q_1), (v_0, v_1)))
    )
    kv_2, mix_2, q_2, v_2 = flip(kv_2, "y"), flip(mix_2, "x"), flip(q_2, "x"), flip(v_2, "y")
    kv_2, mix_2, q_2, v_2, hidden_got, kv_send, chip = tie(
        kv_2, mix_2, q_2, v_2, hidden_got, kv_send, chip
    )
    (got,) = add_up(
        [(kv_0, 0), (kv_1, 0), kv_2],
        [(mix_0, 0), (mix_1, 0), mix_2],
        [(q_0, 0), (q_1, 0), q_2],
        [(v_0, 0), (v_1, 0), v_2],
        joined=True,
    )
    got = owned(got, 2, ("z", "c"))
    chip = flip(chip, "y")
    hidden_part = ((height, 2 * D), BF)
    hidden_near, hidden_core, hidden_chip = run(
        depth_sum_kernel,
        [hidden_part, hidden_part, ((2,) + hidden_part[0], BF)],
        [SM, VM],
        [vmem((FOLD * height, 2 * D), F32)],
        me, hidden_got,
    )
    hidden_chip = flip(hidden_chip, "y")
    (grad_image,) = run(
        image_grad_kernel,
        [((images, D), BF)],
        [VM, VM, SM] + [HB] * 8,
        [vmem((2, depth, 2, 2, 2 * height, D), BF), sems(8)],
        kv_keep, kv_send, me, *pieces_b,
    )
    grad_up, grad_down = run(
        unpack_hidden_kernel, [flat(FOLD)] * 2, [SM] + [VM] * 4,
        [vmem((FOLD, height, 2 * D), BF)],
        me, hidden_near, hidden_chip, flip(hidden_core, "c"), flip(hidden_chip[1], "c"),
    )
    layer_out, grad_tokens = run(
        collect_kernel, [((FOLD, rows // FOLD, D), BF)] * 2, [SM] + [VM] * 4, [],
        me, near, chip, flip(core, "c"), flip(chip[1], "c"),
    )
    grad_cq, grad_ckv, grad_co, grad_out, grad_qkv, grad_small = run(
        unpack_kernel,
        [flat(n) for n in (1, 2, 1, 1, 3)] + [((8, LANES), F32)],
        [VM],
        [],
        got,
        mib=16,
    )
    return (
        layer_out.reshape(tokens.shape),
        grad_tokens.reshape(tokens.shape),
        grad_image.reshape(image_tokens.shape),
        *(
            g.reshape(-1)
            for g in (grad_qkv, grad_out, grad_cq, grad_ckv, grad_co, grad_up, grad_down)
        ),
        grad_small.reshape(-1)[: small_params.shape[0]],
    )


def general_norm_rows(inputs, gain_vec, shift_vec):
    centred = inputs - jnp.mean(inputs, axis=-1, keepdims=True)
    variance = jnp.mean(centred * centred, axis=-1, keepdims=True)
    return centred * lax.rsqrt(variance + epsilon) * gain_vec + shift_vec


def general_norm_back(inputs, gain_vec, shift_vec, grad_normed):
    _, pullback = jax.vjp(general_norm_rows, inputs, gain_vec, shift_vec)
    return pullback(grad_normed)


def general_gelu_exact(inputs):
    return jax.nn.gelu(inputs, approximate=False)


def general_gelu_back(inputs, grad_active):
    _, pullback = jax.vjp(general_gelu_exact, inputs)
    return pullback(grad_active)[0]


def general_slot_index(lengths, arrivals):
    run_ends = jnp.cumsum(lengths)
    starts = run_ends - lengths
    caption = jnp.sum((run_ends[None, :] <= arrivals[:, None]).astype(jnp.int32), axis=1)
    picked = caption[:, None] == jnp.arange(lengths.shape[0], dtype=jnp.int32)[None, :]
    first_row = jnp.sum(jnp.where(picked, starts[None, :], 0), axis=1)
    return caption * CAP_LEN + arrivals - first_row


def general_score_block(queries, keys_in, allowed):
    scores = jnp.einsum(
        "cqhd,ckhd->chqk", queries, keys_in, preferred_element_type=jnp.float32
    ) * HEAD_DIM ** (-0.5)
    return jnp.where(allowed, scores, -masked_fill)


def general_attention(queries, keys_in, values, allowed):
    scores = general_score_block(queries, keys_in, allowed)
    row_max = jnp.max(scores, axis=-1, keepdims=True)
    log_total = row_max + jnp.log(jnp.sum(jnp.exp(scores - row_max), axis=-1, keepdims=True))
    attn_weights = jnp.exp(scores - log_total).astype(jnp.bfloat16)
    mixed_out = jnp.einsum(
        "chqk,ckhd->cqhd", attn_weights, values, preferred_element_type=jnp.float32
    ).astype(jnp.bfloat16)
    return (mixed_out, log_total)


def general_attention_back(queries, keys_in, values, log_total, grad_mixed, allowed):
    scores = general_score_block(queries, keys_in, allowed)
    attn_weights = jnp.exp(scores - log_total)
    grad_weights = jnp.einsum(
        "cqhd,ckhd->chqk", grad_mixed, values, preferred_element_type=jnp.float32
    )
    centre = jnp.sum(attn_weights * grad_weights, axis=-1, keepdims=True)
    grad_scores = (attn_weights * (grad_weights - centre)).astype(jnp.bfloat16)
    grad_queries = jnp.einsum(
        "chqk,ckhd->cqhd", grad_scores, keys_in, preferred_element_type=jnp.float32
    ) * HEAD_DIM ** (-0.5)
    grad_keys = jnp.einsum(
        "chqk,cqhd->ckhd", grad_scores, queries, preferred_element_type=jnp.float32
    ) * HEAD_DIM ** (-0.5)
    grad_values = jnp.einsum(
        "chqk,cqhd->ckhd",
        attn_weights.astype(jnp.bfloat16),
        grad_mixed,
        preferred_element_type=jnp.float32,
    )
    return (grad_queries, grad_keys, grad_values)


def general_unpack_params(gathered):
    (
        flat_qkv,
        flat_out,
        flat_cross_q,
        flat_cross_kv,
        flat_cross_out,
        flat_up,
        flat_down,
        flat_small,
    ) = gathered
    small_vals = flat_small.astype(jnp.float32)
    return (
        flat_qkv.reshape(D, 3 * D),
        flat_out.reshape(D, D),
        flat_cross_q.reshape(D, D),
        flat_cross_kv.reshape(V, 2 * D),
        flat_cross_out.reshape(D, D),
        flat_up.reshape(D, FF),
        flat_down.reshape(FF, D),
        small_vals[: 3 * D].reshape(3, D),
        small_vals[3 * D : 6 * D].reshape(3, D),
        small_vals[6 * D : 6 * D + FF],
        small_vals[6 * D + FF :],
    )


def general_forward(slotted, image_rows, params, allowed, open_mask):
    (
        mat_qkv,
        mat_out,
        mat_cross_q,
        mat_cross_kv,
        mat_cross_out,
        mat_up,
        mat_down,
        norm_gains,
        shifts,
        up_bias,
        down_bias,
    ) = params
    captions = slotted.shape[0] // CAP_LEN
    head_count = D // HEAD_DIM
    normed_self = general_norm_rows(slotted, norm_gains[0], shifts[0]).astype(jnp.bfloat16)
    projected = jnp.dot(normed_self, mat_qkv, preferred_element_type=jnp.float32).astype(
        jnp.bfloat16
    )
    projected = projected.reshape(captions, CAP_LEN, 3, head_count, HEAD_DIM)
    self_mixed, self_total = general_attention(
        projected[:, :, 0], projected[:, :, 1], projected[:, :, 2], allowed
    )
    self_mixed = self_mixed.reshape(-1, D)
    after_self = slotted + jnp.dot(self_mixed, mat_out, preferred_element_type=jnp.float32)
    normed_cross = general_norm_rows(after_self, norm_gains[1], shifts[1]).astype(jnp.bfloat16)
    cross_query = jnp.dot(normed_cross, mat_cross_q, preferred_element_type=jnp.float32).astype(
        jnp.bfloat16
    )
    cross_query = cross_query.reshape(captions, CAP_LEN, head_count, HEAD_DIM)
    image_kv = jnp.dot(image_rows, mat_cross_kv, preferred_element_type=jnp.float32).astype(
        jnp.bfloat16
    )
    image_kv = image_kv.reshape(captions, IMG, 2, head_count, HEAD_DIM)
    cross_mixed, cross_total = general_attention(
        cross_query, image_kv[:, :, 0], image_kv[:, :, 1], open_mask
    )
    cross_mixed = cross_mixed.reshape(-1, D)
    after_cross = after_self + jnp.dot(
        cross_mixed, mat_cross_out, preferred_element_type=jnp.float32
    )
    normed_mlp = general_norm_rows(after_cross, norm_gains[2], shifts[2]).astype(jnp.bfloat16)
    hidden = jnp.dot(normed_mlp, mat_up, preferred_element_type=jnp.float32) + up_bias
    activated = general_gelu_exact(hidden).astype(jnp.bfloat16)
    result = (
        after_cross + jnp.dot(activated, mat_down, preferred_element_type=jnp.float32) + down_bias
    )
    saved_state = (
        slotted,
        normed_self,
        projected,
        self_total,
        self_mixed,
        after_self,
        normed_cross,
        cross_query,
        image_kv,
        cross_total,
        cross_mixed,
        after_cross,
        normed_mlp,
        hidden,
        activated,
    )
    return (result, saved_state)


def general_backward(saved_state, grad_slot, image_rows, params, allowed, open_mask):
    (
        mat_qkv,
        mat_out,
        mat_cross_q,
        mat_cross_kv,
        mat_cross_out,
        mat_up,
        mat_down,
        norm_gains,
        shifts,
        up_bias,
        down_bias,
    ) = params
    (
        slotted,
        normed_self,
        projected,
        self_total,
        self_mixed,
        after_self,
        normed_cross,
        cross_query,
        image_kv,
        cross_total,
        cross_mixed,
        after_cross,
        normed_mlp,
        hidden,
        activated,
    ) = saved_state
    captions = slotted.shape[0] // CAP_LEN
    head_count = D // HEAD_DIM
    grad_branch = grad_slot.astype(jnp.bfloat16)
    grad_down = jnp.einsum("rf,rd->fd", activated, grad_branch, preferred_element_type=jnp.float32)
    grad_down_bias = jnp.sum(grad_slot, axis=0)
    grad_active = jnp.einsum("rd,fd->rf", grad_branch, mat_down, preferred_element_type=jnp.float32)
    grad_hidden = general_gelu_back(hidden, grad_active).astype(jnp.bfloat16)
    grad_up = jnp.einsum("rd,rf->df", normed_mlp, grad_hidden, preferred_element_type=jnp.float32)
    grad_up_bias = jnp.sum(grad_hidden.astype(jnp.float32), axis=0)
    grad_normed = jnp.einsum("rf,df->rd", grad_hidden, mat_up, preferred_element_type=jnp.float32)
    grad_cross_in, grad_gain3, grad_shift3 = general_norm_back(
        after_cross, norm_gains[2], shifts[2], grad_normed
    )
    grad_after_cross = grad_slot + grad_cross_in
    grad_branch = grad_after_cross.astype(jnp.bfloat16)
    grad_cross_out = jnp.einsum(
        "rd,re->de", cross_mixed, grad_branch, preferred_element_type=jnp.float32
    )
    grad_mixed = jnp.einsum(
        "re,de->rd", grad_branch, mat_cross_out, preferred_element_type=jnp.float32
    ).astype(jnp.bfloat16)
    grad_mixed = grad_mixed.reshape(captions, CAP_LEN, head_count, HEAD_DIM)
    grad_query, grad_key, grad_value = general_attention_back(
        cross_query, image_kv[:, :, 0], image_kv[:, :, 1], cross_total, grad_mixed, open_mask
    )
    grad_query = grad_query.reshape(-1, D).astype(jnp.bfloat16)
    grad_kv = jnp.stack([grad_key, grad_value], axis=2).reshape(-1, 2 * D).astype(jnp.bfloat16)
    grad_cross_q = jnp.einsum(
        "rd,re->de", normed_cross, grad_query, preferred_element_type=jnp.float32
    )
    grad_cross_kv = jnp.einsum("iv,ie->ve", image_rows, grad_kv, preferred_element_type=jnp.float32)
    grad_image = jnp.einsum(
        "ie,ve->iv", grad_kv, mat_cross_kv, preferred_element_type=jnp.float32
    ).astype(jnp.bfloat16)
    grad_normed = jnp.einsum(
        "re,de->rd", grad_query, mat_cross_q, preferred_element_type=jnp.float32
    )
    grad_self_in, grad_gain2, grad_shift2 = general_norm_back(
        after_self, norm_gains[1], shifts[1], grad_normed
    )
    grad_after_self = grad_after_cross + grad_self_in
    grad_branch = grad_after_self.astype(jnp.bfloat16)
    grad_out = jnp.einsum("rd,re->de", self_mixed, grad_branch, preferred_element_type=jnp.float32)
    grad_mixed = jnp.einsum(
        "re,de->rd", grad_branch, mat_out, preferred_element_type=jnp.float32
    ).astype(jnp.bfloat16)
    grad_mixed = grad_mixed.reshape(captions, CAP_LEN, head_count, HEAD_DIM)
    grad_query, grad_key, grad_value = general_attention_back(
        projected[:, :, 0], projected[:, :, 1], projected[:, :, 2], self_total, grad_mixed, allowed
    )
    grad_projected = (
        jnp.stack([grad_query, grad_key, grad_value], axis=2)
        .reshape(-1, 3 * D)
        .astype(jnp.bfloat16)
    )
    grad_w_qkv = jnp.einsum(
        "rd,re->de", normed_self, grad_projected, preferred_element_type=jnp.float32
    )
    grad_normed = jnp.einsum(
        "re,de->rd", grad_projected, mat_qkv, preferred_element_type=jnp.float32
    )
    grad_input, grad_gain1, grad_shift1 = general_norm_back(slotted, norm_gains[0], shifts[0], grad_normed)
    grad_input = grad_input + grad_after_self
    grad_small = jnp.concatenate(
        [
            grad_gain1,
            grad_gain2,
            grad_gain3,
            grad_shift1,
            grad_shift2,
            grad_shift3,
            grad_up_bias,
            grad_down_bias,
        ]
    )
    flat_grads = (
        grad_w_qkv.reshape(-1),
        grad_out.reshape(-1),
        grad_cross_q.reshape(-1),
        grad_cross_kv.reshape(-1),
        grad_cross_out.reshape(-1),
        grad_up.reshape(-1),
        grad_down.reshape(-1),
        grad_small,
    )
    return (grad_input, grad_image, flat_grads)


def general_sum_to_owners(flat_grads):
    summed = []
    for grad_vec in flat_grads:
        for axis in ("dp", "fsdp"):
            parts = grad_vec.reshape(lax.axis_size(axis), -1).astype(jnp.bfloat16)
            if axis == "dp":
                parts = grad_vec.reshape(lax.axis_size("dp"), lax.axis_size("fsdp"), -1)
                parts = parts.astype(jnp.bfloat16)
            got = lax.all_to_all(parts, axis, split_axis=0, concat_axis=0, tiled=True)
            grad_vec = jnp.sum(got.astype(jnp.float32), axis=0)
        summed.append(grad_vec)
    return tuple(summed)


def general_device(
    tokens,
    image_tokens,
    caption_lengths,
    arrival_order,
    w_qkv,
    w_out,
    w_cross_q,
    w_cross_kv,
    w_cross_out,
    w_up,
    w_down,
    small_params,
    cotangent,
):
    lengths = caption_lengths[0]
    slot_rows = general_slot_index(lengths, arrival_order[0])
    captions = lengths.shape[0]
    slot_total = captions * CAP_LEN
    arrived, arrived_grad = (
        lax.all_to_all(tokens, "fsdp", split_axis=0, concat_axis=0, tiled=True),
        lax.all_to_all(cotangent, "fsdp", split_axis=0, concat_axis=0, tiled=True),
    )
    slotted = jnp.zeros((slot_total, D), jnp.float32).at[slot_rows].set(arrived.astype(jnp.float32))
    grad_slot = (
        jnp.zeros((slot_total, D), jnp.float32).at[slot_rows].set(arrived_grad.astype(jnp.float32))
    )
    positions = jnp.arange(CAP_LEN, dtype=jnp.int32)
    allowed = (positions[None, :] <= positions[:, None])[None, None] & (
        positions[None, None, None, :] < lengths[:, None, None, None]
    )
    open_mask = jnp.ones((1, 1, 1, 1), jnp.bool_)
    image_rows = image_tokens.reshape(-1, V)
    owned_shards = (w_qkv, w_out, w_cross_q, w_cross_kv, w_cross_out, w_up, w_down, small_params)
    params = general_unpack_params(
        tuple(lax.all_gather(w, ("dp", "fsdp"), axis=0, tiled=True) for w in owned_shards)
    )
    result, saved_state = general_forward(slotted, image_rows, params, allowed, open_mask)
    grad_input, grad_image, flat_grads = general_backward(
        saved_state, grad_slot, image_rows, params, allowed, open_mask
    )
    summed = general_sum_to_owners(flat_grads)
    out_rows = result[slot_rows].astype(jnp.bfloat16)
    grad_rows = grad_input[slot_rows].astype(jnp.bfloat16)
    layer_out, grad_tokens = (
        lax.all_to_all(out_rows, "fsdp", split_axis=0, concat_axis=0, tiled=True),
        lax.all_to_all(grad_rows, "fsdp", split_axis=0, concat_axis=0, tiled=True),
    )
    return (layer_out, grad_tokens, grad_image.reshape(image_tokens.shape)) + tuple(summed)


def solution(mesh):
    dp, fsdp = mesh.shape["dp"], mesh.shape["fsdp"]
    inner, specs_of = on_device, ("dp", "fsdp")
    if fsdp == 4 and dp % 2 == 0 and D % (dp * fsdp * 8) == 0:
        mesh = Mesh(mesh.devices.reshape(dp // 2, 2, 2, 2), AXES)
        specs_of = AXES
    else:
        inner = general_device
    rows, flat, cube = P(specs_of, None), P(specs_of), P(specs_of, None, None)
    return jax.shard_map(
        inner,
        mesh=mesh,
        in_specs=(rows, cube, rows, rows) + (flat,) * 8 + (rows,),
        out_specs=(rows, rows, cube) + (flat,) * 8,
        check_vma=False,
    )
```

```python
import functools

import jax
import jax.numpy as jnp
from jax import lax
from jax.experimental import pallas as pl
from jax.experimental.pallas import tpu as pltpu
from jax.sharding import Mesh
from jax.sharding import PartitionSpec as P

D = 768
HEAD_DIM = 64
FF = 3072
V = 768
IMG = 256
CAP_LEN = 64
LANES = 128
PAIRS = D // LANES
HALF = D // 2
HEADS = 4
WIDE = HEADS * HEAD_DIM
BATCHES = D // WIDE
FOLD = FF // D
GROUP = FOLD * LANES
GROUPS = FF // GROUP
TOKENS_AT = 32
SCALE = HEAD_DIM ** (-0.5)
epsilon = 1e-05
masked_fill = 1e30

BF = jnp.bfloat16
F32 = jnp.float32
AXES = ("z", "x", "y", "c")


def mm(a, b):
    return lax.dot_general(a, b, (((1,), (0,)), ((), ())), preferred_element_type=F32)


def mm_t(a, b):
    return lax.dot_general(a, b, (((1,), (1,)), ((), ())), preferred_element_type=F32)


def t_mm(a, b):
    return lax.dot_general(a, b, (((0,), (0,)), ((), ())), preferred_element_type=F32)


def wide(value):
    return value.astype(F32)


def norm_rows(inputs, gain_vec, shift_vec):
    centred = inputs - jnp.mean(inputs, axis=-1, keepdims=True)
    variance = jnp.mean(centred * centred, axis=-1, keepdims=True)
    return centred * lax.rsqrt(variance + epsilon) * gain_vec + shift_vec


def norm_back(inputs, gain_vec, grad_normed):
    centred = inputs - jnp.mean(inputs, axis=-1, keepdims=True)
    variance = jnp.mean(centred * centred, axis=-1, keepdims=True)
    scale = lax.rsqrt(variance + epsilon)
    unit = centred * scale
    weighted = grad_normed * gain_vec
    grad_in = scale * (
        weighted
        - jnp.mean(weighted, axis=-1, keepdims=True)
        - unit * jnp.mean(weighted * unit, axis=-1, keepdims=True)
    )
    grad_gain = jnp.sum(grad_normed * unit, axis=0, keepdims=True)
    grad_shift = jnp.sum(grad_normed, axis=0, keepdims=True)
    return grad_in, grad_gain, grad_shift


def arrival_pick(arr_ref):
    rows = arr_ref.shape[1]
    place = lax.broadcasted_iota(jnp.int32, (rows, rows), 0)
    return jnp.where(place == arr_ref[...], 1.0, 0.0).astype(BF)


def caption_of(index, lens_ref):
    end = jnp.int32(0)
    found = jnp.zeros_like(index)
    for c in range(lens_ref.shape[1] - 1):
        end = end + lens_ref[0, c]
        found = found + jnp.where(index >= end, 1, 0)
    return found


def slot_pick(lens_ref, rows):
    captions = lens_ref.shape[1]
    shape = (captions * CAP_LEN, rows)
    slot = lax.broadcasted_iota(jnp.int32, shape, 0)
    row = lax.broadcasted_iota(jnp.int32, shape, 1)
    start = jnp.int32(0)
    hit = jnp.zeros(shape, F32)
    for c in range(captions):
        length = lens_ref[0, c]
        inside = slot - c * CAP_LEN
        ok = (inside >= 0) & (inside < length) & (row - start == inside)
        hit = hit + jnp.where(ok, 1.0, 0.0)
        start = start + length
    return hit.astype(BF)


def fold_pick(back):
    source = lax.broadcasted_iota(jnp.int32, (GROUP, GROUP), 1 if back else 0)
    target = lax.broadcasted_iota(jnp.int32, (GROUP, GROUP), 0 if back else 1)
    return jnp.where(target == (source % FOLD) * LANES + source // FOLD, 1.0, 0.0).astype(BF)


def head_mask(rows):
    shape = (HEADS * rows, WIDE)
    head = lax.broadcasted_iota(jnp.int32, shape, 1) // HEAD_DIM
    row = lax.broadcasted_iota(jnp.int32, shape, 0)
    inside = (row >= head * rows) & (row < (head + 1) * rows)
    return jnp.where(inside, 1.0, 0.0).astype(BF)


def stack_heads(block, mask):
    return jnp.concatenate([block] * HEADS, axis=0) * mask


def merge_heads(stacked):
    rows = stacked.shape[0] // HEADS
    head = lax.broadcasted_iota(jnp.int32, (rows, WIDE), 1) // HEAD_DIM
    out = stacked[:rows]
    for n in range(1, HEADS):
        out = jnp.where(head == n, stacked[n * rows : (n + 1) * rows], out)
    return out


def softmax_rows(scores):
    shifted = jnp.exp(scores - jnp.max(scores, axis=-1, keepdims=True))
    return shifted * (1.0 / jnp.sum(shifted, axis=-1, keepdims=True))


def lanes_at(start, width):
    return pl.ds(pl.multiple_of(start, LANES), width)


def pack_halves(shards, out, rows, at=0):
    depth, _, height, _ = out.shape
    pieces = HALF // LANES
    for shard, mats in shards:
        rows[: shard.shape[0], :] = wide(shard[...])
        for mat in range(mats):
            for half in range(2):
                for i in range(pieces):
                    index = mat * PAIRS + half * pieces + i
                    value = rows[pl.ds(index, height, stride=mats * PAIRS), :].astype(BF)
                    lanes = slice(at + i * LANES, at + (i + 1) * LANES)
                    for z in range(depth):
                        out[z, half, :, lanes] = value
            at += HALF
    return at


def pack_self_kernel(w_qkv, w_out, attend, rows):
    pack_halves(((w_qkv, 3), (w_out, 1)), attend, rows)


def pack_cross_kernel(w_cross_q, w_cross_kv, w_cross_out, small, attend, rows):
    at = pack_halves(((w_cross_q, 1), (w_cross_kv, 2), (w_cross_out, 1)), attend, rows)
    depth, _, height, _ = attend.shape
    flat = wide(small[...])
    tail = jnp.zeros((1, LANES - small.shape[1] % LANES), F32)
    flat = jnp.concatenate([flat, tail], axis=1)
    parts = [flat[:, n : n + LANES] for n in range(0, flat.shape[1], LANES)]
    block = jnp.concatenate(parts + [jnp.zeros((height - len(parts), LANES), F32)], axis=0)
    for z in range(depth):
        for half in range(2):
            attend[z, half, :, at:] = block.astype(BF)


def pack_group_kernel(me, w_up, w_down, tokens, cotangent, near, core, chip, rows, parts):
    chunks = FF // LANES
    height = w_up.shape[0] // chunks

    def chunk(index):
        return rows[pl.ds(index, height, stride=chunks), :].astype(BF)

    rows[...] = wide(w_up[...])
    pick = fold_pick(False)
    for t in range(GROUPS):
        group = jnp.concatenate([chunk(t * FOLD + k) for k in range(FOLD)], axis=1)
        folded = mm(group, pick).astype(BF)
        for j in range(FOLD):
            parts[j, :height, t * LANES : (t + 1) * LANES] = folded[
                :, j * LANES : (j + 1) * LANES
            ]
    rows[...] = wide(w_down[...])
    for j in range(FOLD):
        for i in range(PAIRS):
            at = D + i * LANES
            parts[j, :height, at : at + LANES] = chunk(j * PAIRS + i)
        parts[j, TOKENS_AT : TOKENS_AT + tokens.shape[1], :D] = tokens[j]
        parts[j, TOKENS_AT : TOKENS_AT + tokens.shape[1], D:] = cotangent[j]
    near[...] = parts[part_of(me, 0, 0)]
    core[...] = parts[part_of(me, 0, 1)]
    for c in range(2):
        chip[c] = parts[part_of(me, 1, c)]


def transpose_kernel(img, out):
    for n in range(0, img.shape[0], IMG):
        out[:, n : n + IMG] = img[n : n + IMG, :].T


def part_of(me, far_y, far_c):
    return lax.bitwise_xor(me[0, 2], far_y) * 2 + lax.bitwise_xor(me[0, 3], far_c)


def spread_kernel(me, arr, near, chip, core, both, hidden, slotted, grad_slot, arrived):
    height, count = hidden.shape[2], arrived.shape[0] // FOLD
    for value, far_y, far_c in (
        (near[...], 0, 0), (chip[0], 1, 0), (core[...], 0, 1), (both[...], 1, 1),
    ):
        index = part_of(me, far_y, far_c)
        for z in range(hidden.shape[0]):
            hidden[z, index] = value[:height]
        at = pl.multiple_of(index * count, 8)
        arrived[pl.ds(at, count), :] = wide(value[TOKENS_AT : TOKENS_AT + count])
    pick = arrival_pick(arr)
    slotted[...] = mm(pick, arrived[:, :D].astype(BF)).astype(BF)
    grad_slot[...] = mm(pick, arrived[:, D:].astype(BF)).astype(BF)


def fill_table(share, me, pieces, flat, table):
    depth, height = pieces.shape[1], pieces.shape[2] // 2
    lane = lax.broadcasted_iota(jnp.int32, (3, LANES), 1)
    flat[...] = jnp.zeros_like(flat)
    for owner in range(8 * depth):
        z, x, y, c = owner // 8, owner // 4 % 2, owner // 2 % 2, owner % 2
        index = lax.bitwise_xor(me[0, 1], x) * 2 + lax.bitwise_xor(me[0, 2], y)
        value = wide(pieces[index, z])[c * height : c * height + 3, :]
        row, shift = divmod(owner * share, LANES)
        if shift == 0:
            flat[row : row + 3, :] += value
        else:
            moved = pltpu.roll(value, shift, axis=1)
            flat[row : row + 3, :] += jnp.where(lane >= shift, moved, 0.0)
            flat[row + 1 : row + 4, :] += jnp.where(lane < shift, moved, 0.0)
    for n in range(table.shape[0] * PAIRS):
        row, lanes = n // PAIRS, slice(n % PAIRS * LANES, (n % PAIRS + 1) * LANES)
        table[row : row + 1, lanes] = flat[n : n + 1, :]


def depth_sum_kernel(me, got, near, core, chip, total):
    height = near.shape[0]
    value = wide(got[0])
    for z in range(1, got.shape[0]):
        value = value + wide(got[z])
    total[...] = value

    def part(far_y, far_c):
        at = pl.multiple_of(part_of(me, far_y, far_c) * height, 8)
        return total[pl.ds(at, height), :].astype(BF)

    near[...] = part(0, 0)
    core[...] = part(0, 1)
    for c in range(2):
        chip[c] = part(1, c)


def unpack_hidden_kernel(me, near, chip, core, both, up, down, got):
    for value, far_y, far_c in (
        (near[...], 0, 0), (chip[0], 1, 0), (core[...], 0, 1), (both[...], 1, 1),
    ):
        got[part_of(me, far_y, far_c)] = value
    height = got.shape[1]
    chunks = FF // LANES
    pick = fold_pick(True)
    for t in range(GROUPS):
        group = jnp.concatenate(
            [got[j, :, t * LANES : (t + 1) * LANES] for j in range(FOLD)], axis=1
        )
        natural = mm(group, pick)
        for k in range(FOLD):
            up[pl.ds(t * FOLD + k, height, stride=chunks), :] = natural[
                :, k * LANES : (k + 1) * LANES
            ]
    for j in range(FOLD):
        for i in range(PAIRS):
            at = D + i * LANES
            down[pl.ds(j * PAIRS + i, height, stride=chunks), :] = wide(
                got[j, :, at : at + LANES]
            )


def unpack_halves(got, outs):
    depth, height = got.shape[0], got.shape[2]
    parts = HALF // LANES
    place = 0
    for out in outs:
        chunks = out.shape[0] // height
        for mat in range(chunks // PAIRS):
            for half in range(2):
                for i in range(parts):
                    at = place + i * LANES
                    total = wide(got[0, half, :, at : at + LANES])
                    for z in range(1, depth):
                        total = total + wide(got[z, half, :, at : at + LANES])
                    index = mat * PAIRS + half * parts + i
                    out[pl.ds(index, height, stride=chunks), :] = total
            place += HALF
    return place


class Fetch:
    def __init__(self, sems):
        self.sems = sems
        self.used = 0

    def start(self, source, target):
        copy = pltpu.make_async_copy(source, target, self.sems.at[self.used])
        self.used += 1
        copy.start()
        return copy

    def columns(self, pieces, me, piece_at, target, target_at):
        copies = []
        for index, piece in enumerate(pieces):
            half = lax.bitwise_xor(me[0, 3], index // 4)
            x = lax.bitwise_xor(me[0, 1], index // 2 % 2)
            y = lax.bitwise_xor(me[0, 2], index % 2)
            copies.append(
                self.start(
                    piece.at[:, :, pl.ds(piece_at, HALF)],
                    target.at[:, x, y, :, lanes_at(target_at + half * HALF, HALF)],
                )
            )
        return copies


def wait(copies):
    for copy in copies:
        copy.wait()


def matrix(ref):
    shape = ref.shape
    return ref[...].reshape(shape[0] * shape[1] * shape[2] * shape[3], shape[4])


def forward_kernel(share, lens, me, slotted, img, *refs):
    pieces_a, pieces_b = refs[:8], refs[8:16]
    (
        table,
        projected, probs_self, saved, after_self, after_cross, normed_mlp, query_slots,
        kv_out, probs_out, kv, probs_cross, w_qkv, w_out, w_cq, w_kv, w_co, mixed_slots, small, flat, sems,
    ) = refs[16:]
    fetch = Fetch(sems)
    got_small = [
        fetch.start(pieces_b[n].at[:, :, pl.ds(4 * HALF, LANES)], small.at[n]) for n in range(4)
    ]
    got_qkv = []
    for mat in range(3):
        got_qkv += fetch.columns(pieces_a, me, mat * HALF, w_qkv, mat * D)
    got_out = fetch.columns(pieces_a, me, 3 * HALF, w_out, 0)
    got_cq = fetch.columns(pieces_b, me, 0, w_cq, 0)
    got_kv = fetch.columns(pieces_b, me, HALF, w_kv, 0)
    got_kv += fetch.columns(pieces_b, me, 2 * HALF, w_kv, D)
    got_co = fetch.columns(pieces_b, me, 3 * HALF, w_co, 0)
    rows = slotted.shape[0]
    wait(got_small)
    fill_table(share, me, small, flat, table)
    saved[:, :D] = norm_rows(wide(slotted[...]), table[0:1, :], table[3:4, :]).astype(BF)
    wait(got_qkv)
    projected[...] = mm(saved[:, :D], matrix(w_qkv)).astype(BF)
    query_at = lax.broadcasted_iota(jnp.int32, (rows, rows), 0)
    key_at = lax.broadcasted_iota(jnp.int32, (rows, rows), 1)
    same = caption_of(query_at, lens) == caption_of(key_at, lens)
    block = jnp.where(same & (key_at <= query_at), 0.0, -masked_fill)
    barred = jnp.concatenate([block] * HEADS, axis=0)
    mask = head_mask(rows)
    for n in range(BATCHES):
        query, key, value = (
            projected[:, m * D + n * WIDE : m * D + (n + 1) * WIDE] for m in range(3)
        )
        scores = mm_t(stack_heads(query, mask), key) * SCALE + barred
        weights_low = softmax_rows(scores).astype(BF)
        probs_self[n] = weights_low
        saved[:, D + n * WIDE : D + (n + 1) * WIDE] = merge_heads(
            mm(weights_low, value)
        ).astype(BF)
    wait(got_out)
    state = wide(slotted[...]) + mm(saved[:, D : 2 * D], matrix(w_out))
    after_self[...] = state
    low = norm_rows(state, table[1:2, :], table[4:5, :]).astype(BF)
    saved[:, 2 * D : 3 * D] = low
    wait(got_cq)
    pick = slot_pick(lens, rows)
    query_slots[...] = mm(pick, mm(low, matrix(w_cq)).astype(BF)).astype(BF)
    wait(got_kv)
    kv_mat = matrix(w_kv)
    mask = head_mask(CAP_LEN)
    sent = []
    for c in range(lens.shape[1]):
        slots = slice(c * CAP_LEN, (c + 1) * CAP_LEN)
        images = slice(c * IMG, (c + 1) * IMG)
        kv[images, :] = mm(img[images, :], kv_mat).astype(BF)
        for n in range(BATCHES):
            cols = slice(n * WIDE, (n + 1) * WIDE)
            query = stack_heads(query_slots[slots, cols], mask)
            weights_low = softmax_rows(mm_t(query, kv[images, cols]) * SCALE).astype(BF)
            probs_cross[c * BATCHES + n] = weights_low
            value = kv[images, D + n * WIDE : D + (n + 1) * WIDE]
            mixed_slots[slots, cols] = merge_heads(mm(weights_low, value)).astype(BF)
        batch = slice(c * BATCHES, (c + 1) * BATCHES)
        sent.append(fetch.start(kv.at[images], kv_out.at[images]))
        sent.append(fetch.start(probs_cross.at[batch], probs_out.at[batch]))
    low = t_mm(pick, mixed_slots[...]).astype(BF)
    saved[:, 3 * D :] = low
    wait(got_co)
    state = after_self[...] + mm(low, matrix(w_co))
    after_cross[...] = state
    normed_mlp[...] = norm_rows(state, table[2:3, :], table[5:6, :]).astype(BF)
    wait(sent)


def put_small(small, row, value):
    for k in range(PAIRS):
        at = row * PAIRS + k
        small[at : at + 1, :] = value[:, k * LANES : (k + 1) * LANES]


def own_part(value, me):
    part = me[0, 2] * 2 + me[0, 3]
    out = value[:, :LANES]
    for j in range(1, FOLD):
        out = jnp.where(part == j, value[:, j * LANES : (j + 1) * LANES], out)
    return out


def mlp_kernel(me, table, *refs):
    inputs, grads, pieces = refs[:4], refs[4:8], refs[8:10]
    (
        grad_near, grad_keep, grad_send, grad_send_y, out_near, out_keep, out_send, out_send_y,
        active, grad_hidden, small, all_in, all_grad, w_up, w_down, grad_part, out_part, sems,
    ) = refs[10:]
    fetch = Fetch(sems)
    got_up, got_down = [], []
    for index in range(2):
        x = lax.bitwise_xor(me[0, 1], index)
        got_up.append(fetch.start(pieces[index].at[:, :, pl.ds(0, D)], w_up.at[:, x]))
        got_down.append(fetch.start(pieces[index].at[:, :, pl.ds(D, D)], w_down.at[:, x]))
    rows = inputs[0].shape[0]
    for n in range(4):
        all_in[n * rows : (n + 1) * rows, :] = inputs[n][...]
        all_grad[n * rows : (n + 1) * rows, :] = grads[n][...]
    bias = [
        table[6 + n // PAIRS : 7 + n // PAIRS, n % PAIRS * LANES : (n % PAIRS + 1) * LANES]
        for n in range(FF // LANES)
    ]
    bias = jnp.concatenate(
        [jnp.concatenate(bias[t * FOLD : (t + 1) * FOLD], axis=1) for t in range(GROUPS)], axis=0
    )
    bias = own_part(mm(bias.astype(BF), fold_pick(False)), me)
    bias = jnp.concatenate([bias[t : t + 1, :] for t in range(GROUPS)], axis=1)
    wait(got_up)
    up_mat = w_up[...].reshape(D, D)
    wait(got_down)
    down_mat = w_down[...].reshape(D, D)

    def rows_of(n, total):
        at = pl.ds(pl.multiple_of(n * 2 * rows, 64), 2 * rows)
        hidden = mm(all_in[at, :], up_mat) + bias
        half = 0.5 + 0.5 * lax.erf(hidden * (0.5**0.5))
        act = (hidden * half).astype(BF)
        active[at, :] = act
        slope = half + hidden * (jnp.exp(hidden * hidden * -0.5) * 0.3989422804014327)
        grad_hid = (mm_t(all_grad[at, :], down_mat) * slope).astype(BF)
        grad_hidden[at, :] = grad_hid
        grad_part[n] = mm_t(grad_hid, up_mat)
        out_part[n] = mm(act, down_mat)
        return total + jnp.sum(wide(grad_hid), axis=0, keepdims=True)

    sums = lax.fori_loop(0, 2, rows_of, jnp.zeros((1, D), F32)).astype(BF)
    for part, outs in (
        (grad_part, (grad_near, grad_send, grad_keep, grad_send_y)),
        (out_part, (out_near, out_send, out_keep, out_send_y)),
    ):
        for n, out in enumerate(outs):
            out[...] = part[n // 2, n % 2 * rows : (n % 2 + 1) * rows].astype(out.dtype)
    sums = jnp.concatenate(
        [sums[:, t * LANES : (t + 1) * LANES] for t in range(GROUPS)] + [sums[:, :LANES]] * 2,
        axis=0,
    )
    part = me[0, 2] * 2 + me[0, 3]
    spread = jnp.concatenate(
        [jnp.where(part == j, sums, jnp.zeros_like(sums)) for j in range(FOLD)], axis=1
    )
    natural = mm(spread, fold_pick(True))
    small[...] = jnp.zeros_like(small)
    for n in range(FF // LANES):
        at = 6 * PAIRS + n
        small[at : at + 1, :] = natural[
            n // FOLD : n // FOLD + 1, n % FOLD * LANES : (n % FOLD + 1) * LANES
        ]
    put_small(small, 10, jnp.sum(wide(grads[0][...]), axis=0, keepdims=True))


def hidden_grad_kernel(*refs):
    normed, grad_slot = refs[:4], refs[4:8]
    active, grad_hidden, out = refs[8:]
    rows = lambda parts: jnp.concatenate([r[...] for r in parts], axis=0)
    out[:, :D] = t_mm(rows(normed), grad_hidden[...]).astype(BF)
    out[:, D:] = t_mm(active[...], rows(grad_slot)).astype(BF)


def combine_kernel(keep, far, out):
    out[...] = (wide(keep[...]) + wide(far[...])).astype(BF)


def cross_back_kernel(
    lens, me, grad_near, grad_core, grad_far, after_cross, grad_slot, probs_in, query_slots, kv_in,
    after_self, table, small_in, *refs,
):
    pieces = refs[:8]
    (
        grad_state, small, half_keep, half_send, keep_out, send_out,
        w_co, w_cq, mixed_slots, query_grads, grad_kv, kv_keep, kv_send, kv, probs, sems,
    ) = refs[8:]
    fetch = Fetch(sems)
    got_co = fetch.columns(pieces, me, 3 * HALF, w_co, 0)
    got_kv = [fetch.start(kv_in, kv), fetch.start(probs_in, probs)]
    got_cq = fetch.columns(pieces, me, 0, w_cq, 0)
    rows = after_self.shape[0]
    sent = []
    halves = ((0, half_keep, kv_keep), (1, half_send, kv_send))
    small[...] = small_in[...]
    grad_in, grad_gain, grad_shift = norm_back(
        after_cross[...],
        table[2:3, :],
        grad_near[...] + wide(grad_core[...]) + wide(grad_far[...]),
    )
    put_small(small, 2, grad_gain)
    put_small(small, 5, grad_shift)
    grad_after = wide(grad_slot[...]) + grad_in
    grad_state[...] = grad_after
    pick = slot_pick(lens, rows)
    wait(got_co)
    query_grads[:rows, :] = grad_after.astype(BF)
    mixed_slots[...] = mm(pick, mm_t(query_grads[:rows, :], matrix(w_co)).astype(BF)).astype(BF)
    for rel, half_out, _ in halves:
        at = lax.bitwise_xor(me[0, 3], rel) * HALF
        half_out[:, HALF : 2 * HALF] = query_grads[:rows, lanes_at(at, HALF)]
    mask = head_mask(CAP_LEN)
    wait(got_kv)
    for c in range(lens.shape[1]):
        slots = slice(c * CAP_LEN, (c + 1) * CAP_LEN)
        images = slice(c * IMG, (c + 1) * IMG)
        for n in range(BATCHES):
            cols = slice(n * WIDE, (n + 1) * WIDE)
            value_cols = slice(D + n * WIDE, D + (n + 1) * WIDE)
            grad_mixed = stack_heads(mixed_slots[slots, cols], mask)
            query = stack_heads(query_slots[slots, cols], mask)
            weights_low = probs[c * BATCHES + n]
            attn = wide(weights_low)
            grad_weights = mm_t(grad_mixed, kv[images, value_cols])
            centre = jnp.sum(attn * grad_weights, axis=-1, keepdims=True)
            grad_scores = (attn * (grad_weights - centre)).astype(BF)
            query_grads[slots, cols] = (
                merge_heads(mm(grad_scores, kv[images, cols])) * SCALE
            ).astype(BF)
            grad_kv[images, cols] = (t_mm(grad_scores, query) * SCALE).astype(BF)
            grad_kv[images, value_cols] = t_mm(weights_low, grad_mixed).astype(BF)
        for rel, _, kv_half in halves:
            at = lax.bitwise_xor(me[0, 3], rel) * HALF
            kv_half[images, :HALF] = grad_kv[images, lanes_at(at, HALF)]
            kv_half[images, HALF:] = grad_kv[images, lanes_at(at + D, HALF)]
        sent.append(fetch.start(kv_send.at[images], send_out.at[images]))
        sent.append(fetch.start(kv_keep.at[images], keep_out.at[images]))
    mixed_slots[:rows, :] = t_mm(pick, query_grads[...]).astype(BF)
    wait(got_cq)
    grad_in, grad_gain, grad_shift = norm_back(
        after_self[...], table[1:2, :], mm_t(mixed_slots[:rows, :], matrix(w_cq))
    )
    put_small(small, 1, grad_gain)
    put_small(small, 4, grad_shift)
    grad_after = grad_state[...] + grad_in
    grad_state[...] = grad_after
    query_grads[:rows, :] = grad_after.astype(BF)
    for rel, half_out, _ in halves:
        at = lax.bitwise_xor(me[0, 3], rel) * HALF
        half_out[:, :HALF] = mixed_slots[:rows, lanes_at(at, HALF)]
        half_out[:, 2 * HALF :] = query_grads[:rows, lanes_at(at, HALF)]
    wait(sent)


def self_back_kernel(me, grad_state, probs, projected, slotted, table, small_in, *refs):
    pieces = refs[:8]
    (
        grad_rows, small, keep, send,
        w_out, w_qkv, mixed, grad_projected, sems,
    ) = refs[8:]
    fetch = Fetch(sems)
    got_out = fetch.columns(pieces, me, 3 * HALF, w_out, 0)
    got_qkv = []
    for mat in range(3):
        got_qkv += fetch.columns(pieces, me, mat * HALF, w_qkv, mat * D)
    rows = slotted.shape[0]
    wait(got_out)
    mixed[...] = mm_t(grad_state[...].astype(BF), matrix(w_out)).astype(BF)
    mask = head_mask(rows)
    for n in range(BATCHES):
        cols, key_cols, value_cols = (
            slice(m * D + n * WIDE, m * D + (n + 1) * WIDE) for m in range(3)
        )
        grad_mixed = stack_heads(mixed[:, cols], mask)
        query = stack_heads(projected[:, cols], mask)
        weights_low = probs[n]
        attn = wide(weights_low)
        grad_weights = mm_t(grad_mixed, projected[:, value_cols])
        centre = jnp.sum(attn * grad_weights, axis=-1, keepdims=True)
        grad_scores = (attn * (grad_weights - centre)).astype(BF)
        grad_projected[:, cols] = (
            merge_heads(mm(grad_scores, projected[:, key_cols])) * SCALE
        ).astype(BF)
        grad_projected[:, key_cols] = (t_mm(grad_scores, query) * SCALE).astype(BF)
        grad_projected[:, value_cols] = t_mm(weights_low, grad_mixed).astype(BF)
    for mat in range(3):
        for rel, out in ((0, keep), (1, send)):
            at = lax.bitwise_xor(me[0, 3], rel) * HALF + mat * D
            out[:, mat * HALF : (mat + 1) * HALF] = grad_projected[:, lanes_at(at, HALF)]
    wait(got_qkv)
    grad_in, grad_gain, grad_shift = norm_back(
        wide(slotted[...]), table[0:1, :], mm_t(grad_projected[...], matrix(w_qkv))
    )
    grad_slotted = (grad_state[...] + grad_in).astype(BF)
    grad_rows[...] = grad_slotted
    small[...] = small_in[...]
    put_small(small, 0, grad_gain)
    put_small(small, 3, grad_shift)


def put_quadrants(grads, me, outs, at, first):
    depth, height = outs[0].shape[1:3]
    width = grads.shape[1]
    for i, out in enumerate(outs):
        for j in range(2):
            far_x, far_y = (i, j) if first == "x" else (j, i)
            x, y = lax.bitwise_xor(me[0, 1], far_x), lax.bitwise_xor(me[0, 2], far_y)
            for z in range(depth):
                low = pl.multiple_of(((z * 2 + x) * 2 + y) * height, 16)
                out[j, z, :, at : at + width] = grads[pl.ds(low, height), :].astype(BF)


def half_grads(pieces, me, outs, grads, first, at=0):
    for left, far_left, right, far_right in pieces:
        width = right.shape[1]
        grads[:, :width] = t_mm(left, right) + t_mm(far_left, far_right)
        put_quadrants(grads.at[:, :width], me, outs, at, first)
        at += width


def cross_grad_kernel(me, *refs):
    sources, targets, landed, made, grads, sems = (
        refs[:8], refs[8:12], refs[12:20], refs[20:24], refs[24], refs[25],
    )
    fetch = Fetch(sems)
    copies = [fetch.start(source, target) for source, target in zip(sources, landed)]
    saved, saved_far, half, half_far, img_t, img_t_far, kv, kv_far = landed
    part = lambda ref, n, width: ref[:, n * width : (n + 1) * width]
    piece = lambda left, right: (
        part(saved, left, D), part(saved_far, left, D),
        part(half, right, HALF), part(half_far, right, HALF),
    )
    wait(copies[:4])
    half_grads([piece(3, 1), piece(1, 2)], me, made[2:], grads, "y")
    sent = [fetch.start(made[n], targets[n]) for n in (3, 2)]
    half_grads([piece(2, 0)], me, made[:2], grads, "x")
    wait(copies[4:])
    grads[...] = mm(img_t[...], kv[...]) + mm(img_t_far[...], kv_far[...])
    put_quadrants(grads, me, made[:2], HALF, "x")
    sent += [fetch.start(made[n], targets[n]) for n in (1, 0)]
    wait(sent)


def owner_rows(small, blocks, share):
    height = blocks.shape[0] // (small.shape[0] * LANES // share)
    lane = lax.broadcasted_iota(jnp.int32, (3, LANES), 1)
    blocks[...] = jnp.zeros_like(blocks)
    table = jnp.concatenate([small[...], jnp.zeros((6, LANES), F32)], axis=0)
    for owner in range(small.shape[0] * LANES // share):
        row, shift = divmod(owner * share, LANES)
        if shift == 0:
            value = table[row : row + 3]
        else:
            moved = pltpu.roll(table[row : row + 4], LANES - shift, axis=1)
            value = jnp.where(lane < LANES - shift, moved[:3], moved[1:4])
        blocks[owner * height : owner * height + 3, :] = value


def self_grad_kernel(share, me, saved, saved_far, half, half_far, small, *refs):
    first, second, grads = refs[:2], refs[2:4], refs[4]
    own, far = saved[:, :D], saved_far[:, :D]
    half_grads([(own, far, half[:, :D], half_far[:, :D])], me, first, grads, "y")
    half_grads([(own, far, half[:, D:], half_far[:, D:])], me, second, grads, "x")
    blocks = grads.at[:, :LANES]
    owner_rows(small, blocks, share)
    put_quadrants(blocks, me, second, HALF, "x")


def unpack_kernel(got, *outs):
    at = unpack_halves(got, outs[:-1])
    total = jnp.zeros((8, LANES), F32)
    for z in range(got.shape[0]):
        for c in range(2):
            total = total + wide(got[z, c, :8, at:])
    outs[-1][...] = total


def return_kernel(
    me, arr, after_cross, table, out_near, out_core, out_far, grad_rows, near, core, chip, rows
):
    pick = arrival_pick(arr)
    count = near.shape[0]
    result = after_cross[...] + out_near[...] + wide(out_core[...]) + wide(out_far[...])
    result = result + table[10:11, :]
    rows[:, :D] = t_mm(pick, result.astype(BF))
    rows[:, D:] = t_mm(pick, grad_rows[...])

    def part(far_y, far_c):
        at = pl.multiple_of(part_of(me, far_y, far_c) * count, 8)
        return rows[pl.ds(at, count), :].astype(BF)

    near[...] = part(0, 0)
    core[...] = part(0, 1)
    for c in range(2):
        chip[c] = part(1, c)


def collect_kernel(me, near, chip, core, both, layer_out, grad_tokens):
    for value, far_y, far_c in ((near[...], 0, 0), (chip[0], 1, 0), (core[...], 0, 1), (both[...], 1, 1)):
        index = part_of(me, far_y, far_c)
        layer_out[index] = value[:, :D]
        grad_tokens[index] = value[:, D:]


def image_grad_kernel(kv_keep, kv_send, *refs):
    me, pieces = refs[0], refs[1:9]
    grad_image, w_kv, sems = refs[9:]
    fetch = Fetch(sems)
    copies = []
    for index, piece in enumerate(pieces):
        x = lax.bitwise_xor(me[0, 1], index // 2 % 2)
        y = lax.bitwise_xor(me[0, 2], index % 2)
        copies.append(
            fetch.start(piece.at[:, :, pl.ds(HALF, D)], w_kv.at[index // 4, :, x, y])
        )
    wait(copies)
    near, far = w_kv[0].reshape(D, D), w_kv[1].reshape(D, D)
    for c in range(kv_keep.shape[0] // IMG):
        rows = pl.ds(c * IMG, IMG)
        grad_image[rows, :] = (mm_t(kv_keep[rows, :], near) + mm_t(kv_send[rows, :], far)).astype(
            BF
        )


def add_kernel(counts, joined, *refs):
    outs = refs[sum(counts) :]
    first = at = 0
    for n, count in enumerate(counts):
        for z in range(refs[first].shape[0]):
            total = wide(refs[first][z])
            for ref in refs[first + 1 : first + count]:
                total = total + wide(ref[z])
            if joined:
                outs[0][z, :, at : at + total.shape[-1]] = total.astype(BF)
            else:
                outs[n][z] = total.astype(BF)
        at += total.shape[-1]
        first += count


VM = pl.BlockSpec(memory_space=pltpu.VMEM)
SM = pl.BlockSpec(memory_space=pltpu.SMEM)
HB = pl.BlockSpec(memory_space=pl.ANY)


COST_US = {
    "forward_kernel": 12, "mlp_kernel": 9, "hidden_grad_kernel": 6, "cross_back_kernel": 12,
    "self_back_kernel": 8, "cross_grad_kernel": 10, "self_grad_kernel": 4, "return_kernel": 3,
    "image_grad_kernel": 7, "spread_kernel": 3,
}


def costs(kernel):
    name = (kernel.func if isinstance(kernel, functools.partial) else kernel).__name__
    flops = int(COST_US.get(name, 2) * 0.4 * 1e9)
    return pl.CostEstimate(flops=flops, bytes_accessed=2**20, transcendentals=0)


def run(kernel, outs, specs, scratch, *args, mib=58, copied=0, cost=None):
    return pl.pallas_call(
        kernel,
        out_shape=[jax.ShapeDtypeStruct(s, t) for s, t in outs],
        in_specs=specs,
        out_specs=[VM] * (len(outs) - copied) + [HB] * copied,
        scratch_shapes=scratch,
        compiler_params=pltpu.CompilerParams(vmem_limit_bytes=mib * 2**20),
        cost_estimate=cost or costs(kernel),
        name=(kernel.func if isinstance(kernel, functools.partial) else kernel).__name__,
    )(*args)


def add_up(*sums, joined=False):
    args, specs, shapes = [], [], []
    for terms in sums:
        for term in terms:
            array, index = term if isinstance(term, tuple) else (term, None)
            block = array.shape[-3:]
            if index is None:
                specs.append(pl.BlockSpec(block, lambda i: (0, 0, 0)))
            else:
                specs.append(pl.BlockSpec((None,) + block, lambda i, n=index: (n, 0, 0, 0)))
            args.append(array)
        shapes.append(block)
    if joined:
        shapes = [shapes[0][:2] + (sum(s[2] for s in shapes),)]
    return pl.pallas_call(
        functools.partial(add_kernel, [len(terms) for terms in sums], joined),
        grid=(1,),
        out_shape=[jax.ShapeDtypeStruct(s, BF) for s in shapes],
        in_specs=specs,
        out_specs=[pl.BlockSpec(s, lambda i: (0, 0, 0)) for s in shapes],
        compiler_params=pltpu.CompilerParams(vmem_limit_bytes=58 * 2**20),
        name="add_kernel",
    )(*args)


def flip(value, axis):
    return lax.ppermute(value, axis, [(0, 1), (1, 0)])


def swap_all(value, axes):
    return lax.all_to_all(value, axes, split_axis=0, concat_axis=0, tiled=True)


def tie(*values):
    return lax.optimization_barrier(values)


def on_device(
    tokens,
    image_tokens,
    caption_lengths,
    arrival_order,
    w_qkv,
    w_out,
    w_cross_q,
    w_cross_kv,
    w_cross_out,
    w_up,
    w_down,
    small_params,
    cotangent,
):
    depth = lax.axis_size("z")
    height = D // (8 * depth)
    rows = tokens.shape[0]
    captions = caption_lengths.shape[1]
    slots = captions * CAP_LEN
    images = captions * IMG
    lens, arr = caption_lengths, arrival_order
    me = jnp.stack([lax.axis_index(a) for a in AXES]).astype(jnp.int32).reshape(1, 4)
    vmem = pltpu.VMEM
    sems = lambda n: pltpu.SemaphoreType.DMA((n,))
    shards = (w_qkv, w_out, w_cross_q, w_cross_kv, w_cross_out, w_up, w_down)

    share = small_params.shape[0]
    flat_shards = [w.reshape(-1, LANES) for w in shards]
    packed = lambda n: [((depth, 2, height, n), BF)]
    chunked = [vmem((w_up.shape[0] // LANES, LANES), F32)]
    (a,) = run(pack_self_kernel, packed(4 * HALF), [VM] * 2, chunked, *flat_shards[:2])
    (b,) = run(
        pack_cross_kernel, packed(4 * HALF + LANES), [VM] * 4, chunked,
        *flat_shards[2:5], small_params.reshape(1, share),
    )
    part = ((TOKENS_AT + 48, 2 * D), BF)
    near, core, chip = run(
        pack_group_kernel,
        [part, part, ((2,) + part[0], BF)],
        [SM] + [VM] * 4,
        chunked + [vmem((FOLD,) + part[0], BF)],
        me, *flat_shards[5:], tokens.reshape(FOLD, -1, D), cotangent.reshape(FOLD, -1, D),
    )

    def along_z(packed):
        got = swap_all(packed.reshape(2 * depth, height, -1), ("z", "c"))
        return got.reshape(depth, 2 * height, -1)

    a, chip = along_z(a), flip(chip, "y")
    img = image_tokens.reshape(images, V)
    (img_t,) = run(transpose_kernel, [((V, images), BF)], [VM], [], img)
    a, b, chip, core, img_t = tie(a, b, chip, core, img_t)
    b = along_z(b)
    ax, ay = flip(a, "x"), flip(a, "y")
    img_t_far = flip(img_t, "c")
    hidden, slotted, grad_slot = run(
        spread_kernel,
        [((depth, FOLD, height, 2 * D), BF), ((rows, D), BF), ((rows, D), BF)],
        [SM] + [VM] * 5,
        [vmem((rows, 2 * D), F32)],
        me, arr, near, chip, flip(core, "c"), flip(chip[1], "c"),
    )
    a_far = flip(a, "c")
    b, ax, ay, hidden, grad_slot, img_t_far, a_far = tie(
        b, ax, ay, hidden, grad_slot, img_t_far, a_far
    )
    def group_rows(value):
        far = flip(value, "y")
        return (value, flip(value, "c"), far, flip(far, "c"))

    bx, by = flip(b, "x"), flip(b, "y")
    hidden = swap_all(hidden.reshape(depth, FOLD * height, 2 * D), "z")
    b_far, ax_far, ay_far = flip(b, "c"), flip(ax, "c"), flip(ay, "c")
    bx, by, ax, ax_far, ay_far, b_far = tie(bx, by, ax, ax_far, ay_far, b_far)
    axy, byx = flip(ax, "y"), flip(by, "x")
    by_far, bx_far = flip(by, "c"), flip(bx, "c")
    axy, byx, by_far, bx_far = tie(axy, byx, by_far, bx_far)
    pieces_a = (a, ay, ax, axy, a_far, ay_far, ax_far, flip(axy, "c"))
    pieces_b = (b, by, bx, byx, b_far, by_far, bx_far, flip(byx, "c"))
    hidden_far = flip(hidden, "x")
    pieces_a, pieces_b = tie(pieces_a, pieces_b)
    grad_slots = group_rows(grad_slot)

    weight_shape = lambda n: vmem((depth, 2, 2, 2 * height, n * D), BF)
    (
        table, projected, probs_self, saved, after_self, after_cross, normed_mlp, query_slots, kv,
        probs_cross,
    ) = run(
        functools.partial(forward_kernel, share),
        [
            ((8 * depth * share // D, D), F32),
            ((rows, 3 * D), BF),
            ((BATCHES, HEADS * rows, rows), BF),
            ((rows, 4 * D), BF),
            ((rows, D), F32),
            ((rows, D), F32),
            ((rows, D), BF),
            ((slots, D), BF),
            ((images, 2 * D), BF),
            ((captions * BATCHES, HEADS * CAP_LEN, IMG), BF),
        ],
        [SM, SM] + [VM] * 2 + [HB] * 16,
        [
            vmem((images, 2 * D), BF),
            vmem((captions * BATCHES, HEADS * CAP_LEN, IMG), BF),
            weight_shape(3),
            weight_shape(1),
            weight_shape(1),
            weight_shape(2),
            weight_shape(1),
            vmem((slots, D), BF),
            vmem((4, depth, 2 * height, LANES), BF),
            vmem((72, LANES), F32),
            sems(68 + 2 * captions),
        ],
        lens, me, slotted, img, *pieces_a, *pieces_b,
        copied=2,
        cost=pl.CostEstimate(flops=13200000000, bytes_accessed=20 * 2**20, transcendentals=0),
    )
    inputs = group_rows(normed_mlp)
    small_shape = ((11 * PAIRS, LANES), F32)
    saved_far = flip(saved, "c")
    (
        grad_near, grad_keep, grad_send, grad_send_y, out_near, out_keep, out_send, out_send_y,
        active, grad_hidden, small,
    ) = run(
        mlp_kernel,
        [
            ((rows, D), F32),
            ((rows, D), BF),
            ((rows, D), BF),
            ((rows, D), BF),
            ((rows, D), F32),
            ((rows, D), BF),
            ((rows, D), BF),
            ((rows, D), BF),
            ((4 * rows, D), BF),
            ((4 * rows, D), BF),
            small_shape,
        ],
        [SM] + [VM] * 9 + [HB] * 2,
        [
            vmem((4 * rows, D), BF),
            vmem((4 * rows, D), BF),
            vmem((depth, 2, FOLD * height, D), BF),
            vmem((depth, 2, FOLD * height, D), BF),
            vmem((2, 2 * rows, D), F32),
            vmem((2, 2 * rows, D), F32),
            sems(4),
        ],
        me, table, *inputs, *grad_slots,
        hidden, hidden_far,
    )

    def owned(value, parts, axes):
        got = swap_all(value.reshape(parts * depth, height, -1), axes)
        return got.reshape(depth, parts, height, -1)

    flat = lambda n: ((height * n * PAIRS, LANES), F32)

    def combined(keep, far):
        return run(combine_kernel, [((rows, D), BF)], [VM] * 2, [], keep, far, mib=16)[0]

    grad_far = flip(combined(grad_keep, flip(grad_send_y, "c")), "y")
    grad_core = flip(grad_send, "c")
    (hidden_grad,) = run(
        hidden_grad_kernel,
        [((D, 2 * D), BF)],
        [VM] * 10,
        [],
        *inputs, *grad_slots, active, grad_hidden,
    )
    grad_far, grad_core, hidden_grad, saved_far, out_send, out_send_y = tie(
        grad_far, grad_core, hidden_grad, saved_far, out_send, out_send_y
    )
    hidden_got = swap_all(hidden_grad.reshape(2 * depth, FOLD * height, 2 * D), ("z", "x"))
    out_core, out_core_y = flip(out_send, "c"), flip(out_send_y, "c")
    grad_state, small, half_keep, half_send, kv_keep, kv_send = run(
        cross_back_kernel,
        [
            ((rows, D), F32),
            small_shape,
            ((rows, 3 * HALF), BF),
            ((rows, 3 * HALF), BF),
            ((images, D), BF),
            ((images, D), BF),
        ],
        [SM, SM] + [VM] * 5 + [HB, VM, HB] + [VM] * 3 + [HB] * 8,
        [
            weight_shape(1),
            weight_shape(1),
            vmem((slots, D), BF),
            vmem((slots, D), BF),
            vmem((images, 2 * D), BF),
            vmem((images, D), BF),
            vmem((images, D), BF),
            vmem((images, 2 * D), BF),
            vmem((captions * BATCHES, HEADS * CAP_LEN, IMG), BF),
            sems(18 + 2 * captions),
        ],
        lens, me, grad_near, grad_core, grad_far, after_cross, grad_slot, probs_cross, query_slots,
        kv, after_self, table, small, *pieces_b,
        copied=2,
    )
    grad_state, half_send, kv_send, out_core_y = tie(grad_state, half_send, kv_send, out_core_y)
    half_far, kv_far = flip(half_send, "c"), flip(kv_send, "c")
    out_far = flip(combined(out_keep, out_core_y), "y")
    grad_rows, small, self_keep, self_send = run(
        self_back_kernel,
        [
            ((rows, D), BF),
            small_shape,
            ((rows, 3 * HALF), BF),
            ((rows, 3 * HALF), BF),
        ],
        [SM] + [VM] * 6 + [HB] * 8,
        [
            weight_shape(1),
            weight_shape(3),
            vmem((rows, D), BF),
            vmem((rows, 3 * D), BF),
            sems(32),
        ],
        me, grad_state, probs_self, projected, slotted, table, small, *pieces_a,
    )
    self_send, grad_rows, half_far, kv_far, out_far = tie(
        self_send, grad_rows, half_far, kv_far, out_far
    )
    self_far = flip(self_send, "c")
    block = lambda n: ((2, depth, 2 * height, n), BF)
    kv_0, kv_1, mix_0, mix_1 = run(
        cross_grad_kernel,
        [block(3 * HALF)] * 2 + [block(2 * HALF)] * 2,
        [SM] + [HB] * 8,
        [vmem((rows, 4 * D), BF)] * 2
        + [vmem((rows, 3 * HALF), BF)] * 2
        + [vmem((V, images), BF)] * 2
        + [vmem((images, D), BF)] * 2
        + [vmem(block(n * HALF)[0], BF) for n in (3, 3, 2, 2)]
        + [vmem((D, D), F32), sems(12)],
        me, saved, saved_far, half_keep, half_far, img_t, img_t_far, kv_keep, kv_far,
        copied=4,
    )
    kv_0, kv_1, mix_0, mix_1, self_far, grad_rows = tie(
        kv_0, kv_1, mix_0, mix_1, self_far, grad_rows
    )
    kv_1, mix_1 = flip(kv_1, "x"), flip(mix_1, "y")
    q_0, q_1, v_0, v_1 = run(
        functools.partial(self_grad_kernel, share),
        [block(D)] * 2 + [block(HALF + LANES)] * 2,
        [SM] + [VM] * 5,
        [vmem((D, D), F32)],
        me, saved, saved_far, self_keep, self_far, small,
    )
    q_0, q_1, v_0, v_1, grad_rows = tie(q_0, q_1, v_0, v_1, grad_rows)
    q_1, v_1 = flip(q_1, "y"), flip(v_1, "x")
    part = ((rows // FOLD, 2 * D), BF)
    near, core, chip = run(
        return_kernel,
        [part, part, ((2,) + part[0], BF)],
        [SM] + [VM] * 7,
        [vmem((rows, 2 * D), F32)],
        me, arr, after_cross, table, out_near, out_core, out_far, grad_rows,
    )
    kv_1, mix_1, q_1, v_1, chip = tie(kv_1, mix_1, q_1, v_1, chip)
    kv_2, mix_2, q_2, v_2 = add_up(
        *([(near, 1), (got, 1)] for near, got in ((kv_0, kv_1), (mix_0, mix_1), (q_0, q_1), (v_0, v_1)))
    )
    kv_2, mix_2, q_2, v_2 = flip(kv_2, "y"), flip(mix_2, "x"), flip(q_2, "x"), flip(v_2, "y")
    kv_2, mix_2, q_2, v_2, hidden_got, kv_send, chip = tie(
        kv_2, mix_2, q_2, v_2, hidden_got, kv_send, chip
    )
    (got,) = add_up(
        [(kv_0, 0), (kv_1, 0), kv_2],
        [(mix_0, 0), (mix_1, 0), mix_2],
        [(q_0, 0), (q_1, 0), q_2],
        [(v_0, 0), (v_1, 0), v_2],
        joined=True,
    )
    got = owned(got, 2, ("z", "c"))
    chip = flip(chip, "y")
    hidden_part = ((height, 2 * D), BF)
    hidden_near, hidden_core, hidden_chip = run(
        depth_sum_kernel,
        [hidden_part, hidden_part, ((2,) + hidden_part[0], BF)],
        [SM, VM],
        [vmem((FOLD * height, 2 * D), F32)],
        me, hidden_got,
    )
    hidden_chip = flip(hidden_chip, "y")
    (grad_image,) = run(
        image_grad_kernel,
        [((images, D), BF)],
        [VM, VM, SM] + [HB] * 8,
        [vmem((2, depth, 2, 2, 2 * height, D), BF), sems(8)],
        kv_keep, kv_send, me, *pieces_b,
    )
    grad_up, grad_down = run(
        unpack_hidden_kernel, [flat(FOLD)] * 2, [SM] + [VM] * 4,
        [vmem((FOLD, height, 2 * D), BF)],
        me, hidden_near, hidden_chip, flip(hidden_core, "c"), flip(hidden_chip[1], "c"),
    )
    layer_out, grad_tokens = run(
        collect_kernel, [((FOLD, rows // FOLD, D), BF)] * 2, [SM] + [VM] * 4, [],
        me, near, chip, flip(core, "c"), flip(chip[1], "c"),
    )
    grad_cq, grad_ckv, grad_co, grad_out, grad_qkv, grad_small = run(
        unpack_kernel,
        [flat(n) for n in (1, 2, 1, 1, 3)] + [((8, LANES), F32)],
        [VM],
        [],
        got,
        mib=16,
    )
    return (
        layer_out.reshape(tokens.shape),
        grad_tokens.reshape(tokens.shape),
        grad_image.reshape(image_tokens.shape),
        *(
            g.reshape(-1)
            for g in (grad_qkv, grad_out, grad_cq, grad_ckv, grad_co, grad_up, grad_down)
        ),
        grad_small.reshape(-1)[: small_params.shape[0]],
    )


def general_norm_rows(inputs, gain_vec, shift_vec):
    centred = inputs - jnp.mean(inputs, axis=-1, keepdims=True)
    variance = jnp.mean(centred * centred, axis=-1, keepdims=True)
    return centred * lax.rsqrt(variance + epsilon) * gain_vec + shift_vec


def general_norm_back(inputs, gain_vec, shift_vec, grad_normed):
    _, pullback = jax.vjp(general_norm_rows, inputs, gain_vec, shift_vec)
    return pullback(grad_normed)


def general_gelu_exact(inputs):
    return jax.nn.gelu(inputs, approximate=False)


def general_gelu_back(inputs, grad_active):
    _, pullback = jax.vjp(general_gelu_exact, inputs)
    return pullback(grad_active)[0]


def general_slot_index(lengths, arrivals):
    run_ends = jnp.cumsum(lengths)
    starts = run_ends - lengths
    caption = jnp.sum((run_ends[None, :] <= arrivals[:, None]).astype(jnp.int32), axis=1)
    picked = caption[:, None] == jnp.arange(lengths.shape[0], dtype=jnp.int32)[None, :]
    first_row = jnp.sum(jnp.where(picked, starts[None, :], 0), axis=1)
    return caption * CAP_LEN + arrivals - first_row


def general_score_block(queries, keys_in, allowed):
    scores = jnp.einsum(
        "cqhd,ckhd->chqk", queries, keys_in, preferred_element_type=jnp.float32
    ) * HEAD_DIM ** (-0.5)
    return jnp.where(allowed, scores, -masked_fill)


def general_attention(queries, keys_in, values, allowed):
    scores = general_score_block(queries, keys_in, allowed)
    row_max = jnp.max(scores, axis=-1, keepdims=True)
    log_total = row_max + jnp.log(jnp.sum(jnp.exp(scores - row_max), axis=-1, keepdims=True))
    attn_weights = jnp.exp(scores - log_total).astype(jnp.bfloat16)
    mixed_out = jnp.einsum(
        "chqk,ckhd->cqhd", attn_weights, values, preferred_element_type=jnp.float32
    ).astype(jnp.bfloat16)
    return (mixed_out, log_total)


def general_attention_back(queries, keys_in, values, log_total, grad_mixed, allowed):
    scores = general_score_block(queries, keys_in, allowed)
    attn_weights = jnp.exp(scores - log_total)
    grad_weights = jnp.einsum(
        "cqhd,ckhd->chqk", grad_mixed, values, preferred_element_type=jnp.float32
    )
    centre = jnp.sum(attn_weights * grad_weights, axis=-1, keepdims=True)
    grad_scores = (attn_weights * (grad_weights - centre)).astype(jnp.bfloat16)
    grad_queries = jnp.einsum(
        "chqk,ckhd->cqhd", grad_scores, keys_in, preferred_element_type=jnp.float32
    ) * HEAD_DIM ** (-0.5)
    grad_keys = jnp.einsum(
        "chqk,cqhd->ckhd", grad_scores, queries, preferred_element_type=jnp.float32
    ) * HEAD_DIM ** (-0.5)
    grad_values = jnp.einsum(
        "chqk,cqhd->ckhd",
        attn_weights.astype(jnp.bfloat16),
        grad_mixed,
        preferred_element_type=jnp.float32,
    )
    return (grad_queries, grad_keys, grad_values)


def general_unpack_params(gathered):
    (
        flat_qkv,
        flat_out,
        flat_cross_q,
        flat_cross_kv,
        flat_cross_out,
        flat_up,
        flat_down,
        flat_small,
    ) = gathered
    small_vals = flat_small.astype(jnp.float32)
    return (
        flat_qkv.reshape(D, 3 * D),
        flat_out.reshape(D, D),
        flat_cross_q.reshape(D, D),
        flat_cross_kv.reshape(V, 2 * D),
        flat_cross_out.reshape(D, D),
        flat_up.reshape(D, FF),
        flat_down.reshape(FF, D),
        small_vals[: 3 * D].reshape(3, D),
        small_vals[3 * D : 6 * D].reshape(3, D),
        small_vals[6 * D : 6 * D + FF],
        small_vals[6 * D + FF :],
    )


def general_forward(slotted, image_rows, params, allowed, open_mask):
    (
        mat_qkv,
        mat_out,
        mat_cross_q,
        mat_cross_kv,
        mat_cross_out,
        mat_up,
        mat_down,
        norm_gains,
        shifts,
        up_bias,
        down_bias,
    ) = params
    captions = slotted.shape[0] // CAP_LEN
    head_count = D // HEAD_DIM
    normed_self = general_norm_rows(slotted, norm_gains[0], shifts[0]).astype(jnp.bfloat16)
    projected = jnp.dot(normed_self, mat_qkv, preferred_element_type=jnp.float32).astype(
        jnp.bfloat16
    )
    projected = projected.reshape(captions, CAP_LEN, 3, head_count, HEAD_DIM)
    self_mixed, self_total = general_attention(
        projected[:, :, 0], projected[:, :, 1], projected[:, :, 2], allowed
    )
    self_mixed = self_mixed.reshape(-1, D)
    after_self = slotted + jnp.dot(self_mixed, mat_out, preferred_element_type=jnp.float32)
    normed_cross = general_norm_rows(after_self, norm_gains[1], shifts[1]).astype(jnp.bfloat16)
    cross_query = jnp.dot(normed_cross, mat_cross_q, preferred_element_type=jnp.float32).astype(
        jnp.bfloat16
    )
    cross_query = cross_query.reshape(captions, CAP_LEN, head_count, HEAD_DIM)
    image_kv = jnp.dot(image_rows, mat_cross_kv, preferred_element_type=jnp.float32).astype(
        jnp.bfloat16
    )
    image_kv = image_kv.reshape(captions, IMG, 2, head_count, HEAD_DIM)
    cross_mixed, cross_total = general_attention(
        cross_query, image_kv[:, :, 0], image_kv[:, :, 1], open_mask
    )
    cross_mixed = cross_mixed.reshape(-1, D)
    after_cross = after_self + jnp.dot(
        cross_mixed, mat_cross_out, preferred_element_type=jnp.float32
    )
    normed_mlp = general_norm_rows(after_cross, norm_gains[2], shifts[2]).astype(jnp.bfloat16)
    hidden = jnp.dot(normed_mlp, mat_up, preferred_element_type=jnp.float32) + up_bias
    activated = general_gelu_exact(hidden).astype(jnp.bfloat16)
    result = (
        after_cross + jnp.dot(activated, mat_down, preferred_element_type=jnp.float32) + down_bias
    )
    saved_state = (
        slotted,
        normed_self,
        projected,
        self_total,
        self_mixed,
        after_self,
        normed_cross,
        cross_query,
        image_kv,
        cross_total,
        cross_mixed,
        after_cross,
        normed_mlp,
        hidden,
        activated,
    )
    return (result, saved_state)


def general_backward(saved_state, grad_slot, image_rows, params, allowed, open_mask):
    (
        mat_qkv,
        mat_out,
        mat_cross_q,
        mat_cross_kv,
        mat_cross_out,
        mat_up,
        mat_down,
        norm_gains,
        shifts,
        up_bias,
        down_bias,
    ) = params
    (
        slotted,
        normed_self,
        projected,
        self_total,
        self_mixed,
        after_self,
        normed_cross,
        cross_query,
        image_kv,
        cross_total,
        cross_mixed,
        after_cross,
        normed_mlp,
        hidden,
        activated,
    ) = saved_state
    captions = slotted.shape[0] // CAP_LEN
    head_count = D // HEAD_DIM
    grad_branch = grad_slot.astype(jnp.bfloat16)
    grad_down = jnp.einsum("rf,rd->fd", activated, grad_branch, preferred_element_type=jnp.float32)
    grad_down_bias = jnp.sum(grad_slot, axis=0)
    grad_active = jnp.einsum("rd,fd->rf", grad_branch, mat_down, preferred_element_type=jnp.float32)
    grad_hidden = general_gelu_back(hidden, grad_active).astype(jnp.bfloat16)
    grad_up = jnp.einsum("rd,rf->df", normed_mlp, grad_hidden, preferred_element_type=jnp.float32)
    grad_up_bias = jnp.sum(grad_hidden.astype(jnp.float32), axis=0)
    grad_normed = jnp.einsum("rf,df->rd", grad_hidden, mat_up, preferred_element_type=jnp.float32)
    grad_cross_in, grad_gain3, grad_shift3 = general_norm_back(
        after_cross, norm_gains[2], shifts[2], grad_normed
    )
    grad_after_cross = grad_slot + grad_cross_in
    grad_branch = grad_after_cross.astype(jnp.bfloat16)
    grad_cross_out = jnp.einsum(
        "rd,re->de", cross_mixed, grad_branch, preferred_element_type=jnp.float32
    )
    grad_mixed = jnp.einsum(
        "re,de->rd", grad_branch, mat_cross_out, preferred_element_type=jnp.float32
    ).astype(jnp.bfloat16)
    grad_mixed = grad_mixed.reshape(captions, CAP_LEN, head_count, HEAD_DIM)
    grad_query, grad_key, grad_value = general_attention_back(
        cross_query, image_kv[:, :, 0], image_kv[:, :, 1], cross_total, grad_mixed, open_mask
    )
    grad_query = grad_query.reshape(-1, D).astype(jnp.bfloat16)
    grad_kv = jnp.stack([grad_key, grad_value], axis=2).reshape(-1, 2 * D).astype(jnp.bfloat16)
    grad_cross_q = jnp.einsum(
        "rd,re->de", normed_cross, grad_query, preferred_element_type=jnp.float32
    )
    grad_cross_kv = jnp.einsum("iv,ie->ve", image_rows, grad_kv, preferred_element_type=jnp.float32)
    grad_image = jnp.einsum(
        "ie,ve->iv", grad_kv, mat_cross_kv, preferred_element_type=jnp.float32
    ).astype(jnp.bfloat16)
    grad_normed = jnp.einsum(
        "re,de->rd", grad_query, mat_cross_q, preferred_element_type=jnp.float32
    )
    grad_self_in, grad_gain2, grad_shift2 = general_norm_back(
        after_self, norm_gains[1], shifts[1], grad_normed
    )
    grad_after_self = grad_after_cross + grad_self_in
    grad_branch = grad_after_self.astype(jnp.bfloat16)
    grad_out = jnp.einsum("rd,re->de", self_mixed, grad_branch, preferred_element_type=jnp.float32)
    grad_mixed = jnp.einsum(
        "re,de->rd", grad_branch, mat_out, preferred_element_type=jnp.float32
    ).astype(jnp.bfloat16)
    grad_mixed = grad_mixed.reshape(captions, CAP_LEN, head_count, HEAD_DIM)
    grad_query, grad_key, grad_value = general_attention_back(
        projected[:, :, 0], projected[:, :, 1], projected[:, :, 2], self_total, grad_mixed, allowed
    )
    grad_projected = (
        jnp.stack([grad_query, grad_key, grad_value], axis=2)
        .reshape(-1, 3 * D)
        .astype(jnp.bfloat16)
    )
    grad_w_qkv = jnp.einsum(
        "rd,re->de", normed_self, grad_projected, preferred_element_type=jnp.float32
    )
    grad_normed = jnp.einsum(
        "re,de->rd", grad_projected, mat_qkv, preferred_element_type=jnp.float32
    )
    grad_input, grad_gain1, grad_shift1 = general_norm_back(slotted, norm_gains[0], shifts[0], grad_normed)
    grad_input = grad_input + grad_after_self
    grad_small = jnp.concatenate(
        [
            grad_gain1,
            grad_gain2,
            grad_gain3,
            grad_shift1,
            grad_shift2,
            grad_shift3,
            grad_up_bias,
            grad_down_bias,
        ]
    )
    flat_grads = (
        grad_w_qkv.reshape(-1),
        grad_out.reshape(-1),
        grad_cross_q.reshape(-1),
        grad_cross_kv.reshape(-1),
        grad_cross_out.reshape(-1),
        grad_up.reshape(-1),
        grad_down.reshape(-1),
        grad_small,
    )
    return (grad_input, grad_image, flat_grads)


def general_sum_to_owners(flat_grads):
    summed = []
    for grad_vec in flat_grads:
        for axis in ("dp", "fsdp"):
            parts = grad_vec.reshape(lax.axis_size(axis), -1).astype(jnp.bfloat16)
            if axis == "dp":
                parts = grad_vec.reshape(lax.axis_size("dp"), lax.axis_size("fsdp"), -1)
                parts = parts.astype(jnp.bfloat16)
            got = lax.all_to_all(parts, axis, split_axis=0, concat_axis=0, tiled=True)
            grad_vec = jnp.sum(got.astype(jnp.float32), axis=0)
        summed.append(grad_vec)
    return tuple(summed)


def general_device(
    tokens,
    image_tokens,
    caption_lengths,
    arrival_order,
    w_qkv,
    w_out,
    w_cross_q,
    w_cross_kv,
    w_cross_out,
    w_up,
    w_down,
    small_params,
    cotangent,
):
    lengths = caption_lengths[0]
    slot_rows = general_slot_index(lengths, arrival_order[0])
    captions = lengths.shape[0]
    slot_total = captions * CAP_LEN
    arrived, arrived_grad = (
        lax.all_to_all(tokens, "fsdp", split_axis=0, concat_axis=0, tiled=True),
        lax.all_to_all(cotangent, "fsdp", split_axis=0, concat_axis=0, tiled=True),
    )
    slotted = jnp.zeros((slot_total, D), jnp.float32).at[slot_rows].set(arrived.astype(jnp.float32))
    grad_slot = (
        jnp.zeros((slot_total, D), jnp.float32).at[slot_rows].set(arrived_grad.astype(jnp.float32))
    )
    positions = jnp.arange(CAP_LEN, dtype=jnp.int32)
    allowed = (positions[None, :] <= positions[:, None])[None, None] & (
        positions[None, None, None, :] < lengths[:, None, None, None]
    )
    open_mask = jnp.ones((1, 1, 1, 1), jnp.bool_)
    image_rows = image_tokens.reshape(-1, V)
    owned_shards = (w_qkv, w_out, w_cross_q, w_cross_kv, w_cross_out, w_up, w_down, small_params)
    params = general_unpack_params(
        tuple(lax.all_gather(w, ("dp", "fsdp"), axis=0, tiled=True) for w in owned_shards)
    )
    result, saved_state = general_forward(slotted, image_rows, params, allowed, open_mask)
    grad_input, grad_image, flat_grads = general_backward(
        saved_state, grad_slot, image_rows, params, allowed, open_mask
    )
    summed = general_sum_to_owners(flat_grads)
    out_rows = result[slot_rows].astype(jnp.bfloat16)
    grad_rows = grad_input[slot_rows].astype(jnp.bfloat16)
    layer_out, grad_tokens = (
        lax.all_to_all(out_rows, "fsdp", split_axis=0, concat_axis=0, tiled=True),
        lax.all_to_all(grad_rows, "fsdp", split_axis=0, concat_axis=0, tiled=True),
    )
    return (layer_out, grad_tokens, grad_image.reshape(image_tokens.shape)) + tuple(summed)


def solution(mesh):
    dp, fsdp = mesh.shape["dp"], mesh.shape["fsdp"]
    inner, specs_of = on_device, ("dp", "fsdp")
    if fsdp == 4 and dp % 2 == 0 and D % (dp * fsdp * 8) == 0:
        mesh = Mesh(mesh.devices.reshape(dp // 2, 2, 2, 2), AXES)
        specs_of = AXES
    else:
        inner = general_device
    rows, flat, cube = P(specs_of, None), P(specs_of), P(specs_of, None, None)
    return jax.shard_map(
        inner,
        mesh=mesh,
        in_specs=(rows, cube, rows, rows) + (flat,) * 8 + (rows,),
        out_specs=(rows, rows, cube) + (flat,) * 8,
        check_vma=False,
    )
```

```python
import functools

import jax
import jax.numpy as jnp
from jax import lax
from jax.experimental import pallas as pl
from jax.experimental.pallas import tpu as pltpu
from jax.sharding import Mesh
from jax.sharding import PartitionSpec as P

D = 768
HEAD_DIM = 64
FF = 3072
V = 768
IMG = 256
CAP_LEN = 64
LANES = 128
PAIRS = D // LANES
HALF = D // 2
HEADS = 4
WIDE = HEADS * HEAD_DIM
BATCHES = D // WIDE
FOLD = FF // D
GROUP = FOLD * LANES
GROUPS = FF // GROUP
TOKENS_AT = 32
SCALE = HEAD_DIM ** (-0.5)
epsilon = 1e-05
masked_fill = 1e30

BF = jnp.bfloat16
F32 = jnp.float32
AXES = ("z", "x", "y", "c")


def mm(a, b):
    return lax.dot_general(a, b, (((1,), (0,)), ((), ())), preferred_element_type=F32)


def mm_t(a, b):
    return lax.dot_general(a, b, (((1,), (1,)), ((), ())), preferred_element_type=F32)


def t_mm(a, b):
    return lax.dot_general(a, b, (((0,), (0,)), ((), ())), preferred_element_type=F32)


def wide(value):
    return value.astype(F32)


def norm_rows(inputs, gain_vec, shift_vec):
    centred = inputs - jnp.mean(inputs, axis=-1, keepdims=True)
    variance = jnp.mean(centred * centred, axis=-1, keepdims=True)
    return centred * lax.rsqrt(variance + epsilon) * gain_vec + shift_vec


def norm_back(inputs, gain_vec, grad_normed):
    centred = inputs - jnp.mean(inputs, axis=-1, keepdims=True)
    variance = jnp.mean(centred * centred, axis=-1, keepdims=True)
    scale = lax.rsqrt(variance + epsilon)
    unit = centred * scale
    weighted = grad_normed * gain_vec
    grad_in = scale * (
        weighted
        - jnp.mean(weighted, axis=-1, keepdims=True)
        - unit * jnp.mean(weighted * unit, axis=-1, keepdims=True)
    )
    grad_gain = jnp.sum(grad_normed * unit, axis=0, keepdims=True)
    grad_shift = jnp.sum(grad_normed, axis=0, keepdims=True)
    return grad_in, grad_gain, grad_shift


def arrival_pick(arr_ref):
    rows = arr_ref.shape[1]
    place = lax.broadcasted_iota(jnp.int32, (rows, rows), 0)
    return jnp.where(place == arr_ref[...], 1.0, 0.0).astype(BF)


def caption_of(index, lens_ref):
    end = jnp.int32(0)
    found = jnp.zeros_like(index)
    for c in range(lens_ref.shape[1] - 1):
        end = end + lens_ref[0, c]
        found = found + jnp.where(index >= end, 1, 0)
    return found


def slot_pick(lens_ref, rows):
    captions = lens_ref.shape[1]
    shape = (captions * CAP_LEN, rows)
    slot = lax.broadcasted_iota(jnp.int32, shape, 0)
    row = lax.broadcasted_iota(jnp.int32, shape, 1)
    start = jnp.int32(0)
    hit = jnp.zeros(shape, F32)
    for c in range(captions):
        length = lens_ref[0, c]
        inside = slot - c * CAP_LEN
        ok = (inside >= 0) & (inside < length) & (row - start == inside)
        hit = hit + jnp.where(ok, 1.0, 0.0)
        start = start + length
    return hit.astype(BF)


def fold_pick(back):
    source = lax.broadcasted_iota(jnp.int32, (GROUP, GROUP), 1 if back else 0)
    target = lax.broadcasted_iota(jnp.int32, (GROUP, GROUP), 0 if back else 1)
    return jnp.where(target == (source % FOLD) * LANES + source // FOLD, 1.0, 0.0).astype(BF)


def head_mask(rows):
    shape = (HEADS * rows, WIDE)
    head = lax.broadcasted_iota(jnp.int32, shape, 1) // HEAD_DIM
    row = lax.broadcasted_iota(jnp.int32, shape, 0)
    inside = (row >= head * rows) & (row < (head + 1) * rows)
    return jnp.where(inside, 1.0, 0.0).astype(BF)


def stack_heads(block, mask):
    return jnp.concatenate([block] * HEADS, axis=0) * mask


def merge_heads(stacked):
    rows = stacked.shape[0] // HEADS
    head = lax.broadcasted_iota(jnp.int32, (rows, WIDE), 1) // HEAD_DIM
    out = stacked[:rows]
    for n in range(1, HEADS):
        out = jnp.where(head == n, stacked[n * rows : (n + 1) * rows], out)
    return out


def softmax_rows(scores):
    shifted = jnp.exp(scores - jnp.max(scores, axis=-1, keepdims=True))
    return shifted * (1.0 / jnp.sum(shifted, axis=-1, keepdims=True))


def lanes_at(start, width):
    return pl.ds(pl.multiple_of(start, LANES), width)


def pack_halves(shards, out, rows, at=0):
    depth, _, height, _ = out.shape
    pieces = HALF // LANES
    for shard, mats in shards:
        rows[: shard.shape[0], :] = wide(shard[...])
        for mat in range(mats):
            for half in range(2):
                for i in range(pieces):
                    index = mat * PAIRS + half * pieces + i
                    value = rows[pl.ds(index, height, stride=mats * PAIRS), :].astype(BF)
                    lanes = slice(at + i * LANES, at + (i + 1) * LANES)
                    for z in range(depth):
                        out[z, half, :, lanes] = value
            at += HALF
    return at


def pack_self_kernel(w_qkv, w_out, attend, rows):
    pack_halves(((w_qkv, 3), (w_out, 1)), attend, rows)


def pack_cross_kernel(w_cross_q, w_cross_kv, w_cross_out, small, attend, rows):
    at = pack_halves(((w_cross_q, 1), (w_cross_kv, 2), (w_cross_out, 1)), attend, rows)
    depth, _, height, _ = attend.shape
    flat = wide(small[...])
    tail = jnp.zeros((1, LANES - small.shape[1] % LANES), F32)
    flat = jnp.concatenate([flat, tail], axis=1)
    parts = [flat[:, n : n + LANES] for n in range(0, flat.shape[1], LANES)]
    block = jnp.concatenate(parts + [jnp.zeros((height - len(parts), LANES), F32)], axis=0)
    for z in range(depth):
        for half in range(2):
            attend[z, half, :, at:] = block.astype(BF)


def pack_group_kernel(me, w_up, w_down, tokens, cotangent, near, core, chip, rows, parts):
    chunks = FF // LANES
    height = w_up.shape[0] // chunks

    def chunk(index):
        return rows[pl.ds(index, height, stride=chunks), :].astype(BF)

    rows[...] = wide(w_up[...])
    pick = fold_pick(False)
    for t in range(GROUPS):
        group = jnp.concatenate([chunk(t * FOLD + k) for k in range(FOLD)], axis=1)
        folded = mm(group, pick).astype(BF)
        for j in range(FOLD):
            parts[j, :height, t * LANES : (t + 1) * LANES] = folded[
                :, j * LANES : (j + 1) * LANES
            ]
    rows[...] = wide(w_down[...])
    for j in range(FOLD):
        for i in range(PAIRS):
            at = D + i * LANES
            parts[j, :height, at : at + LANES] = chunk(j * PAIRS + i)
        parts[j, TOKENS_AT : TOKENS_AT + tokens.shape[1], :D] = tokens[j]
        parts[j, TOKENS_AT : TOKENS_AT + tokens.shape[1], D:] = cotangent[j]
    near[...] = parts[part_of(me, 0, 0)]
    core[...] = parts[part_of(me, 0, 1)]
    for c in range(2):
        chip[c] = parts[part_of(me, 1, c)]


def transpose_kernel(img, out):
    for n in range(0, img.shape[0], IMG):
        out[:, n : n + IMG] = img[n : n + IMG, :].T


def part_of(me, far_y, far_c):
    return lax.bitwise_xor(me[0, 2], far_y) * 2 + lax.bitwise_xor(me[0, 3], far_c)


def spread_kernel(me, arr, near, chip, core, both, hidden, slotted, grad_slot, arrived):
    height, count = hidden.shape[2], arrived.shape[0] // FOLD
    for value, far_y, far_c in (
        (near[...], 0, 0), (chip[0], 1, 0), (core[...], 0, 1), (both[...], 1, 1),
    ):
        index = part_of(me, far_y, far_c)
        for z in range(hidden.shape[0]):
            hidden[z, index] = value[:height]
        at = pl.multiple_of(index * count, 8)
        arrived[pl.ds(at, count), :] = wide(value[TOKENS_AT : TOKENS_AT + count])
    pick = arrival_pick(arr)
    slotted[...] = mm(pick, arrived[:, :D].astype(BF)).astype(BF)
    grad_slot[...] = mm(pick, arrived[:, D:].astype(BF)).astype(BF)


def fill_table(share, me, pieces, flat, table):
    depth, height = pieces.shape[1], pieces.shape[2] // 2
    lane = lax.broadcasted_iota(jnp.int32, (3, LANES), 1)
    flat[...] = jnp.zeros_like(flat)
    for owner in range(8 * depth):
        z, x, y, c = owner // 8, owner // 4 % 2, owner // 2 % 2, owner % 2
        index = lax.bitwise_xor(me[0, 1], x) * 2 + lax.bitwise_xor(me[0, 2], y)
        value = wide(pieces[index, z])[c * height : c * height + 3, :]
        row, shift = divmod(owner * share, LANES)
        if shift == 0:
            flat[row : row + 3, :] += value
        else:
            moved = pltpu.roll(value, shift, axis=1)
            flat[row : row + 3, :] += jnp.where(lane >= shift, moved, 0.0)
            flat[row + 1 : row + 4, :] += jnp.where(lane < shift, moved, 0.0)
    for n in range(table.shape[0] * PAIRS):
        row, lanes = n // PAIRS, slice(n % PAIRS * LANES, (n % PAIRS + 1) * LANES)
        table[row : row + 1, lanes] = flat[n : n + 1, :]


def depth_sum_kernel(me, got, near, core, chip, total):
    height = near.shape[0]
    value = wide(got[0])
    for z in range(1, got.shape[0]):
        value = value + wide(got[z])
    total[...] = value

    def part(far_y, far_c):
        at = pl.multiple_of(part_of(me, far_y, far_c) * height, 8)
        return total[pl.ds(at, height), :].astype(BF)

    near[...] = part(0, 0)
    core[...] = part(0, 1)
    for c in range(2):
        chip[c] = part(1, c)


def unpack_hidden_kernel(me, near, chip, core, both, up, down, got):
    for value, far_y, far_c in (
        (near[...], 0, 0), (chip[0], 1, 0), (core[...], 0, 1), (both[...], 1, 1),
    ):
        got[part_of(me, far_y, far_c)] = value
    height = got.shape[1]
    chunks = FF // LANES
    pick = fold_pick(True)
    for t in range(GROUPS):
        group = jnp.concatenate(
            [got[j, :, t * LANES : (t + 1) * LANES] for j in range(FOLD)], axis=1
        )
        natural = mm(group, pick)
        for k in range(FOLD):
            up[pl.ds(t * FOLD + k, height, stride=chunks), :] = natural[
                :, k * LANES : (k + 1) * LANES
            ]
    for j in range(FOLD):
        for i in range(PAIRS):
            at = D + i * LANES
            down[pl.ds(j * PAIRS + i, height, stride=chunks), :] = wide(
                got[j, :, at : at + LANES]
            )


def unpack_halves(got, outs):
    depth, height = got.shape[0], got.shape[2]
    parts = HALF // LANES
    place = 0
    for out in outs:
        chunks = out.shape[0] // height
        for mat in range(chunks // PAIRS):
            for half in range(2):
                for i in range(parts):
                    at = place + i * LANES
                    total = wide(got[0, half, :, at : at + LANES])
                    for z in range(1, depth):
                        total = total + wide(got[z, half, :, at : at + LANES])
                    index = mat * PAIRS + half * parts + i
                    out[pl.ds(index, height, stride=chunks), :] = total
            place += HALF
    return place


class Fetch:
    def __init__(self, sems):
        self.sems = sems
        self.used = 0

    def start(self, source, target):
        copy = pltpu.make_async_copy(source, target, self.sems.at[self.used])
        self.used += 1
        copy.start()
        return copy

    def columns(self, pieces, me, piece_at, target, target_at):
        copies = []
        for index, piece in enumerate(pieces):
            half = lax.bitwise_xor(me[0, 3], index // 4)
            x = lax.bitwise_xor(me[0, 1], index // 2 % 2)
            y = lax.bitwise_xor(me[0, 2], index % 2)
            copies.append(
                self.start(
                    piece.at[:, :, pl.ds(piece_at, HALF)],
                    target.at[:, x, y, :, lanes_at(target_at + half * HALF, HALF)],
                )
            )
        return copies


def wait(copies):
    for copy in copies:
        copy.wait()


def matrix(ref):
    shape = ref.shape
    return ref[...].reshape(shape[0] * shape[1] * shape[2] * shape[3], shape[4])


def forward_kernel(share, lens, me, slotted, img, *refs):
    pieces_a, pieces_b = refs[:8], refs[8:16]
    (
        table,
        projected, probs_self, saved, after_self, after_cross, normed_mlp, query_slots,
        kv_out, probs_out, kv, probs_cross, w_qkv, w_out, w_cq, w_kv, w_co, mixed_slots, small, flat, sems,
    ) = refs[16:]
    fetch = Fetch(sems)
    got_small = [
        fetch.start(pieces_b[n].at[:, :, pl.ds(4 * HALF, LANES)], small.at[n]) for n in range(4)
    ]
    got_qkv = []
    for mat in range(3):
        got_qkv += fetch.columns(pieces_a, me, mat * HALF, w_qkv, mat * D)
    got_out = fetch.columns(pieces_a, me, 3 * HALF, w_out, 0)
    got_cq = fetch.columns(pieces_b, me, 0, w_cq, 0)
    got_kv = fetch.columns(pieces_b, me, HALF, w_kv, 0)
    got_kv += fetch.columns(pieces_b, me, 2 * HALF, w_kv, D)
    got_co = fetch.columns(pieces_b, me, 3 * HALF, w_co, 0)
    rows = slotted.shape[0]
    wait(got_small)
    fill_table(share, me, small, flat, table)
    saved[:, :D] = norm_rows(wide(slotted[...]), table[0:1, :], table[3:4, :]).astype(BF)
    wait(got_qkv)
    projected[...] = mm(saved[:, :D], matrix(w_qkv)).astype(BF)
    query_at = lax.broadcasted_iota(jnp.int32, (rows, rows), 0)
    key_at = lax.broadcasted_iota(jnp.int32, (rows, rows), 1)
    same = caption_of(query_at, lens) == caption_of(key_at, lens)
    block = jnp.where(same & (key_at <= query_at), 0.0, -masked_fill)
    barred = jnp.concatenate([block] * HEADS, axis=0)
    mask = head_mask(rows)
    for n in range(BATCHES):
        query, key, value = (
            projected[:, m * D + n * WIDE : m * D + (n + 1) * WIDE] for m in range(3)
        )
        scores = mm_t(stack_heads(query, mask), key) * SCALE + barred
        weights_low = softmax_rows(scores).astype(BF)
        probs_self[n] = weights_low
        saved[:, D + n * WIDE : D + (n + 1) * WIDE] = merge_heads(
            mm(weights_low, value)
        ).astype(BF)
    wait(got_out)
    state = wide(slotted[...]) + mm(saved[:, D : 2 * D], matrix(w_out))
    after_self[...] = state
    low = norm_rows(state, table[1:2, :], table[4:5, :]).astype(BF)
    saved[:, 2 * D : 3 * D] = low
    wait(got_cq)
    pick = slot_pick(lens, rows)
    query_slots[...] = mm(pick, mm(low, matrix(w_cq)).astype(BF)).astype(BF)
    wait(got_kv)
    kv_mat = matrix(w_kv)
    mask = head_mask(CAP_LEN)
    sent = []
    for c in range(lens.shape[1]):
        slots = slice(c * CAP_LEN, (c + 1) * CAP_LEN)
        images = slice(c * IMG, (c + 1) * IMG)
        kv[images, :] = mm(img[images, :], kv_mat).astype(BF)
        for n in range(BATCHES):
            cols = slice(n * WIDE, (n + 1) * WIDE)
            query = stack_heads(query_slots[slots, cols], mask)
            weights_low = softmax_rows(mm_t(query, kv[images, cols]) * SCALE).astype(BF)
            probs_cross[c * BATCHES + n] = weights_low
            value = kv[images, D + n * WIDE : D + (n + 1) * WIDE]
            mixed_slots[slots, cols] = merge_heads(mm(weights_low, value)).astype(BF)
        batch = slice(c * BATCHES, (c + 1) * BATCHES)
        sent.append(fetch.start(kv.at[images], kv_out.at[images]))
        sent.append(fetch.start(probs_cross.at[batch], probs_out.at[batch]))
    low = t_mm(pick, mixed_slots[...]).astype(BF)
    saved[:, 3 * D :] = low
    wait(got_co)
    state = after_self[...] + mm(low, matrix(w_co))
    after_cross[...] = state
    normed_mlp[...] = norm_rows(state, table[2:3, :], table[5:6, :]).astype(BF)
    wait(sent)


def put_small(small, row, value):
    for k in range(PAIRS):
        at = row * PAIRS + k
        small[at : at + 1, :] = value[:, k * LANES : (k + 1) * LANES]


def own_part(value, me):
    part = me[0, 2] * 2 + me[0, 3]
    out = value[:, :LANES]
    for j in range(1, FOLD):
        out = jnp.where(part == j, value[:, j * LANES : (j + 1) * LANES], out)
    return out


def mlp_kernel(me, table, *refs):
    inputs, grads, pieces = refs[:4], refs[4:8], refs[8:10]
    (
        grad_near, grad_keep, grad_send, grad_send_y, out_near, out_keep, out_send, out_send_y,
        active, grad_hidden, small, all_in, all_grad, w_up, w_down, grad_part, out_part, sems,
    ) = refs[10:]
    fetch = Fetch(sems)
    got_up, got_down = [], []
    for index in range(2):
        x = lax.bitwise_xor(me[0, 1], index)
        got_up.append(fetch.start(pieces[index].at[:, :, pl.ds(0, D)], w_up.at[:, x]))
        got_down.append(fetch.start(pieces[index].at[:, :, pl.ds(D, D)], w_down.at[:, x]))
    rows = inputs[0].shape[0]
    for n in range(4):
        all_in[n * rows : (n + 1) * rows, :] = inputs[n][...]
        all_grad[n * rows : (n + 1) * rows, :] = grads[n][...]
    bias = [
        table[6 + n // PAIRS : 7 + n // PAIRS, n % PAIRS * LANES : (n % PAIRS + 1) * LANES]
        for n in range(FF // LANES)
    ]
    bias = jnp.concatenate(
        [jnp.concatenate(bias[t * FOLD : (t + 1) * FOLD], axis=1) for t in range(GROUPS)], axis=0
    )
    bias = own_part(mm(bias.astype(BF), fold_pick(False)), me)
    bias = jnp.concatenate([bias[t : t + 1, :] for t in range(GROUPS)], axis=1)
    wait(got_up)
    up_mat = w_up[...].reshape(D, D)
    wait(got_down)
    down_mat = w_down[...].reshape(D, D)

    def rows_of(n, total):
        at = pl.ds(pl.multiple_of(n * 2 * rows, 64), 2 * rows)
        hidden = mm(all_in[at, :], up_mat) + bias
        half = 0.5 + 0.5 * lax.erf(hidden * (0.5**0.5))
        act = (hidden * half).astype(BF)
        active[at, :] = act
        slope = half + hidden * (jnp.exp(hidden * hidden * -0.5) * 0.3989422804014327)
        grad_hid = (mm_t(all_grad[at, :], down_mat) * slope).astype(BF)
        grad_hidden[at, :] = grad_hid
        grad_part[n] = mm_t(grad_hid, up_mat)
        out_part[n] = mm(act, down_mat)
        return total + jnp.sum(wide(grad_hid), axis=0, keepdims=True)

    sums = lax.fori_loop(0, 2, rows_of, jnp.zeros((1, D), F32)).astype(BF)
    for part, outs in (
        (grad_part, (grad_near, grad_send, grad_keep, grad_send_y)),
        (out_part, (out_near, out_send, out_keep, out_send_y)),
    ):
        for n, out in enumerate(outs):
            out[...] = part[n // 2, n % 2 * rows : (n % 2 + 1) * rows].astype(out.dtype)
    sums = jnp.concatenate(
        [sums[:, t * LANES : (t + 1) * LANES] for t in range(GROUPS)] + [sums[:, :LANES]] * 2,
        axis=0,
    )
    part = me[0, 2] * 2 + me[0, 3]
    spread = jnp.concatenate(
        [jnp.where(part == j, sums, jnp.zeros_like(sums)) for j in range(FOLD)], axis=1
    )
    natural = mm(spread, fold_pick(True))
    small[...] = jnp.zeros_like(small)
    for n in range(FF // LANES):
        at = 6 * PAIRS + n
        small[at : at + 1, :] = natural[
            n // FOLD : n // FOLD + 1, n % FOLD * LANES : (n % FOLD + 1) * LANES
        ]
    put_small(small, 10, jnp.sum(wide(grads[0][...]), axis=0, keepdims=True))


def hidden_grad_kernel(*refs):
    normed, grad_slot = refs[:4], refs[4:8]
    active, grad_hidden, out = refs[8:]
    rows = lambda parts: jnp.concatenate([r[...] for r in parts], axis=0)
    out[:, :D] = t_mm(rows(normed), grad_hidden[...]).astype(BF)
    out[:, D:] = t_mm(active[...], rows(grad_slot)).astype(BF)


def combine_kernel(keep, far, out):
    out[...] = (wide(keep[...]) + wide(far[...])).astype(BF)


def cross_back_kernel(
    lens, me, grad_near, grad_core, grad_far, after_cross, grad_slot, probs_in, query_slots, kv_in,
    after_self, table, small_in, *refs,
):
    pieces = refs[:8]
    (
        grad_state, small, half_keep, half_send, keep_out, send_out,
        w_co, w_cq, mixed_slots, query_grads, grad_kv, kv_keep, kv_send, kv, probs, sems,
    ) = refs[8:]
    fetch = Fetch(sems)
    got_co = fetch.columns(pieces, me, 3 * HALF, w_co, 0)
    got_kv = [fetch.start(kv_in, kv), fetch.start(probs_in, probs)]
    got_cq = fetch.columns(pieces, me, 0, w_cq, 0)
    rows = after_self.shape[0]
    sent = []
    halves = ((0, half_keep, kv_keep), (1, half_send, kv_send))
    small[...] = small_in[...]
    grad_in, grad_gain, grad_shift = norm_back(
        after_cross[...],
        table[2:3, :],
        grad_near[...] + wide(grad_core[...]) + wide(grad_far[...]),
    )
    put_small(small, 2, grad_gain)
    put_small(small, 5, grad_shift)
    grad_after = wide(grad_slot[...]) + grad_in
    grad_state[...] = grad_after
    pick = slot_pick(lens, rows)
    wait(got_co)
    query_grads[:rows, :] = grad_after.astype(BF)
    mixed_slots[...] = mm(pick, mm_t(query_grads[:rows, :], matrix(w_co)).astype(BF)).astype(BF)
    for rel, half_out, _ in halves:
        at = lax.bitwise_xor(me[0, 3], rel) * HALF
        half_out[:, HALF : 2 * HALF] = query_grads[:rows, lanes_at(at, HALF)]
    mask = head_mask(CAP_LEN)
    wait(got_kv)
    for c in range(lens.shape[1]):
        slots = slice(c * CAP_LEN, (c + 1) * CAP_LEN)
        images = slice(c * IMG, (c + 1) * IMG)
        for n in range(BATCHES):
            cols = slice(n * WIDE, (n + 1) * WIDE)
            value_cols = slice(D + n * WIDE, D + (n + 1) * WIDE)
            grad_mixed = stack_heads(mixed_slots[slots, cols], mask)
            query = stack_heads(query_slots[slots, cols], mask)
            weights_low = probs[c * BATCHES + n]
            attn = wide(weights_low)
            grad_weights = mm_t(grad_mixed, kv[images, value_cols])
            centre = jnp.sum(attn * grad_weights, axis=-1, keepdims=True)
            grad_scores = (attn * (grad_weights - centre)).astype(BF)
            query_grads[slots, cols] = (
                merge_heads(mm(grad_scores, kv[images, cols])) * SCALE
            ).astype(BF)
            grad_kv[images, cols] = (t_mm(grad_scores, query) * SCALE).astype(BF)
            grad_kv[images, value_cols] = t_mm(weights_low, grad_mixed).astype(BF)
        for rel, _, kv_half in halves:
            at = lax.bitwise_xor(me[0, 3], rel) * HALF
            kv_half[images, :HALF] = grad_kv[images, lanes_at(at, HALF)]
            kv_half[images, HALF:] = grad_kv[images, lanes_at(at + D, HALF)]
        sent.append(fetch.start(kv_send.at[images], send_out.at[images]))
        sent.append(fetch.start(kv_keep.at[images], keep_out.at[images]))
    mixed_slots[:rows, :] = t_mm(pick, query_grads[...]).astype(BF)
    wait(got_cq)
    grad_in, grad_gain, grad_shift = norm_back(
        after_self[...], table[1:2, :], mm_t(mixed_slots[:rows, :], matrix(w_cq))
    )
    put_small(small, 1, grad_gain)
    put_small(small, 4, grad_shift)
    grad_after = grad_state[...] + grad_in
    grad_state[...] = grad_after
    query_grads[:rows, :] = grad_after.astype(BF)
    for rel, half_out, _ in halves:
        at = lax.bitwise_xor(me[0, 3], rel) * HALF
        half_out[:, :HALF] = mixed_slots[:rows, lanes_at(at, HALF)]
        half_out[:, 2 * HALF :] = query_grads[:rows, lanes_at(at, HALF)]
    wait(sent)


def self_back_kernel(me, grad_state, probs, projected, slotted, table, small_in, *refs):
    pieces = refs[:8]
    (
        grad_rows, small, keep, send,
        w_out, w_qkv, mixed, grad_projected, sems,
    ) = refs[8:]
    fetch = Fetch(sems)
    got_out = fetch.columns(pieces, me, 3 * HALF, w_out, 0)
    got_qkv = []
    for mat in range(3):
        got_qkv += fetch.columns(pieces, me, mat * HALF, w_qkv, mat * D)
    rows = slotted.shape[0]
    wait(got_out)
    mixed[...] = mm_t(grad_state[...].astype(BF), matrix(w_out)).astype(BF)
    mask = head_mask(rows)
    for n in range(BATCHES):
        cols, key_cols, value_cols = (
            slice(m * D + n * WIDE, m * D + (n + 1) * WIDE) for m in range(3)
        )
        grad_mixed = stack_heads(mixed[:, cols], mask)
        query = stack_heads(projected[:, cols], mask)
        weights_low = probs[n]
        attn = wide(weights_low)
        grad_weights = mm_t(grad_mixed, projected[:, value_cols])
        centre = jnp.sum(attn * grad_weights, axis=-1, keepdims=True)
        grad_scores = (attn * (grad_weights - centre)).astype(BF)
        grad_projected[:, cols] = (
            merge_heads(mm(grad_scores, projected[:, key_cols])) * SCALE
        ).astype(BF)
        grad_projected[:, key_cols] = (t_mm(grad_scores, query) * SCALE).astype(BF)
        grad_projected[:, value_cols] = t_mm(weights_low, grad_mixed).astype(BF)
    for mat in range(3):
        for rel, out in ((0, keep), (1, send)):
            at = lax.bitwise_xor(me[0, 3], rel) * HALF + mat * D
            out[:, mat * HALF : (mat + 1) * HALF] = grad_projected[:, lanes_at(at, HALF)]
    wait(got_qkv)
    grad_in, grad_gain, grad_shift = norm_back(
        wide(slotted[...]), table[0:1, :], mm_t(grad_projected[...], matrix(w_qkv))
    )
    grad_slotted = (grad_state[...] + grad_in).astype(BF)
    grad_rows[...] = grad_slotted
    small[...] = small_in[...]
    put_small(small, 0, grad_gain)
    put_small(small, 3, grad_shift)


def put_quadrants(grads, me, outs, at, first):
    depth, height = outs[0].shape[1:3]
    width = grads.shape[1]
    for i, out in enumerate(outs):
        for j in range(2):
            far_x, far_y = (i, j) if first == "x" else (j, i)
            x, y = lax.bitwise_xor(me[0, 1], far_x), lax.bitwise_xor(me[0, 2], far_y)
            for z in range(depth):
                low = pl.multiple_of(((z * 2 + x) * 2 + y) * height, 16)
                out[j, z, :, at : at + width] = grads[pl.ds(low, height), :].astype(BF)


def half_grads(pieces, me, outs, grads, first, at=0):
    for left, far_left, right, far_right in pieces:
        width = right.shape[1]
        grads[:, :width] = t_mm(left, right) + t_mm(far_left, far_right)
        put_quadrants(grads.at[:, :width], me, outs, at, first)
        at += width


def cross_grad_kernel(me, *refs):
    sources, targets, landed, made, grads, sems = (
        refs[:8], refs[8:12], refs[12:20], refs[20:24], refs[24], refs[25],
    )
    fetch = Fetch(sems)
    copies = [fetch.start(source, target) for source, target in zip(sources, landed)]
    saved, saved_far, half, half_far, img_t, img_t_far, kv, kv_far = landed
    part = lambda ref, n, width: ref[:, n * width : (n + 1) * width]
    piece = lambda left, right: (
        part(saved, left, D), part(saved_far, left, D),
        part(half, right, HALF), part(half_far, right, HALF),
    )
    wait(copies[:4])
    half_grads([piece(3, 1), piece(1, 2)], me, made[2:], grads, "y")
    sent = [fetch.start(made[n], targets[n]) for n in (3, 2)]
    half_grads([piece(2, 0)], me, made[:2], grads, "x")
    wait(copies[4:])
    grads[...] = mm(img_t[...], kv[...]) + mm(img_t_far[...], kv_far[...])
    put_quadrants(grads, me, made[:2], HALF, "x")
    sent += [fetch.start(made[n], targets[n]) for n in (1, 0)]
    wait(sent)


def owner_rows(small, blocks, share):
    height = blocks.shape[0] // (small.shape[0] * LANES // share)
    lane = lax.broadcasted_iota(jnp.int32, (3, LANES), 1)
    blocks[...] = jnp.zeros_like(blocks)
    table = jnp.concatenate([small[...], jnp.zeros((6, LANES), F32)], axis=0)
    for owner in range(small.shape[0] * LANES // share):
        row, shift = divmod(owner * share, LANES)
        if shift == 0:
            value = table[row : row + 3]
        else:
            moved = pltpu.roll(table[row : row + 4], LANES - shift, axis=1)
            value = jnp.where(lane < LANES - shift, moved[:3], moved[1:4])
        blocks[owner * height : owner * height + 3, :] = value


def self_grad_kernel(share, me, saved, saved_far, half, half_far, small, *refs):
    first, second, grads = refs[:2], refs[2:4], refs[4]
    own, far = saved[:, :D], saved_far[:, :D]
    half_grads([(own, far, half[:, :D], half_far[:, :D])], me, first, grads, "y")
    half_grads([(own, far, half[:, D:], half_far[:, D:])], me, second, grads, "x")
    blocks = grads.at[:, :LANES]
    owner_rows(small, blocks, share)
    put_quadrants(blocks, me, second, HALF, "x")


def unpack_kernel(got, *outs):
    at = unpack_halves(got, outs[:-1])
    total = jnp.zeros((8, LANES), F32)
    for z in range(got.shape[0]):
        for c in range(2):
            total = total + wide(got[z, c, :8, at:])
    outs[-1][...] = total


def return_kernel(
    me, arr, after_cross, table, out_near, out_core, out_far, grad_rows, near, core, chip, rows
):
    pick = arrival_pick(arr)
    count = near.shape[0]
    result = after_cross[...] + out_near[...] + wide(out_core[...]) + wide(out_far[...])
    result = result + table[10:11, :]
    rows[:, :D] = t_mm(pick, result.astype(BF))
    rows[:, D:] = t_mm(pick, grad_rows[...])

    def part(far_y, far_c):
        at = pl.multiple_of(part_of(me, far_y, far_c) * count, 8)
        return rows[pl.ds(at, count), :].astype(BF)

    near[...] = part(0, 0)
    core[...] = part(0, 1)
    for c in range(2):
        chip[c] = part(1, c)


def collect_kernel(me, near, chip, core, both, layer_out, grad_tokens):
    for value, far_y, far_c in ((near[...], 0, 0), (chip[0], 1, 0), (core[...], 0, 1), (both[...], 1, 1)):
        index = part_of(me, far_y, far_c)
        layer_out[index] = value[:, :D]
        grad_tokens[index] = value[:, D:]


def image_grad_kernel(kv_keep, kv_send, *refs):
    me, pieces = refs[0], refs[1:9]
    grad_image, w_kv, sems = refs[9:]
    fetch = Fetch(sems)
    copies = []
    for index, piece in enumerate(pieces):
        x = lax.bitwise_xor(me[0, 1], index // 2 % 2)
        y = lax.bitwise_xor(me[0, 2], index % 2)
        copies.append(
            fetch.start(piece.at[:, :, pl.ds(HALF, D)], w_kv.at[index // 4, :, x, y])
        )
    wait(copies)
    near, far = w_kv[0].reshape(D, D), w_kv[1].reshape(D, D)
    for c in range(kv_keep.shape[0] // IMG):
        rows = pl.ds(c * IMG, IMG)
        grad_image[rows, :] = (mm_t(kv_keep[rows, :], near) + mm_t(kv_send[rows, :], far)).astype(
            BF
        )


def add_kernel(counts, joined, *refs):
    outs = refs[sum(counts) :]
    first = at = 0
    for n, count in enumerate(counts):
        for z in range(refs[first].shape[0]):
            total = wide(refs[first][z])
            for ref in refs[first + 1 : first + count]:
                total = total + wide(ref[z])
            if joined:
                outs[0][z, :, at : at + total.shape[-1]] = total.astype(BF)
            else:
                outs[n][z] = total.astype(BF)
        at += total.shape[-1]
        first += count


def last_add_kernel(so_far, *refs):
    out, at = refs[-1], 0
    for ref in refs[:-1]:
        lanes = slice(at, at + ref.shape[-1])
        for z in range(out.shape[0]):
            out[z, :, lanes] = (wide(so_far[z, :, lanes]) + wide(ref[z])).astype(BF)
        at += ref.shape[-1]


VM = pl.BlockSpec(memory_space=pltpu.VMEM)
SM = pl.BlockSpec(memory_space=pltpu.SMEM)
HB = pl.BlockSpec(memory_space=pl.ANY)


COST_US = {
    "forward_kernel": 12, "mlp_kernel": 9, "hidden_grad_kernel": 6, "cross_back_kernel": 12,
    "self_back_kernel": 8, "cross_grad_kernel": 10, "self_grad_kernel": 4, "return_kernel": 3,
    "image_grad_kernel": 7, "spread_kernel": 3,
}


def costs(kernel):
    name = (kernel.func if isinstance(kernel, functools.partial) else kernel).__name__
    flops = int(COST_US.get(name, 2) * 0.4 * 1e9)
    return pl.CostEstimate(flops=flops, bytes_accessed=2**20, transcendentals=0)


def run(kernel, outs, specs, scratch, *args, mib=58, copied=0, cost=None):
    return pl.pallas_call(
        kernel,
        out_shape=[jax.ShapeDtypeStruct(s, t) for s, t in outs],
        in_specs=specs,
        out_specs=[VM] * (len(outs) - copied) + [HB] * copied,
        scratch_shapes=scratch,
        compiler_params=pltpu.CompilerParams(vmem_limit_bytes=mib * 2**20),
        cost_estimate=cost or costs(kernel),
        name=(kernel.func if isinstance(kernel, functools.partial) else kernel).__name__,
    )(*args)


def add_up(*sums, joined=False):
    args, specs, shapes = [], [], []
    for terms in sums:
        for term in terms:
            array, index = term if isinstance(term, tuple) else (term, None)
            block = array.shape[-3:]
            if index is None:
                specs.append(pl.BlockSpec(block, lambda i: (0, 0, 0)))
            else:
                specs.append(pl.BlockSpec((None,) + block, lambda i, n=index: (n, 0, 0, 0)))
            args.append(array)
        shapes.append(block)
    if joined:
        shapes = [shapes[0][:2] + (sum(s[2] for s in shapes),)]
    return pl.pallas_call(
        functools.partial(add_kernel, [len(terms) for terms in sums], joined),
        grid=(1,),
        out_shape=[jax.ShapeDtypeStruct(s, BF) for s in shapes],
        in_specs=specs,
        out_specs=[pl.BlockSpec(s, lambda i: (0, 0, 0)) for s in shapes],
        compiler_params=pltpu.CompilerParams(vmem_limit_bytes=58 * 2**20),
        name="add_kernel",
    )(*args)


def flip(value, axis):
    return lax.ppermute(value, axis, [(0, 1), (1, 0)])


def swap_all(value, axes):
    return lax.all_to_all(value, axes, split_axis=0, concat_axis=0, tiled=True)


def tie(*values):
    return lax.optimization_barrier(values)


def on_device(
    tokens,
    image_tokens,
    caption_lengths,
    arrival_order,
    w_qkv,
    w_out,
    w_cross_q,
    w_cross_kv,
    w_cross_out,
    w_up,
    w_down,
    small_params,
    cotangent,
):
    depth = lax.axis_size("z")
    height = D // (8 * depth)
    rows = tokens.shape[0]
    captions = caption_lengths.shape[1]
    slots = captions * CAP_LEN
    images = captions * IMG
    lens, arr = caption_lengths, arrival_order
    me = jnp.stack([lax.axis_index(a) for a in AXES]).astype(jnp.int32).reshape(1, 4)
    vmem = pltpu.VMEM
    sems = lambda n: pltpu.SemaphoreType.DMA((n,))
    shards = (w_qkv, w_out, w_cross_q, w_cross_kv, w_cross_out, w_up, w_down)

    share = small_params.shape[0]
    flat_shards = [w.reshape(-1, LANES) for w in shards]
    packed = lambda n: [((depth, 2, height, n), BF)]
    chunked = [vmem((w_up.shape[0] // LANES, LANES), F32)]
    (a,) = run(pack_self_kernel, packed(4 * HALF), [VM] * 2, chunked, *flat_shards[:2])
    (b,) = run(
        pack_cross_kernel, packed(4 * HALF + LANES), [VM] * 4, chunked,
        *flat_shards[2:5], small_params.reshape(1, share),
    )
    part = ((TOKENS_AT + 48, 2 * D), BF)
    near, core, chip = run(
        pack_group_kernel,
        [part, part, ((2,) + part[0], BF)],
        [SM] + [VM] * 4,
        chunked + [vmem((FOLD,) + part[0], BF)],
        me, *flat_shards[5:], tokens.reshape(FOLD, -1, D), cotangent.reshape(FOLD, -1, D),
    )

    def along_z(packed):
        got = swap_all(packed.reshape(2 * depth, height, -1), ("z", "c"))
        return got.reshape(depth, 2 * height, -1)

    a, chip = along_z(a), flip(chip, "y")
    img = image_tokens.reshape(images, V)
    (img_t,) = run(transpose_kernel, [((V, images), BF)], [VM], [], img)
    a, b, chip, core, img_t = tie(a, b, chip, core, img_t)
    b = along_z(b)
    ax, ay = flip(a, "x"), flip(a, "y")
    img_t_far = flip(img_t, "c")
    hidden, slotted, grad_slot = run(
        spread_kernel,
        [((depth, FOLD, height, 2 * D), BF), ((rows, D), BF), ((rows, D), BF)],
        [SM] + [VM] * 5,
        [vmem((rows, 2 * D), F32)],
        me, arr, near, chip, flip(core, "c"), flip(chip[1], "c"),
    )
    a_far = flip(a, "c")
    b, ax, ay, hidden, grad_slot, img_t_far, a_far = tie(
        b, ax, ay, hidden, grad_slot, img_t_far, a_far
    )
    def group_rows(value):
        far = flip(value, "y")
        return (value, flip(value, "c"), far, flip(far, "c"))

    bx, by = flip(b, "x"), flip(b, "y")
    hidden = swap_all(hidden.reshape(depth, FOLD * height, 2 * D), "z")
    b_far, ax_far, ay_far = flip(b, "c"), flip(ax, "c"), flip(ay, "c")
    bx, by, ax, ax_far, ay_far, b_far = tie(bx, by, ax, ax_far, ay_far, b_far)
    axy, byx = flip(ax, "y"), flip(by, "x")
    by_far, bx_far = flip(by, "c"), flip(bx, "c")
    axy, byx, by_far, bx_far = tie(axy, byx, by_far, bx_far)
    pieces_a = (a, ay, ax, axy, a_far, ay_far, ax_far, flip(axy, "c"))
    pieces_b = (b, by, bx, byx, b_far, by_far, bx_far, flip(byx, "c"))
    hidden_far = flip(hidden, "x")
    pieces_a, pieces_b = tie(pieces_a, pieces_b)
    grad_slots = group_rows(grad_slot)

    weight_shape = lambda n: vmem((depth, 2, 2, 2 * height, n * D), BF)
    (
        table, projected, probs_self, saved, after_self, after_cross, normed_mlp, query_slots, kv,
        probs_cross,
    ) = run(
        functools.partial(forward_kernel, share),
        [
            ((8 * depth * share // D, D), F32),
            ((rows, 3 * D), BF),
            ((BATCHES, HEADS * rows, rows), BF),
            ((rows, 4 * D), BF),
            ((rows, D), F32),
            ((rows, D), F32),
            ((rows, D), BF),
            ((slots, D), BF),
            ((images, 2 * D), BF),
            ((captions * BATCHES, HEADS * CAP_LEN, IMG), BF),
        ],
        [SM, SM] + [VM] * 2 + [HB] * 16,
        [
            vmem((images, 2 * D), BF),
            vmem((captions * BATCHES, HEADS * CAP_LEN, IMG), BF),
            weight_shape(3),
            weight_shape(1),
            weight_shape(1),
            weight_shape(2),
            weight_shape(1),
            vmem((slots, D), BF),
            vmem((4, depth, 2 * height, LANES), BF),
            vmem((72, LANES), F32),
            sems(68 + 2 * captions),
        ],
        lens, me, slotted, img, *pieces_a, *pieces_b,
        copied=2,
        cost=pl.CostEstimate(flops=13200000000, bytes_accessed=20 * 2**20, transcendentals=0),
    )
    inputs = group_rows(normed_mlp)
    small_shape = ((11 * PAIRS, LANES), F32)
    saved_far = flip(saved, "c")
    (
        grad_near, grad_keep, grad_send, grad_send_y, out_near, out_keep, out_send, out_send_y,
        active, grad_hidden, small,
    ) = run(
        mlp_kernel,
        [
            ((rows, D), F32),
            ((rows, D), BF),
            ((rows, D), BF),
            ((rows, D), BF),
            ((rows, D), F32),
            ((rows, D), BF),
            ((rows, D), BF),
            ((rows, D), BF),
            ((4 * rows, D), BF),
            ((4 * rows, D), BF),
            small_shape,
        ],
        [SM] + [VM] * 9 + [HB] * 2,
        [
            vmem((4 * rows, D), BF),
            vmem((4 * rows, D), BF),
            vmem((depth, 2, FOLD * height, D), BF),
            vmem((depth, 2, FOLD * height, D), BF),
            vmem((2, 2 * rows, D), F32),
            vmem((2, 2 * rows, D), F32),
            sems(4),
        ],
        me, table, *inputs, *grad_slots,
        hidden, hidden_far,
    )

    def owned(value, parts, axes):
        got = swap_all(value.reshape(parts * depth, height, -1), axes)
        return got.reshape(depth, parts, height, -1)

    flat = lambda n: ((height * n * PAIRS, LANES), F32)

    def combined(keep, far):
        return run(combine_kernel, [((rows, D), BF)], [VM] * 2, [], keep, far, mib=16)[0]

    grad_far = flip(combined(grad_keep, flip(grad_send_y, "c")), "y")
    grad_core = flip(grad_send, "c")
    (hidden_grad,) = run(
        hidden_grad_kernel,
        [((D, 2 * D), BF)],
        [VM] * 10,
        [],
        *inputs, *grad_slots, active, grad_hidden,
    )
    grad_far, grad_core, hidden_grad, saved_far, out_send, out_send_y = tie(
        grad_far, grad_core, hidden_grad, saved_far, out_send, out_send_y
    )
    hidden_got = swap_all(hidden_grad.reshape(2 * depth, FOLD * height, 2 * D), ("z", "x"))
    out_core, out_core_y = flip(out_send, "c"), flip(out_send_y, "c")
    grad_state, small, half_keep, half_send, kv_keep, kv_send = run(
        cross_back_kernel,
        [
            ((rows, D), F32),
            small_shape,
            ((rows, 3 * HALF), BF),
            ((rows, 3 * HALF), BF),
            ((images, D), BF),
            ((images, D), BF),
        ],
        [SM, SM] + [VM] * 5 + [HB, VM, HB] + [VM] * 3 + [HB] * 8,
        [
            weight_shape(1),
            weight_shape(1),
            vmem((slots, D), BF),
            vmem((slots, D), BF),
            vmem((images, 2 * D), BF),
            vmem((images, D), BF),
            vmem((images, D), BF),
            vmem((images, 2 * D), BF),
            vmem((captions * BATCHES, HEADS * CAP_LEN, IMG), BF),
            sems(18 + 2 * captions),
        ],
        lens, me, grad_near, grad_core, grad_far, after_cross, grad_slot, probs_cross, query_slots,
        kv, after_self, table, small, *pieces_b,
        copied=2,
    )
    grad_state, half_send, kv_send, out_core_y = tie(grad_state, half_send, kv_send, out_core_y)
    half_far, kv_far = flip(half_send, "c"), flip(kv_send, "c")
    out_far = flip(combined(out_keep, out_core_y), "y")
    grad_rows, small, self_keep, self_send = run(
        self_back_kernel,
        [
            ((rows, D), BF),
            small_shape,
            ((rows, 3 * HALF), BF),
            ((rows, 3 * HALF), BF),
        ],
        [SM] + [VM] * 6 + [HB] * 8,
        [
            weight_shape(1),
            weight_shape(3),
            vmem((rows, D), BF),
            vmem((rows, 3 * D), BF),
            sems(32),
        ],
        me, grad_state, probs_self, projected, slotted, table, small, *pieces_a,
    )
    self_send, grad_rows, half_far, kv_far, out_far = tie(
        self_send, grad_rows, half_far, kv_far, out_far
    )
    self_far = flip(self_send, "c")
    block = lambda n: ((2, depth, 2 * height, n), BF)
    kv_0, kv_1, mix_0, mix_1 = run(
        cross_grad_kernel,
        [block(3 * HALF)] * 2 + [block(2 * HALF)] * 2,
        [SM] + [HB] * 8,
        [vmem((rows, 4 * D), BF)] * 2
        + [vmem((rows, 3 * HALF), BF)] * 2
        + [vmem((V, images), BF)] * 2
        + [vmem((images, D), BF)] * 2
        + [vmem(block(n * HALF)[0], BF) for n in (3, 3, 2, 2)]
        + [vmem((D, D), F32), sems(12)],
        me, saved, saved_far, half_keep, half_far, img_t, img_t_far, kv_keep, kv_far,
        copied=4,
    )
    kv_0, kv_1, mix_0, mix_1, self_far, grad_rows = tie(
        kv_0, kv_1, mix_0, mix_1, self_far, grad_rows
    )
    kv_1, mix_1 = flip(kv_1, "x"), flip(mix_1, "y")
    q_0, q_1, v_0, v_1 = run(
        functools.partial(self_grad_kernel, share),
        [block(D)] * 2 + [block(HALF + LANES)] * 2,
        [SM] + [VM] * 5,
        [vmem((D, D), F32)],
        me, saved, saved_far, self_keep, self_far, small,
    )
    q_0, q_1, v_0, v_1, grad_rows = tie(q_0, q_1, v_0, v_1, grad_rows)
    q_1, v_1 = flip(q_1, "y"), flip(v_1, "x")
    part = ((rows // FOLD, 2 * D), BF)
    near, core, chip = run(
        return_kernel,
        [part, part, ((2,) + part[0], BF)],
        [SM] + [VM] * 7,
        [vmem((rows, 2 * D), F32)],
        me, arr, after_cross, table, out_near, out_core, out_far, grad_rows,
    )
    kv_1, mix_1, q_1, v_1, chip = tie(kv_1, mix_1, q_1, v_1, chip)
    kv_2, mix_2, q_2, v_2 = add_up(
        *([(near, 1), (got, 1)] for near, got in ((kv_0, kv_1), (mix_0, mix_1), (q_0, q_1), (v_0, v_1)))
    )
    kv_2, mix_2, q_2, v_2 = flip(kv_2, "y"), flip(mix_2, "x"), flip(q_2, "x"), flip(v_2, "y")
    (so_far,) = add_up(
        *([(near, 0), (got, 0)] for near, got in ((kv_0, kv_1), (mix_0, mix_1), (q_0, q_1), (v_0, v_1))),
        joined=True,
    )
    kv_2, mix_2, q_2, v_2, hidden_got, kv_send, chip, so_far = tie(
        kv_2, mix_2, q_2, v_2, hidden_got, kv_send, chip, so_far
    )
    (got,) = run(
        last_add_kernel, [(so_far.shape, BF)], [VM] * 5, [], so_far, kv_2, mix_2, q_2, v_2
    )
    got = owned(got, 2, ("z", "c"))
    chip = flip(chip, "y")
    hidden_part = ((height, 2 * D), BF)
    hidden_near, hidden_core, hidden_chip = run(
        depth_sum_kernel,
        [hidden_part, hidden_part, ((2,) + hidden_part[0], BF)],
        [SM, VM],
        [vmem((FOLD * height, 2 * D), F32)],
        me, hidden_got,
    )
    hidden_chip = flip(hidden_chip, "y")
    (grad_image,) = run(
        image_grad_kernel,
        [((images, D), BF)],
        [VM, VM, SM] + [HB] * 8,
        [vmem((2, depth, 2, 2, 2 * height, D), BF), sems(8)],
        kv_keep, kv_send, me, *pieces_b,
    )
    grad_up, grad_down = run(
        unpack_hidden_kernel, [flat(FOLD)] * 2, [SM] + [VM] * 4,
        [vmem((FOLD, height, 2 * D), BF)],
        me, hidden_near, hidden_chip, flip(hidden_core, "c"), flip(hidden_chip[1], "c"),
    )
    layer_out, grad_tokens = run(
        collect_kernel, [((FOLD, rows // FOLD, D), BF)] * 2, [SM] + [VM] * 4, [],
        me, near, chip, flip(core, "c"), flip(chip[1], "c"),
    )
    grad_cq, grad_ckv, grad_co, grad_out, grad_qkv, grad_small = run(
        unpack_kernel,
        [flat(n) for n in (1, 2, 1, 1, 3)] + [((8, LANES), F32)],
        [VM],
        [],
        got,
        mib=16,
    )
    return (
        layer_out.reshape(tokens.shape),
        grad_tokens.reshape(tokens.shape),
        grad_image.reshape(image_tokens.shape),
        *(
            g.reshape(-1)
            for g in (grad_qkv, grad_out, grad_cq, grad_ckv, grad_co, grad_up, grad_down)
        ),
        grad_small.reshape(-1)[: small_params.shape[0]],
    )


def general_norm_rows(inputs, gain_vec, shift_vec):
    centred = inputs - jnp.mean(inputs, axis=-1, keepdims=True)
    variance = jnp.mean(centred * centred, axis=-1, keepdims=True)
    return centred * lax.rsqrt(variance + epsilon) * gain_vec + shift_vec


def general_norm_back(inputs, gain_vec, shift_vec, grad_normed):
    _, pullback = jax.vjp(general_norm_rows, inputs, gain_vec, shift_vec)
    return pullback(grad_normed)


def general_gelu_exact(inputs):
    return jax.nn.gelu(inputs, approximate=False)


def general_gelu_back(inputs, grad_active):
    _, pullback = jax.vjp(general_gelu_exact, inputs)
    return pullback(grad_active)[0]


def general_slot_index(lengths, arrivals):
    run_ends = jnp.cumsum(lengths)
    starts = run_ends - lengths
    caption = jnp.sum((run_ends[None, :] <= arrivals[:, None]).astype(jnp.int32), axis=1)
    picked = caption[:, None] == jnp.arange(lengths.shape[0], dtype=jnp.int32)[None, :]
    first_row = jnp.sum(jnp.where(picked, starts[None, :], 0), axis=1)
    return caption * CAP_LEN + arrivals - first_row


def general_score_block(queries, keys_in, allowed):
    scores = jnp.einsum(
        "cqhd,ckhd->chqk", queries, keys_in, preferred_element_type=jnp.float32
    ) * HEAD_DIM ** (-0.5)
    return jnp.where(allowed, scores, -masked_fill)


def general_attention(queries, keys_in, values, allowed):
    scores = general_score_block(queries, keys_in, allowed)
    row_max = jnp.max(scores, axis=-1, keepdims=True)
    log_total = row_max + jnp.log(jnp.sum(jnp.exp(scores - row_max), axis=-1, keepdims=True))
    attn_weights = jnp.exp(scores - log_total).astype(jnp.bfloat16)
    mixed_out = jnp.einsum(
        "chqk,ckhd->cqhd", attn_weights, values, preferred_element_type=jnp.float32
    ).astype(jnp.bfloat16)
    return (mixed_out, log_total)


def general_attention_back(queries, keys_in, values, log_total, grad_mixed, allowed):
    scores = general_score_block(queries, keys_in, allowed)
    attn_weights = jnp.exp(scores - log_total)
    grad_weights = jnp.einsum(
        "cqhd,ckhd->chqk", grad_mixed, values, preferred_element_type=jnp.float32
    )
    centre = jnp.sum(attn_weights * grad_weights, axis=-1, keepdims=True)
    grad_scores = (attn_weights * (grad_weights - centre)).astype(jnp.bfloat16)
    grad_queries = jnp.einsum(
        "chqk,ckhd->cqhd", grad_scores, keys_in, preferred_element_type=jnp.float32
    ) * HEAD_DIM ** (-0.5)
    grad_keys = jnp.einsum(
        "chqk,cqhd->ckhd", grad_scores, queries, preferred_element_type=jnp.float32
    ) * HEAD_DIM ** (-0.5)
    grad_values = jnp.einsum(
        "chqk,cqhd->ckhd",
        attn_weights.astype(jnp.bfloat16),
        grad_mixed,
        preferred_element_type=jnp.float32,
    )
    return (grad_queries, grad_keys, grad_values)


def general_unpack_params(gathered):
    (
        flat_qkv,
        flat_out,
        flat_cross_q,
        flat_cross_kv,
        flat_cross_out,
        flat_up,
        flat_down,
        flat_small,
    ) = gathered
    small_vals = flat_small.astype(jnp.float32)
    return (
        flat_qkv.reshape(D, 3 * D),
        flat_out.reshape(D, D),
        flat_cross_q.reshape(D, D),
        flat_cross_kv.reshape(V, 2 * D),
        flat_cross_out.reshape(D, D),
        flat_up.reshape(D, FF),
        flat_down.reshape(FF, D),
        small_vals[: 3 * D].reshape(3, D),
        small_vals[3 * D : 6 * D].reshape(3, D),
        small_vals[6 * D : 6 * D + FF],
        small_vals[6 * D + FF :],
    )


def general_forward(slotted, image_rows, params, allowed, open_mask):
    (
        mat_qkv,
        mat_out,
        mat_cross_q,
        mat_cross_kv,
        mat_cross_out,
        mat_up,
        mat_down,
        norm_gains,
        shifts,
        up_bias,
        down_bias,
    ) = params
    captions = slotted.shape[0] // CAP_LEN
    head_count = D // HEAD_DIM
    normed_self = general_norm_rows(slotted, norm_gains[0], shifts[0]).astype(jnp.bfloat16)
    projected = jnp.dot(normed_self, mat_qkv, preferred_element_type=jnp.float32).astype(
        jnp.bfloat16
    )
    projected = projected.reshape(captions, CAP_LEN, 3, head_count, HEAD_DIM)
    self_mixed, self_total = general_attention(
        projected[:, :, 0], projected[:, :, 1], projected[:, :, 2], allowed
    )
    self_mixed = self_mixed.reshape(-1, D)
    after_self = slotted + jnp.dot(self_mixed, mat_out, preferred_element_type=jnp.float32)
    normed_cross = general_norm_rows(after_self, norm_gains[1], shifts[1]).astype(jnp.bfloat16)
    cross_query = jnp.dot(normed_cross, mat_cross_q, preferred_element_type=jnp.float32).astype(
        jnp.bfloat16
    )
    cross_query = cross_query.reshape(captions, CAP_LEN, head_count, HEAD_DIM)
    image_kv = jnp.dot(image_rows, mat_cross_kv, preferred_element_type=jnp.float32).astype(
        jnp.bfloat16
    )
    image_kv = image_kv.reshape(captions, IMG, 2, head_count, HEAD_DIM)
    cross_mixed, cross_total = general_attention(
        cross_query, image_kv[:, :, 0], image_kv[:, :, 1], open_mask
    )
    cross_mixed = cross_mixed.reshape(-1, D)
    after_cross = after_self + jnp.dot(
        cross_mixed, mat_cross_out, preferred_element_type=jnp.float32
    )
    normed_mlp = general_norm_rows(after_cross, norm_gains[2], shifts[2]).astype(jnp.bfloat16)
    hidden = jnp.dot(normed_mlp, mat_up, preferred_element_type=jnp.float32) + up_bias
    activated = general_gelu_exact(hidden).astype(jnp.bfloat16)
    result = (
        after_cross + jnp.dot(activated, mat_down, preferred_element_type=jnp.float32) + down_bias
    )
    saved_state = (
        slotted,
        normed_self,
        projected,
        self_total,
        self_mixed,
        after_self,
        normed_cross,
        cross_query,
        image_kv,
        cross_total,
        cross_mixed,
        after_cross,
        normed_mlp,
        hidden,
        activated,
    )
    return (result, saved_state)


def general_backward(saved_state, grad_slot, image_rows, params, allowed, open_mask):
    (
        mat_qkv,
        mat_out,
        mat_cross_q,
        mat_cross_kv,
        mat_cross_out,
        mat_up,
        mat_down,
        norm_gains,
        shifts,
        up_bias,
        down_bias,
    ) = params
    (
        slotted,
        normed_self,
        projected,
        self_total,
        self_mixed,
        after_self,
        normed_cross,
        cross_query,
        image_kv,
        cross_total,
        cross_mixed,
        after_cross,
        normed_mlp,
        hidden,
        activated,
    ) = saved_state
    captions = slotted.shape[0] // CAP_LEN
    head_count = D // HEAD_DIM
    grad_branch = grad_slot.astype(jnp.bfloat16)
    grad_down = jnp.einsum("rf,rd->fd", activated, grad_branch, preferred_element_type=jnp.float32)
    grad_down_bias = jnp.sum(grad_slot, axis=0)
    grad_active = jnp.einsum("rd,fd->rf", grad_branch, mat_down, preferred_element_type=jnp.float32)
    grad_hidden = general_gelu_back(hidden, grad_active).astype(jnp.bfloat16)
    grad_up = jnp.einsum("rd,rf->df", normed_mlp, grad_hidden, preferred_element_type=jnp.float32)
    grad_up_bias = jnp.sum(grad_hidden.astype(jnp.float32), axis=0)
    grad_normed = jnp.einsum("rf,df->rd", grad_hidden, mat_up, preferred_element_type=jnp.float32)
    grad_cross_in, grad_gain3, grad_shift3 = general_norm_back(
        after_cross, norm_gains[2], shifts[2], grad_normed
    )
    grad_after_cross = grad_slot + grad_cross_in
    grad_branch = grad_after_cross.astype(jnp.bfloat16)
    grad_cross_out = jnp.einsum(
        "rd,re->de", cross_mixed, grad_branch, preferred_element_type=jnp.float32
    )
    grad_mixed = jnp.einsum(
        "re,de->rd", grad_branch, mat_cross_out, preferred_element_type=jnp.float32
    ).astype(jnp.bfloat16)
    grad_mixed = grad_mixed.reshape(captions, CAP_LEN, head_count, HEAD_DIM)
    grad_query, grad_key, grad_value = general_attention_back(
        cross_query, image_kv[:, :, 0], image_kv[:, :, 1], cross_total, grad_mixed, open_mask
    )
    grad_query = grad_query.reshape(-1, D).astype(jnp.bfloat16)
    grad_kv = jnp.stack([grad_key, grad_value], axis=2).reshape(-1, 2 * D).astype(jnp.bfloat16)
    grad_cross_q = jnp.einsum(
        "rd,re->de", normed_cross, grad_query, preferred_element_type=jnp.float32
    )
    grad_cross_kv = jnp.einsum("iv,ie->ve", image_rows, grad_kv, preferred_element_type=jnp.float32)
    grad_image = jnp.einsum(
        "ie,ve->iv", grad_kv, mat_cross_kv, preferred_element_type=jnp.float32
    ).astype(jnp.bfloat16)
    grad_normed = jnp.einsum(
        "re,de->rd", grad_query, mat_cross_q, preferred_element_type=jnp.float32
    )
    grad_self_in, grad_gain2, grad_shift2 = general_norm_back(
        after_self, norm_gains[1], shifts[1], grad_normed
    )
    grad_after_self = grad_after_cross + grad_self_in
    grad_branch = grad_after_self.astype(jnp.bfloat16)
    grad_out = jnp.einsum("rd,re->de", self_mixed, grad_branch, preferred_element_type=jnp.float32)
    grad_mixed = jnp.einsum(
        "re,de->rd", grad_branch, mat_out, preferred_element_type=jnp.float32
    ).astype(jnp.bfloat16)
    grad_mixed = grad_mixed.reshape(captions, CAP_LEN, head_count, HEAD_DIM)
    grad_query, grad_key, grad_value = general_attention_back(
        projected[:, :, 0], projected[:, :, 1], projected[:, :, 2], self_total, grad_mixed, allowed
    )
    grad_projected = (
        jnp.stack([grad_query, grad_key, grad_value], axis=2)
        .reshape(-1, 3 * D)
        .astype(jnp.bfloat16)
    )
    grad_w_qkv = jnp.einsum(
        "rd,re->de", normed_self, grad_projected, preferred_element_type=jnp.float32
    )
    grad_normed = jnp.einsum(
        "re,de->rd", grad_projected, mat_qkv, preferred_element_type=jnp.float32
    )
    grad_input, grad_gain1, grad_shift1 = general_norm_back(slotted, norm_gains[0], shifts[0], grad_normed)
    grad_input = grad_input + grad_after_self
    grad_small = jnp.concatenate(
        [
            grad_gain1,
            grad_gain2,
            grad_gain3,
            grad_shift1,
            grad_shift2,
            grad_shift3,
            grad_up_bias,
            grad_down_bias,
        ]
    )
    flat_grads = (
        grad_w_qkv.reshape(-1),
        grad_out.reshape(-1),
        grad_cross_q.reshape(-1),
        grad_cross_kv.reshape(-1),
        grad_cross_out.reshape(-1),
        grad_up.reshape(-1),
        grad_down.reshape(-1),
        grad_small,
    )
    return (grad_input, grad_image, flat_grads)


def general_sum_to_owners(flat_grads):
    summed = []
    for grad_vec in flat_grads:
        for axis in ("dp", "fsdp"):
            parts = grad_vec.reshape(lax.axis_size(axis), -1).astype(jnp.bfloat16)
            if axis == "dp":
                parts = grad_vec.reshape(lax.axis_size("dp"), lax.axis_size("fsdp"), -1)
                parts = parts.astype(jnp.bfloat16)
            got = lax.all_to_all(parts, axis, split_axis=0, concat_axis=0, tiled=True)
            grad_vec = jnp.sum(got.astype(jnp.float32), axis=0)
        summed.append(grad_vec)
    return tuple(summed)


def general_device(
    tokens,
    image_tokens,
    caption_lengths,
    arrival_order,
    w_qkv,
    w_out,
    w_cross_q,
    w_cross_kv,
    w_cross_out,
    w_up,
    w_down,
    small_params,
    cotangent,
):
    lengths = caption_lengths[0]
    slot_rows = general_slot_index(lengths, arrival_order[0])
    captions = lengths.shape[0]
    slot_total = captions * CAP_LEN
    arrived, arrived_grad = (
        lax.all_to_all(tokens, "fsdp", split_axis=0, concat_axis=0, tiled=True),
        lax.all_to_all(cotangent, "fsdp", split_axis=0, concat_axis=0, tiled=True),
    )
    slotted = jnp.zeros((slot_total, D), jnp.float32).at[slot_rows].set(arrived.astype(jnp.float32))
    grad_slot = (
        jnp.zeros((slot_total, D), jnp.float32).at[slot_rows].set(arrived_grad.astype(jnp.float32))
    )
    positions = jnp.arange(CAP_LEN, dtype=jnp.int32)
    allowed = (positions[None, :] <= positions[:, None])[None, None] & (
        positions[None, None, None, :] < lengths[:, None, None, None]
    )
    open_mask = jnp.ones((1, 1, 1, 1), jnp.bool_)
    image_rows = image_tokens.reshape(-1, V)
    owned_shards = (w_qkv, w_out, w_cross_q, w_cross_kv, w_cross_out, w_up, w_down, small_params)
    params = general_unpack_params(
        tuple(lax.all_gather(w, ("dp", "fsdp"), axis=0, tiled=True) for w in owned_shards)
    )
    result, saved_state = general_forward(slotted, image_rows, params, allowed, open_mask)
    grad_input, grad_image, flat_grads = general_backward(
        saved_state, grad_slot, image_rows, params, allowed, open_mask
    )
    summed = general_sum_to_owners(flat_grads)
    out_rows = result[slot_rows].astype(jnp.bfloat16)
    grad_rows = grad_input[slot_rows].astype(jnp.bfloat16)
    layer_out, grad_tokens = (
        lax.all_to_all(out_rows, "fsdp", split_axis=0, concat_axis=0, tiled=True),
        lax.all_to_all(grad_rows, "fsdp", split_axis=0, concat_axis=0, tiled=True),
    )
    return (layer_out, grad_tokens, grad_image.reshape(image_tokens.shape)) + tuple(summed)


def solution(mesh):
    dp, fsdp = mesh.shape["dp"], mesh.shape["fsdp"]
    inner, specs_of = on_device, ("dp", "fsdp")
    if fsdp == 4 and dp % 2 == 0 and D % (dp * fsdp * 8) == 0:
        mesh = Mesh(mesh.devices.reshape(dp // 2, 2, 2, 2), AXES)
        specs_of = AXES
    else:
        inner = general_device
    rows, flat, cube = P(specs_of, None), P(specs_of), P(specs_of, None, None)
    return jax.shard_map(
        inner,
        mesh=mesh,
        in_specs=(rows, cube, rows, rows) + (flat,) * 8 + (rows,),
        out_specs=(rows, rows, cube) + (flat,) * 8,
        check_vma=False,
    )
```
